32 devices in a mesh: groups: 2 (over y), ctx: 16 (over z, x, core).
Axes of the slice: x: 2, y: 2, z: 4, core: 2. Of those that a mesh axis runs over, the one named last changes fastest.
Arguments:
- queries: bfloat16 [64, 73728], P(('groups', 'ctx')), parts along dimension 0, may hold values from -10 to 10
- prefix_latents: bfloat16 [8128, 576], P(('groups', 'ctx')), parts along dimension 0, may hold values from -4 to 4
- span_latents: bfloat16 [64, 576], P(('groups', 'ctx')), parts along dimension 0, may hold values from -4 to 4
- value_up: bfloat16 [128, 512, 128], P('ctx'), may hold values from -2.109375 to 2.109375
- prefix_length: int32 [2], P('groups'), parts along dimension 0, may hold values from 2032 to 4064
- span_offset: int32 [2], P('groups'), parts along dimension 0, may hold values from 0 to 16
Outputs:
- attended: bfloat16 [64, 16384], P(('groups', 'ctx')), parts along dimension 0
The draws below stay inside these ranges and needn't reach their ends.
There are 2 independent parts, one for each index of `groups`. The reference program is written for one: setup_inputs(seed, part) draws one part's arguments, and reference() takes and returns one part's arrays. A program takes and returns all parts, laid end to end along the dimension named above; an argument that names none is the same for every part. Nothing has to cross between parts.
Inputs may be any that keep to these rules, and one draw needn't show every extreme that they name: Only the first prefix_length of the 4064 cache slots hold valid latents. Block rows before span_offset belong to an earlier prompt and are no keys.
All inputs are finite; a program needn't handle non-finite values.
Results may differ from the reference program's by a relative error of at most 0.0075.
Values may be sent and summed in bfloat16 or wider, within the bound.
No kernel may reach another device: no remote copies, remote signals or barrier semaphores. Data moves between devices by JAX's collectives and lax.ppermute only.
A program may use at most 128 MiB of HBM per device.

```python
import jax
import jax.numpy as jnp
from jax import lax

H = 128
LATENT = 512
ROPE = 64
V_HEAD = 128
PREFIX = 4064
SPAN = 32


def draw_prefix_latents(key, part):
    key = jax.random.fold_in(key, 11)
    base = jnp.clip(jax.random.normal(key, (PREFIX, LATENT + ROPE), jnp.float32), -4.0, 4.0)
    return base.astype(jnp.bfloat16)


def draw_queries(key, part):
    key = jax.random.fold_in(key, 23)
    latent_width = LATENT + ROPE
    base = jnp.clip(jax.random.normal(key, (SPAN, H * latent_width), jnp.float32), -8.0, 8.0)
    return base.astype(jnp.bfloat16)


def block_scale(own_key, shape, cuts, least, largest):
    def one(axis_at, shards_of):
        draws = jax.random.uniform(jax.random.fold_in(jax.random.fold_in(own_key, 6), axis_at), (shards_of,), jnp.float32, least / len(cuts), largest / len(cuts))
        return jnp.repeat(jnp.exp(draws), shape[axis_at] // shards_of).reshape((-1,) + (1,) * (len(shape) - axis_at - 1))

    gain = one(*cuts[0])
    for cut in cuts[1:]:
        gain = gain * one(*cut)
    return gain


def noise(stream_key, extent, deviation, reach, cuts=(), held_as=jnp.bfloat16):
    result = jax.random.normal(stream_key, extent, jnp.float32) * deviation
    if len(cuts) > 0:
        result = block_scale(stream_key, extent, cuts, -0.22, 0.18) * result
    return jnp.clip(result, min=-reach, max=reach).astype(held_as)


def setup_inputs(seed: int = 0, part: int = 0) -> dict:
    streams_of = jax.random.split(jax.random.key(seed), 7)
    own_keys = jax.random.split(jax.random.fold_in(streams_of[6], part), 7)
    return {
        "queries": draw_queries(jax.random.fold_in(jax.random.fold_in(streams_of[6], part), 71), part),
        "prefix_latents": draw_prefix_latents(jax.random.fold_in(jax.random.fold_in(streams_of[6], part), 71), part),
        "span_latents": noise(own_keys[2], (SPAN, LATENT + ROPE), 1.0, 4.0, ((0, 16),)),
        "value_up": noise(streams_of[3], (H, LATENT, V_HEAD), (8 * LATENT ** -0.5), 2.109375, ((0, 16),)),
        "prefix_length": jax.random.randint(own_keys[4], (1,), PREFIX // 2, PREFIX + 1).astype(jnp.int32),
        "span_offset": jax.random.randint(own_keys[5], (1,), 0, SPAN // 2 + 1).astype(jnp.int32),
    }


score_scale = 192.0 ** -0.5


def reference(queries, prefix_latents, span_latents, value_up, prefix_length, span_offset):
    latent_width = LATENT + ROPE
    all_keys = jnp.concatenate([prefix_latents, span_latents], axis=0)
    values = all_keys[:, :LATENT]
    query_row = jnp.arange(SPAN, dtype=jnp.int32)[:, None]
    key_row = jnp.arange(PREFIX + SPAN, dtype=jnp.int32)[None, :]
    span_row = key_row - PREFIX
    visible = jnp.where(key_row < PREFIX, key_row < prefix_length[0],
                        (span_row >= span_offset[0]) & (span_row <= query_row))
    grouped = queries.reshape(SPAN, H, latent_width)

    def one_head(head):
        head_queries = lax.dynamic_index_in_dim(grouped, head, 1, keepdims=False)
        scores = jnp.dot(head_queries, all_keys.T, preferred_element_type=jnp.float32) * score_scale
        masked = jnp.where(visible, scores, -1e30)
        row_max = jnp.max(masked, axis=1, keepdims=True)
        probs = jnp.where(visible, jnp.exp(masked - row_max), 0.0)
        denominator = jnp.sum(probs, axis=1, keepdims=True)
        weights = probs.astype(jnp.bfloat16)
        summed = jnp.dot(weights, values, preferred_element_type=jnp.float32)
        context = (summed / denominator).astype(jnp.bfloat16)
        head_weights = lax.dynamic_index_in_dim(value_up, head, 0, keepdims=False)
        return jnp.dot(context, head_weights, preferred_element_type=jnp.float32).astype(jnp.bfloat16)

    per_head = lax.map(one_head, jnp.arange(H, dtype=jnp.int32))
    return jnp.transpose(per_head, (1, 0, 2)).reshape(SPAN, H * V_HEAD)
```

```python
import functools
import math

import jax
import jax.numpy as jnp
import numpy as np
from jax import lax
from jax.experimental import pallas as pl
from jax.experimental.pallas import tpu as pltpu
from jax.sharding import PartitionSpec as P

LATENT = 512
V_HEAD = 128
CORES = 2
LANES = 128

score_scale = 192.0 ** (-0.5) * math.log2(math.e)
neg_large = -1e30
f32 = jnp.float32
bf16 = jnp.bfloat16


def chip_cycle(chips):
    wide = max(1, int(round(chips ** (1 / 3))))
    tall = chips // wide
    if wide * tall != chips or wide < 2 or tall < 2:
        return list(range(chips))
    walk = []
    for z in range(tall):
        across = range(1, wide) if z % 2 == 0 else range(wide - 1, 0, -1)
        walk += [z * wide + x for x in across]
    return walk + [z * wide for z in reversed(range(tall))]


def fold_shard(q_ref, key_ref, base, length, m_ref, l_ref, acc_ref):
    rows = q_ref.shape[0]
    block = min(256, rows)
    slots = key_ref.shape[1]
    shown = base + lax.broadcasted_iota(jnp.int32, (1, slots), 1) < length
    for start in range(0, rows, block):
        part = pl.ds(start, block)
        s = jnp.dot(q_ref[part, :], key_ref[...], preferred_element_type=f32) * score_scale
        s = jnp.where(shown, s, neg_large)
        m_old = m_ref[part, :][:, :1]
        m_new = jnp.maximum(m_old, jnp.max(s, axis=1, keepdims=True))
        probs = jnp.where(shown, jnp.exp2(s - m_new), 0.0)
        shrink = jnp.exp2(m_old - m_new)
        l_new = l_ref[part, :][:, :1] * shrink + jnp.sum(probs, axis=1, keepdims=True)
        summed = lax.dot_general(
            probs.astype(bf16), key_ref[:LATENT, :], (((1,), (1,)), ((), ())),
            preferred_element_type=f32,
        )
        acc_ref[part, :] = acc_ref[part, :] * shrink + summed
        m_ref[part, :] = jnp.broadcast_to(m_new, (block, LANES))
        l_ref[part, :] = jnp.broadcast_to(l_new, (block, LANES))


def first_kernel(tokens, heads, scal_ref, here_ref, there_ref, row_token_ref, key_token_ref,
                 key_ref, q_ref, m_ref, l_ref, acc_ref, span_ref):
    chips = here_ref.shape[0]
    rows = tokens * heads
    for core, piece_ref in enumerate((here_ref, there_ref)):
        for o in range(chips):
            at = core * chips + o
            q_ref[at * rows:(at + 1) * rows, :] = piece_ref[o, :rows, :]
            if core == 0:
                span_ref[o * tokens:(o + 1) * tokens, :] = (
                    piece_ref[o, rows:rows + tokens, :].astype(f32)
                )
    span = span_ref[...].astype(bf16)
    total = q_ref.shape[0]
    block = min(256, total)
    key_token = key_token_ref[...]
    for start in range(0, total, block):
        part = pl.ds(start, block)
        s = lax.dot_general(
            q_ref[part, :], span, (((1,), (1,)), ((), ())), preferred_element_type=f32
        ) * score_scale
        shown = (key_token >= scal_ref[1]) & (key_token <= row_token_ref[part, :])
        s = jnp.where(shown, s, neg_large)
        m_new = jnp.max(s, axis=1, keepdims=True)
        probs = jnp.where(shown, jnp.exp2(s - m_new), 0.0)
        l_new = jnp.sum(probs, axis=1, keepdims=True)
        acc_ref[part, :] = jnp.dot(
            probs.astype(bf16), span[:, :LATENT], preferred_element_type=f32
        )
        m_ref[part, :] = jnp.broadcast_to(m_new, (block, LANES))
        l_ref[part, :] = jnp.broadcast_to(l_new, (block, LANES))
    fold_shard(q_ref, key_ref, scal_ref[3], scal_ref[0], m_ref, l_ref, acc_ref)


def middle_kernel(at, count, scal_ref, q_ref, m_in, l_in, acc_in, *rest):
    keys, (m_ref, l_ref, acc_ref) = rest[:count], rest[count:]
    m_ref[...] = m_in[...]
    l_ref[...] = l_in[...]
    acc_ref[...] = acc_in[...]
    for j, key_ref in enumerate(keys):
        base = scal_ref[3 + at + j]

        @pl.when(base < scal_ref[0])
        def _():
            fold_shard(q_ref, key_ref, base, scal_ref[0], m_ref, l_ref, acc_ref)


def last_kernel(at, count, tokens, heads, scal_ref, place_ref, q_ref, m_in, l_in, acc_in, *rest):
    keys = rest[:count]
    own_up, far_up, out_ref, m_ref, l_ref, acc_ref, context_ref, flat_ref = rest[count:]
    middle_kernel(at, count, scal_ref, q_ref, m_in, l_in, acc_in, *keys, m_ref, l_ref, acc_ref)
    for k in range(LATENT // LANES):
        lanes = slice(k * LANES, (k + 1) * LANES)
        context_ref[k] = acc_ref[:, lanes] / l_ref[...]
    m_ref[...] = m_ref[...] + jnp.log2(l_ref[...])
    everyone = flat_ref.shape[0]
    core = scal_ref[2]
    per_core = heads // CORES
    tail = jnp.zeros((everyone, LANES), f32)
    lane = lax.broadcasted_iota(jnp.int32, (everyone, LANES), 1)
    for side, up_ref in enumerate((own_up, far_up)):
        for j in range(per_core):
            head = (core ^ side) * per_core + j
            rows = pl.ds(head, everyone, stride=heads)
            context = jnp.concatenate(
                [context_ref[k, rows, :] for k in range(LATENT // LANES)], axis=1
            ).astype(bf16)
            lifted = jnp.dot(context, up_ref[j], preferred_element_type=f32)
            flat_ref[:, pl.ds(pl.multiple_of(head * V_HEAD, V_HEAD), V_HEAD)] = lifted
            weight = m_ref[rows, :]
            high = weight.astype(bf16).astype(f32)
            mid = (weight - high).astype(bf16).astype(f32)
            low = weight - high - mid
            tail = jnp.where(lane == head, high, tail)
            tail = jnp.where(lane == head + heads, mid, tail)
            tail = jnp.where(lane == head + 2 * heads, low, tail)
    flat_ref[:, heads * V_HEAD:] = tail
    for i in range(everyone // tokens):
        out_ref[place_ref[i]] = flat_ref[i * tokens:(i + 1) * tokens, :].astype(bf16)


def merge_kernel(heads, parts_ref, out_ref):
    width = heads * V_HEAD
    for chip in range(parts_ref.shape[0] // CORES):
        one = parts_ref[2 * chip].astype(f32)
        two = parts_ref[2 * chip + 1].astype(f32)
        gap = one[:, width:] - two[:, width:]
        delta = gap[:, :heads] + (gap[:, heads:2 * heads] + gap[:, 2 * heads:3 * heads])
        share = 1.0 / (1.0 + jnp.exp2(-delta))
        rest = 1.0 / (1.0 + jnp.exp2(delta))
        for j in range(heads):
            lanes = slice(j * V_HEAD, (j + 1) * V_HEAD)
            mixed = one[:, lanes] * share[:, j:j + 1] + two[:, lanes] * rest[:, j:j + 1]
            out_ref[:, chip * width + j * V_HEAD:chip * width + (j + 1) * V_HEAD] = (
                mixed.astype(bf16)
            )


VMEM = pl.BlockSpec(memory_space=pltpu.VMEM)
SMEM = pl.BlockSpec(memory_space=pltpu.SMEM)
PARAMS = pltpu.CompilerParams(vmem_limit_bytes=32 * 1024 * 1024)


def shape(*dims, dtype=f32):
    return jax.ShapeDtypeStruct(dims, dtype)


def on_device(ctx, queries, prefix_latents, span_latents, value_up, prefix_length, span_offset):
    slots, width = prefix_latents.shape
    tokens = queries.shape[0]
    all_heads = queries.shape[1] // width
    chips = ctx // CORES
    heads = all_heads // chips
    rows = tokens * heads
    total = rows * ctx
    everyone = tokens * ctx
    walk = chip_cycle(chips)
    spot = np.argsort(np.array(walk))
    onward = (chips - 1 + 1) // 2
    backward = chips - 1 - onward

    me = lax.axis_index("ctx")
    chip, core = me // CORES, me % CORES

    def across(step):
        return [
            (walk[r] * CORES + c, walk[(r + step) % chips] * CORES + c)
            for r in range(chips) for c in range(CORES)
        ]

    other_core = [(d, d ^ 1) for d in range(ctx)]

    own = prefix_latents.T
    right, left = [own], [own]
    for _ in range(onward):
        right.append(lax.ppermute(right[-1], "ctx", across(1)))
    for _ in range(backward):
        left.append(lax.ppermute(left[-1], "ctx", across(-1)))

    grouped = queries.reshape(tokens, all_heads, width)
    pad = -(rows + tokens) % 8
    span_rows = jnp.concatenate([span_latents, jnp.zeros((pad, width), bf16)], axis=0)
    pieces = []
    for o in range(chips):
        piece = lax.dynamic_slice(grouped, (0, (chip ^ o) * heads, 0), (tokens, heads, width))
        piece = jnp.concatenate([piece.reshape(rows, width), span_rows], axis=0)
        if o:
            swap = [(d, d ^ (o * CORES)) for d in range(ctx)]
            piece = lax.ppermute(piece, "ctx", swap)
        pieces.append(piece)
    here = jnp.stack(pieces)
    there = lax.ppermute(here, "ctx", other_core)
    far_up = lax.ppermute(value_up, "ctx", other_core)

    turns = [0]
    for s in range(1, onward + 1):
        turns.append(-s)
        if s <= backward:
            turns.append(s)
    owner_table = np.array(
        [[walk[(spot[p] + t) % chips] for t in turns] for p in range(chips)], np.int32
    )
    owners = lax.dynamic_index_in_dim(jnp.asarray(owner_table), chip, 0, keepdims=False)
    bases = (owners * CORES + core) * slots
    scal = jnp.concatenate([prefix_length, span_offset, core[None], bases]).astype(jnp.int32)
    index = jnp.arange(ctx, dtype=jnp.int32)
    place = ((chip ^ (index % chips)) * CORES + (core ^ (index // chips))).astype(jnp.int32)
    key_token = (place[:, None] * tokens + jnp.arange(tokens, dtype=jnp.int32)[None, :]).reshape(-1)
    row_token = jnp.repeat(key_token, heads, total_repeat_length=total)[:, None]

    state_shapes = [shape(total, LANES), shape(total, LANES), shape(total, LATENT)]
    q, *state = pl.pallas_call(
        functools.partial(first_kernel, tokens, heads),
        out_shape=[shape(total, width, dtype=bf16)] + state_shapes,
        in_specs=[SMEM] + [VMEM] * 5,
        out_specs=[VMEM] * 4,
        scratch_shapes=[pltpu.VMEM((everyone // CORES, width), f32)],
        compiler_params=PARAMS,
        name="first",
    )(scal, here, there, row_token, key_token[None, :everyone // CORES], own)

    at = 1
    for s in range(1, onward):
        keys = [right[s]] + ([left[s]] if s <= backward else [])
        state = pl.pallas_call(
            functools.partial(middle_kernel, at, len(keys)),
            out_shape=state_shapes,
            in_specs=[SMEM] + [VMEM] * (4 + len(keys)),
            out_specs=[VMEM] * 3,
            compiler_params=PARAMS,
            name="middle",
        )(scal, q, *state, *keys)
        at += len(keys)
    keys = [right[onward]] + ([left[onward]] if onward <= backward else [])
    flat = heads * V_HEAD + LANES
    parts = pl.pallas_call(
        functools.partial(last_kernel, at, len(keys), tokens, heads),
        out_shape=shape(ctx, tokens, flat, dtype=bf16),
        in_specs=[SMEM, SMEM] + [VMEM] * (6 + len(keys)),
        out_specs=VMEM,
        scratch_shapes=[
            pltpu.VMEM((total, LANES), f32),
            pltpu.VMEM((total, LANES), f32),
            pltpu.VMEM((total, LATENT), f32),
            pltpu.VMEM((LATENT // LANES, total, LANES), f32),
            pltpu.VMEM((everyone, flat), f32),
        ],
        compiler_params=PARAMS,
        name="last",
    )(scal, place, q, *state, *keys, value_up, far_up)
    returned = lax.all_to_all(parts, "ctx", split_axis=0, concat_axis=0, tiled=True)
    return pl.pallas_call(
        functools.partial(merge_kernel, heads),
        out_shape=shape(tokens, all_heads * V_HEAD, dtype=bf16),
        in_specs=[VMEM],
        out_specs=VMEM,
        compiler_params=PARAMS,
        name="merge",
    )(returned)


def solution(mesh):
    return jax.shard_map(
        functools.partial(on_device, mesh.shape["ctx"]),
        mesh=mesh,
        in_specs=(
            P(("groups", "ctx"), None),
            P(("groups", "ctx"), None),
            P(("groups", "ctx"), None),
            P("ctx", None, None),
            P("groups"),
            P("groups"),
        ),
        out_specs=P(("groups", "ctx"), None),
        check_vma=False,
    )
```

```python
import functools
import math

import jax
import jax.numpy as jnp
import numpy as np
from jax import lax
from jax.experimental import pallas as pl
from jax.experimental.pallas import tpu as pltpu
from jax.sharding import PartitionSpec as P

LATENT = 512
V_HEAD = 128
CORES = 2
LANES = 128

score_scale = 192.0 ** (-0.5) * math.log2(math.e)
neg_large = -1e30
f32 = jnp.float32
bf16 = jnp.bfloat16


def chip_cycle(chips):
    wide = max(1, int(round(chips ** (1 / 3))))
    tall = chips // wide
    if wide * tall != chips or wide < 2 or tall < 2:
        return list(range(chips))
    walk = []
    for z in range(tall):
        across = range(1, wide) if z % 2 == 0 else range(wide - 1, 0, -1)
        walk += [z * wide + x for x in across]
    return walk + [z * wide for z in reversed(range(tall))]


def fold_shard(q_ref, key_ref, base, length, m_ref, l_ref, acc_ref):
    rows = q_ref.shape[0]
    block = min(256, rows)
    slots = key_ref.shape[1]
    shown = base + lax.broadcasted_iota(jnp.int32, (1, slots), 1) < length
    for start in range(0, rows, block):
        part = pl.ds(start, block)
        s = jnp.dot(q_ref[part, :], key_ref[...], preferred_element_type=f32) * score_scale
        s = jnp.where(shown, s, neg_large)
        m_old = m_ref[part, :][:, :1]
        m_new = jnp.maximum(m_old, jnp.max(s, axis=1, keepdims=True))
        probs = jnp.where(shown, jnp.exp2(s - m_new), 0.0)
        shrink = jnp.exp2(m_old - m_new)
        l_new = l_ref[part, :][:, :1] * shrink + jnp.sum(probs, axis=1, keepdims=True)
        summed = lax.dot_general(
            probs.astype(bf16), key_ref[:LATENT, :], (((1,), (1,)), ((), ())),
            preferred_element_type=f32,
        )
        acc_ref[part, :] = acc_ref[part, :] * shrink + summed
        m_ref[part, :] = jnp.broadcast_to(m_new, (block, LANES))
        l_ref[part, :] = jnp.broadcast_to(l_new, (block, LANES))


def parted(index, size):
    return index >> (size.bit_length() - 1), index & (size - 1)


def token_of(index, tokens, chips):
    me = lax.axis_index("ctx")
    device, t = parted(index, tokens)
    core, offset = parted(device, chips)
    return (((me // CORES) ^ offset) * CORES + ((me % CORES) ^ core)) * tokens + t


def base_of(table_ref, at, slots):
    me = lax.axis_index("ctx")
    count = table_ref.shape[0] // (lax.axis_size("ctx") // CORES)
    return (table_ref[(me // CORES) * count + at] * CORES + me % CORES) * slots


def first_kernel(tokens, heads, length_ref, offset_ref, table_ref, here_ref, there_ref,
                 key_ref, q_ref, m_ref, l_ref, acc_ref, span_ref):
    chips = here_ref.shape[0]
    rows = tokens * heads
    for core, piece_ref in enumerate((here_ref, there_ref)):
        for o in range(chips):
            at = core * chips + o
            q_ref[at * rows:(at + 1) * rows, :] = piece_ref[o, :rows, :]
            if core == 0:
                span_ref[o * tokens:(o + 1) * tokens, :] = (
                    piece_ref[o, rows:rows + tokens, :].astype(f32)
                )
    span = span_ref[...].astype(bf16)
    total = q_ref.shape[0]
    block = min(256, total)
    key_index = lax.broadcasted_iota(jnp.int32, (1, span.shape[0]), 1)
    key_token = token_of(key_index, tokens, chips)
    for start in range(0, total, block):
        part = pl.ds(start, block)
        s = lax.dot_general(
            q_ref[part, :], span, (((1,), (1,)), ((), ())), preferred_element_type=f32
        ) * score_scale
        row_index = start + lax.broadcasted_iota(jnp.int32, (block, 1), 0)
        row_token = token_of(row_index >> (heads.bit_length() - 1), tokens, chips)
        shown = (key_token >= offset_ref[0]) & (key_token <= row_token)
        s = jnp.where(shown, s, neg_large)
        m_new = jnp.max(s, axis=1, keepdims=True)
        probs = jnp.where(shown, jnp.exp2(s - m_new), 0.0)
        l_new = jnp.sum(probs, axis=1, keepdims=True)
        acc_ref[part, :] = jnp.dot(
            probs.astype(bf16), span[:, :LATENT], preferred_element_type=f32
        )
        m_ref[part, :] = jnp.broadcast_to(m_new, (block, LANES))
        l_ref[part, :] = jnp.broadcast_to(l_new, (block, LANES))
    base = base_of(table_ref, 0, key_ref.shape[1])
    fold_shard(q_ref, key_ref, base, length_ref[0], m_ref, l_ref, acc_ref)


def middle_kernel(at, count, length_ref, table_ref, q_ref, m_in, l_in, acc_in, *rest):
    keys, (m_ref, l_ref, acc_ref) = rest[:count], rest[count:]
    m_ref[...] = m_in[...]
    l_ref[...] = l_in[...]
    acc_ref[...] = acc_in[...]
    for j, key_ref in enumerate(keys):
        base = base_of(table_ref, at + j, key_ref.shape[1])

        @pl.when(base < length_ref[0])
        def _():
            fold_shard(q_ref, key_ref, base, length_ref[0], m_ref, l_ref, acc_ref)


def last_kernel(at, count, tokens, heads, length_ref, table_ref, q_ref, m_in, l_in, acc_in, *rest):
    keys = rest[:count]
    own_up, far_up, out_ref, m_ref, l_ref, acc_ref, context_ref, flat_ref = rest[count:]
    middle_kernel(at, count, length_ref, table_ref, q_ref, m_in, l_in, acc_in, *keys, m_ref, l_ref, acc_ref)
    for k in range(LATENT // LANES):
        lanes = slice(k * LANES, (k + 1) * LANES)
        context_ref[k] = acc_ref[:, lanes] / l_ref[...]
    m_ref[...] = m_ref[...] + jnp.log2(l_ref[...])
    everyone = flat_ref.shape[0]
    me = lax.axis_index("ctx")
    core = me % CORES
    per_core = heads // CORES
    tail = jnp.zeros((everyone, LANES), f32)
    lane = lax.broadcasted_iota(jnp.int32, (everyone, LANES), 1)
    for side, up_ref in enumerate((own_up, far_up)):
        for j in range(per_core):
            head = (core ^ side) * per_core + j
            rows = pl.ds(head, everyone, stride=heads)
            context = jnp.concatenate(
                [context_ref[k, rows, :] for k in range(LATENT // LANES)], axis=1
            ).astype(bf16)
            lifted = jnp.dot(context, up_ref[j], preferred_element_type=f32)
            flat_ref[:, pl.ds(pl.multiple_of(head * V_HEAD, V_HEAD), V_HEAD)] = lifted
            weight = m_ref[rows, :]
            high = weight.astype(bf16).astype(f32)
            mid = (weight - high).astype(bf16).astype(f32)
            low = weight - high - mid
            tail = jnp.where(lane == head, high, tail)
            tail = jnp.where(lane == head + heads, mid, tail)
            tail = jnp.where(lane == head + 2 * heads, low, tail)
    flat_ref[:, heads * V_HEAD:] = tail
    devices = everyone // tokens
    for i in range(devices):
        place = (me // CORES) ^ (i % (devices // CORES))
        place = place * CORES + (core ^ (i // (devices // CORES)))
        out_ref[place] = flat_ref[i * tokens:(i + 1) * tokens, :].astype(bf16)


def merge_kernel(heads, parts_ref, out_ref):
    width = heads * V_HEAD
    for chip in range(parts_ref.shape[0] // CORES):
        one = parts_ref[2 * chip].astype(f32)
        two = parts_ref[2 * chip + 1].astype(f32)
        gap = one[:, width:] - two[:, width:]
        delta = gap[:, :heads] + (gap[:, heads:2 * heads] + gap[:, 2 * heads:3 * heads])
        share = 1.0 / (1.0 + jnp.exp2(-delta))
        rest = 1.0 / (1.0 + jnp.exp2(delta))
        for j in range(heads):
            lanes = slice(j * V_HEAD, (j + 1) * V_HEAD)
            mixed = one[:, lanes] * share[:, j:j + 1] + two[:, lanes] * rest[:, j:j + 1]
            out_ref[:, chip * width + j * V_HEAD:chip * width + (j + 1) * V_HEAD] = (
                mixed.astype(bf16)
            )


VMEM = pl.BlockSpec(memory_space=pltpu.VMEM)
SMEM = pl.BlockSpec(memory_space=pltpu.SMEM)
PARAMS = pltpu.CompilerParams(vmem_limit_bytes=32 * 1024 * 1024)


def shape(*dims, dtype=f32):
    return jax.ShapeDtypeStruct(dims, dtype)


def on_device(ctx, queries, prefix_latents, span_latents, value_up, prefix_length, span_offset):
    slots, width = prefix_latents.shape
    tokens = queries.shape[0]
    all_heads = queries.shape[1] // width
    chips = ctx // CORES
    heads = all_heads // chips
    rows = tokens * heads
    total = rows * ctx
    everyone = tokens * ctx
    walk = chip_cycle(chips)
    spot = np.argsort(np.array(walk))
    onward = (chips - 1 + 1) // 2
    backward = chips - 1 - onward

    me = lax.axis_index("ctx")
    chip = me // CORES

    def across(step):
        return [
            (walk[r] * CORES + c, walk[(r + step) % chips] * CORES + c)
            for r in range(chips) for c in range(CORES)
        ]

    other_core = [(d, d ^ 1) for d in range(ctx)]

    own = prefix_latents.T
    right, left = [own], [own]
    for _ in range(onward):
        right.append(lax.ppermute(right[-1], "ctx", across(1)))
    for _ in range(backward):
        left.append(lax.ppermute(left[-1], "ctx", across(-1)))

    grouped = queries.reshape(tokens, all_heads, width)
    pad = -(rows + tokens) % 8
    span_rows = jnp.concatenate([span_latents, jnp.zeros((pad, width), bf16)], axis=0)
    pieces = []
    for o in range(chips):
        piece = lax.dynamic_slice(grouped, (0, (chip ^ o) * heads, 0), (tokens, heads, width))
        pieces.append(jnp.concatenate([piece.reshape(rows, width), span_rows], axis=0))
    bit = 1
    while bit < chips:
        away = [o for o in range(chips) if o & bit]
        swap = [(d, d ^ (bit * CORES)) for d in range(ctx)]
        moved = lax.ppermute(jnp.stack([pieces[o] for o in away]), "ctx", swap)
        for j, o in enumerate(away):
            pieces[o] = moved[j]
        bit *= 2
    here = jnp.stack(pieces)
    there = lax.ppermute(here, "ctx", other_core)
    far_up = lax.ppermute(value_up, "ctx", other_core)

    turns = [0]
    for s in range(1, onward + 1):
        turns.append(-s)
        if s <= backward:
            turns.append(s)
    owner_table = np.array(
        [[walk[(spot[p] + t) % chips] for t in turns] for p in range(chips)], np.int32
    )
    table = jnp.asarray(owner_table.reshape(-1))

    state_shapes = [shape(total, LANES), shape(total, LANES), shape(total, LATENT)]
    q, *state = pl.pallas_call(
        functools.partial(first_kernel, tokens, heads),
        out_shape=[shape(total, width, dtype=bf16)] + state_shapes,
        in_specs=[SMEM] * 3 + [VMEM] * 3,
        out_specs=[VMEM] * 4,
        scratch_shapes=[pltpu.VMEM((everyone // CORES, width), f32)],
        compiler_params=PARAMS,
        name="first",
    )(prefix_length, span_offset, table, here, there, own)

    at = 1
    for s in range(1, onward):
        keys = [right[s]] + ([left[s]] if s <= backward else [])
        state = pl.pallas_call(
            functools.partial(middle_kernel, at, len(keys)),
            out_shape=state_shapes,
            in_specs=[SMEM] * 2 + [VMEM] * (4 + len(keys)),
            out_specs=[VMEM] * 3,
            compiler_params=PARAMS,
            name="middle",
        )(prefix_length, table, q, *state, *keys)
        at += len(keys)
    keys = [right[onward]] + ([left[onward]] if onward <= backward else [])
    flat = heads * V_HEAD + LANES
    parts = pl.pallas_call(
        functools.partial(last_kernel, at, len(keys), tokens, heads),
        out_shape=shape(ctx, tokens, flat, dtype=bf16),
        in_specs=[SMEM, SMEM] + [VMEM] * (6 + len(keys)),
        out_specs=VMEM,
        scratch_shapes=[
            pltpu.VMEM((total, LANES), f32),
            pltpu.VMEM((total, LANES), f32),
            pltpu.VMEM((total, LATENT), f32),
            pltpu.VMEM((LATENT // LANES, total, LANES), f32),
            pltpu.VMEM((everyone, flat), f32),
        ],
        compiler_params=PARAMS,
        name="last",
    )(prefix_length, table, q, *state, *keys, value_up, far_up)
    returned = lax.all_to_all(parts, "ctx", split_axis=0, concat_axis=0, tiled=True)
    return pl.pallas_call(
        functools.partial(merge_kernel, heads),
        out_shape=shape(tokens, all_heads * V_HEAD, dtype=bf16),
        in_specs=[VMEM],
        out_specs=VMEM,
        compiler_params=PARAMS,
        name="merge",
    )(returned)


def solution(mesh):
    return jax.shard_map(
        functools.partial(on_device, mesh.shape["ctx"]),
        mesh=mesh,
        in_specs=(
            P(("groups", "ctx"), None),
            P(("groups", "ctx"), None),
            P(("groups", "ctx"), None),
            P("ctx", None, None),
            P("groups"),
            P("groups"),
        ),
        out_specs=P(("groups", "ctx"), None),
        check_vma=False,
    )
```

```python
import functools
import math

import jax
import jax.numpy as jnp
import numpy as np
from jax import lax
from jax.experimental import pallas as pl
from jax.experimental.pallas import tpu as pltpu
from jax.sharding import PartitionSpec as P

LATENT = 512
V_HEAD = 128
CORES = 2
LANES = 128

score_scale = 192.0 ** (-0.5) * math.log2(math.e)
neg_large = -1e30
least_max = -1e29
f32 = jnp.float32
bf16 = jnp.bfloat16


def chip_cycle(chips):
    wide = max(1, int(round(chips ** (1 / 3))))
    tall = chips // wide
    if wide * tall != chips or wide < 2 or tall < 2:
        return list(range(chips))
    walk = []
    for z in range(tall):
        across = range(1, wide) if z % 2 == 0 else range(wide - 1, 0, -1)
        walk += [z * wide + x for x in across]
    return walk + [z * wide for z in reversed(range(tall))]


def fold_shards(q_ref, shards, length, m_ref, l_ref, acc_ref):
    rows = q_ref.shape[0]
    block = min(128, rows)
    for start in range(0, rows, block):
        part = pl.ds(start, block)
        m_old = m_ref[part, :][:, :1]
        m_new = m_old
        scores = []
        for base, key_ref in shards:
            slot = base + lax.broadcasted_iota(jnp.int32, (1, key_ref.shape[1]), 1)
            s = jnp.dot(q_ref[part, :], key_ref[...], preferred_element_type=f32) * score_scale
            s = jnp.where(slot < length, s, neg_large)
            m_new = jnp.maximum(m_new, jnp.max(s, axis=1, keepdims=True))
            scores.append(s)
        shrink = jnp.exp2(m_old - m_new)
        l_new = l_ref[part, :][:, :1] * shrink
        summed = acc_ref[part, :] * shrink
        for s, (_, key_ref) in zip(scores, shards):
            probs = jnp.exp2(s - m_new)
            l_new += jnp.sum(probs, axis=1, keepdims=True)
            summed += lax.dot_general(
                probs.astype(bf16), key_ref[:LATENT, :], (((1,), (1,)), ((), ())),
                preferred_element_type=f32,
            )
        acc_ref[part, :] = summed
        m_ref[part, :] = jnp.broadcast_to(m_new, (block, LANES))
        l_ref[part, :] = jnp.broadcast_to(l_new, (block, LANES))


def parted(index, size):
    return index >> (size.bit_length() - 1), index & (size - 1)


def token_of(index, tokens, chips):
    device, t = parted(index, tokens)
    core, chip = parted(device, chips)
    return (chip * CORES + ((lax.axis_index("ctx") % CORES) ^ core)) * tokens + t


def with_base(table_ref, at, key_refs):
    me = lax.axis_index("ctx")
    count = table_ref.shape[0] // (lax.axis_size("ctx") // CORES)
    shards = []
    for j, key_ref in enumerate(key_refs):
        chip = table_ref[(me // CORES) * count + at + j]
        shards.append(((chip * CORES + me % CORES) * key_ref.shape[1], key_ref))
    return shards


def first_kernel(tokens, heads, count, length_ref, offset_ref, table_ref, here_ref, there_ref, *rest):
    keys, (q_ref, m_ref, l_ref, acc_ref, span_ref) = rest[:count], rest[count:]
    chips = here_ref.shape[0]
    rows = tokens * heads
    for core, piece_ref in enumerate((here_ref, there_ref)):
        for chip in range(chips):
            at = core * chips + chip
            q_ref[at * rows:(at + 1) * rows, :] = piece_ref[chip, :rows, :]
            if core == 0:
                span_ref[chip * tokens:(chip + 1) * tokens, :] = (
                    piece_ref[chip, rows:rows + tokens, :].astype(f32)
                )
    span = span_ref[...].astype(bf16)
    total = q_ref.shape[0]
    block = min(256, total)
    key_index = lax.broadcasted_iota(jnp.int32, (1, span.shape[0]), 1)
    key_token = token_of(key_index, tokens, chips)
    for start in range(0, total, block):
        part = pl.ds(start, block)
        s = lax.dot_general(
            q_ref[part, :], span, (((1,), (1,)), ((), ())), preferred_element_type=f32
        ) * score_scale
        row_index = start + lax.broadcasted_iota(jnp.int32, (block, 1), 0)
        row_token = token_of(row_index >> (heads.bit_length() - 1), tokens, chips)
        shown = (key_token >= offset_ref[0]) & (key_token <= row_token)
        s = jnp.where(shown, s, neg_large)
        m_new = jnp.maximum(jnp.max(s, axis=1, keepdims=True), least_max)
        probs = jnp.exp2(s - m_new)
        l_new = jnp.sum(probs, axis=1, keepdims=True)
        acc_ref[part, :] = jnp.dot(
            probs.astype(bf16), span[:, :LATENT], preferred_element_type=f32
        )
        m_ref[part, :] = jnp.broadcast_to(m_new, (block, LANES))
        l_ref[part, :] = jnp.broadcast_to(l_new, (block, LANES))
    fold_shards(q_ref, with_base(table_ref, 0, keys), length_ref[0], m_ref, l_ref, acc_ref)


def middle_kernel(at, count, length_ref, table_ref, q_ref, m_in, l_in, acc_in, *rest):
    keys, (m_ref, l_ref, acc_ref) = rest[:count], rest[count:]
    m_ref[...] = m_in[...]
    l_ref[...] = l_in[...]
    acc_ref[...] = acc_in[...]
    fold_shards(q_ref, with_base(table_ref, at, keys), length_ref[0], m_ref, l_ref, acc_ref)


def last_kernel(at, tokens, heads, length_ref, table_ref, q_ref, m_in, l_in, acc_in,
                top_ref, bottom_ref, own_up, far_up, out_ref,
                key_ref, m_ref, l_ref, acc_ref, context_ref, flat_ref):
    cut = top_ref.shape[0]
    key_ref[:cut, :] = top_ref[...]
    key_ref[cut:, :] = bottom_ref[...]
    middle_kernel(at, 1, length_ref, table_ref, q_ref, m_in, l_in, acc_in,
                  key_ref, m_ref, l_ref, acc_ref)
    for k in range(LATENT // LANES):
        lanes = slice(k * LANES, (k + 1) * LANES)
        context_ref[k] = acc_ref[:, lanes] / l_ref[...]
    m_ref[...] = m_ref[...] + jnp.log2(l_ref[...])
    everyone = flat_ref.shape[0]
    core = lax.axis_index("ctx") % CORES
    per_core = heads // CORES
    tail = jnp.zeros((everyone, LANES), f32)
    lane = lax.broadcasted_iota(jnp.int32, (everyone, LANES), 1)
    for side, up_ref in enumerate((own_up, far_up)):
        for j in range(per_core):
            head = (core ^ side) * per_core + j
            rows = pl.ds(head, everyone, stride=heads)
            context = jnp.concatenate(
                [context_ref[k, rows, :] for k in range(LATENT // LANES)], axis=1
            ).astype(bf16)
            lifted = jnp.dot(context, up_ref[j], preferred_element_type=f32)
            flat_ref[:, pl.ds(pl.multiple_of(head * V_HEAD, V_HEAD), V_HEAD)] = lifted
            weight = m_ref[rows, :]
            high = weight.astype(bf16).astype(f32)
            mid = (weight - high).astype(bf16).astype(f32)
            low = weight - high - mid
            tail = jnp.where(lane == head, high, tail)
            tail = jnp.where(lane == head + heads, mid, tail)
            tail = jnp.where(lane == head + 2 * heads, low, tail)
    flat_ref[:, heads * V_HEAD:] = tail
    chips = everyone // tokens // CORES
    for i in range(chips * CORES):
        out_ref[(i % chips) * CORES + (core ^ (i // chips))] = (
            flat_ref[i * tokens:(i + 1) * tokens, :].astype(bf16)
        )


def merge_kernel(heads, parts_ref, out_ref):
    width = heads * V_HEAD
    for chip in range(parts_ref.shape[0] // CORES):
        one = parts_ref[2 * chip].astype(f32)
        two = parts_ref[2 * chip + 1].astype(f32)
        gap = one[:, width:] - two[:, width:]
        delta = gap[:, :heads] + (gap[:, heads:2 * heads] + gap[:, 2 * heads:3 * heads])
        share = 1.0 / (1.0 + jnp.exp2(-delta))
        rest = 1.0 / (1.0 + jnp.exp2(delta))
        for j in range(heads):
            lanes = slice(j * V_HEAD, (j + 1) * V_HEAD)
            mixed = one[:, lanes] * share[:, j:j + 1] + two[:, lanes] * rest[:, j:j + 1]
            out_ref[:, chip * width + j * V_HEAD:chip * width + (j + 1) * V_HEAD] = (
                mixed.astype(bf16)
            )


VMEM = pl.BlockSpec(memory_space=pltpu.VMEM)
SMEM = pl.BlockSpec(memory_space=pltpu.SMEM)
PARAMS = pltpu.CompilerParams(vmem_limit_bytes=32 * 1024 * 1024)


def shape(*dims, dtype=f32):
    return jax.ShapeDtypeStruct(dims, dtype)


def on_device(ctx, queries, prefix_latents, span_latents, value_up, prefix_length, span_offset):
    slots, width = prefix_latents.shape
    tokens = queries.shape[0]
    all_heads = queries.shape[1] // width
    chips = ctx // CORES
    heads = all_heads // chips
    rows = tokens * heads
    total = rows * ctx
    everyone = tokens * ctx
    walk = chip_cycle(chips)
    spot = np.argsort(np.array(walk))
    steps = chips // 2

    def across(step):
        return [
            (walk[r] * CORES + c, walk[(r + step) % chips] * CORES + c)
            for r in range(chips) for c in range(CORES)
        ]

    other_core = [(d, d ^ 1) for d in range(ctx)]
    same_core = [[p * CORES + c for p in range(chips)] for c in range(CORES)]

    grouped = queries.reshape(tokens, chips, heads, width).transpose(1, 0, 2, 3)
    pad = -(rows + tokens) % 8
    span_rows = jnp.pad(span_latents, ((0, pad), (0, 0)))
    span_rows = jnp.broadcast_to(span_rows[None], (chips, tokens + pad, width))
    pieces = jnp.concatenate([grouped.reshape(chips, rows, width), span_rows], axis=1)
    here = lax.all_to_all(
        pieces, "ctx", split_axis=0, concat_axis=0, axis_index_groups=same_core, tiled=True
    )

    turns = [0]
    for s in range(1, steps):
        turns += [-s, s]
    turns.append(steps)
    owner_table = np.array(
        [[walk[(spot[p] + t) % chips] for t in turns] for p in range(chips)], np.int32
    )
    table = jnp.asarray(owner_table.reshape(-1))
    state_shapes = [shape(total, LANES), shape(total, LANES), shape(total, LATENT)]

    def fold_first(keys):
        return pl.pallas_call(
            functools.partial(first_kernel, tokens, heads, len(keys)),
            out_shape=[shape(total, width, dtype=bf16)] + state_shapes,
            in_specs=[SMEM] * 3 + [VMEM] * (2 + len(keys)),
            out_specs=[VMEM] * 4,
            scratch_shapes=[pltpu.VMEM((everyone // CORES, width), f32)],
            compiler_params=PARAMS,
            name="first",
        )(prefix_length, span_offset, table, here, there, *keys)

    def fold_more(at, q, state, keys):
        return pl.pallas_call(
            functools.partial(middle_kernel, at, len(keys)),
            out_shape=state_shapes,
            in_specs=[SMEM] * 2 + [VMEM] * (4 + len(keys)),
            out_specs=[VMEM] * 3,
            compiler_params=PARAMS,
            name="middle",
        )(prefix_length, table, q, *state, *keys)

    own = prefix_latents.T
    right = lax.ppermute(own, "ctx", across(1))
    left = lax.ppermute(own, "ctx", across(-1))
    right, left, here = lax.optimization_barrier((right, left, here))
    there = lax.ppermute(here, "ctx", other_core)
    far_up = lax.ppermute(value_up, "ctx", other_core)
    cut = LATENT // 2
    for s in range(2, steps + 1):
        onward = right if s < steps else right[:cut]
        backward = left if s < steps else left[cut:]
        onward = lax.ppermute(onward, "ctx", across(1))
        backward = lax.ppermute(backward, "ctx", across(-1))
        if s == 2:
            q, *state = fold_first([own, right, left])
        else:
            state = fold_more(2 * s - 3, q, state, [right, left])
        right, left = onward, backward
        if s < steps:
            right, left, state = lax.optimization_barrier((right, left, state))
    flat = heads * V_HEAD + LANES
    parts = pl.pallas_call(
        functools.partial(last_kernel, chips - 1, tokens, heads),
        out_shape=shape(ctx, tokens, flat, dtype=bf16),
        in_specs=[SMEM] * 2 + [VMEM] * 8,
        out_specs=VMEM,
        scratch_shapes=[
            pltpu.VMEM((width, slots), bf16),
            pltpu.VMEM((total, LANES), f32),
            pltpu.VMEM((total, LANES), f32),
            pltpu.VMEM((total, LATENT), f32),
            pltpu.VMEM((LATENT // LANES, total, LANES), f32),
            pltpu.VMEM((everyone, flat), f32),
        ],
        compiler_params=PARAMS,
        name="last",
    )(prefix_length, table, q, *state, right, left, value_up, far_up)
    returned = lax.all_to_all(parts, "ctx", split_axis=0, concat_axis=0, tiled=True)
    return pl.pallas_call(
        functools.partial(merge_kernel, heads),
        out_shape=shape(tokens, all_heads * V_HEAD, dtype=bf16),
        in_specs=[VMEM],
        out_specs=VMEM,
        compiler_params=PARAMS,
        name="merge",
    )(returned)


def solution(mesh):
    return jax.shard_map(
        functools.partial(on_device, mesh.shape["ctx"]),
        mesh=mesh,
        in_specs=(
            P(("groups", "ctx"), None),
            P(("groups", "ctx"), None),
            P(("groups", "ctx"), None),
            P("ctx", None, None),
            P("groups"),
            P("groups"),
        ),
        out_specs=P(("groups", "ctx"), None),
        check_vma=False,
    )
```

```python
import functools
import math

import jax
import jax.numpy as jnp
import numpy as np
from jax import lax
from jax.experimental import pallas as pl
from jax.experimental.pallas import tpu as pltpu
from jax.sharding import PartitionSpec as P

LATENT = 512
V_HEAD = 128
CORES = 2
LANES = 128

score_scale = 192.0 ** (-0.5) * math.log2(math.e)
neg_large = -1e30
least_max = -1e29
f32 = jnp.float32
bf16 = jnp.bfloat16


def chip_cycle(chips):
    wide = max(1, int(round(chips ** (1 / 3))))
    tall = chips // wide
    if wide * tall != chips or wide < 2 or tall < 2:
        return list(range(chips))
    walk = []
    for z in range(tall):
        across = range(1, wide) if z % 2 == 0 else range(wide - 1, 0, -1)
        walk += [z * wide + x for x in across]
    return walk + [z * wide for z in reversed(range(tall))]


def fold_shards(q_ref, shards, length, m_ref, l_ref, acc_ref):
    rows = q_ref.shape[0]
    block = min(128, rows)
    for start in range(0, rows, block):
        part = pl.ds(start, block)
        m_old = m_ref[part, :][:, :1]
        m_new = m_old
        scores = []
        for base, (top_ref, bottom_ref) in shards:
            cut, slots = top_ref.shape
            slot = base + lax.broadcasted_iota(jnp.int32, (1, slots), 1)
            s = jnp.dot(q_ref[part, :cut], top_ref[...], preferred_element_type=f32)
            s += jnp.dot(q_ref[part, cut:], bottom_ref[...], preferred_element_type=f32)
            s = jnp.where(slot < length, s * score_scale, neg_large)
            m_new = jnp.maximum(m_new, jnp.max(s, axis=1, keepdims=True))
            scores.append(s)
        shrink = jnp.exp2(m_old - m_new)
        l_new = l_ref[part, :][:, :1] * shrink
        weights = []
        for s in scores:
            probs = jnp.exp2(s - m_new)
            l_new += jnp.sum(probs, axis=1, keepdims=True)
            weights.append(probs.astype(bf16))
        cut = shards[0][1][0].shape[0]
        for half, lanes in enumerate((slice(0, cut), slice(cut, LATENT))):
            summed = acc_ref[part, lanes] * shrink
            for w, (_, pair) in zip(weights, shards):
                summed += lax.dot_general(
                    w, pair[half][:lanes.stop - lanes.start, :], (((1,), (1,)), ((), ())),
                    preferred_element_type=f32,
                )
            acc_ref[part, lanes] = summed
        m_ref[part, :] = jnp.broadcast_to(m_new, (block, LANES))
        l_ref[part, :] = jnp.broadcast_to(l_new, (block, LANES))


def parted(index, size):
    return index >> (size.bit_length() - 1), index & (size - 1)


def token_of(index, tokens, chips):
    device, t = parted(index, tokens)
    core, chip = parted(device, chips)
    return (chip * CORES + ((lax.axis_index("ctx") % CORES) ^ core)) * tokens + t


def with_base(table_ref, at, key_refs):
    me = lax.axis_index("ctx")
    count = table_ref.shape[0] // (lax.axis_size("ctx") // CORES)
    shards = []
    for j, pair in enumerate(zip(key_refs[::2], key_refs[1::2])):
        chip = table_ref[(me // CORES) * count + at + j]
        shards.append(((chip * CORES + me % CORES) * pair[0].shape[1], pair))
    return shards


def first_kernel(tokens, heads, count, length_ref, offset_ref, table_ref, here_ref, there_ref, *rest):
    keys, (q_ref, m_ref, l_ref, acc_ref, span_ref) = rest[:count], rest[count:]
    chips = here_ref.shape[0]
    rows = tokens * heads
    for core, piece_ref in enumerate((here_ref, there_ref)):
        for chip in range(chips):
            at = core * chips + chip
            q_ref[at * rows:(at + 1) * rows, :] = piece_ref[chip, :rows, :]
            if core == 0:
                span_ref[chip * tokens:(chip + 1) * tokens, :] = (
                    piece_ref[chip, rows:rows + tokens, :].astype(f32)
                )
    span = span_ref[...].astype(bf16)
    total = q_ref.shape[0]
    block = min(256, total)
    key_index = lax.broadcasted_iota(jnp.int32, (1, span.shape[0]), 1)
    key_token = token_of(key_index, tokens, chips)
    for start in range(0, total, block):
        part = pl.ds(start, block)
        s = lax.dot_general(
            q_ref[part, :], span, (((1,), (1,)), ((), ())), preferred_element_type=f32
        ) * score_scale
        row_index = start + lax.broadcasted_iota(jnp.int32, (block, 1), 0)
        row_token = token_of(row_index >> (heads.bit_length() - 1), tokens, chips)
        shown = (key_token >= offset_ref[0]) & (key_token <= row_token)
        s = jnp.where(shown, s, neg_large)
        m_new = jnp.maximum(jnp.max(s, axis=1, keepdims=True), least_max)
        probs = jnp.exp2(s - m_new)
        l_new = jnp.sum(probs, axis=1, keepdims=True)
        acc_ref[part, :] = jnp.dot(
            probs.astype(bf16), span[:, :LATENT], preferred_element_type=f32
        )
        m_ref[part, :] = jnp.broadcast_to(m_new, (block, LANES))
        l_ref[part, :] = jnp.broadcast_to(l_new, (block, LANES))
    fold_shards(q_ref, with_base(table_ref, 0, keys), length_ref[0], m_ref, l_ref, acc_ref)


def middle_kernel(at, count, length_ref, table_ref, q_ref, m_in, l_in, acc_in, *rest):
    keys, (m_ref, l_ref, acc_ref) = rest[:count], rest[count:]
    m_ref[...] = m_in[...]
    l_ref[...] = l_in[...]
    acc_ref[...] = acc_in[...]
    fold_shards(q_ref, with_base(table_ref, at, keys), length_ref[0], m_ref, l_ref, acc_ref)


def last_kernel(at, tokens, heads, length_ref, table_ref, q_ref, m_in, l_in, acc_in,
                top_ref, bottom_ref, own_up, far_up, out_ref,
                m_ref, l_ref, acc_ref, context_ref, flat_ref):
    middle_kernel(at, 2, length_ref, table_ref, q_ref, m_in, l_in, acc_in,
                  top_ref, bottom_ref, m_ref, l_ref, acc_ref)
    for k in range(LATENT // LANES):
        lanes = slice(k * LANES, (k + 1) * LANES)
        context_ref[k] = acc_ref[:, lanes] / l_ref[...]
    m_ref[...] = m_ref[...] + jnp.log2(l_ref[...])
    everyone = flat_ref.shape[0]
    core = lax.axis_index("ctx") % CORES
    per_core = heads // CORES
    tail = jnp.zeros((everyone, LANES), f32)
    lane = lax.broadcasted_iota(jnp.int32, (everyone, LANES), 1)
    for side, up_ref in enumerate((own_up, far_up)):
        for j in range(per_core):
            head = (core ^ side) * per_core + j
            rows = pl.ds(head, everyone, stride=heads)
            context = jnp.concatenate(
                [context_ref[k, rows, :] for k in range(LATENT // LANES)], axis=1
            ).astype(bf16)
            lifted = jnp.dot(context, up_ref[j], preferred_element_type=f32)
            flat_ref[:, pl.ds(pl.multiple_of(head * V_HEAD, V_HEAD), V_HEAD)] = lifted
            weight = m_ref[rows, :]
            high = weight.astype(bf16).astype(f32)
            mid = (weight - high).astype(bf16).astype(f32)
            low = weight - high - mid
            tail = jnp.where(lane == head, high, tail)
            tail = jnp.where(lane == head + heads, mid, tail)
            tail = jnp.where(lane == head + 2 * heads, low, tail)
    flat_ref[:, heads * V_HEAD:] = tail
    chips = everyone // tokens // CORES
    for i in range(chips * CORES):
        out_ref[(i % chips) * CORES + (core ^ (i // chips))] = (
            flat_ref[i * tokens:(i + 1) * tokens, :].astype(bf16)
        )


def merge_kernel(heads, parts_ref, out_ref):
    width = heads * V_HEAD
    for chip in range(parts_ref.shape[0] // CORES):
        one = parts_ref[2 * chip].astype(f32)
        two = parts_ref[2 * chip + 1].astype(f32)
        gap = one[:, width:] - two[:, width:]
        delta = gap[:, :heads] + (gap[:, heads:2 * heads] + gap[:, 2 * heads:3 * heads])
        share = 1.0 / (1.0 + jnp.exp2(-delta))
        rest = 1.0 / (1.0 + jnp.exp2(delta))
        for j in range(heads):
            lanes = slice(j * V_HEAD, (j + 1) * V_HEAD)
            mixed = one[:, lanes] * share[:, j:j + 1] + two[:, lanes] * rest[:, j:j + 1]
            out_ref[:, chip * width + j * V_HEAD:chip * width + (j + 1) * V_HEAD] = (
                mixed.astype(bf16)
            )


VMEM = pl.BlockSpec(memory_space=pltpu.VMEM)
SMEM = pl.BlockSpec(memory_space=pltpu.SMEM)
PARAMS = pltpu.CompilerParams(vmem_limit_bytes=32 * 1024 * 1024)


def shape(*dims, dtype=f32):
    return jax.ShapeDtypeStruct(dims, dtype)


def on_device(ctx, queries, prefix_latents, span_latents, value_up, prefix_length, span_offset):
    slots, width = prefix_latents.shape
    tokens = queries.shape[0]
    all_heads = queries.shape[1] // width
    chips = ctx // CORES
    heads = all_heads // chips
    rows = tokens * heads
    total = rows * ctx
    everyone = tokens * ctx
    walk = chip_cycle(chips)
    spot = np.argsort(np.array(walk))
    steps = chips // 2

    def across(step):
        return [
            (walk[r] * CORES + c, walk[(r + step) % chips] * CORES + c)
            for r in range(chips) for c in range(CORES)
        ]

    other_core = [(d, d ^ 1) for d in range(ctx)]
    same_core = [[p * CORES + c for p in range(chips)] for c in range(CORES)]

    turns = [0]
    for s in range(1, steps):
        turns += [-s, s]
    turns.append(steps)
    owner_table = np.array(
        [[walk[(spot[p] + t) % chips] for t in turns] for p in range(chips)], np.int32
    )
    table = jnp.asarray(owner_table.reshape(-1))
    state_shapes = [shape(total, LANES), shape(total, LANES), shape(total, LATENT)]

    def fold_first(keys):
        return pl.pallas_call(
            functools.partial(first_kernel, tokens, heads, len(keys)),
            out_shape=[shape(total, width, dtype=bf16)] + state_shapes,
            in_specs=[SMEM] * 3 + [VMEM] * (2 + len(keys)),
            out_specs=[VMEM] * 4,
            scratch_shapes=[pltpu.VMEM((everyone // CORES, width), f32)],
            compiler_params=PARAMS,
            name="first",
        )(prefix_length, span_offset, table, here, there, *keys)

    def fold_more(at, q, state, keys):
        return pl.pallas_call(
            functools.partial(middle_kernel, at, len(keys)),
            out_shape=state_shapes,
            in_specs=[SMEM] * 2 + [VMEM] * (4 + len(keys)),
            out_specs=[VMEM] * 3,
            compiler_params=PARAMS,
            name="middle",
        )(prefix_length, table, q, *state, *keys)

    cut = LATENT // 2
    onward = functools.partial(lax.ppermute, axis_name="ctx", perm=across(1))
    backward = functools.partial(lax.ppermute, axis_name="ctx", perm=across(-1))
    own = prefix_latents.T
    top, bottom = own[:cut], own[cut:]
    right = [onward(top), onward(bottom)]
    left = [backward(top), backward(bottom)]

    grouped = queries.reshape(tokens, chips, heads, width).transpose(1, 0, 2, 3)
    pad = -(rows + tokens) % 8
    span_rows = jnp.pad(span_latents, ((0, pad), (0, 0)))
    span_rows = jnp.broadcast_to(span_rows[None], (chips, tokens + pad, width))
    pieces = jnp.concatenate([grouped.reshape(chips, rows, width), span_rows], axis=1)
    pieces, right[0], left[0] = lax.optimization_barrier((pieces, right[0], left[0]))
    here = lax.all_to_all(
        pieces, "ctx", split_axis=0, concat_axis=0, axis_index_groups=same_core, tiled=True
    )

    there = lax.ppermute(here, "ctx", other_core)
    far_up = lax.ppermute(value_up, "ctx", other_core)

    keys, state, q = [top, bottom, *right, *left], None, None
    for s in range(2, steps + 1):
        if state is not None:
            right[1], left[1], state = lax.optimization_barrier((right[1], left[1], state))
        if s < steps:
            right = [onward(right[0]), onward(right[1])]
            left = [backward(left[0]), backward(left[1])]
        else:
            right, left = [onward(right[0])], [backward(left[1])]
        if state is None:
            q, *state = fold_first(keys)
        else:
            state = fold_more(2 * s - 3, q, state, keys)
        keys = [*right, *left]
    flat = heads * V_HEAD + LANES
    parts = pl.pallas_call(
        functools.partial(last_kernel, chips - 1, tokens, heads),
        out_shape=shape(ctx, tokens, flat, dtype=bf16),
        in_specs=[SMEM] * 2 + [VMEM] * 8,
        out_specs=VMEM,
        scratch_shapes=[
            pltpu.VMEM((total, LANES), f32),
            pltpu.VMEM((total, LANES), f32),
            pltpu.VMEM((total, LATENT), f32),
            pltpu.VMEM((LATENT // LANES, total, LANES), f32),
            pltpu.VMEM((everyone, flat), f32),
        ],
        compiler_params=PARAMS,
        name="last",
    )(prefix_length, table, q, *state, *keys, value_up, far_up)
    returned = lax.all_to_all(parts, "ctx", split_axis=0, concat_axis=0, tiled=True)
    return pl.pallas_call(
        functools.partial(merge_kernel, heads),
        out_shape=shape(tokens, all_heads * V_HEAD, dtype=bf16),
        in_specs=[VMEM],
        out_specs=VMEM,
        compiler_params=PARAMS,
        name="merge",
    )(returned)


def solution(mesh):
    return jax.shard_map(
        functools.partial(on_device, mesh.shape["ctx"]),
        mesh=mesh,
        in_specs=(
            P(("groups", "ctx"), None),
            P(("groups", "ctx"), None),
            P(("groups", "ctx"), None),
            P("ctx", None, None),
            P("groups"),
            P("groups"),
        ),
        out_specs=P(("groups", "ctx"), None),
        check_vma=False,
    )
```

```python
import functools
import math

import jax
import jax.numpy as jnp
import numpy as np
from jax import lax
from jax.experimental import pallas as pl
from jax.experimental.pallas import tpu as pltpu
from jax.sharding import PartitionSpec as P

LATENT = 512
V_HEAD = 128
CORES = 2
LANES = 128

score_scale = 192.0 ** (-0.5) * math.log2(math.e)
neg_large = -1e30
least_max = -1e29
f32 = jnp.float32
bf16 = jnp.bfloat16


def chip_cycle(chips):
    wide = max(1, int(round(chips ** (1 / 3))))
    tall = chips // wide
    if wide * tall != chips or wide < 2 or tall < 2:
        return list(range(chips))
    walk = []
    for z in range(tall):
        across = range(1, wide) if z % 2 == 0 else range(wide - 1, 0, -1)
        walk += [z * wide + x for x in across]
    return walk + [z * wide for z in reversed(range(tall))]


def fold_shards(q_ref, shards, length, old, new):
    rows = q_ref.shape[0]
    block = min(256, rows)
    for start in range(0, rows, block):
        part = pl.ds(start, block)
        m_old = old[0][part, :][:, :1]
        m_new = m_old
        scores = []
        for base, key_ref in shards:
            slot = base + lax.broadcasted_iota(jnp.int32, (1, key_ref.shape[1]), 1)
            s = jnp.dot(q_ref[part, :], key_ref[...], preferred_element_type=f32) * score_scale
            s = jnp.where(slot < length, s, neg_large)
            m_new = jnp.maximum(m_new, jnp.max(s, axis=1, keepdims=True))
            scores.append(s)
        shrink = jnp.exp2(m_old - m_new)
        l_new = old[1][part, :][:, :1] * shrink
        summed = old[2][part, :] * shrink
        for s, (_, key_ref) in zip(scores, shards):
            probs = jnp.exp2(s - m_new)
            l_new += jnp.sum(probs, axis=1, keepdims=True)
            summed += lax.dot_general(
                probs.astype(bf16), key_ref[:LATENT, :], (((1,), (1,)), ((), ())),
                preferred_element_type=f32,
            )
        new[0][part, :] = jnp.broadcast_to(m_new, (block, LANES))
        new[1][part, :] = jnp.broadcast_to(l_new, (block, LANES))
        new[2][part, :] = summed


def parted(index, size):
    return index >> (size.bit_length() - 1), index & (size - 1)


def token_of(index, tokens, chips):
    device, t = parted(index, tokens)
    core, chip = parted(device, chips)
    return (chip * CORES + ((lax.axis_index("ctx") % CORES) ^ core)) * tokens + t


def with_base(table_ref, at, key_refs):
    me = lax.axis_index("ctx")
    count = table_ref.shape[0] // (lax.axis_size("ctx") // CORES)
    shards = []
    for j, key_ref in enumerate(key_refs):
        chip = table_ref[(me // CORES) * count + at + j]
        shards.append(((chip * CORES + me % CORES) * key_ref.shape[1], key_ref))
    return shards


def first_kernel(tokens, heads, count, length_ref, offset_ref, table_ref, here_ref, there_ref, *rest):
    keys, (q_ref, m_ref, l_ref, acc_ref, span_ref) = rest[:count], rest[count:]
    chips = here_ref.shape[0]
    rows = tokens * heads
    for core, piece_ref in enumerate((here_ref, there_ref)):
        for chip in range(chips):
            at = core * chips + chip
            q_ref[at * rows:(at + 1) * rows, :] = piece_ref[chip, :rows, :]
            if core == 0:
                span_ref[chip * tokens:(chip + 1) * tokens, :] = (
                    piece_ref[chip, rows:rows + tokens, :].astype(f32)
                )
    span = span_ref[...].astype(bf16)
    total = q_ref.shape[0]
    block = min(256, total)
    key_index = lax.broadcasted_iota(jnp.int32, (1, span.shape[0]), 1)
    key_token = token_of(key_index, tokens, chips)
    for start in range(0, total, block):
        part = pl.ds(start, block)
        s = lax.dot_general(
            q_ref[part, :], span, (((1,), (1,)), ((), ())), preferred_element_type=f32
        ) * score_scale
        row_index = start + lax.broadcasted_iota(jnp.int32, (block, 1), 0)
        row_token = token_of(row_index >> (heads.bit_length() - 1), tokens, chips)
        shown = (key_token >= offset_ref[0]) & (key_token <= row_token)
        s = jnp.where(shown, s, neg_large)
        m_new = jnp.maximum(jnp.max(s, axis=1, keepdims=True), least_max)
        probs = jnp.exp2(s - m_new)
        l_new = jnp.sum(probs, axis=1, keepdims=True)
        acc_ref[part, :] = jnp.dot(
            probs.astype(bf16), span[:, :LATENT], preferred_element_type=f32
        )
        m_ref[part, :] = jnp.broadcast_to(m_new, (block, LANES))
        l_ref[part, :] = jnp.broadcast_to(l_new, (block, LANES))
    state = (m_ref, l_ref, acc_ref)
    fold_shards(q_ref, with_base(table_ref, 0, keys), length_ref[0], state, state)


def middle_kernel(at, count, length_ref, table_ref, q_ref, m_in, l_in, acc_in, *rest):
    keys, new = rest[:count], rest[count:]
    fold_shards(q_ref, with_base(table_ref, at, keys), length_ref[0], (m_in, l_in, acc_in), new)


def last_kernel(at, tokens, heads, length_ref, table_ref, q_ref, m_in, l_in, acc_in,
                top_ref, bottom_ref, own_up, far_up, out_ref,
                key_ref, m_ref, l_ref, acc_ref, context_ref, flat_ref):
    cut = top_ref.shape[0]
    key_ref[:cut, :] = top_ref[...]
    key_ref[cut:, :] = bottom_ref[...]
    middle_kernel(at, 1, length_ref, table_ref, q_ref, m_in, l_in, acc_in,
                  key_ref, m_ref, l_ref, acc_ref)
    for k in range(LATENT // LANES):
        lanes = slice(k * LANES, (k + 1) * LANES)
        context_ref[k] = acc_ref[:, lanes] / l_ref[...]
    m_ref[...] = m_ref[...] + jnp.log2(l_ref[...])
    everyone = flat_ref.shape[0]
    core = lax.axis_index("ctx") % CORES
    per_core = heads // CORES
    tail = jnp.zeros((everyone, LANES), f32)
    lane = lax.broadcasted_iota(jnp.int32, (everyone, LANES), 1)
    pair = min(2, per_core)
    for side, up_ref in enumerate((own_up, far_up)):
        for j in range(0, per_core, pair):
            first_head = (core ^ side) * per_core + j
            contexts = []
            for head in [first_head + i for i in range(pair)]:
                rows = pl.ds(head, everyone, stride=heads)
                contexts.append(jnp.concatenate(
                    [context_ref[k, rows, :] for k in range(LATENT // LANES)], axis=1
                ).astype(bf16))
                weight = m_ref[rows, :]
                high = weight.astype(bf16).astype(f32)
                mid = (weight - high).astype(bf16).astype(f32)
                low = weight - high - mid
                tail = jnp.where(lane == head, high, tail)
                tail = jnp.where(lane == head + heads, mid, tail)
                tail = jnp.where(lane == head + 2 * heads, low, tail)
            lifted = jnp.dot(
                jnp.concatenate(contexts, axis=0),
                jnp.concatenate([up_ref[j + i] for i in range(pair)], axis=1),
                preferred_element_type=f32,
            )
            for i in range(pair):
                lanes = pl.ds(pl.multiple_of((first_head + i) * V_HEAD, V_HEAD), V_HEAD)
                flat_ref[:, lanes] = lifted[
                    i * everyone:(i + 1) * everyone, i * V_HEAD:(i + 1) * V_HEAD
                ]
    flat_ref[:, heads * V_HEAD:] = tail
    chips = everyone // tokens // CORES
    for i in range(chips * CORES):
        out_ref[(i % chips) * CORES + (core ^ (i // chips))] = (
            flat_ref[i * tokens:(i + 1) * tokens, :].astype(bf16)
        )


def merge_kernel(heads, parts_ref, out_ref):
    width = heads * V_HEAD
    for chip in range(parts_ref.shape[0] // CORES):
        one = parts_ref[2 * chip].astype(f32)
        two = parts_ref[2 * chip + 1].astype(f32)
        gap = one[:, width:] - two[:, width:]
        delta = gap[:, :heads] + (gap[:, heads:2 * heads] + gap[:, 2 * heads:3 * heads])
        share = 1.0 / (1.0 + jnp.exp2(-delta))
        rest = 1.0 / (1.0 + jnp.exp2(delta))
        for j in range(heads):
            lanes = slice(j * V_HEAD, (j + 1) * V_HEAD)
            mixed = one[:, lanes] * share[:, j:j + 1] + two[:, lanes] * rest[:, j:j + 1]
            out_ref[:, chip * width + j * V_HEAD:chip * width + (j + 1) * V_HEAD] = (
                mixed.astype(bf16)
            )


VMEM = pl.BlockSpec(memory_space=pltpu.VMEM)
SMEM = pl.BlockSpec(memory_space=pltpu.SMEM)
PARAMS = pltpu.CompilerParams(vmem_limit_bytes=32 * 1024 * 1024)


def shape(*dims, dtype=f32):
    return jax.ShapeDtypeStruct(dims, dtype)


def on_device(ctx, queries, prefix_latents, span_latents, value_up, prefix_length, span_offset):
    slots, width = prefix_latents.shape
    tokens = queries.shape[0]
    all_heads = queries.shape[1] // width
    chips = ctx // CORES
    heads = all_heads // chips
    rows = tokens * heads
    total = rows * ctx
    everyone = tokens * ctx
    walk = chip_cycle(chips)
    spot = np.argsort(np.array(walk))
    steps = chips // 2

    def across(step):
        return [
            (walk[r] * CORES + c, walk[(r + step) % chips] * CORES + c)
            for r in range(chips) for c in range(CORES)
        ]

    other_core = [(d, d ^ 1) for d in range(ctx)]
    same_core = [[p * CORES + c for p in range(chips)] for c in range(CORES)]

    turns = [0]
    for s in range(1, steps):
        turns += [-s, s]
    turns.append(steps)
    owner_table = np.array(
        [[walk[(spot[p] + t) % chips] for t in turns] for p in range(chips)], np.int32
    )
    table = jnp.asarray(owner_table.reshape(-1))
    state_shapes = [shape(total, LANES), shape(total, LANES), shape(total, LATENT)]

    def fold_first(keys):
        return pl.pallas_call(
            functools.partial(first_kernel, tokens, heads, len(keys)),
            out_shape=[shape(total, width, dtype=bf16)] + state_shapes,
            in_specs=[SMEM] * 3 + [VMEM] * (2 + len(keys)),
            out_specs=[VMEM] * 4,
            scratch_shapes=[pltpu.VMEM((everyone // CORES, width), f32)],
            compiler_params=PARAMS,
            name="first",
        )(prefix_length, span_offset, table, here, there, *keys)

    def fold_more(at, q, state, keys):
        return pl.pallas_call(
            functools.partial(middle_kernel, at, len(keys)),
            out_shape=state_shapes,
            in_specs=[SMEM] * 2 + [VMEM] * (4 + len(keys)),
            out_specs=[VMEM] * 3,
            compiler_params=PARAMS,
            name="middle",
        )(prefix_length, table, q, *state, *keys)

    onward = functools.partial(lax.ppermute, axis_name="ctx", perm=across(1))
    backward = functools.partial(lax.ppermute, axis_name="ctx", perm=across(-1))
    cut = LATENT // 2
    own = prefix_latents.T
    right, left = onward(own), backward(own)

    grouped = queries.reshape(tokens, chips, heads, width).transpose(1, 0, 2, 3)
    pad = -(rows + tokens) % 8
    span_rows = jnp.pad(span_latents, ((0, pad), (0, 0)))
    span_rows = jnp.broadcast_to(span_rows[None], (chips, tokens + pad, width))
    pieces = jnp.concatenate([grouped.reshape(chips, rows, width), span_rows], axis=1)
    pieces, right, left = lax.optimization_barrier((pieces, right, left))
    here = lax.all_to_all(
        pieces, "ctx", split_axis=0, concat_axis=0, axis_index_groups=same_core, tiled=True
    )

    there = lax.ppermute(here, "ctx", other_core)
    far_up = lax.ppermute(value_up, "ctx", other_core)

    keys, state, at = [own, right, left], None, 0
    for s in range(2, steps):
        right, left = onward(right), backward(left)
        keys += [right, left]
        if s == 2:
            continue
        if state is None:
            q, *state = fold_first(keys[:-2])
        else:
            state = fold_more(at, q, state, keys[:-2])
        at += len(keys) - 2
        keys = keys[-2:]
    right, left, state = lax.optimization_barrier((right, left, state))
    right, left = onward(right[:cut]), backward(left[cut:])
    state = fold_more(at, q, state, keys)
    keys = [right, left]
    flat = heads * V_HEAD + LANES
    parts = pl.pallas_call(
        functools.partial(last_kernel, chips - 1, tokens, heads),
        out_shape=shape(ctx, tokens, flat, dtype=bf16),
        in_specs=[SMEM] * 2 + [VMEM] * 8,
        out_specs=VMEM,
        scratch_shapes=[
            pltpu.VMEM((width, slots), bf16),
            pltpu.VMEM((total, LANES), f32),
            pltpu.VMEM((total, LANES), f32),
            pltpu.VMEM((total, LATENT), f32),
            pltpu.VMEM((LATENT // LANES, total, LANES), f32),
            pltpu.VMEM((everyone, flat), f32),
        ],
        compiler_params=PARAMS,
        name="last",
    )(prefix_length, table, q, *state, *keys, value_up, far_up)
    returned = lax.all_to_all(parts, "ctx", split_axis=0, concat_axis=0, tiled=True)
    return pl.pallas_call(
        functools.partial(merge_kernel, heads),
        out_shape=shape(tokens, all_heads * V_HEAD, dtype=bf16),
        in_specs=[VMEM],
        out_specs=VMEM,
        compiler_params=PARAMS,
        name="merge",
    )(returned)


def solution(mesh):
    return jax.shard_map(
        functools.partial(on_device, mesh.shape["ctx"]),
        mesh=mesh,
        in_specs=(
            P(("groups", "ctx"), None),
            P(("groups", "ctx"), None),
            P(("groups", "ctx"), None),
            P("ctx", None, None),
            P("groups"),
            P("groups"),
        ),
        out_specs=P(("groups", "ctx"), None),
        check_vma=False,
    )
```

```python
import functools
import math

import jax
import jax.numpy as jnp
import numpy as np
from jax import lax
from jax.experimental import pallas as pl
from jax.experimental.pallas import tpu as pltpu
from jax.sharding import PartitionSpec as P

LATENT = 512
V_HEAD = 128
CORES = 2
LANES = 128

score_scale = 192.0 ** (-0.5) * math.log2(math.e)
neg_large = -1e30
least_max = -1e29
f32 = jnp.float32
bf16 = jnp.bfloat16


def chip_cycle(chips):
    wide = max(1, int(round(chips ** (1 / 3))))
    tall = chips // wide
    if wide * tall != chips or wide < 2 or tall < 2:
        return list(range(chips))
    walk = []
    for z in range(tall):
        across = range(1, wide) if z % 2 == 0 else range(wide - 1, 0, -1)
        walk += [z * wide + x for x in across]
    return walk + [z * wide for z in reversed(range(tall))]


def fold_shards(q_ref, shards, length, old, new):
    rows = q_ref.shape[0]
    block = min(256, rows)
    for start in range(0, rows, block):
        part = pl.ds(start, block)
        m_old = old[0][part, :][:, :1]
        m_new = m_old
        scores = []
        for base, key_ref in shards:
            slot = base + lax.broadcasted_iota(jnp.int32, (1, key_ref.shape[1]), 1)
            s = jnp.dot(q_ref[part, :], key_ref[...], preferred_element_type=f32) * score_scale
            s = jnp.where(slot < length, s, neg_large)
            m_new = jnp.maximum(m_new, jnp.max(s, axis=1, keepdims=True))
            scores.append(s)
        shrink = jnp.exp2(m_old - m_new)
        l_new = old[1][part, :][:, :1] * shrink
        summed = old[2][part, :] * shrink
        for s, (_, key_ref) in zip(scores, shards):
            probs = jnp.exp2(s - m_new)
            l_new += jnp.sum(probs, axis=1, keepdims=True)
            summed += lax.dot_general(
                probs.astype(bf16), key_ref[:LATENT, :], (((1,), (1,)), ((), ())),
                preferred_element_type=f32,
            )
        new[0][part, :] = jnp.broadcast_to(m_new, (block, LANES))
        new[1][part, :] = jnp.broadcast_to(l_new, (block, LANES))
        new[2][part, :] = summed


def parted(index, size):
    return index >> (size.bit_length() - 1), index & (size - 1)


def token_of(index, tokens, chips):
    device, t = parted(index, tokens)
    core, chip = parted(device, chips)
    return (chip * CORES + ((lax.axis_index("ctx") % CORES) ^ core)) * tokens + t


def with_base(table_ref, at, key_refs):
    me = lax.axis_index("ctx")
    count = table_ref.shape[0] // (lax.axis_size("ctx") // CORES)
    shards = []
    for j, key_ref in enumerate(key_refs):
        chip = table_ref[(me // CORES) * count + at + j]
        shards.append(((chip * CORES + me % CORES) * key_ref.shape[1], key_ref))
    return shards


def first_kernel(heads, count, length_ref, offset_ref, table_ref, here_ref, there_ref, *rest):
    keys, (q_ref, m_ref, l_ref, acc_ref) = rest[:count], rest[count:]
    chips = lax.axis_size("ctx") // CORES
    half = here_ref.shape[0]
    tokens = half // chips
    width = q_ref.shape[1]
    for core, piece_ref in enumerate((here_ref, there_ref)):
        for head in range(heads):
            row = (head * CORES + core) * half
            q_ref[row:row + half, :] = piece_ref[:, head * width:(head + 1) * width]
    span = here_ref[:, heads * width:]
    total = q_ref.shape[0]
    block = min(256, total)
    key_index = lax.broadcasted_iota(jnp.int32, (1, span.shape[0]), 1)
    key_token = token_of(key_index, tokens, chips)
    for start in range(0, total, block):
        part = pl.ds(start, block)
        s = lax.dot_general(
            q_ref[part, :], span, (((1,), (1,)), ((), ())), preferred_element_type=f32
        ) * score_scale
        row_index = start + lax.broadcasted_iota(jnp.int32, (block, 1), 0)
        row_token = token_of(row_index & (half * CORES - 1), tokens, chips)
        shown = (key_token >= offset_ref[0]) & (key_token <= row_token)
        s = jnp.where(shown, s, neg_large)
        m_new = jnp.maximum(jnp.max(s, axis=1, keepdims=True), least_max)
        probs = jnp.exp2(s - m_new)
        l_new = jnp.sum(probs, axis=1, keepdims=True)
        acc_ref[part, :] = jnp.dot(
            probs.astype(bf16), span[:, :LATENT], preferred_element_type=f32
        )
        m_ref[part, :] = jnp.broadcast_to(m_new, (block, LANES))
        l_ref[part, :] = jnp.broadcast_to(l_new, (block, LANES))
    state = (m_ref, l_ref, acc_ref)
    fold_shards(q_ref, with_base(table_ref, 0, keys), length_ref[0], state, state)


def middle_kernel(at, count, length_ref, table_ref, q_ref, m_in, l_in, acc_in, *rest):
    keys, new = rest[:count], rest[count:]
    fold_shards(q_ref, with_base(table_ref, at, keys), length_ref[0], (m_in, l_in, acc_in), new)


def last_kernel(at, tokens, heads, length_ref, table_ref, q_ref, m_in, l_in, acc_in,
                top_ref, bottom_ref, own_up, far_up, out_ref,
                key_ref, m_ref, l_ref, acc_ref, flat_ref):
    cut = top_ref.shape[0]
    key_ref[:cut, :] = top_ref[...]
    key_ref[cut:, :] = bottom_ref[...]
    middle_kernel(at, 1, length_ref, table_ref, q_ref, m_in, l_in, acc_in,
                  key_ref, m_ref, l_ref, acc_ref)
    acc_ref[...] = acc_ref[...] / l_ref[:, :1]
    m_ref[...] = m_ref[...] + jnp.log2(l_ref[...])
    everyone = flat_ref.shape[0]
    core = lax.axis_index("ctx") % CORES
    per_core = heads // CORES
    tail = jnp.zeros((everyone, LANES), f32)
    lane = lax.broadcasted_iota(jnp.int32, (everyone, LANES), 1)
    pair = min(2, per_core)
    for side, up_ref in enumerate((own_up, far_up)):
        for j in range(0, per_core, pair):
            first_head = (core ^ side) * per_core + j
            contexts = []
            for head in [first_head + i for i in range(pair)]:
                rows = pl.ds(pl.multiple_of(head * everyone, everyone), everyone)
                contexts.append(acc_ref[rows, :].astype(bf16))
                weight = m_ref[rows, :]
                high = weight.astype(bf16).astype(f32)
                mid = (weight - high).astype(bf16).astype(f32)
                low = weight - high - mid
                tail = jnp.where(lane == head, high, tail)
                tail = jnp.where(lane == head + heads, mid, tail)
                tail = jnp.where(lane == head + 2 * heads, low, tail)
            lifted = jnp.dot(
                jnp.concatenate(contexts, axis=0),
                jnp.concatenate([up_ref[j + i] for i in range(pair)], axis=1),
                preferred_element_type=f32,
            )
            for i in range(pair):
                lanes = pl.ds(pl.multiple_of((first_head + i) * V_HEAD, V_HEAD), V_HEAD)
                flat_ref[:, lanes] = lifted[
                    i * everyone:(i + 1) * everyone, i * V_HEAD:(i + 1) * V_HEAD
                ]
    flat_ref[:, heads * V_HEAD:] = tail
    chips = everyone // tokens // CORES
    for i in range(chips * CORES):
        out_ref[(i % chips) * CORES + (core ^ (i // chips))] = (
            flat_ref[i * tokens:(i + 1) * tokens, :].astype(bf16)
        )


def merge_kernel(heads, parts_ref, out_ref):
    width = heads * V_HEAD
    for chip in range(parts_ref.shape[0] // CORES):
        one = parts_ref[2 * chip].astype(f32)
        two = parts_ref[2 * chip + 1].astype(f32)
        gap = one[:, width:] - two[:, width:]
        delta = gap[:, :heads] + (gap[:, heads:2 * heads] + gap[:, 2 * heads:3 * heads])
        share = 1.0 / (1.0 + jnp.exp2(-delta))
        rest = 1.0 / (1.0 + jnp.exp2(delta))
        for j in range(heads):
            lanes = slice(j * V_HEAD, (j + 1) * V_HEAD)
            mixed = one[:, lanes] * share[:, j:j + 1] + two[:, lanes] * rest[:, j:j + 1]
            out_ref[:, chip * width + j * V_HEAD:chip * width + (j + 1) * V_HEAD] = (
                mixed.astype(bf16)
            )


VMEM = pl.BlockSpec(memory_space=pltpu.VMEM)
SMEM = pl.BlockSpec(memory_space=pltpu.SMEM)
PARAMS = pltpu.CompilerParams(vmem_limit_bytes=32 * 1024 * 1024)


def shape(*dims, dtype=f32):
    return jax.ShapeDtypeStruct(dims, dtype)


def on_device(ctx, queries, prefix_latents, span_latents, value_up, prefix_length, span_offset):
    slots, width = prefix_latents.shape
    tokens = queries.shape[0]
    all_heads = queries.shape[1] // width
    chips = ctx // CORES
    heads = all_heads // chips
    rows = tokens * heads
    total = rows * ctx
    everyone = tokens * ctx
    walk = chip_cycle(chips)
    spot = np.argsort(np.array(walk))
    steps = chips // 2

    def across(step):
        return [
            (walk[r] * CORES + c, walk[(r + step) % chips] * CORES + c)
            for r in range(chips) for c in range(CORES)
        ]

    other_core = [(d, d ^ 1) for d in range(ctx)]
    same_core = [[p * CORES + c for p in range(chips)] for c in range(CORES)]

    turns = [0]
    for s in range(1, steps):
        turns += [-s, s]
    turns.append(steps)
    owner_table = np.array(
        [[walk[(spot[p] + t) % chips] for t in turns] for p in range(chips)], np.int32
    )
    table = jnp.asarray(owner_table.reshape(-1))
    state_shapes = [shape(total, LANES), shape(total, LANES), shape(total, LATENT)]

    def fold_first(keys):
        return pl.pallas_call(
            functools.partial(first_kernel, heads, len(keys)),
            out_shape=[shape(total, width, dtype=bf16)] + state_shapes,
            in_specs=[SMEM] * 3 + [VMEM] * (2 + len(keys)),
            out_specs=[VMEM] * 4,
            compiler_params=PARAMS,
            name="first",
        )(prefix_length, span_offset, table, here, there, *keys)

    def fold_more(at, q, state, keys):
        return pl.pallas_call(
            functools.partial(middle_kernel, at, len(keys)),
            out_shape=state_shapes,
            in_specs=[SMEM] * 2 + [VMEM] * (4 + len(keys)),
            out_specs=[VMEM] * 3,
            compiler_params=PARAMS,
            name="middle",
        )(prefix_length, table, q, *state, *keys)

    onward = functools.partial(lax.ppermute, axis_name="ctx", perm=across(1))
    backward = functools.partial(lax.ppermute, axis_name="ctx", perm=across(-1))
    cut = LATENT // 2
    own = prefix_latents.T
    right, left = onward(own), backward(own)

    grouped = queries.reshape(tokens, chips, heads * width).transpose(1, 0, 2)
    spans = jnp.broadcast_to(span_latents[None], (chips, tokens, width))
    pieces = jnp.concatenate([grouped, spans], axis=2)
    here = lax.all_to_all(
        pieces, "ctx", split_axis=0, concat_axis=0, axis_index_groups=same_core, tiled=True
    )
    far_up = lax.ppermute(value_up, "ctx", other_core)

    keys, state, at = [own, right, left], None, 0
    for s in range(2, steps):
        right, left = onward(right), backward(left)
        keys += [right, left]
        if s == 2:
            right, left, here = lax.optimization_barrier((right, left, here))
            keys[-2:] = right, left
            here = here.reshape(chips * tokens, (heads + 1) * width)
            there = lax.ppermute(here, "ctx", other_core)
            continue
        if state is None:
            q, *state = fold_first(keys[:-2])
        else:
            state = fold_more(at, q, state, keys[:-2])
        at += len(keys) - 2
        keys = keys[-2:]
    right, left, state = lax.optimization_barrier((right, left, state))
    right, left = onward(right[:cut]), backward(left[cut:])
    state = fold_more(at, q, state, keys)
    keys = [right, left]
    flat = heads * V_HEAD + LANES
    parts = pl.pallas_call(
        functools.partial(last_kernel, chips - 1, tokens, heads),
        out_shape=shape(ctx, tokens, flat, dtype=bf16),
        in_specs=[SMEM] * 2 + [VMEM] * 8,
        out_specs=VMEM,
        scratch_shapes=[
            pltpu.VMEM((width, slots), bf16),
            pltpu.VMEM((total, LANES), f32),
            pltpu.VMEM((total, LANES), f32),
            pltpu.VMEM((total, LATENT), f32),
            pltpu.VMEM((everyone, flat), f32),
        ],
        compiler_params=PARAMS,
        name="last",
    )(prefix_length, table, q, *state, *keys, value_up, far_up)
    returned = lax.all_to_all(parts, "ctx", split_axis=0, concat_axis=0, tiled=True)
    return pl.pallas_call(
        functools.partial(merge_kernel, heads),
        out_shape=shape(tokens, all_heads * V_HEAD, dtype=bf16),
        in_specs=[VMEM],
        out_specs=VMEM,
        compiler_params=PARAMS,
        name="merge",
    )(returned)


def solution(mesh):
    return jax.shard_map(
        functools.partial(on_device, mesh.shape["ctx"]),
        mesh=mesh,
        in_specs=(
            P(("groups", "ctx"), None),
            P(("groups", "ctx"), None),
            P(("groups", "ctx"), None),
            P("ctx", None, None),
            P("groups"),
            P("groups"),
        ),
        out_specs=P(("groups", "ctx"), None),
        check_vma=False,
    )
```

```python
import functools
import math

import jax
import jax.numpy as jnp
import numpy as np
from jax import lax
from jax.experimental import pallas as pl
from jax.experimental.pallas import tpu as pltpu
from jax.sharding import PartitionSpec as P

LATENT = 512
V_HEAD = 128
CORES = 2
LANES = 128

score_scale = 192.0 ** (-0.5) * math.log2(math.e)
neg_large = -1e30
least_max = -1e29
f32 = jnp.float32
bf16 = jnp.bfloat16


def chip_cycle(chips):
    wide = max(1, int(round(chips ** (1 / 3))))
    tall = chips // wide
    if wide * tall != chips or wide < 2 or tall < 2:
        return list(range(chips))
    walk = []
    for z in range(tall):
        across = range(1, wide) if z % 2 == 0 else range(wide - 1, 0, -1)
        walk += [z * wide + x for x in across]
    return walk + [z * wide for z in reversed(range(tall))]


def fold_shards(q_ref, shards, length, old, new):
    rows = q_ref.shape[0]
    block = min(256, rows)
    for start in range(0, rows, block):
        part = pl.ds(start, block)
        m_old = old[0][part, :][:, :1]
        m_new = m_old
        scores = []
        for base, key_ref in shards:
            slot = base + lax.broadcasted_iota(jnp.int32, (1, key_ref.shape[1]), 1)
            s = jnp.dot(q_ref[part, :], key_ref[...], preferred_element_type=f32) * score_scale
            s = jnp.where(slot < length, s, neg_large)
            m_new = jnp.maximum(m_new, jnp.max(s, axis=1, keepdims=True))
            scores.append(s)
        shrink = jnp.exp2(m_old - m_new)
        l_new = old[1][part, :][:, :1] * shrink
        summed = old[2][part, :] * shrink
        for s, (_, key_ref) in zip(scores, shards):
            probs = jnp.exp2(s - m_new)
            l_new += jnp.sum(probs, axis=1, keepdims=True)
            summed += lax.dot_general(
                probs.astype(bf16), key_ref[:LATENT, :], (((1,), (1,)), ((), ())),
                preferred_element_type=f32,
            )
        new[0][part, :] = jnp.broadcast_to(m_new, (block, LANES))
        new[1][part, :] = jnp.broadcast_to(l_new, (block, LANES))
        new[2][part, :] = summed


def parted(index, size):
    return index >> (size.bit_length() - 1), index & (size - 1)


def token_of(index, tokens, chips):
    device, t = parted(index, tokens)
    core, chip = parted(device, chips)
    return (chip * CORES + ((lax.axis_index("ctx") % CORES) ^ core)) * tokens + t


def with_base(table_ref, at, key_refs):
    me = lax.axis_index("ctx")
    count = table_ref.shape[0] // (lax.axis_size("ctx") // CORES)
    shards = []
    for j, key_ref in enumerate(key_refs):
        chip = table_ref[(me // CORES) * count + at + j]
        shards.append(((chip * CORES + me % CORES) * key_ref.shape[1], key_ref))
    return shards


def first_kernel(heads, count, length_ref, offset_ref, table_ref, here_ref, there_ref, *rest):
    keys, (q_ref, m_ref, l_ref, acc_ref) = rest[:count], rest[count:]
    chips = lax.axis_size("ctx") // CORES
    half = here_ref.shape[0]
    tokens = half // chips
    width = q_ref.shape[1]
    for core, piece_ref in enumerate((here_ref, there_ref)):
        for head in range(heads):
            row = (head * CORES + core) * half
            q_ref[row:row + half, :] = piece_ref[:, head * width:(head + 1) * width]
    span = here_ref[:, heads * width:]
    total = q_ref.shape[0]
    block = min(256, total)
    key_index = lax.broadcasted_iota(jnp.int32, (1, span.shape[0]), 1)
    key_token = token_of(key_index, tokens, chips)
    for start in range(0, total, block):
        part = pl.ds(start, block)
        s = lax.dot_general(
            q_ref[part, :], span, (((1,), (1,)), ((), ())), preferred_element_type=f32
        ) * score_scale
        row_index = start + lax.broadcasted_iota(jnp.int32, (block, 1), 0)
        row_token = token_of(row_index & (half * CORES - 1), tokens, chips)
        shown = (key_token >= offset_ref[0]) & (key_token <= row_token)
        s = jnp.where(shown, s, neg_large)
        m_new = jnp.maximum(jnp.max(s, axis=1, keepdims=True), least_max)
        probs = jnp.exp2(s - m_new)
        l_new = jnp.sum(probs, axis=1, keepdims=True)
        acc_ref[part, :] = jnp.dot(
            probs.astype(bf16), span[:, :LATENT], preferred_element_type=f32
        )
        m_ref[part, :] = jnp.broadcast_to(m_new, (block, LANES))
        l_ref[part, :] = jnp.broadcast_to(l_new, (block, LANES))
    state = (m_ref, l_ref, acc_ref)
    fold_shards(q_ref, with_base(table_ref, 0, keys), length_ref[0], state, state)


def middle_kernel(at, count, length_ref, table_ref, q_ref, m_in, l_in, acc_in, *rest):
    keys, new = rest[:count], rest[count:]
    fold_shards(q_ref, with_base(table_ref, at, keys), length_ref[0], (m_in, l_in, acc_in), new)


def last_kernel(at, heads, length_ref, table_ref, q_ref, m_in, l_in, acc_in,
                top_ref, bottom_ref, own_up, far_up, keep_ref, give_ref,
                key_ref, m_ref, l_ref, acc_ref, flat_ref):
    cut = top_ref.shape[0]
    key_ref[:cut, :] = top_ref[...]
    key_ref[cut:, :] = bottom_ref[...]
    middle_kernel(at, 1, length_ref, table_ref, q_ref, m_in, l_in, acc_in,
                  key_ref, m_ref, l_ref, acc_ref)
    acc_ref[...] = acc_ref[...] / l_ref[:, :1]
    m_ref[...] = m_ref[...] + jnp.log2(l_ref[...])
    everyone = flat_ref.shape[0]
    core = lax.axis_index("ctx") % CORES
    per_core = heads // CORES
    tail = jnp.zeros((everyone, LANES), f32)
    lane = lax.broadcasted_iota(jnp.int32, (everyone, LANES), 1)
    pair = min(2, per_core)
    for side, up_ref in enumerate((own_up, far_up)):
        for j in range(0, per_core, pair):
            first_head = (core ^ side) * per_core + j
            contexts = []
            for head in [first_head + i for i in range(pair)]:
                rows = pl.ds(pl.multiple_of(head * everyone, everyone), everyone)
                contexts.append(acc_ref[rows, :].astype(bf16))
                weight = m_ref[rows, :]
                high = weight.astype(bf16).astype(f32)
                mid = (weight - high).astype(bf16).astype(f32)
                low = weight - high - mid
                tail = jnp.where(lane == head, high, tail)
                tail = jnp.where(lane == head + heads, mid, tail)
                tail = jnp.where(lane == head + 2 * heads, low, tail)
            lifted = jnp.dot(
                jnp.concatenate(contexts, axis=0),
                jnp.concatenate([up_ref[j + i] for i in range(pair)], axis=1),
                preferred_element_type=f32,
            )
            for i in range(pair):
                lanes = pl.ds(pl.multiple_of((first_head + i) * V_HEAD, V_HEAD), V_HEAD)
                flat_ref[:, lanes] = lifted[
                    i * everyone:(i + 1) * everyone, i * V_HEAD:(i + 1) * V_HEAD
                ]
    flat_ref[:, heads * V_HEAD:] = tail
    keep_ref[...] = flat_ref[:everyone // CORES, :]
    give_ref[...] = flat_ref[everyone // CORES:, :].astype(bf16)


def merge_kernel(heads, keep_ref, got_ref, out_ref, flat_ref):
    width = heads * V_HEAD
    gap = keep_ref[:, width:] - got_ref[:, width:].astype(f32)
    delta = gap[:, :heads] + (gap[:, heads:2 * heads] + gap[:, 2 * heads:3 * heads])
    share = 1.0 / (1.0 + jnp.exp2(-delta))
    rest = 1.0 / (1.0 + jnp.exp2(delta))
    for j in range(heads):
        lanes = slice(j * V_HEAD, (j + 1) * V_HEAD)
        flat_ref[:, lanes] = (
            keep_ref[:, lanes] * share[:, j:j + 1]
            + got_ref[:, lanes].astype(f32) * rest[:, j:j + 1]
        )
    chips, tokens, _ = out_ref.shape
    for chip in range(chips):
        out_ref[chip] = flat_ref[chip * tokens:(chip + 1) * tokens, :].astype(bf16)


VMEM = pl.BlockSpec(memory_space=pltpu.VMEM)
SMEM = pl.BlockSpec(memory_space=pltpu.SMEM)
PARAMS = pltpu.CompilerParams(vmem_limit_bytes=32 * 1024 * 1024)


def shape(*dims, dtype=f32):
    return jax.ShapeDtypeStruct(dims, dtype)


def on_device(ctx, queries, prefix_latents, span_latents, value_up, prefix_length, span_offset):
    slots, width = prefix_latents.shape
    tokens = queries.shape[0]
    all_heads = queries.shape[1] // width
    chips = ctx // CORES
    heads = all_heads // chips
    rows = tokens * heads
    total = rows * ctx
    everyone = tokens * ctx
    walk = chip_cycle(chips)
    spot = np.argsort(np.array(walk))
    steps = chips // 2

    def across(step):
        return [
            (walk[r] * CORES + c, walk[(r + step) % chips] * CORES + c)
            for r in range(chips) for c in range(CORES)
        ]

    other_core = [(d, d ^ 1) for d in range(ctx)]
    same_core = [[p * CORES + c for p in range(chips)] for c in range(CORES)]

    turns = [0]
    for s in range(1, steps):
        turns += [-s, s]
    turns.append(steps)
    owner_table = np.array(
        [[walk[(spot[p] + t) % chips] for t in turns] for p in range(chips)], np.int32
    )
    table = jnp.asarray(owner_table.reshape(-1))
    state_shapes = [shape(total, LANES), shape(total, LANES), shape(total, LATENT)]

    def fold_first(keys):
        return pl.pallas_call(
            functools.partial(first_kernel, heads, len(keys)),
            out_shape=[shape(total, width, dtype=bf16)] + state_shapes,
            in_specs=[SMEM] * 3 + [VMEM] * (2 + len(keys)),
            out_specs=[VMEM] * 4,
            compiler_params=PARAMS,
            name="first",
        )(prefix_length, span_offset, table, here, there, *keys)

    def fold_more(at, q, state, keys):
        return pl.pallas_call(
            functools.partial(middle_kernel, at, len(keys)),
            out_shape=state_shapes,
            in_specs=[SMEM] * 2 + [VMEM] * (4 + len(keys)),
            out_specs=[VMEM] * 3,
            compiler_params=PARAMS,
            name="middle",
        )(prefix_length, table, q, *state, *keys)

    onward = functools.partial(lax.ppermute, axis_name="ctx", perm=across(1))
    backward = functools.partial(lax.ppermute, axis_name="ctx", perm=across(-1))
    cut = LATENT // 2
    own = prefix_latents.T
    right, left = onward(own), backward(own)

    grouped = queries.reshape(tokens, chips, heads * width).transpose(1, 0, 2)
    spans = jnp.broadcast_to(span_latents[None], (chips, tokens, width))
    pieces = jnp.concatenate([grouped, spans], axis=2)
    here = lax.all_to_all(
        pieces, "ctx", split_axis=0, concat_axis=0, axis_index_groups=same_core, tiled=True
    )
    far_up = lax.ppermute(value_up, "ctx", other_core)

    keys, state, at = [own, right, left], None, 0
    for s in range(2, steps):
        right, left = onward(right), backward(left)
        keys += [right, left]
        if s == 2:
            right, left, here = lax.optimization_barrier((right, left, here))
            keys[-2:] = right, left
            here = here.reshape(chips * tokens, (heads + 1) * width)
            there = lax.ppermute(here, "ctx", other_core)
            continue
        if state is None:
            q, *state = fold_first(keys[:-2])
        else:
            state = fold_more(at, q, state, keys[:-2])
        at += len(keys) - 2
        keys = keys[-2:]
    right, left, state = lax.optimization_barrier((right, left, state))
    right, left = onward(right[:cut]), backward(left[cut:])
    state = fold_more(at, q, state, keys)
    keys = [right, left]
    flat = heads * V_HEAD + LANES
    half = everyone // CORES
    keep, give = pl.pallas_call(
        functools.partial(last_kernel, chips - 1, heads),
        out_shape=[shape(half, flat), shape(half, flat, dtype=bf16)],
        in_specs=[SMEM] * 2 + [VMEM] * 8,
        out_specs=[VMEM] * 2,
        scratch_shapes=[
            pltpu.VMEM((width, slots), bf16),
            pltpu.VMEM((total, LANES), f32),
            pltpu.VMEM((total, LANES), f32),
            pltpu.VMEM((total, LATENT), f32),
            pltpu.VMEM((everyone, flat), f32),
        ],
        compiler_params=PARAMS,
        name="last",
    )(prefix_length, table, q, *state, *keys, value_up, far_up)
    got = lax.ppermute(give, "ctx", other_core)
    merged = pl.pallas_call(
        functools.partial(merge_kernel, heads),
        out_shape=shape(chips, tokens, heads * V_HEAD, dtype=bf16),
        in_specs=[VMEM] * 2,
        out_specs=VMEM,
        scratch_shapes=[pltpu.VMEM((half, heads * V_HEAD), f32)],
        compiler_params=PARAMS,
        name="merge",
    )(keep, got)
    returned = lax.all_to_all(
        merged, "ctx", split_axis=0, concat_axis=0, axis_index_groups=same_core, tiled=True
    )
    return returned.transpose(1, 0, 2).reshape(tokens, all_heads * V_HEAD)


def solution(mesh):
    return jax.shard_map(
        functools.partial(on_device, mesh.shape["ctx"]),
        mesh=mesh,
        in_specs=(
            P(("groups", "ctx"), None),
            P(("groups", "ctx"), None),
            P(("groups", "ctx"), None),
            P("ctx", None, None),
            P("groups"),
            P("groups"),
        ),
        out_specs=P(("groups", "ctx"), None),
        check_vma=False,
    )
```

```python
import functools
import math

import jax
import jax.numpy as jnp
import numpy as np
from jax import lax
from jax.experimental import pallas as pl
from jax.experimental.pallas import tpu as pltpu
from jax.sharding import PartitionSpec as P

LATENT = 512
V_HEAD = 128
CORES = 2
LANES = 128

score_scale = 192.0 ** (-0.5) * math.log2(math.e)
neg_large = -1e30
least_max = -1e29
f32 = jnp.float32
bf16 = jnp.bfloat16


def chip_cycle(chips):
    wide = max(1, int(round(chips ** (1 / 3))))
    tall = chips // wide
    if wide * tall != chips or wide < 2 or tall < 2:
        return list(range(chips))
    walk = []
    for z in range(tall):
        across = range(1, wide) if z % 2 == 0 else range(wide - 1, 0, -1)
        walk += [z * wide + x for x in across]
    return walk + [z * wide for z in reversed(range(tall))]


def fold_shards(q_ref, shards, length, old, new):
    rows = q_ref.shape[0]
    block = min(256, rows)
    for start in range(0, rows, block):
        part = pl.ds(start, block)
        m_old = old[0][part, :][:, :1]
        m_new = m_old
        scores = []
        for base, key_ref in shards:
            slot = base + lax.broadcasted_iota(jnp.int32, (1, key_ref.shape[1]), 1)
            s = jnp.dot(q_ref[part, :], key_ref[...], preferred_element_type=f32) * score_scale
            s = jnp.where(slot < length, s, neg_large)
            m_new = jnp.maximum(m_new, jnp.max(s, axis=1, keepdims=True))
            scores.append(s)
        shrink = jnp.exp2(m_old - m_new)
        l_new = old[1][part, :][:, :1] * shrink
        summed = old[2][part, :] * shrink
        for s, (_, key_ref) in zip(scores, shards):
            probs = jnp.exp2(s - m_new)
            l_new += jnp.sum(probs, axis=1, keepdims=True)
            summed += lax.dot_general(
                probs.astype(bf16), key_ref[:LATENT, :], (((1,), (1,)), ((), ())),
                preferred_element_type=f32,
            )
        new[0][part, :] = jnp.broadcast_to(m_new, (block, LANES))
        new[1][part, :] = jnp.broadcast_to(l_new, (block, LANES))
        new[2][part, :] = summed


def parted(index, size):
    return index >> (size.bit_length() - 1), index & (size - 1)


def token_of(index, tokens, chips):
    device, t = parted(index, tokens)
    core, chip = parted(device, chips)
    return (chip * CORES + ((lax.axis_index("ctx") % CORES) ^ core)) * tokens + t


def with_base(table_ref, at, key_refs):
    me = lax.axis_index("ctx")
    count = table_ref.shape[0] // (lax.axis_size("ctx") // CORES)
    shards = []
    for j, key_ref in enumerate(key_refs):
        chip = table_ref[(me // CORES) * count + at + j]
        shards.append(((chip * CORES + me % CORES) * key_ref.shape[1], key_ref))
    return shards


def first_kernel(heads, count, scal_ref, table_ref, here_ref, there_ref, *rest):
    keys, (q_ref, m_ref, l_ref, acc_ref) = rest[:count], rest[count:]
    chips = lax.axis_size("ctx") // CORES
    half = here_ref.shape[0]
    tokens = half // chips
    width = q_ref.shape[1]
    for core, piece_ref in enumerate((here_ref, there_ref)):
        for head in range(heads):
            row = (head * CORES + core) * half
            q_ref[row:row + half, :] = piece_ref[:, head * width:(head + 1) * width]
    span = here_ref[:, heads * width:]
    total = q_ref.shape[0]
    block = min(256, total)
    key_index = lax.broadcasted_iota(jnp.int32, (1, span.shape[0]), 1)
    key_token = token_of(key_index, tokens, chips)
    for start in range(0, total, block):
        part = pl.ds(start, block)
        s = lax.dot_general(
            q_ref[part, :], span, (((1,), (1,)), ((), ())), preferred_element_type=f32
        ) * score_scale
        row_index = start + lax.broadcasted_iota(jnp.int32, (block, 1), 0)
        row_token = token_of(row_index & (half * CORES - 1), tokens, chips)
        shown = (key_token >= scal_ref[1]) & (key_token <= row_token)
        s = jnp.where(shown, s, neg_large)
        m_new = jnp.maximum(jnp.max(s, axis=1, keepdims=True), least_max)
        probs = jnp.exp2(s - m_new)
        l_new = jnp.sum(probs, axis=1, keepdims=True)
        acc_ref[part, :] = jnp.dot(
            probs.astype(bf16), span[:, :LATENT], preferred_element_type=f32
        )
        m_ref[part, :] = jnp.broadcast_to(m_new, (block, LANES))
        l_ref[part, :] = jnp.broadcast_to(l_new, (block, LANES))
    state = (m_ref, l_ref, acc_ref)
    fold_shards(q_ref, with_base(table_ref, 0, keys), scal_ref[0], state, state)


def middle_kernel(at, count, scal_ref, table_ref, q_ref, m_in, l_in, acc_in, *rest):
    keys, new = rest[:count], rest[count:]
    fold_shards(q_ref, with_base(table_ref, at, keys), scal_ref[0], (m_in, l_in, acc_in), new)


def join_halves(halves, key_refs):
    for top_ref, bottom_ref, key_ref in zip(halves[::2], halves[1::2], key_refs):
        cut = top_ref.shape[0]
        key_ref[:cut, :] = top_ref[...]
        key_ref[cut:, :] = bottom_ref[...]


def halves_kernel(at, scal_ref, table_ref, q_ref, m_in, l_in, acc_in, *rest):
    halves, new, keys = rest[:4], rest[4:7], rest[7:]
    join_halves(halves, keys)
    middle_kernel(at, 2, scal_ref, table_ref, q_ref, m_in, l_in, acc_in, *keys, *new)


def last_kernel(at, heads, scal_ref, table_ref, q_ref, m_in, l_in, acc_in,
                top_ref, bottom_ref, own_up, far_up, keep_ref, give_ref,
                key_ref, m_ref, l_ref, acc_ref, flat_ref):
    join_halves((top_ref, bottom_ref), (key_ref,))
    middle_kernel(at, 1, scal_ref, table_ref, q_ref, m_in, l_in, acc_in,
                  key_ref, m_ref, l_ref, acc_ref)
    acc_ref[...] = acc_ref[...] / l_ref[:, :1]
    m_ref[...] = m_ref[...] + jnp.log2(l_ref[...])
    everyone = flat_ref.shape[0]
    core = lax.axis_index("ctx") % CORES
    per_core = heads // CORES
    tail = jnp.zeros((everyone, LANES), f32)
    lane = lax.broadcasted_iota(jnp.int32, (everyone, LANES), 1)
    pair = min(2, per_core)
    for side, up_ref in enumerate((own_up, far_up)):
        for j in range(0, per_core, pair):
            first_head = (core ^ side) * per_core + j
            contexts = []
            for head in [first_head + i for i in range(pair)]:
                rows = pl.ds(pl.multiple_of(head * everyone, everyone), everyone)
                contexts.append(acc_ref[rows, :].astype(bf16))
                weight = m_ref[rows, :]
                high = weight.astype(bf16).astype(f32)
                mid = (weight - high).astype(bf16).astype(f32)
                low = weight - high - mid
                tail = jnp.where(lane == head, high, tail)
                tail = jnp.where(lane == head + heads, mid, tail)
                tail = jnp.where(lane == head + 2 * heads, low, tail)
            lifted = jnp.dot(
                jnp.concatenate(contexts, axis=0),
                jnp.concatenate([up_ref[j + i] for i in range(pair)], axis=1),
                preferred_element_type=f32,
            )
            for i in range(pair):
                lanes = pl.ds(pl.multiple_of((first_head + i) * V_HEAD, V_HEAD), V_HEAD)
                flat_ref[:, lanes] = lifted[
                    i * everyone:(i + 1) * everyone, i * V_HEAD:(i + 1) * V_HEAD
                ]
    flat_ref[:, heads * V_HEAD:] = tail
    keep_ref[...] = flat_ref[:everyone // CORES, :]
    give_ref[...] = flat_ref[everyone // CORES:, :].astype(bf16)


def merge_kernel(heads, keep_ref, got_ref, out_ref, flat_ref):
    width = heads * V_HEAD
    gap = keep_ref[:, width:] - got_ref[:, width:].astype(f32)
    delta = gap[:, :heads] + (gap[:, heads:2 * heads] + gap[:, 2 * heads:3 * heads])
    share = 1.0 / (1.0 + jnp.exp2(-delta))
    rest = 1.0 / (1.0 + jnp.exp2(delta))
    for j in range(heads):
        lanes = slice(j * V_HEAD, (j + 1) * V_HEAD)
        flat_ref[:, lanes] = (
            keep_ref[:, lanes] * share[:, j:j + 1]
            + got_ref[:, lanes].astype(f32) * rest[:, j:j + 1]
        )
    chips, tokens, _ = out_ref.shape
    here = lax.axis_index("ctx") // CORES
    for chip in range(chips):
        out_ref[here ^ chip] = flat_ref[chip * tokens:(chip + 1) * tokens, :].astype(bf16)


def place_kernel(kept_ref, moved_ref, out_ref):
    here = lax.axis_index("ctx") // CORES
    half, _, width = kept_ref.shape
    for o in range(half):
        for far, ref in enumerate((kept_ref, moved_ref)):
            lanes = pl.ds(pl.multiple_of((here ^ (o + far * half)) * width, width), width)
            out_ref[:, lanes] = ref[o]


VMEM = pl.BlockSpec(memory_space=pltpu.VMEM)
SMEM = pl.BlockSpec(memory_space=pltpu.SMEM)
PARAMS = pltpu.CompilerParams(vmem_limit_bytes=32 * 1024 * 1024)


def shape(*dims, dtype=f32):
    return jax.ShapeDtypeStruct(dims, dtype)


def on_device(ctx, queries, prefix_latents, span_latents, value_up, prefix_length, span_offset):
    slots, width = prefix_latents.shape
    tokens = queries.shape[0]
    all_heads = queries.shape[1] // width
    chips = ctx // CORES
    heads = all_heads // chips
    rows = tokens * heads
    total = rows * ctx
    everyone = tokens * ctx
    walk = chip_cycle(chips)
    spot = np.argsort(np.array(walk))
    steps = chips // 2

    def across(step):
        return [
            (walk[r] * CORES + c, walk[(r + step) % chips] * CORES + c)
            for r in range(chips) for c in range(CORES)
        ]

    other_core = [(d, d ^ 1) for d in range(ctx)]
    same_core = [[p * CORES + c for p in range(chips)] for c in range(CORES)]

    turns = [0]
    for s in range(1, steps):
        turns += [-s, s]
    turns.append(steps)
    owner_table = np.array(
        [[walk[(spot[p] + t) % chips] for t in turns] for p in range(chips)], np.int32
    )
    table = jnp.asarray(owner_table.reshape(-1))
    state_shapes = [shape(total, LANES), shape(total, LANES), shape(total, LATENT)]

    def fold_first(keys):
        return pl.pallas_call(
            functools.partial(first_kernel, heads, len(keys)),
            out_shape=[shape(total, width, dtype=bf16)] + state_shapes,
            in_specs=[SMEM] * 2 + [VMEM] * (2 + len(keys)),
            out_specs=[VMEM] * 4,
            compiler_params=PARAMS,
            name="first",
        )(scal, table, here, there, *keys)

    def fold_more(at, q, state, keys):
        return pl.pallas_call(
            functools.partial(middle_kernel, at, len(keys)),
            out_shape=state_shapes,
            in_specs=[SMEM] * 2 + [VMEM] * (4 + len(keys)),
            out_specs=[VMEM] * 3,
            compiler_params=PARAMS,
            name="middle",
        )(scal, table, q, *state, *keys)

    onward = functools.partial(lax.ppermute, axis_name="ctx", perm=across(1))
    backward = functools.partial(lax.ppermute, axis_name="ctx", perm=across(-1))
    cut = LATENT // 2
    own = prefix_latents.T
    right, left = onward(own), backward(own)

    grouped = queries.reshape(tokens, chips, heads * width).transpose(1, 0, 2)
    spans = jnp.broadcast_to(span_latents[None], (chips, tokens, width))
    pieces = jnp.concatenate([grouped, spans], axis=2)
    scal = jnp.concatenate([prefix_length, span_offset])
    pieces, scal = lax.optimization_barrier((pieces, scal))
    here = lax.all_to_all(
        pieces, "ctx", split_axis=0, concat_axis=0, axis_index_groups=same_core, tiled=True
    )
    far_up = lax.ppermute(value_up, "ctx", other_core)

    keys, state, at = [own, right, left], None, 0
    for s in range(2, steps - 1):
        right, left = onward(right), backward(left)
        keys += [right, left]
        if s == 2:
            here, _, _ = lax.optimization_barrier((here, right, left))
            here = here.reshape(chips * tokens, (heads + 1) * width)
            there = lax.ppermute(here, "ctx", other_core)
            continue
        if state is None:
            q, *state = fold_first(keys[:-2])
        else:
            state = fold_more(at, q, state, keys[:-2])
        at += len(keys) - 2
        keys = keys[-2:]
    right_top, left_bottom = onward(right[:cut]), backward(left[cut:])
    right_bottom, left_top = onward(right[cut:]), backward(left[:cut])
    far_top, far_bottom = onward(right_top), backward(left_bottom)
    if state is None:
        q, *state = fold_first(keys)
    else:
        state = fold_more(at, q, state, keys)
    at += len(keys)
    state = pl.pallas_call(
        functools.partial(halves_kernel, at),
        out_shape=state_shapes,
        in_specs=[SMEM] * 2 + [VMEM] * 8,
        out_specs=[VMEM] * 3,
        scratch_shapes=[pltpu.VMEM((width, slots), bf16)] * 2,
        compiler_params=PARAMS,
        name="halves",
    )(scal, table, q, *state, right_top, right_bottom, left_top, left_bottom)
    keys = [far_top, far_bottom]
    flat = heads * V_HEAD + LANES
    half = everyone // CORES
    keep, give = pl.pallas_call(
        functools.partial(last_kernel, chips - 1, heads),
        out_shape=[shape(half, flat), shape(half, flat, dtype=bf16)],
        in_specs=[SMEM] * 2 + [VMEM] * 8,
        out_specs=[VMEM] * 2,
        scratch_shapes=[
            pltpu.VMEM((width, slots), bf16),
            pltpu.VMEM((total, LANES), f32),
            pltpu.VMEM((total, LANES), f32),
            pltpu.VMEM((total, LATENT), f32),
            pltpu.VMEM((everyone, flat), f32),
        ],
        compiler_params=PARAMS,
        name="last",
    )(scal, table, q, *state, *keys, value_up, far_up)
    got = lax.ppermute(give, "ctx", other_core)
    merged = pl.pallas_call(
        functools.partial(merge_kernel, heads),
        out_shape=shape(chips, tokens, heads * V_HEAD, dtype=bf16),
        in_specs=[VMEM] * 2,
        out_specs=VMEM,
        scratch_shapes=[pltpu.VMEM((half, heads * V_HEAD), f32)],
        compiler_params=PARAMS,
        name="merge",
    )(keep, got)
    slot = [merged[o] for o in range(chips)]
    bit = 1
    while bit < chips:
        away = [o for o in range(chips) if o & bit]
        swap = [(d, d ^ (bit * CORES)) for d in range(ctx)]
        moved = lax.ppermute(jnp.stack([slot[o] for o in away]), "ctx", swap)
        for j, o in enumerate(away):
            slot[o] = moved[j]
        bit *= 2
    return pl.pallas_call(
        place_kernel,
        out_shape=shape(tokens, all_heads * V_HEAD, dtype=bf16),
        in_specs=[VMEM] * 2,
        out_specs=VMEM,
        compiler_params=PARAMS,
        name="place",
    )(jnp.stack(slot[:chips // 2]), moved)


def solution(mesh):
    return jax.shard_map(
        functools.partial(on_device, mesh.shape["ctx"]),
        mesh=mesh,
        in_specs=(
            P(("groups", "ctx"), None),
            P(("groups", "ctx"), None),
            P(("groups", "ctx"), None),
            P("ctx", None, None),
            P("groups"),
            P("groups"),
        ),
        out_specs=P(("groups", "ctx"), None),
        check_vma=False,
    )
```

```python
import functools
import math

import jax
import jax.numpy as jnp
import numpy as np
from jax import lax
from jax.experimental import pallas as pl
from jax.experimental.pallas import tpu as pltpu
from jax.sharding import PartitionSpec as P

LATENT = 512
V_HEAD = 128
CORES = 2
LANES = 128

score_scale = 192.0 ** (-0.5) * math.log2(math.e)
neg_large = -1e30
least_max = -1e29
f32 = jnp.float32
bf16 = jnp.bfloat16


def chip_cycle(chips):
    wide = max(1, int(round(chips ** (1 / 3))))
    tall = chips // wide
    if wide * tall != chips or wide < 2 or tall < 2:
        return list(range(chips))
    walk = []
    for z in range(tall):
        across = range(1, wide) if z % 2 == 0 else range(wide - 1, 0, -1)
        walk += [z * wide + x for x in across]
    return walk + [z * wide for z in reversed(range(tall))]


def fold_shards(q_ref, shards, length, old, new):
    rows = q_ref.shape[0]
    block = min(256, rows)
    for start in range(0, rows, block):
        part = pl.ds(start, block)
        m_old = old[0][part, :][:, :1]
        m_new = m_old
        scores = []
        for base, key_ref in shards:
            slot = base + lax.broadcasted_iota(jnp.int32, (1, key_ref.shape[1]), 1)
            s = jnp.dot(q_ref[part, :], key_ref[...], preferred_element_type=f32) * score_scale
            s = jnp.where(slot < length, s, neg_large)
            m_new = jnp.maximum(m_new, jnp.max(s, axis=1, keepdims=True))
            scores.append(s)
        shrink = jnp.exp2(m_old - m_new)
        l_new = old[1][part, :][:, :1] * shrink
        summed = old[2][part, :] * shrink
        for s, (_, key_ref) in zip(scores, shards):
            probs = jnp.exp2(s - m_new)
            l_new += jnp.sum(probs, axis=1, keepdims=True)
            summed += lax.dot_general(
                probs.astype(bf16), key_ref[:LATENT, :], (((1,), (1,)), ((), ())),
                preferred_element_type=f32,
            )
        new[0][part, :] = jnp.broadcast_to(m_new, (block, LANES))
        new[1][part, :] = jnp.broadcast_to(l_new, (block, LANES))
        new[2][part, :] = summed


def parted(index, size):
    return index >> (size.bit_length() - 1), index & (size - 1)


def token_of(index, tokens, chips):
    device, t = parted(index, tokens)
    core, chip = parted(device, chips)
    return (chip * CORES + ((lax.axis_index("ctx") % CORES) ^ core)) * tokens + t


def with_base(table_ref, at, key_refs):
    me = lax.axis_index("ctx")
    count = table_ref.shape[0] // lax.axis_size("ctx")
    return [
        (table_ref[me * count + at + j] * key_ref.shape[1], key_ref)
        for j, key_ref in enumerate(key_refs)
    ]


def pieces_kernel(queries_ref, span_ref, out_ref):
    chips = out_ref.shape[0]
    part = queries_ref.shape[1] // chips
    for chip in range(chips):
        out_ref[chip, :, :part] = queries_ref[:, chip * part:(chip + 1) * part]
        out_ref[chip, :, part:] = span_ref[...]


def first_kernel(heads, count, length_ref, offset_ref, table_ref, here_ref, there_ref, *rest):
    keys, (q_ref, m_ref, l_ref, acc_ref) = rest[:count], rest[count:]
    chips = lax.axis_size("ctx") // CORES
    half = here_ref.shape[0]
    tokens = half // chips
    width = q_ref.shape[1]
    for core, piece_ref in enumerate((here_ref, there_ref)):
        for head in range(heads):
            row = (head * CORES + core) * half
            q_ref[row:row + half, :] = piece_ref[:, head * width:(head + 1) * width]
    span = here_ref[:, heads * width:]
    total = q_ref.shape[0]
    block = min(256, total)
    key_index = lax.broadcasted_iota(jnp.int32, (1, span.shape[0]), 1)
    key_token = token_of(key_index, tokens, chips)
    for start in range(0, total, block):
        part = pl.ds(start, block)
        s = lax.dot_general(
            q_ref[part, :], span, (((1,), (1,)), ((), ())), preferred_element_type=f32
        ) * score_scale
        row_index = start + lax.broadcasted_iota(jnp.int32, (block, 1), 0)
        row_token = token_of(row_index & (half * CORES - 1), tokens, chips)
        shown = (key_token >= offset_ref[0]) & (key_token <= row_token)
        s = jnp.where(shown, s, neg_large)
        m_new = jnp.maximum(jnp.max(s, axis=1, keepdims=True), least_max)
        probs = jnp.exp2(s - m_new)
        l_new = jnp.sum(probs, axis=1, keepdims=True)
        acc_ref[part, :] = jnp.dot(
            probs.astype(bf16), span[:, :LATENT], preferred_element_type=f32
        )
        m_ref[part, :] = jnp.broadcast_to(m_new, (block, LANES))
        l_ref[part, :] = jnp.broadcast_to(l_new, (block, LANES))
    state = (m_ref, l_ref, acc_ref)
    fold_shards(q_ref, with_base(table_ref, 0, keys), length_ref[0], state, state)


def middle_kernel(at, count, length_ref, table_ref, q_ref, m_in, l_in, acc_in, *rest):
    keys, new = rest[:count], rest[count:]
    fold_shards(q_ref, with_base(table_ref, at, keys), length_ref[0], (m_in, l_in, acc_in), new)


def last_kernel(at, heads, length_ref, table_ref, q_ref, m_in, l_in, acc_in,
                top_ref, bottom_ref, own_up, far_up, keep_ref, give_ref,
                key_ref, m_ref, l_ref, acc_ref, flat_ref):
    cut = top_ref.shape[0]
    key_ref[:cut, :] = top_ref[...]
    key_ref[cut:, :] = bottom_ref[...]
    middle_kernel(at, 1, length_ref, table_ref, q_ref, m_in, l_in, acc_in,
                  key_ref, m_ref, l_ref, acc_ref)
    acc_ref[...] = acc_ref[...] / l_ref[:, :1]
    m_ref[...] = m_ref[...] + jnp.log2(l_ref[...])
    everyone = flat_ref.shape[0]
    core = lax.axis_index("ctx") % CORES
    per_core = heads // CORES
    tail = jnp.zeros((everyone, LANES), f32)
    lane = lax.broadcasted_iota(jnp.int32, (everyone, LANES), 1)
    pair = min(2, per_core)
    for side, up_ref in enumerate((own_up, far_up)):
        for j in range(0, per_core, pair):
            first_head = (core ^ side) * per_core + j
            contexts = []
            for head in [first_head + i for i in range(pair)]:
                rows = pl.ds(pl.multiple_of(head * everyone, everyone), everyone)
                contexts.append(acc_ref[rows, :].astype(bf16))
                weight = m_ref[rows, :]
                high = weight.astype(bf16).astype(f32)
                mid = (weight - high).astype(bf16).astype(f32)
                low = weight - high - mid
                tail = jnp.where(lane == head, high, tail)
                tail = jnp.where(lane == head + heads, mid, tail)
                tail = jnp.where(lane == head + 2 * heads, low, tail)
            lifted = jnp.dot(
                jnp.concatenate(contexts, axis=0),
                jnp.concatenate([up_ref[j + i] for i in range(pair)], axis=1),
                preferred_element_type=f32,
            )
            for i in range(pair):
                lanes = pl.ds(pl.multiple_of((first_head + i) * V_HEAD, V_HEAD), V_HEAD)
                flat_ref[:, lanes] = lifted[
                    i * everyone:(i + 1) * everyone, i * V_HEAD:(i + 1) * V_HEAD
                ]
    flat_ref[:, heads * V_HEAD:] = tail
    keep_ref[...] = flat_ref[:everyone // CORES, :]
    give_ref[...] = flat_ref[everyone // CORES:, :].astype(bf16)


def merge_kernel(heads, keep_ref, got_ref, out_ref, flat_ref):
    width = heads * V_HEAD
    gap = keep_ref[:, width:] - got_ref[:, width:].astype(f32)
    delta = gap[:, :heads] + (gap[:, heads:2 * heads] + gap[:, 2 * heads:3 * heads])
    share = 1.0 / (1.0 + jnp.exp2(-delta))
    rest = 1.0 / (1.0 + jnp.exp2(delta))
    for j in range(heads):
        lanes = slice(j * V_HEAD, (j + 1) * V_HEAD)
        flat_ref[:, lanes] = (
            keep_ref[:, lanes] * share[:, j:j + 1]
            + got_ref[:, lanes].astype(f32) * rest[:, j:j + 1]
        )
    chips, tokens, _ = out_ref.shape
    for chip in range(chips):
        out_ref[chip] = flat_ref[chip * tokens:(chip + 1) * tokens, :].astype(bf16)


VMEM = pl.BlockSpec(memory_space=pltpu.VMEM)
SMEM = pl.BlockSpec(memory_space=pltpu.SMEM)
PARAMS = pltpu.CompilerParams(vmem_limit_bytes=32 * 1024 * 1024)


def shape(*dims, dtype=f32):
    return jax.ShapeDtypeStruct(dims, dtype)


def on_device(ctx, queries, prefix_latents, span_latents, value_up, prefix_length, span_offset):
    slots, width = prefix_latents.shape
    tokens = queries.shape[0]
    all_heads = queries.shape[1] // width
    chips = ctx // CORES
    heads = all_heads // chips
    rows = tokens * heads
    total = rows * ctx
    everyone = tokens * ctx
    walk = chip_cycle(chips)
    spot = np.argsort(np.array(walk))
    steps = chips // 2

    def across(step):
        return [
            (walk[r] * CORES + c, walk[(r + (-step if c else step)) % chips] * CORES + c)
            for r in range(chips) for c in range(CORES)
        ]

    other_core = [(d, d ^ 1) for d in range(ctx)]
    same_core = [[p * CORES + c for p in range(chips)] for c in range(CORES)]

    turns = [0]
    for s in range(1, steps):
        turns += [-s, s]
    turns.append(steps)
    owner_table = np.array(
        [
            [walk[(spot[p] + (-t if c else t)) % chips] * CORES + c for t in turns]
            for p in range(chips) for c in range(CORES)
        ],
        np.int32,
    )
    table = jnp.asarray(owner_table.reshape(-1))
    state_shapes = [shape(total, LANES), shape(total, LANES), shape(total, LATENT)]

    def fold_first(keys):
        return pl.pallas_call(
            functools.partial(first_kernel, heads, len(keys)),
            out_shape=[shape(total, width, dtype=bf16)] + state_shapes,
            in_specs=[SMEM] * 3 + [VMEM] * (2 + len(keys)),
            out_specs=[VMEM] * 4,
            compiler_params=PARAMS,
            name="first",
        )(prefix_length, span_offset, table, here, there, *keys)

    def fold_more(at, q, state, keys):
        return pl.pallas_call(
            functools.partial(middle_kernel, at, len(keys)),
            out_shape=state_shapes,
            in_specs=[SMEM] * 2 + [VMEM] * (4 + len(keys)),
            out_specs=[VMEM] * 3,
            compiler_params=PARAMS,
            name="middle",
        )(prefix_length, table, q, *state, *keys)

    onward = functools.partial(lax.ppermute, axis_name="ctx", perm=across(1))
    backward = functools.partial(lax.ppermute, axis_name="ctx", perm=across(-1))
    cut = LATENT // 2
    own = prefix_latents.T
    right, left = onward(own), backward(own)

    pieces = pl.pallas_call(
        pieces_kernel,
        out_shape=shape(chips, tokens, (heads + 1) * width, dtype=bf16),
        in_specs=[VMEM] * 2,
        out_specs=VMEM,
        compiler_params=PARAMS,
        name="pieces",
    )(queries, span_latents)
    here = lax.all_to_all(
        pieces, "ctx", split_axis=0, concat_axis=0, axis_index_groups=same_core, tiled=True
    )
    far_up = lax.ppermute(value_up, "ctx", other_core)

    keys, state, at = [own, right, left], None, 0
    for s in range(2, steps):
        right, left = onward(right), backward(left)
        keys += [right, left]
        if s == 2:
            right, left, here = lax.optimization_barrier((right, left, here))
            keys[-2:] = right, left
            here = here.reshape(chips * tokens, (heads + 1) * width)
            there = lax.ppermute(here, "ctx", other_core)
            continue
        if state is None:
            q, *state = fold_first(keys[:-2])
        else:
            state = fold_more(at, q, state, keys[:-2])
        at += len(keys) - 2
        keys = keys[-2:]
    right, left, state = lax.optimization_barrier((right, left, state))
    right, left = onward(right[:cut]), backward(left[cut:])
    state = fold_more(at, q, state, keys)
    keys = [right, left]
    flat = heads * V_HEAD + LANES
    half = everyone // CORES
    keep, give = pl.pallas_call(
        functools.partial(last_kernel, chips - 1, heads),
        out_shape=[shape(half, flat), shape(half, flat, dtype=bf16)],
        in_specs=[SMEM] * 2 + [VMEM] * 8,
        out_specs=[VMEM] * 2,
        scratch_shapes=[
            pltpu.VMEM((width, slots), bf16),
            pltpu.VMEM((total, LANES), f32),
            pltpu.VMEM((total, LANES), f32),
            pltpu.VMEM((total, LATENT), f32),
            pltpu.VMEM((everyone, flat), f32),
        ],
        compiler_params=PARAMS,
        name="last",
    )(prefix_length, table, q, *state, *keys, value_up, far_up)
    got = lax.ppermute(give, "ctx", other_core)
    merged = pl.pallas_call(
        functools.partial(merge_kernel, heads),
        out_shape=shape(chips, tokens, heads * V_HEAD, dtype=bf16),
        in_specs=[VMEM] * 2,
        out_specs=VMEM,
        scratch_shapes=[pltpu.VMEM((half, heads * V_HEAD), f32)],
        compiler_params=PARAMS,
        name="merge",
    )(keep, got)
    returned = lax.all_to_all(
        merged, "ctx", split_axis=0, concat_axis=0, axis_index_groups=same_core, tiled=True
    )
    return returned.transpose(1, 0, 2).reshape(tokens, all_heads * V_HEAD)


def solution(mesh):
    return jax.shard_map(
        functools.partial(on_device, mesh.shape["ctx"]),
        mesh=mesh,
        in_specs=(
            P(("groups", "ctx"), None),
            P(("groups", "ctx"), None),
            P(("groups", "ctx"), None),
            P("ctx", None, None),
            P("groups"),
            P("groups"),
        ),
        out_specs=P(("groups", "ctx"), None),
        check_vma=False,
    )
```

```python
import functools
import math

import jax
import jax.numpy as jnp
import numpy as np
from jax import lax
from jax.experimental import pallas as pl
from jax.experimental.pallas import tpu as pltpu
from jax.sharding import PartitionSpec as P

LATENT = 512
V_HEAD = 128
CORES = 2
LANES = 128

score_scale = 192.0 ** (-0.5) * math.log2(math.e)
neg_large = -1e30
least_max = -1e29
f32 = jnp.float32
bf16 = jnp.bfloat16


def chip_cycle(chips):
    wide = max(1, int(round(chips ** (1 / 3))))
    tall = chips // wide
    if wide * tall != chips or wide < 2 or tall < 2:
        return list(range(chips))
    walk = []
    for z in range(tall):
        across = range(1, wide) if z % 2 == 0 else range(wide - 1, 0, -1)
        walk += [z * wide + x for x in across]
    return walk + [z * wide for z in reversed(range(tall))]


def fold_shards(q_ref, shards, length, old, new):
    rows = q_ref.shape[0]
    block = min(256, rows)
    for start in range(0, rows, block):
        part = pl.ds(start, block)
        m_old = old[0][part, :][:, :1]
        m_new = m_old
        scores = []
        for base, key_ref in shards:
            slot = base + lax.broadcasted_iota(jnp.int32, (1, key_ref.shape[1]), 1)
            s = jnp.dot(q_ref[part, :], key_ref[...], preferred_element_type=f32) * score_scale
            s = jnp.where(slot < length, s, neg_large)
            m_new = jnp.maximum(m_new, jnp.max(s, axis=1, keepdims=True))
            scores.append(s)
        shrink = jnp.exp2(m_old - m_new)
        l_new = old[1][part, :][:, :1] * shrink
        summed = old[2][part, :] * shrink
        for s, (_, key_ref) in zip(scores, shards):
            probs = jnp.exp2(s - m_new)
            l_new += jnp.sum(probs, axis=1, keepdims=True)
            summed += lax.dot_general(
                probs.astype(bf16), key_ref[:LATENT, :], (((1,), (1,)), ((), ())),
                preferred_element_type=f32,
            )
        new[0][part, :] = jnp.broadcast_to(m_new, (block, LANES))
        new[1][part, :] = jnp.broadcast_to(l_new, (block, LANES))
        new[2][part, :] = summed


def parted(index, size):
    return index >> (size.bit_length() - 1), index & (size - 1)


def token_of(index, tokens, chips):
    device, t = parted(index, tokens)
    core, chip = parted(device, chips)
    return (chip * CORES + ((lax.axis_index("ctx") % CORES) ^ core)) * tokens + t


def with_base(table_ref, at, key_refs):
    me = lax.axis_index("ctx")
    count = table_ref.shape[0] // lax.axis_size("ctx")
    return [
        (table_ref[me * count + at + j] * key_ref.shape[1], key_ref)
        for j, key_ref in enumerate(key_refs)
    ]


def pieces_kernel(queries_ref, span_ref, out_ref):
    chips = out_ref.shape[0]
    part = queries_ref.shape[1] // chips
    for chip in range(chips):
        out_ref[chip, :, :part] = queries_ref[:, chip * part:(chip + 1) * part]
        out_ref[chip, :, part:] = span_ref[...]


def first_kernel(heads, count, length_ref, offset_ref, table_ref, here_ref, there_ref, *rest):
    keys, (q_ref, m_ref, l_ref, acc_ref) = rest[:count], rest[count:]
    chips = lax.axis_size("ctx") // CORES
    half = here_ref.shape[0]
    tokens = half // chips
    width = q_ref.shape[1]
    for core, piece_ref in enumerate((here_ref, there_ref)):
        for head in range(heads):
            row = (head * CORES + core) * half
            q_ref[row:row + half, :] = piece_ref[:, head * width:(head + 1) * width]
    span = here_ref[:, heads * width:]
    total = q_ref.shape[0]
    block = min(256, total)
    key_index = lax.broadcasted_iota(jnp.int32, (1, span.shape[0]), 1)
    key_token = token_of(key_index, tokens, chips)
    for start in range(0, total, block):
        part = pl.ds(start, block)
        s = lax.dot_general(
            q_ref[part, :], span, (((1,), (1,)), ((), ())), preferred_element_type=f32
        ) * score_scale
        row_index = start + lax.broadcasted_iota(jnp.int32, (block, 1), 0)
        row_token = token_of(row_index & (half * CORES - 1), tokens, chips)
        shown = (key_token >= offset_ref[...]) & (key_token <= row_token)
        s = jnp.where(shown, s, neg_large)
        m_new = jnp.maximum(jnp.max(s, axis=1, keepdims=True), least_max)
        probs = jnp.exp2(s - m_new)
        l_new = jnp.sum(probs, axis=1, keepdims=True)
        acc_ref[part, :] = jnp.dot(
            probs.astype(bf16), span[:, :LATENT], preferred_element_type=f32
        )
        m_ref[part, :] = jnp.broadcast_to(m_new, (block, LANES))
        l_ref[part, :] = jnp.broadcast_to(l_new, (block, LANES))
    state = (m_ref, l_ref, acc_ref)
    fold_shards(q_ref, with_base(table_ref, 0, keys), length_ref[...], state, state)


def middle_kernel(at, count, length_ref, table_ref, q_ref, m_in, l_in, acc_in, *rest):
    keys, new = rest[:count], rest[count:]
    fold_shards(q_ref, with_base(table_ref, at, keys), length_ref[...], (m_in, l_in, acc_in), new)


def last_kernel(at, heads, length_ref, table_ref, q_ref, m_in, l_in, acc_in,
                key_ref, own_up, far_up, keep_ref, give_ref,
                m_ref, l_ref, acc_ref, flat_ref):
    middle_kernel(at, 1, length_ref, table_ref, q_ref, m_in, l_in, acc_in,
                  key_ref, m_ref, l_ref, acc_ref)
    acc_ref[...] = acc_ref[...] / l_ref[:, :1]
    m_ref[...] = m_ref[...] + jnp.log2(l_ref[...])
    everyone = flat_ref.shape[0]
    core = lax.axis_index("ctx") % CORES
    per_core = heads // CORES
    tail = jnp.zeros((everyone, LANES), f32)
    lane = lax.broadcasted_iota(jnp.int32, (everyone, LANES), 1)
    pair = min(2, per_core)
    for side, up_ref in enumerate((own_up, far_up)):
        for j in range(0, per_core, pair):
            first_head = (core ^ side) * per_core + j
            contexts = []
            for head in [first_head + i for i in range(pair)]:
                rows = pl.ds(pl.multiple_of(head * everyone, everyone), everyone)
                contexts.append(acc_ref[rows, :].astype(bf16))
                weight = m_ref[rows, :]
                high = weight.astype(bf16).astype(f32)
                mid = (weight - high).astype(bf16).astype(f32)
                low = weight - high - mid
                tail = jnp.where(lane == head, high, tail)
                tail = jnp.where(lane == head + heads, mid, tail)
                tail = jnp.where(lane == head + 2 * heads, low, tail)
            lifted = jnp.dot(
                jnp.concatenate(contexts, axis=0),
                jnp.concatenate([up_ref[j + i] for i in range(pair)], axis=1),
                preferred_element_type=f32,
            )
            for i in range(pair):
                lanes = pl.ds(pl.multiple_of((first_head + i) * V_HEAD, V_HEAD), V_HEAD)
                flat_ref[:, lanes] = lifted[
                    i * everyone:(i + 1) * everyone, i * V_HEAD:(i + 1) * V_HEAD
                ]
    flat_ref[:, heads * V_HEAD:] = tail
    keep_ref[...] = flat_ref[:everyone // CORES, :]
    give_ref[...] = flat_ref[everyone // CORES:, :].astype(bf16)


def merge_kernel(heads, keep_ref, got_ref, out_ref, flat_ref):
    width = heads * V_HEAD
    gap = keep_ref[:, width:] - got_ref[:, width:].astype(f32)
    delta = gap[:, :heads] + (gap[:, heads:2 * heads] + gap[:, 2 * heads:3 * heads])
    share = 1.0 / (1.0 + jnp.exp2(-delta))
    rest = 1.0 / (1.0 + jnp.exp2(delta))
    for j in range(heads):
        lanes = slice(j * V_HEAD, (j + 1) * V_HEAD)
        flat_ref[:, lanes] = (
            keep_ref[:, lanes] * share[:, j:j + 1]
            + got_ref[:, lanes].astype(f32) * rest[:, j:j + 1]
        )
    chips, tokens, _ = out_ref.shape
    for chip in range(chips):
        out_ref[chip] = flat_ref[chip * tokens:(chip + 1) * tokens, :].astype(bf16)


VMEM = pl.BlockSpec(memory_space=pltpu.VMEM)
SMEM = pl.BlockSpec(memory_space=pltpu.SMEM)
PARAMS = pltpu.CompilerParams(vmem_limit_bytes=32 * 1024 * 1024)


def shape(*dims, dtype=f32):
    return jax.ShapeDtypeStruct(dims, dtype)


def on_device(ctx, queries, prefix_latents, span_latents, value_up, prefix_length, span_offset):
    slots, width = prefix_latents.shape
    tokens = queries.shape[0]
    all_heads = queries.shape[1] // width
    chips = ctx // CORES
    heads = all_heads // chips
    rows = tokens * heads
    total = rows * ctx
    everyone = tokens * ctx
    walk = chip_cycle(chips)
    spot = np.argsort(np.array(walk))
    steps = chips // 2

    def across(step):
        return [
            (walk[r] * CORES + c, walk[(r + (-step if c else step)) % chips] * CORES + c)
            for r in range(chips) for c in range(CORES)
        ]

    other_core = [(d, d ^ 1) for d in range(ctx)]
    same_core = [[p * CORES + c for p in range(chips)] for c in range(CORES)]

    turns = [0]
    for s in range(1, steps):
        turns += [-s, s]
    turns.append(steps)
    owner_table = np.array(
        [
            [walk[(spot[p] + (-t if c else t)) % chips] * CORES + c for t in turns]
            for p in range(chips) for c in range(CORES)
        ],
        np.int32,
    )
    table = jnp.asarray(owner_table.reshape(-1))
    length, offset = prefix_length.reshape(1, 1), span_offset.reshape(1, 1)
    state_shapes = [shape(total, LANES), shape(total, LANES), shape(total, LATENT)]

    def fold_first(keys):
        return pl.pallas_call(
            functools.partial(first_kernel, heads, len(keys)),
            out_shape=[shape(total, width, dtype=bf16)] + state_shapes,
            in_specs=[VMEM, VMEM, SMEM] + [VMEM] * (2 + len(keys)),
            out_specs=[VMEM] * 4,
            compiler_params=PARAMS,
            name="first",
        )(length, offset, table, here, there, *keys)

    def fold_more(at, q, state, keys):
        return pl.pallas_call(
            functools.partial(middle_kernel, at, len(keys)),
            out_shape=state_shapes,
            in_specs=[VMEM, SMEM] + [VMEM] * (4 + len(keys)),
            out_specs=[VMEM] * 3,
            compiler_params=PARAMS,
            name="middle",
        )(length, table, q, *state, *keys)

    onward = functools.partial(lax.ppermute, axis_name="ctx", perm=across(1))
    backward = functools.partial(lax.ppermute, axis_name="ctx", perm=across(-1))
    own = prefix_latents.T
    right, left = onward(own), backward(own)

    pieces = pl.pallas_call(
        pieces_kernel,
        out_shape=shape(chips, tokens, (heads + 1) * width, dtype=bf16),
        in_specs=[VMEM] * 2,
        out_specs=VMEM,
        compiler_params=PARAMS,
        name="pieces",
    )(queries, span_latents)
    here = lax.all_to_all(
        pieces, "ctx", split_axis=0, concat_axis=0, axis_index_groups=same_core, tiled=True
    )
    far_up = lax.ppermute(value_up, "ctx", other_core)

    keys, state, at = [own, right, left], None, 0
    for s in range(2, steps):
        right, left = onward(right), backward(left)
        if s == 2:
            here, right = lax.optimization_barrier((here, right))
            here = here.reshape(chips * tokens, (heads + 1) * width)
            there = lax.ppermute(here, "ctx", other_core)
            keys += [right, left]
            continue
        if state is None:
            q, *state = fold_first(keys)
        else:
            state = fold_more(at, q, state, keys)
        at += len(keys)
        keys = [right, left]
    right, state = lax.optimization_barrier((right, state))
    right = onward(right)
    state = fold_more(at, q, state, keys)
    flat = heads * V_HEAD + LANES
    half = everyone // CORES
    keep, give = pl.pallas_call(
        functools.partial(last_kernel, chips - 1, heads),
        out_shape=[shape(half, flat), shape(half, flat, dtype=bf16)],
        in_specs=[VMEM, SMEM] + [VMEM] * 7,
        out_specs=[VMEM] * 2,
        scratch_shapes=[
            pltpu.VMEM((total, LANES), f32),
            pltpu.VMEM((total, LANES), f32),
            pltpu.VMEM((total, LATENT), f32),
            pltpu.VMEM((everyone, flat), f32),
        ],
        compiler_params=PARAMS,
        name="last",
    )(length, table, q, *state, right, value_up, far_up)
    got = lax.ppermute(give, "ctx", other_core)
    merged = pl.pallas_call(
        functools.partial(merge_kernel, heads),
        out_shape=shape(chips, tokens, heads * V_HEAD, dtype=bf16),
        in_specs=[VMEM] * 2,
        out_specs=VMEM,
        scratch_shapes=[pltpu.VMEM((half, heads * V_HEAD), f32)],
        compiler_params=PARAMS,
        name="merge",
    )(keep, got)
    returned = lax.all_to_all(
        merged, "ctx", split_axis=0, concat_axis=0, axis_index_groups=same_core, tiled=True
    )
    return returned.transpose(1, 0, 2).reshape(tokens, all_heads * V_HEAD)


def solution(mesh):
    return jax.shard_map(
        functools.partial(on_device, mesh.shape["ctx"]),
        mesh=mesh,
        in_specs=(
            P(("groups", "ctx"), None),
            P(("groups", "ctx"), None),
            P(("groups", "ctx"), None),
            P("ctx", None, None),
            P("groups"),
            P("groups"),
        ),
        out_specs=P(("groups", "ctx"), None),
        check_vma=False,
    )
```

```python
import functools
import math

import jax
import jax.numpy as jnp
import numpy as np
from jax import lax
from jax.experimental import pallas as pl
from jax.experimental.pallas import tpu as pltpu
from jax.sharding import PartitionSpec as P

LATENT = 512
V_HEAD = 128
CORES = 2
LANES = 128

score_scale = 192.0 ** (-0.5) * math.log2(math.e)
neg_large = -1e30
least_max = -1e29
f32 = jnp.float32
bf16 = jnp.bfloat16


def chip_cycle(chips):
    wide = max(1, int(round(chips ** (1 / 3))))
    tall = chips // wide
    if wide * tall != chips or wide < 2 or tall < 2:
        return list(range(chips))
    walk = []
    for z in range(tall):
        across = range(1, wide) if z % 2 == 0 else range(wide - 1, 0, -1)
        walk += [z * wide + x for x in across]
    return walk + [z * wide for z in reversed(range(tall))]


def fold_block(part, q_ref, shards, length, old):
    m_old = old[0][part, :][:, :1]
    m_new = m_old
    scores = []
    for base, key_ref in shards:
        slot = base + lax.broadcasted_iota(jnp.int32, (1, key_ref.shape[1]), 1)
        s = jnp.dot(q_ref[part, :], key_ref[...], preferred_element_type=f32) * score_scale
        s = jnp.where(slot < length, s, neg_large)
        m_new = jnp.maximum(m_new, jnp.max(s, axis=1, keepdims=True))
        scores.append(s)
    shrink = jnp.exp2(m_old - m_new)
    l_new = old[1][part, :][:, :1] * shrink
    summed = old[2][part, :] * shrink
    for s, (_, key_ref) in zip(scores, shards):
        probs = jnp.exp2(s - m_new)
        l_new += jnp.sum(probs, axis=1, keepdims=True)
        summed += lax.dot_general(
            probs.astype(bf16), key_ref[:LATENT, :], (((1,), (1,)), ((), ())),
            preferred_element_type=f32,
        )
    return m_new, l_new, summed


def fold_shards(q_ref, shards, length, old, new):
    rows = q_ref.shape[0]
    block = min(256, rows)
    for start in range(0, rows, block):
        part = pl.ds(start, block)
        m_new, l_new, summed = fold_block(part, q_ref, shards, length, old)
        new[0][part, :] = jnp.broadcast_to(m_new, (block, LANES))
        new[1][part, :] = jnp.broadcast_to(l_new, (block, LANES))
        new[2][part, :] = summed


def parted(index, size):
    return index >> (size.bit_length() - 1), index & (size - 1)


def token_of(index, tokens, chips):
    device, t = parted(index, tokens)
    core, chip = parted(device, chips)
    return (chip * CORES + ((lax.axis_index("ctx") % CORES) ^ core)) * tokens + t


def with_base(table_ref, at, key_refs):
    me = lax.axis_index("ctx")
    count = table_ref.shape[0] // lax.axis_size("ctx")
    return [
        (table_ref[me * count + at + j] * key_ref.shape[1], key_ref)
        for j, key_ref in enumerate(key_refs)
    ]


def pieces_kernel(queries_hbm, span_hbm, out_ref, queries_ref, span_ref, sems):
    copies = [
        pltpu.make_async_copy(queries_hbm, queries_ref, sems.at[0]),
        pltpu.make_async_copy(span_hbm, span_ref, sems.at[1]),
    ]
    for copy in copies:
        copy.start()
    for copy in copies:
        copy.wait()
    chips = out_ref.shape[0]
    part = queries_ref.shape[1] // chips
    for chip in range(chips):
        out_ref[chip, :, :part] = queries_ref[:, chip * part:(chip + 1) * part]
        out_ref[chip, :, part:] = span_ref[...]


def first_kernel(heads, count, length_ref, offset_ref, table_ref, here_ref, there_ref, *rest):
    keys, (q_ref, m_ref, l_ref, acc_ref) = rest[:count], rest[count:]
    chips = lax.axis_size("ctx") // CORES
    half = here_ref.shape[0]
    tokens = half // chips
    width = q_ref.shape[1]
    for core, piece_ref in enumerate((here_ref, there_ref)):
        for head in range(heads):
            row = (head * CORES + core) * half
            q_ref[row:row + half, :] = piece_ref[:, head * width:(head + 1) * width]
    span = here_ref[:, heads * width:]
    total = q_ref.shape[0]
    block = min(256, total)
    key_index = lax.broadcasted_iota(jnp.int32, (1, span.shape[0]), 1)
    key_token = token_of(key_index, tokens, chips)
    for start in range(0, total, block):
        part = pl.ds(start, block)
        s = lax.dot_general(
            q_ref[part, :], span, (((1,), (1,)), ((), ())), preferred_element_type=f32
        ) * score_scale
        row_index = start + lax.broadcasted_iota(jnp.int32, (block, 1), 0)
        row_token = token_of(row_index & (half * CORES - 1), tokens, chips)
        shown = (key_token >= offset_ref[0]) & (key_token <= row_token)
        s = jnp.where(shown, s, neg_large)
        m_new = jnp.maximum(jnp.max(s, axis=1, keepdims=True), least_max)
        probs = jnp.exp2(s - m_new)
        l_new = jnp.sum(probs, axis=1, keepdims=True)
        acc_ref[part, :] = jnp.dot(
            probs.astype(bf16), span[:, :LATENT], preferred_element_type=f32
        )
        m_ref[part, :] = jnp.broadcast_to(m_new, (block, LANES))
        l_ref[part, :] = jnp.broadcast_to(l_new, (block, LANES))
    state = (m_ref, l_ref, acc_ref)
    fold_shards(q_ref, with_base(table_ref, 0, keys), length_ref[0], state, state)


def middle_kernel(at, count, length_ref, table_ref, q_ref, m_in, l_in, acc_in, *rest):
    keys, new = rest[:count], rest[count:]
    fold_shards(q_ref, with_base(table_ref, at, keys), length_ref[0], (m_in, l_in, acc_in), new)


def last_kernel(at, heads, length_ref, table_ref, q_ref, m_ref, l_ref, acc_ref,
                key_ref, own_up, far_up, keep_ref, give_ref, flat_ref):
    core = lax.axis_index("ctx") % CORES
    shards = with_base(table_ref, at, (key_ref,))
    everyone = flat_ref.shape[0]
    per_core = heads // CORES
    rows = per_core * everyone
    pair = min(2, per_core)
    tail = jnp.zeros((everyone, LANES), f32)
    lane = lax.broadcasted_iota(jnp.int32, (everyone, LANES), 1)
    for side, up_ref in enumerate((own_up, far_up)):
        part = pl.ds(pl.multiple_of((core ^ side) * rows, rows), rows)
        m_new, l_new, summed = fold_block(
            part, q_ref, shards, length_ref[0], (m_ref, l_ref, acc_ref)
        )
        context = (summed * (1.0 / l_new)).astype(bf16)
        weight = m_new + jnp.log2(l_new)
        high = weight.astype(bf16).astype(f32)
        mid = (weight - high).astype(bf16).astype(f32)
        low = weight - high - mid
        for j in range(0, per_core, pair):
            lifted = jnp.dot(
                context[j * everyone:(j + pair) * everyone, :],
                jnp.concatenate([up_ref[j + i] for i in range(pair)], axis=1),
                preferred_element_type=f32,
            )
            for i in range(pair):
                head = (core ^ side) * per_core + j + i
                here = slice((j + i) * everyone, (j + i + 1) * everyone)
                tail = jnp.where(lane == head, high[here], tail)
                tail = jnp.where(lane == head + heads, mid[here], tail)
                tail = jnp.where(lane == head + 2 * heads, low[here], tail)
                lanes = pl.ds(pl.multiple_of(head * V_HEAD, V_HEAD), V_HEAD)
                flat_ref[:, lanes] = lifted[
                    i * everyone:(i + 1) * everyone, i * V_HEAD:(i + 1) * V_HEAD
                ]
    flat_ref[:, heads * V_HEAD:] = tail
    keep_ref[...] = flat_ref[:everyone // CORES, :]
    give_ref[...] = flat_ref[everyone // CORES:, :].astype(bf16)


def merge_kernel(heads, keep_ref, got_ref, out_ref, flat_ref):
    width = heads * V_HEAD
    gap = keep_ref[:, width:] - got_ref[:, width:].astype(f32)
    delta = gap[:, :heads] + (gap[:, heads:2 * heads] + gap[:, 2 * heads:3 * heads])
    share = 1.0 / (1.0 + jnp.exp2(-delta))
    rest = 1.0 / (1.0 + jnp.exp2(delta))
    for j in range(heads):
        lanes = slice(j * V_HEAD, (j + 1) * V_HEAD)
        flat_ref[:, lanes] = (
            keep_ref[:, lanes] * share[:, j:j + 1]
            + got_ref[:, lanes].astype(f32) * rest[:, j:j + 1]
        )
    chips, tokens, _ = out_ref.shape
    for chip in range(chips):
        out_ref[chip] = flat_ref[chip * tokens:(chip + 1) * tokens, :].astype(bf16)


VMEM = pl.BlockSpec(memory_space=pltpu.VMEM)
SMEM = pl.BlockSpec(memory_space=pltpu.SMEM)
PARAMS = pltpu.CompilerParams(vmem_limit_bytes=32 * 1024 * 1024)


def shape(*dims, dtype=f32):
    return jax.ShapeDtypeStruct(dims, dtype)


def on_device(ctx, queries, prefix_latents, span_latents, value_up, prefix_length, span_offset):
    slots, width = prefix_latents.shape
    tokens = queries.shape[0]
    all_heads = queries.shape[1] // width
    chips = ctx // CORES
    heads = all_heads // chips
    rows = tokens * heads
    total = rows * ctx
    everyone = tokens * ctx
    walk = chip_cycle(chips)
    spot = np.argsort(np.array(walk))
    steps = chips // 2

    def across(step):
        return [
            (walk[r] * CORES + c, walk[(r + (-step if c else step)) % chips] * CORES + c)
            for r in range(chips) for c in range(CORES)
        ]

    other_core = [(d, d ^ 1) for d in range(ctx)]
    same_core = [[p * CORES + c for p in range(chips)] for c in range(CORES)]

    turns = [0]
    for s in range(1, steps):
        turns += [-s, s]
    turns.append(steps)
    owner_table = np.array(
        [
            [walk[(spot[p] + (-t if c else t)) % chips] * CORES + c for t in turns]
            for p in range(chips) for c in range(CORES)
        ],
        np.int32,
    )
    table = jnp.asarray(owner_table.reshape(-1))
    state_shapes = [shape(total, LANES), shape(total, LANES), shape(total, LATENT)]

    def fold_first(keys):
        return pl.pallas_call(
            functools.partial(first_kernel, heads, len(keys)),
            out_shape=[shape(total, width, dtype=bf16)] + state_shapes,
            in_specs=[SMEM] * 3 + [VMEM] * (2 + len(keys)),
            out_specs=[VMEM] * 4,
            compiler_params=PARAMS,
            name="first",
        )(prefix_length, span_offset, table, here, there, *keys)

    def fold_more(at, q, state, keys):
        return pl.pallas_call(
            functools.partial(middle_kernel, at, len(keys)),
            out_shape=state_shapes,
            in_specs=[SMEM] * 2 + [VMEM] * (4 + len(keys)),
            out_specs=[VMEM] * 3,
            compiler_params=PARAMS,
            name="middle",
        )(prefix_length, table, q, *state, *keys)

    onward = functools.partial(lax.ppermute, axis_name="ctx", perm=across(1))
    backward = functools.partial(lax.ppermute, axis_name="ctx", perm=across(-1))
    own = prefix_latents.T
    right, left = onward(own), backward(own)

    anywhere = pl.BlockSpec(memory_space=pl.ANY)
    pieces = pl.pallas_call(
        pieces_kernel,
        out_shape=shape(chips, tokens, (heads + 1) * width, dtype=bf16),
        in_specs=[anywhere] * 2,
        out_specs=VMEM,
        scratch_shapes=[
            pltpu.VMEM(queries.shape, bf16),
            pltpu.VMEM(span_latents.shape, bf16),
            pltpu.SemaphoreType.DMA((2,)),
        ],
        compiler_params=pltpu.CompilerParams(vmem_limit_bytes=56 * 1024 * 1024),
        name="pieces",
    )(queries, span_latents)
    here = lax.all_to_all(
        pieces, "ctx", split_axis=0, concat_axis=0, axis_index_groups=same_core, tiled=True
    )
    far_up = lax.ppermute(value_up, "ctx", other_core)

    keys, state, at = [own, right, left], None, 0
    for s in range(2, steps):
        right, left = onward(right), backward(left)
        keys += [right, left]
        if s == 2:
            right, left, here = lax.optimization_barrier((right, left, here))
            keys[-2:] = right, left
            here = here.reshape(chips * tokens, (heads + 1) * width)
            there = lax.ppermute(here, "ctx", other_core)
            continue
        if state is None:
            q, *state = fold_first(keys[:-2])
        else:
            state = fold_more(at, q, state, keys[:-2])
        at += len(keys) - 2
        keys = keys[-2:]
    right, left, state = lax.optimization_barrier((right, left, state))
    right = onward(right)
    state = fold_more(at, q, state, keys)
    flat = heads * V_HEAD + LANES
    half = everyone // CORES
    keep, give = pl.pallas_call(
        functools.partial(last_kernel, chips - 1, heads),
        out_shape=[shape(half, flat), shape(half, flat, dtype=bf16)],
        in_specs=[SMEM] * 2 + [VMEM] * 7,
        out_specs=[VMEM] * 2,
        scratch_shapes=[pltpu.VMEM((everyone, flat), f32)],
        compiler_params=PARAMS,
        name="last",
    )(prefix_length, table, q, *state, right, value_up, far_up)
    got = lax.ppermute(give, "ctx", other_core)
    merged = pl.pallas_call(
        functools.partial(merge_kernel, heads),
        out_shape=shape(chips, tokens, heads * V_HEAD, dtype=bf16),
        in_specs=[VMEM] * 2,
        out_specs=VMEM,
        scratch_shapes=[pltpu.VMEM((half, heads * V_HEAD), f32)],
        compiler_params=PARAMS,
        name="merge",
    )(keep, got)
    returned = lax.all_to_all(
        merged, "ctx", split_axis=0, concat_axis=0, axis_index_groups=same_core, tiled=True
    )
    return returned.transpose(1, 0, 2).reshape(tokens, all_heads * V_HEAD)


def solution(mesh):
    return jax.shard_map(
        functools.partial(on_device, mesh.shape["ctx"]),
        mesh=mesh,
        in_specs=(
            P(("groups", "ctx"), None),
            P(("groups", "ctx"), None),
            P(("groups", "ctx"), None),
            P("ctx", None, None),
            P("groups"),
            P("groups"),
        ),
        out_specs=P(("groups", "ctx"), None),
        check_vma=False,
    )
```

```python
import functools
import math

import jax
import jax.numpy as jnp
import numpy as np
from jax import lax
from jax.experimental import pallas as pl
from jax.experimental.pallas import tpu as pltpu
from jax.sharding import PartitionSpec as P

LATENT = 512
V_HEAD = 128
CORES = 2
LANES = 128

score_scale = 192.0 ** (-0.5) * math.log2(math.e)
neg_large = -1e30
least_max = -1e29
f32 = jnp.float32
bf16 = jnp.bfloat16


def chip_cycle(chips):
    wide = max(1, int(round(chips ** (1 / 3))))
    tall = chips // wide
    if wide * tall != chips or wide < 2 or tall < 2:
        return list(range(chips))
    walk = []
    for z in range(tall):
        across = range(1, wide) if z % 2 == 0 else range(wide - 1, 0, -1)
        walk += [z * wide + x for x in across]
    return walk + [z * wide for z in reversed(range(tall))]


def fold_block(part, q_ref, shards, length, old=None, span=None):
    m_old = least_max if old is None else old[0][part, :][:, :1]
    m_new = m_old
    scores = []
    for base, key_ref in shards:
        slot = base + lax.broadcasted_iota(jnp.int32, (1, key_ref.shape[1]), 1)
        s = jnp.dot(q_ref[part, :], key_ref[...], preferred_element_type=f32) * score_scale
        s = jnp.where(slot < length, s, neg_large)
        m_new = jnp.maximum(m_new, jnp.max(s, axis=1, keepdims=True))
        scores.append(s)
    if span is not None:
        keys, shown = span
        s = lax.dot_general(
            q_ref[part, :], keys, (((1,), (1,)), ((), ())), preferred_element_type=f32
        )
        span_s = jnp.where(shown, s * score_scale, neg_large)
        m_new = jnp.maximum(m_new, jnp.max(span_s, axis=1, keepdims=True))
    l_new, summed = 0.0, 0.0
    if old is not None:
        shrink = jnp.exp2(m_old - m_new)
        l_new = old[1][part, :][:, :1] * shrink
        summed = old[2][part, :] * shrink
    for s, (_, key_ref) in zip(scores, shards):
        probs = jnp.exp2(s - m_new)
        l_new += jnp.sum(probs, axis=1, keepdims=True)
        summed += lax.dot_general(
            probs.astype(bf16), key_ref[:LATENT, :], (((1,), (1,)), ((), ())),
            preferred_element_type=f32,
        )
    if span is not None:
        probs = jnp.exp2(span_s - m_new)
        l_new += jnp.sum(probs, axis=1, keepdims=True)
        summed += jnp.dot(
            probs.astype(bf16), keys[:, :LATENT], preferred_element_type=f32
        )
    return m_new, l_new, summed


def fold_shards(q_ref, shards, length, old, new, span=None):
    rows = q_ref.shape[0]
    block = min(256, rows)
    for start in range(0, rows, block):
        part = pl.ds(start, block)
        shown = None if span is None else (span[0], span[1](start, block))
        m_new, l_new, summed = fold_block(part, q_ref, shards, length, old, shown)
        new[0][part, :] = jnp.broadcast_to(m_new, (block, LANES))
        new[1][part, :] = jnp.broadcast_to(l_new, (block, LANES))
        new[2][part, :] = summed


def parted(index, size):
    return index >> (size.bit_length() - 1), index & (size - 1)


def token_of(index, tokens, chips):
    device, t = parted(index, tokens)
    core, chip = parted(device, chips)
    return (chip * CORES + ((lax.axis_index("ctx") % CORES) ^ core)) * tokens + t


def with_base(table_ref, at, key_refs):
    me = lax.axis_index("ctx")
    count = table_ref.shape[0] // lax.axis_size("ctx")
    return [
        (table_ref[me * count + at + j] * key_ref.shape[1], key_ref)
        for j, key_ref in enumerate(key_refs)
    ]


def pieces_kernel(queries_ref, span_ref, out_ref):
    chips = out_ref.shape[0]
    part = queries_ref.shape[1] // chips
    for chip in range(chips):
        out_ref[chip, :, :part] = queries_ref[:, chip * part:(chip + 1) * part]
        out_ref[chip, :, part:] = span_ref[...]


def first_kernel(heads, count, length_ref, table_ref, here_ref, there_ref, *rest):
    keys, (q_ref, m_ref, l_ref, acc_ref) = rest[:count], rest[count:]
    half = here_ref.shape[0]
    width = q_ref.shape[1]
    for core, piece_ref in enumerate((here_ref, there_ref)):
        for head in range(heads):
            row = (head * CORES + core) * half
            q_ref[row:row + half, :] = piece_ref[:, head * width:(head + 1) * width]
    shards = with_base(table_ref, 0, keys)
    fold_shards(q_ref, shards, length_ref[0], None, (m_ref, l_ref, acc_ref))


def middle_kernel(at, count, length_ref, table_ref, q_ref, m_in, l_in, acc_in, *rest):
    keys, new = rest[:count], rest[count:]
    fold_shards(q_ref, with_base(table_ref, at, keys), length_ref[0], (m_in, l_in, acc_in), new)


def span_kernel(at, count, length_ref, offset_ref, table_ref, q_ref, m_in, l_in, acc_in,
                here_ref, *rest):
    keys, new = rest[:count], rest[count:]
    chips = lax.axis_size("ctx") // CORES
    half = here_ref.shape[0]
    tokens = half // chips
    width = q_ref.shape[1]
    key_index = lax.broadcasted_iota(jnp.int32, (1, half), 1)
    key_token = token_of(key_index, tokens, chips)

    def shown(start, block):
        row_index = start + lax.broadcasted_iota(jnp.int32, (block, 1), 0)
        row_token = token_of(row_index & (half * CORES - 1), tokens, chips)
        return (key_token >= offset_ref[0]) & (key_token <= row_token)

    fold_shards(
        q_ref, with_base(table_ref, at, keys), length_ref[0], (m_in, l_in, acc_in), new,
        (here_ref[:, here_ref.shape[1] - width:], shown),
    )


def join_halves(top_ref, bottom_ref, key_ref):
    cut = top_ref.shape[0]
    key_ref[:cut, :] = top_ref[...]
    key_ref[cut:, :] = bottom_ref[...]


def last_kernel(at, heads, length_ref, table_ref, q_ref, m_ref, l_ref, acc_ref,
                top_ref, bottom_ref, own_up, far_up, keep_ref, give_ref, key_ref, flat_ref):
    join_halves(top_ref, bottom_ref, key_ref)
    core = lax.axis_index("ctx") % CORES
    shards = with_base(table_ref, at, (key_ref,))
    everyone = flat_ref.shape[0]
    per_core = heads // CORES
    rows = per_core * everyone
    pair = min(2, per_core)
    tail = jnp.zeros((everyone, LANES), f32)
    lane = lax.broadcasted_iota(jnp.int32, (everyone, LANES), 1)
    for side, up_ref in enumerate((own_up, far_up)):
        part = pl.ds(pl.multiple_of((core ^ side) * rows, rows), rows)
        m_new, l_new, summed = fold_block(
            part, q_ref, shards, length_ref[0], (m_ref, l_ref, acc_ref)
        )
        context = (summed * (1.0 / l_new)).astype(bf16)
        weight = m_new + jnp.log2(l_new)
        high = weight.astype(bf16).astype(f32)
        mid = (weight - high).astype(bf16).astype(f32)
        low = weight - high - mid
        for j in range(0, per_core, pair):
            lifted = jnp.dot(
                context[j * everyone:(j + pair) * everyone, :],
                jnp.concatenate([up_ref[j + i] for i in range(pair)], axis=1),
                preferred_element_type=f32,
            )
            for i in range(pair):
                head = (core ^ side) * per_core + j + i
                here = slice((j + i) * everyone, (j + i + 1) * everyone)
                tail = jnp.where(lane == head, high[here], tail)
                tail = jnp.where(lane == head + heads, mid[here], tail)
                tail = jnp.where(lane == head + 2 * heads, low[here], tail)
                lanes = pl.ds(pl.multiple_of(head * V_HEAD, V_HEAD), V_HEAD)
                flat_ref[:, lanes] = lifted[
                    i * everyone:(i + 1) * everyone, i * V_HEAD:(i + 1) * V_HEAD
                ]
    flat_ref[:, heads * V_HEAD:] = tail
    keep_ref[...] = flat_ref[:everyone // CORES, :]
    give_ref[...] = flat_ref[everyone // CORES:, :].astype(bf16)


def merge_kernel(heads, keep_ref, got_ref, out_ref, flat_ref):
    width = heads * V_HEAD
    gap = keep_ref[:, width:] - got_ref[:, width:].astype(f32)
    delta = gap[:, :heads] + (gap[:, heads:2 * heads] + gap[:, 2 * heads:3 * heads])
    share = 1.0 / (1.0 + jnp.exp2(-delta))
    rest = 1.0 / (1.0 + jnp.exp2(delta))
    for j in range(heads):
        lanes = slice(j * V_HEAD, (j + 1) * V_HEAD)
        flat_ref[:, lanes] = (
            keep_ref[:, lanes] * share[:, j:j + 1]
            + got_ref[:, lanes].astype(f32) * rest[:, j:j + 1]
        )
    chips, tokens, _ = out_ref.shape
    for chip in range(chips):
        out_ref[chip] = flat_ref[chip * tokens:(chip + 1) * tokens, :].astype(bf16)


VMEM = pl.BlockSpec(memory_space=pltpu.VMEM)
SMEM = pl.BlockSpec(memory_space=pltpu.SMEM)
PARAMS = pltpu.CompilerParams(vmem_limit_bytes=32 * 1024 * 1024)


def shape(*dims, dtype=f32):
    return jax.ShapeDtypeStruct(dims, dtype)


def on_device(ctx, queries, prefix_latents, span_latents, value_up, prefix_length, span_offset):
    slots, width = prefix_latents.shape
    tokens = queries.shape[0]
    all_heads = queries.shape[1] // width
    chips = ctx // CORES
    heads = all_heads // chips
    rows = tokens * heads
    total = rows * ctx
    everyone = tokens * ctx
    walk = chip_cycle(chips)
    spot = np.argsort(np.array(walk))
    steps = chips // 2

    def across(step):
        return [
            (walk[r] * CORES + c, walk[(r + (-step if c else step)) % chips] * CORES + c)
            for r in range(chips) for c in range(CORES)
        ]

    other_core = [(d, d ^ 1) for d in range(ctx)]
    same_core = [[p * CORES + c for p in range(chips)] for c in range(CORES)]

    turns = [0]
    for s in range(1, steps):
        turns += [-s, s]
    turns.append(steps)
    owner_table = np.array(
        [
            [walk[(spot[p] + (-t if c else t)) % chips] * CORES + c for t in turns]
            for p in range(chips) for c in range(CORES)
        ],
        np.int32,
    )
    table = jnp.asarray(owner_table.reshape(-1))
    state_shapes = [shape(total, LANES), shape(total, LANES), shape(total, LATENT)]

    def fold_first(keys):
        return pl.pallas_call(
            functools.partial(first_kernel, heads, len(keys)),
            out_shape=[shape(total, width, dtype=bf16)] + state_shapes,
            in_specs=[SMEM] * 2 + [VMEM] * (2 + len(keys)),
            out_specs=[VMEM] * 4,
            compiler_params=PARAMS,
            name="first",
        )(prefix_length, table, here, there, *keys)

    def fold_more(at, q, state, keys):
        return pl.pallas_call(
            functools.partial(middle_kernel, at, len(keys)),
            out_shape=state_shapes,
            in_specs=[SMEM] * 2 + [VMEM] * (4 + len(keys)),
            out_specs=[VMEM] * 3,
            compiler_params=PARAMS,
            name="middle",
        )(prefix_length, table, q, *state, *keys)

    onward = functools.partial(lax.ppermute, axis_name="ctx", perm=across(1))
    backward = functools.partial(lax.ppermute, axis_name="ctx", perm=across(-1))
    cut = LATENT // 2
    own = prefix_latents.T
    right, left = onward(own), backward(own)

    pieces = pl.pallas_call(
        pieces_kernel,
        out_shape=shape(chips, tokens, (heads + 1) * width, dtype=bf16),
        in_specs=[VMEM] * 2,
        out_specs=VMEM,
        compiler_params=PARAMS,
        name="pieces",
    )(queries, span_latents)
    here = lax.all_to_all(
        pieces, "ctx", split_axis=0, concat_axis=0, axis_index_groups=same_core, tiled=True
    )
    far_up = lax.ppermute(value_up, "ctx", other_core)

    keys, state, at = [own, right, left], None, 0
    for s in range(2, steps):
        right, left = onward(right), backward(left)
        if s == 2:
            here, right = lax.optimization_barrier((here, right))
            here = here.reshape(chips * tokens, (heads + 1) * width)
            there = lax.ppermute(here, "ctx", other_core)
            keys += [right, left]
            continue
        if state is None:
            q, *state = fold_first(keys)
        else:
            state = fold_more(at, q, state, keys)
        at += len(keys)
        keys = [right, left]
    top = onward(right[:cut])
    left, state = lax.optimization_barrier((left, state))
    bottom = backward(left[cut:])
    state = pl.pallas_call(
        functools.partial(span_kernel, at, len(keys)),
        out_shape=state_shapes,
        in_specs=[SMEM] * 3 + [VMEM] * (5 + len(keys)),
        out_specs=[VMEM] * 3,
        compiler_params=PARAMS,
        name="middle",
    )(prefix_length, span_offset, table, q, *state, here, *keys)
    flat = heads * V_HEAD + LANES
    half = everyone // CORES
    keep, give = pl.pallas_call(
        functools.partial(last_kernel, chips - 1, heads),
        out_shape=[shape(half, flat), shape(half, flat, dtype=bf16)],
        in_specs=[SMEM] * 2 + [VMEM] * 8,
        out_specs=[VMEM] * 2,
        scratch_shapes=[pltpu.VMEM((width, slots), bf16), pltpu.VMEM((everyone, flat), f32)],
        compiler_params=PARAMS,
        name="last",
    )(prefix_length, table, q, *state, top, bottom, value_up, far_up)
    got = lax.ppermute(give, "ctx", other_core)
    merged = pl.pallas_call(
        functools.partial(merge_kernel, heads),
        out_shape=shape(chips, tokens, heads * V_HEAD, dtype=bf16),
        in_specs=[VMEM] * 2,
        out_specs=VMEM,
        scratch_shapes=[pltpu.VMEM((half, heads * V_HEAD), f32)],
        compiler_params=PARAMS,
        name="merge",
    )(keep, got)
    returned = lax.all_to_all(
        merged, "ctx", split_axis=0, concat_axis=0, axis_index_groups=same_core, tiled=True
    )
    return returned.transpose(1, 0, 2).reshape(tokens, all_heads * V_HEAD)


def solution(mesh):
    return jax.shard_map(
        functools.partial(on_device, mesh.shape["ctx"]),
        mesh=mesh,
        in_specs=(
            P(("groups", "ctx"), None),
            P(("groups", "ctx"), None),
            P(("groups", "ctx"), None),
            P("ctx", None, None),
            P("groups"),
            P("groups"),
        ),
        out_specs=P(("groups", "ctx"), None),
        check_vma=False,
    )
```

```python
import functools
import math

import jax
import jax.numpy as jnp
import numpy as np
from jax import lax
from jax.experimental import pallas as pl
from jax.experimental.pallas import tpu as pltpu
from jax.sharding import PartitionSpec as P

LATENT = 512
V_HEAD = 128
CORES = 2
LANES = 128

score_scale = 192.0 ** (-0.5) * math.log2(math.e)
neg_large = -1e30
least_max = -1e29
f32 = jnp.float32
bf16 = jnp.bfloat16


def chip_cycle(chips):
    wide = max(1, int(round(chips ** (1 / 3))))
    tall = chips // wide
    if wide * tall != chips or wide < 2 or tall < 2:
        return list(range(chips))
    walk = []
    for z in range(tall):
        across = range(1, wide) if z % 2 == 0 else range(wide - 1, 0, -1)
        walk += [z * wide + x for x in across]
    return walk + [z * wide for z in reversed(range(tall))]


def fold_block(part, q_ref, shards, length, old=None, span=None):
    m_old = least_max if old is None else old[0][part, :][:, :1]
    m_new = m_old
    scores = []
    for base, key_ref in shards:
        slot = base + lax.broadcasted_iota(jnp.int32, (1, key_ref.shape[1]), 1)
        s = jnp.dot(q_ref[part, :], key_ref[...], preferred_element_type=f32) * score_scale
        s = jnp.where(slot < length, s, neg_large)
        m_new = jnp.maximum(m_new, jnp.max(s, axis=1, keepdims=True))
        scores.append(s)
    if span is not None:
        keys, shown = span
        s = lax.dot_general(
            q_ref[part, :], keys, (((1,), (1,)), ((), ())), preferred_element_type=f32
        )
        span_s = jnp.where(shown, s * score_scale, neg_large)
        m_new = jnp.maximum(m_new, jnp.max(span_s, axis=1, keepdims=True))
    l_new, summed = 0.0, 0.0
    if old is not None:
        shrink = jnp.exp2(m_old - m_new)
        l_new = old[1][part, :][:, :1] * shrink
        summed = old[2][part, :] * shrink
    for s, (_, key_ref) in zip(scores, shards):
        probs = jnp.exp2(s - m_new)
        l_new += jnp.sum(probs, axis=1, keepdims=True)
        summed += lax.dot_general(
            probs.astype(bf16), key_ref[:LATENT, :], (((1,), (1,)), ((), ())),
            preferred_element_type=f32,
        )
    if span is not None:
        probs = jnp.exp2(span_s - m_new)
        l_new += jnp.sum(probs, axis=1, keepdims=True)
        summed += jnp.dot(
            probs.astype(bf16), keys[:, :LATENT], preferred_element_type=f32
        )
    return m_new, l_new, summed


def fold_shards(q_ref, shards, length, old, new, span=None):
    rows = q_ref.shape[0]
    block = min(256, rows)
    for start in range(0, rows, block):
        part = pl.ds(start, block)
        shown = None if span is None else (span[0], span[1](start, block))
        m_new, l_new, summed = fold_block(part, q_ref, shards, length, old, shown)
        new[0][part, :] = jnp.broadcast_to(m_new, (block, LANES))
        new[1][part, :] = jnp.broadcast_to(l_new, (block, LANES))
        new[2][part, :] = summed


def parted(index, size):
    return index >> (size.bit_length() - 1), index & (size - 1)


def token_of(index, tokens, chips):
    device, t = parted(index, tokens)
    core, chip = parted(device, chips)
    return (chip * CORES + ((lax.axis_index("ctx") % CORES) ^ core)) * tokens + t


def with_base(table_ref, at, key_refs):
    me = lax.axis_index("ctx")
    count = table_ref.shape[0] // lax.axis_size("ctx")
    return [
        (table_ref[me * count + at + j] * key_ref.shape[1], key_ref)
        for j, key_ref in enumerate(key_refs)
    ]


def pieces_kernel(queries_ref, span_ref, out_ref):
    chips = out_ref.shape[0]
    part = queries_ref.shape[1] // chips
    for chip in range(chips):
        out_ref[chip, :, :part] = queries_ref[:, chip * part:(chip + 1) * part]
        out_ref[chip, :, part:] = span_ref[...]


def first_kernel(heads, count, length_ref, table_ref, here_ref, there_ref, *rest):
    keys, (q_ref, m_ref, l_ref, acc_ref) = rest[:count], rest[count:]
    half = here_ref.shape[0]
    width = q_ref.shape[1]
    for core, piece_ref in enumerate((here_ref, there_ref)):
        for head in range(heads):
            row = (head * CORES + core) * half
            q_ref[row:row + half, :] = piece_ref[:, head * width:(head + 1) * width]
    shards = with_base(table_ref, 0, keys)
    fold_shards(q_ref, shards, length_ref[0], None, (m_ref, l_ref, acc_ref))


def middle_kernel(at, count, length_ref, table_ref, q_ref, m_in, l_in, acc_in, *rest):
    keys, new = rest[:count], rest[count:]
    fold_shards(q_ref, with_base(table_ref, at, keys), length_ref[0], (m_in, l_in, acc_in), new)


def span_kernel(at, count, length_ref, offset_ref, table_ref, q_ref, m_in, l_in, acc_in,
                here_ref, *rest):
    keys, new = rest[:count], rest[count:]
    chips = lax.axis_size("ctx") // CORES
    half = here_ref.shape[0]
    tokens = half // chips
    width = q_ref.shape[1]
    key_index = lax.broadcasted_iota(jnp.int32, (1, half), 1)
    key_token = token_of(key_index, tokens, chips)

    def shown(start, block):
        row_index = start + lax.broadcasted_iota(jnp.int32, (block, 1), 0)
        row_token = token_of(row_index & (half * CORES - 1), tokens, chips)
        return (key_token >= offset_ref[0]) & (key_token <= row_token)

    fold_shards(
        q_ref, with_base(table_ref, at, keys), length_ref[0], (m_in, l_in, acc_in), new,
        (here_ref[:, here_ref.shape[1] - width:], shown),
    )


def join_halves(top_ref, bottom_ref, key_ref):
    cut = top_ref.shape[0]
    key_ref[:cut, :] = top_ref[...]
    key_ref[cut:, :] = bottom_ref[...]


def last_kernel(at, heads, length_ref, table_ref, q_ref, m_ref, l_ref, acc_ref,
                top_ref, bottom_ref, own_up, far_up, keep_ref, give_ref, key_ref, flat_ref):
    join_halves(top_ref, bottom_ref, key_ref)
    core = lax.axis_index("ctx") % CORES
    shards = with_base(table_ref, at, (key_ref,))
    everyone = flat_ref.shape[0]
    per_core = heads // CORES
    rows = per_core * everyone
    pair = min(2, per_core)
    tail = jnp.zeros((everyone, LANES), f32)
    lane = lax.broadcasted_iota(jnp.int32, (everyone, LANES), 1)
    for side, up_ref in enumerate((own_up, far_up)):
        part = pl.ds(pl.multiple_of((core ^ side) * rows, rows), rows)
        m_new, l_new, summed = fold_block(
            part, q_ref, shards, length_ref[0], (m_ref, l_ref, acc_ref)
        )
        context = (summed * (1.0 / l_new)).astype(bf16)
        weight = m_new + jnp.log2(l_new)
        high = weight.astype(bf16).astype(f32)
        mid = (weight - high).astype(bf16).astype(f32)
        low = weight - high - mid
        for j in range(0, per_core, pair):
            lifted = jnp.dot(
                context[j * everyone:(j + pair) * everyone, :],
                jnp.concatenate([up_ref[j + i] for i in range(pair)], axis=1),
                preferred_element_type=f32,
            )
            for i in range(pair):
                head = (core ^ side) * per_core + j + i
                here = slice((j + i) * everyone, (j + i + 1) * everyone)
                tail = jnp.where(lane == head, high[here], tail)
                tail = jnp.where(lane == head + heads, mid[here], tail)
                tail = jnp.where(lane == head + 2 * heads, low[here], tail)
                lanes = pl.ds(pl.multiple_of(head * V_HEAD, V_HEAD), V_HEAD)
                flat_ref[:, lanes] = lifted[
                    i * everyone:(i + 1) * everyone, i * V_HEAD:(i + 1) * V_HEAD
                ]
    flat_ref[:, heads * V_HEAD:] = tail
    keep_ref[...] = flat_ref[:everyone // CORES, :]
    give_ref[...] = flat_ref[everyone // CORES:, :].astype(bf16)


def merge_kernel(heads, keep_ref, got_ref, out_ref, flat_ref):
    width = heads * V_HEAD
    gap = keep_ref[:, width:] - got_ref[:, width:].astype(f32)
    delta = gap[:, :heads] + (gap[:, heads:2 * heads] + gap[:, 2 * heads:3 * heads])
    share = 1.0 / (1.0 + jnp.exp2(-delta))
    rest = 1.0 / (1.0 + jnp.exp2(delta))
    for j in range(heads):
        lanes = slice(j * V_HEAD, (j + 1) * V_HEAD)
        flat_ref[:, lanes] = (
            keep_ref[:, lanes] * share[:, j:j + 1]
            + got_ref[:, lanes].astype(f32) * rest[:, j:j + 1]
        )
    chips, tokens, _ = out_ref.shape
    for chip in range(chips):
        out_ref[chip] = flat_ref[chip * tokens:(chip + 1) * tokens, :].astype(bf16)


VMEM = pl.BlockSpec(memory_space=pltpu.VMEM)
SMEM = pl.BlockSpec(memory_space=pltpu.SMEM)
PARAMS = pltpu.CompilerParams(vmem_limit_bytes=32 * 1024 * 1024)


def shape(*dims, dtype=f32):
    return jax.ShapeDtypeStruct(dims, dtype)


def on_device(ctx, queries, prefix_latents, span_latents, value_up, prefix_length, span_offset):
    slots, width = prefix_latents.shape
    tokens = queries.shape[0]
    all_heads = queries.shape[1] // width
    chips = ctx // CORES
    heads = all_heads // chips
    rows = tokens * heads
    total = rows * ctx
    everyone = tokens * ctx
    walk = chip_cycle(chips)
    spot = np.argsort(np.array(walk))
    steps = chips // 2

    def across(step):
        return [
            (walk[r] * CORES + c, walk[(r + (-step if c else step)) % chips] * CORES + c)
            for r in range(chips) for c in range(CORES)
        ]

    other_core = [(d, d ^ 1) for d in range(ctx)]
    same_core = [[p * CORES + c for p in range(chips)] for c in range(CORES)]

    turns = [0]
    for s in range(1, steps):
        turns += [-s, s]
    turns.append(steps)
    owner_table = np.array(
        [
            [walk[(spot[p] + (-t if c else t)) % chips] * CORES + c for t in turns]
            for p in range(chips) for c in range(CORES)
        ],
        np.int32,
    )
    table = jnp.asarray(owner_table.reshape(-1))
    state_shapes = [shape(total, LANES), shape(total, LANES), shape(total, LATENT)]

    def fold_first(keys):
        return pl.pallas_call(
            functools.partial(first_kernel, heads, len(keys)),
            out_shape=[shape(total, width, dtype=bf16)] + state_shapes,
            in_specs=[SMEM] * 2 + [VMEM] * (2 + len(keys)),
            out_specs=[VMEM] * 4,
            compiler_params=PARAMS,
            name="first",
        )(prefix_length, table, here, there, *keys)

    def fold_more(at, q, state, keys):
        return pl.pallas_call(
            functools.partial(middle_kernel, at, len(keys)),
            out_shape=state_shapes,
            in_specs=[SMEM] * 2 + [VMEM] * (4 + len(keys)),
            out_specs=[VMEM] * 3,
            compiler_params=PARAMS,
            name="middle",
        )(prefix_length, table, q, *state, *keys)

    onward = functools.partial(lax.ppermute, axis_name="ctx", perm=across(1))
    backward = functools.partial(lax.ppermute, axis_name="ctx", perm=across(-1))
    cut = LATENT // 2
    own = prefix_latents.T
    right, left = onward(own), backward(own)

    pieces = pl.pallas_call(
        pieces_kernel,
        out_shape=shape(chips, tokens, (heads + 1) * width, dtype=bf16),
        in_specs=[VMEM] * 2,
        out_specs=VMEM,
        compiler_params=PARAMS,
        name="pieces",
    )(queries, span_latents)
    here = lax.all_to_all(
        pieces, "ctx", split_axis=0, concat_axis=0, axis_index_groups=same_core, tiled=True
    )
    far_up = lax.ppermute(value_up, "ctx", other_core)

    keys, state, at = [own, right, left], None, 0
    for s in range(2, steps):
        right, left = onward(right), backward(left)
        if s == 2:
            here = here.reshape(chips * tokens, (heads + 1) * width)
            there = lax.ppermute(here, "ctx", other_core)
            keys += [right, left]
            continue
        if state is None:
            q, *state = fold_first(keys)
        else:
            state = fold_more(at, q, state, keys)
        at += len(keys)
        keys = [right, left]
    top = onward(right[:cut])
    left, state = lax.optimization_barrier((left, state))
    bottom = backward(left[cut:])
    state = pl.pallas_call(
        functools.partial(span_kernel, at, len(keys)),
        out_shape=state_shapes,
        in_specs=[SMEM] * 3 + [VMEM] * (5 + len(keys)),
        out_specs=[VMEM] * 3,
        compiler_params=PARAMS,
        name="middle",
    )(prefix_length, span_offset, table, q, *state, here, *keys)
    flat = heads * V_HEAD + LANES
    half = everyone // CORES
    keep, give = pl.pallas_call(
        functools.partial(last_kernel, chips - 1, heads),
        out_shape=[shape(half, flat), shape(half, flat, dtype=bf16)],
        in_specs=[SMEM] * 2 + [VMEM] * 8,
        out_specs=[VMEM] * 2,
        scratch_shapes=[pltpu.VMEM((width, slots), bf16), pltpu.VMEM((everyone, flat), f32)],
        compiler_params=PARAMS,
        name="last",
    )(prefix_length, table, q, *state, top, bottom, value_up, far_up)
    got = lax.ppermute(give, "ctx", other_core)
    merged = pl.pallas_call(
        functools.partial(merge_kernel, heads),
        out_shape=shape(chips, tokens, heads * V_HEAD, dtype=bf16),
        in_specs=[VMEM] * 2,
        out_specs=VMEM,
        scratch_shapes=[pltpu.VMEM((half, heads * V_HEAD), f32)],
        compiler_params=PARAMS,
        name="merge",
    )(keep, got)
    returned = lax.all_to_all(
        merged, "ctx", split_axis=0, concat_axis=0, axis_index_groups=same_core, tiled=True
    )
    return returned.transpose(1, 0, 2).reshape(tokens, all_heads * V_HEAD)


def solution(mesh):
    return jax.shard_map(
        functools.partial(on_device, mesh.shape["ctx"]),
        mesh=mesh,
        in_specs=(
            P(("groups", "ctx"), None),
            P(("groups", "ctx"), None),
            P(("groups", "ctx"), None),
            P("ctx", None, None),
            P("groups"),
            P("groups"),
        ),
        out_specs=P(("groups", "ctx"), None),
        check_vma=False,
    )
```

```python
import functools
import math

import jax
import jax.numpy as jnp
import numpy as np
from jax import lax
from jax.experimental import pallas as pl
from jax.experimental.pallas import tpu as pltpu
from jax.sharding import PartitionSpec as P

LATENT = 512
V_HEAD = 128
CORES = 2
LANES = 128

score_scale = 192.0 ** (-0.5) * math.log2(math.e)
neg_large = -1e30
least_max = -1e29
f32 = jnp.float32
bf16 = jnp.bfloat16


def chip_cycle(chips):
    wide = max(1, int(round(chips ** (1 / 3))))
    tall = chips // wide
    if wide * tall != chips or wide < 2 or tall < 2:
        return list(range(chips))
    walk = []
    for z in range(tall):
        across = range(1, wide) if z % 2 == 0 else range(wide - 1, 0, -1)
        walk += [z * wide + x for x in across]
    return walk + [z * wide for z in reversed(range(tall))]


def fold_block(part, q_ref, shards, length, old=None, span=None):
    m_old = least_max if old is None else old[0][part, :][:, :1]
    m_new = m_old
    scores = []
    for base, key_ref in shards:
        slot = base + lax.broadcasted_iota(jnp.int32, (1, key_ref.shape[1]), 1)
        s = jnp.dot(q_ref[part, :], key_ref[...], preferred_element_type=f32) * score_scale
        s = jnp.where(slot < length, s, neg_large)
        m_new = jnp.maximum(m_new, jnp.max(s, axis=1, keepdims=True))
        scores.append(s)
    if span is not None:
        keys, shown = span
        s = lax.dot_general(
            q_ref[part, :], keys, (((1,), (1,)), ((), ())), preferred_element_type=f32
        )
        span_s = jnp.where(shown, s * score_scale, neg_large)
        m_new = jnp.maximum(m_new, jnp.max(span_s, axis=1, keepdims=True))
    l_new, summed = 0.0, 0.0
    if old is not None:
        shrink = jnp.exp2(m_old - m_new)
        l_new = old[1][part, :][:, :1] * shrink
        summed = old[2][part, :] * shrink
    for s, (_, key_ref) in zip(scores, shards):
        probs = jnp.exp2(s - m_new)
        l_new += jnp.sum(probs, axis=1, keepdims=True)
        summed += lax.dot_general(
            probs.astype(bf16), key_ref[:LATENT, :], (((1,), (1,)), ((), ())),
            preferred_element_type=f32,
        )
    if span is not None:
        probs = jnp.exp2(span_s - m_new)
        l_new += jnp.sum(probs, axis=1, keepdims=True)
        summed += jnp.dot(
            probs.astype(bf16), keys[:, :LATENT], preferred_element_type=f32
        )
    return m_new, l_new, summed


def fold_shards(q_ref, shards, length, old, new, span=None):
    rows = q_ref.shape[0]
    block = min(256, rows)
    for start in range(0, rows, block):
        part = pl.ds(start, block)
        shown = None if span is None else (span[0], span[1](start, block))
        m_new, l_new, summed = fold_block(part, q_ref, shards, length, old, shown)
        new[0][part, :] = jnp.broadcast_to(m_new, (block, LANES))
        new[1][part, :] = jnp.broadcast_to(l_new, (block, LANES))
        new[2][part, :] = summed


def parted(index, size):
    return index >> (size.bit_length() - 1), index & (size - 1)


def token_of(index, tokens, chips):
    device, t = parted(index, tokens)
    core, chip = parted(device, chips)
    return (chip * CORES + ((lax.axis_index("ctx") % CORES) ^ core)) * tokens + t


def with_base(table_ref, at, key_refs):
    me = lax.axis_index("ctx")
    count = table_ref.shape[0] // lax.axis_size("ctx")
    return [
        (table_ref[me * count + at + j] * key_ref.shape[1], key_ref)
        for j, key_ref in enumerate(key_refs)
    ]


def pieces_kernel(queries_ref, span_ref, out_ref):
    chips = out_ref.shape[0]
    part = queries_ref.shape[1] // chips
    for chip in range(chips):
        out_ref[chip, :, :part] = queries_ref[:, chip * part:(chip + 1) * part]
        out_ref[chip, :, part:] = span_ref[...]


def first_kernel(heads, count, length_ref, table_ref, here_ref, there_ref, *rest):
    keys, (q_ref, m_ref, l_ref, acc_ref) = rest[:count], rest[count:]
    half = here_ref.shape[0]
    width = q_ref.shape[1]
    for core, piece_ref in enumerate((here_ref, there_ref)):
        for head in range(heads):
            row = (head * CORES + core) * half
            q_ref[row:row + half, :] = piece_ref[:, head * width:(head + 1) * width]
    shards = with_base(table_ref, 0, keys)
    fold_shards(q_ref, shards, length_ref[0], None, (m_ref, l_ref, acc_ref))


def middle_kernel(at, count, length_ref, table_ref, q_ref, m_in, l_in, acc_in, *rest):
    keys, new = rest[:count], rest[count:]
    fold_shards(q_ref, with_base(table_ref, at, keys), length_ref[0], (m_in, l_in, acc_in), new)


def span_kernel(at, count, length_ref, offset_ref, table_ref, q_ref, m_in, l_in, acc_in,
                here_ref, *rest):
    keys, new = rest[:count], rest[count:]
    chips = lax.axis_size("ctx") // CORES
    half = here_ref.shape[0]
    tokens = half // chips
    width = q_ref.shape[1]
    key_index = lax.broadcasted_iota(jnp.int32, (1, half), 1)
    key_token = token_of(key_index, tokens, chips)

    def shown(start, block):
        row_index = start + lax.broadcasted_iota(jnp.int32, (block, 1), 0)
        row_token = token_of(row_index & (half * CORES - 1), tokens, chips)
        return (key_token >= offset_ref[0]) & (key_token <= row_token)

    fold_shards(
        q_ref, with_base(table_ref, at, keys), length_ref[0], (m_in, l_in, acc_in), new,
        (here_ref[:, here_ref.shape[1] - width:], shown),
    )


def join_halves(top_ref, bottom_ref, key_ref):
    cut = top_ref.shape[0]
    key_ref[:cut, :] = top_ref[...]
    key_ref[cut:, :] = bottom_ref[...]


def last_kernel(at, heads, length_ref, table_ref, q_ref, m_ref, l_ref, acc_ref,
                top_ref, bottom_ref, own_up, far_up, keep_ref, give_ref, key_ref, flat_ref):
    join_halves(top_ref, bottom_ref, key_ref)
    core = lax.axis_index("ctx") % CORES
    shards = with_base(table_ref, at, (key_ref,))
    everyone = flat_ref.shape[0]
    per_core = heads // CORES
    rows = per_core * everyone
    pair = min(2, per_core)
    tail = jnp.zeros((everyone, LANES), f32)
    lane = lax.broadcasted_iota(jnp.int32, (everyone, LANES), 1)
    for side, up_ref in enumerate((own_up, far_up)):
        part = pl.ds(pl.multiple_of((core ^ side) * rows, rows), rows)
        m_new, l_new, summed = fold_block(
            part, q_ref, shards, length_ref[0], (m_ref, l_ref, acc_ref)
        )
        context = (summed * (1.0 / l_new)).astype(bf16)
        weight = m_new + jnp.log2(l_new)
        high = weight.astype(bf16).astype(f32)
        mid = (weight - high).astype(bf16).astype(f32)
        low = weight - high - mid
        for j in range(0, per_core, pair):
            lifted = jnp.dot(
                context[j * everyone:(j + pair) * everyone, :],
                jnp.concatenate([up_ref[j + i] for i in range(pair)], axis=1),
                preferred_element_type=f32,
            )
            for i in range(pair):
                head = (core ^ side) * per_core + j + i
                here = slice((j + i) * everyone, (j + i + 1) * everyone)
                tail = jnp.where(lane == head, high[here], tail)
                tail = jnp.where(lane == head + heads, mid[here], tail)
                tail = jnp.where(lane == head + 2 * heads, low[here], tail)
                lanes = pl.ds(pl.multiple_of(head * V_HEAD, V_HEAD), V_HEAD)
                flat_ref[:, lanes] = lifted[
                    i * everyone:(i + 1) * everyone, i * V_HEAD:(i + 1) * V_HEAD
                ]
    flat_ref[:, heads * V_HEAD:] = tail
    keep_ref[...] = flat_ref[:everyone // CORES, :]
    give_ref[...] = flat_ref[everyone // CORES:, :].astype(bf16)


def merge_kernel(heads, keep_ref, got_ref, out_ref, flat_ref):
    width = heads * V_HEAD
    gap = keep_ref[:, width:] - got_ref[:, width:].astype(f32)
    delta = gap[:, :heads] + (gap[:, heads:2 * heads] + gap[:, 2 * heads:3 * heads])
    share = 1.0 / (1.0 + jnp.exp2(-delta))
    rest = 1.0 / (1.0 + jnp.exp2(delta))
    for j in range(heads):
        lanes = slice(j * V_HEAD, (j + 1) * V_HEAD)
        flat_ref[:, lanes] = (
            keep_ref[:, lanes] * share[:, j:j + 1]
            + got_ref[:, lanes].astype(f32) * rest[:, j:j + 1]
        )
    chips, tokens, _ = out_ref.shape
    for chip in range(chips):
        out_ref[chip] = flat_ref[chip * tokens:(chip + 1) * tokens, :].astype(bf16)


VMEM = pl.BlockSpec(memory_space=pltpu.VMEM)
SMEM = pl.BlockSpec(memory_space=pltpu.SMEM)
PARAMS = pltpu.CompilerParams(vmem_limit_bytes=32 * 1024 * 1024)


def shape(*dims, dtype=f32):
    return jax.ShapeDtypeStruct(dims, dtype)


def on_device(ctx, queries, prefix_latents, span_latents, value_up, prefix_length, span_offset):
    slots, width = prefix_latents.shape
    tokens = queries.shape[0]
    all_heads = queries.shape[1] // width
    chips = ctx // CORES
    heads = all_heads // chips
    rows = tokens * heads
    total = rows * ctx
    everyone = tokens * ctx
    walk = chip_cycle(chips)
    spot = np.argsort(np.array(walk))
    steps = chips // 2

    def across(step):
        return [
            (walk[r] * CORES + c, walk[(r + (-step if c else step)) % chips] * CORES + c)
            for r in range(chips) for c in range(CORES)
        ]

    other_core = [(d, d ^ 1) for d in range(ctx)]
    same_core = [[p * CORES + c for p in range(chips)] for c in range(CORES)]

    turns = [0]
    for s in range(1, steps):
        turns += [-s, s]
    turns.append(steps)
    owner_table = np.array(
        [
            [walk[(spot[p] + (-t if c else t)) % chips] * CORES + c for t in turns]
            for p in range(chips) for c in range(CORES)
        ],
        np.int32,
    )
    table = jnp.asarray(owner_table.reshape(-1))
    state_shapes = [shape(total, LANES), shape(total, LANES), shape(total, LATENT)]

    def fold_first(keys):
        return pl.pallas_call(
            functools.partial(first_kernel, heads, len(keys)),
            out_shape=[shape(total, width, dtype=bf16)] + state_shapes,
            in_specs=[SMEM] * 2 + [VMEM] * (2 + len(keys)),
            out_specs=[VMEM] * 4,
            compiler_params=PARAMS,
            name="first",
        )(prefix_length, table, here, there, *keys)

    def fold_more(at, q, state, keys):
        return pl.pallas_call(
            functools.partial(middle_kernel, at, len(keys)),
            out_shape=state_shapes,
            in_specs=[SMEM] * 2 + [VMEM] * (4 + len(keys)),
            out_specs=[VMEM] * 3,
            compiler_params=PARAMS,
            name="middle",
        )(prefix_length, table, q, *state, *keys)

    onward = functools.partial(lax.ppermute, axis_name="ctx", perm=across(1))
    backward = functools.partial(lax.ppermute, axis_name="ctx", perm=across(-1))
    cut = LATENT // 2
    own = prefix_latents.T
    right, left = onward(own), backward(own)

    pieces = pl.pallas_call(
        pieces_kernel,
        out_shape=shape(chips, tokens, (heads + 1) * width, dtype=bf16),
        in_specs=[VMEM] * 2,
        out_specs=VMEM,
        compiler_params=PARAMS,
        name="pieces",
    )(queries, span_latents)
    here = lax.all_to_all(
        pieces, "ctx", split_axis=0, concat_axis=0, axis_index_groups=same_core, tiled=True
    )
    far_up = lax.ppermute(value_up, "ctx", other_core)

    right, left = lax.optimization_barrier((right, left))
    keys, state, at = [own, right, left], None, 0
    for s in range(2, steps):
        right, left = onward(right), backward(left)
        if s == 2:
            here = here.reshape(chips * tokens, (heads + 1) * width)
            there = lax.ppermute(here, "ctx", other_core)
            keys += [right, left]
            continue
        if state is None:
            q, *state = fold_first(keys)
        else:
            state = fold_more(at, q, state, keys)
        at += len(keys)
        keys = [right, left]
    top = onward(right[:cut])
    left, state = lax.optimization_barrier((left, state))
    bottom = backward(left[cut:])
    state = pl.pallas_call(
        functools.partial(span_kernel, at, len(keys)),
        out_shape=state_shapes,
        in_specs=[SMEM] * 3 + [VMEM] * (5 + len(keys)),
        out_specs=[VMEM] * 3,
        compiler_params=PARAMS,
        name="middle",
    )(prefix_length, span_offset, table, q, *state, here, *keys)
    flat = heads * V_HEAD + LANES
    half = everyone // CORES
    keep, give = pl.pallas_call(
        functools.partial(last_kernel, chips - 1, heads),
        out_shape=[shape(half, flat), shape(half, flat, dtype=bf16)],
        in_specs=[SMEM] * 2 + [VMEM] * 8,
        out_specs=[VMEM] * 2,
        scratch_shapes=[pltpu.VMEM((width, slots), bf16), pltpu.VMEM((everyone, flat), f32)],
        compiler_params=PARAMS,
        name="last",
    )(prefix_length, table, q, *state, top, bottom, value_up, far_up)
    got = lax.ppermute(give, "ctx", other_core)
    merged = pl.pallas_call(
        functools.partial(merge_kernel, heads),
        out_shape=shape(chips, tokens, heads * V_HEAD, dtype=bf16),
        in_specs=[VMEM] * 2,
        out_specs=VMEM,
        scratch_shapes=[pltpu.VMEM((half, heads * V_HEAD), f32)],
        compiler_params=PARAMS,
        name="merge",
    )(keep, got)
    returned = lax.all_to_all(
        merged, "ctx", split_axis=0, concat_axis=0, axis_index_groups=same_core, tiled=True
    )
    return returned.transpose(1, 0, 2).reshape(tokens, all_heads * V_HEAD)


def solution(mesh):
    return jax.shard_map(
        functools.partial(on_device, mesh.shape["ctx"]),
        mesh=mesh,
        in_specs=(
            P(("groups", "ctx"), None),
            P(("groups", "ctx"), None),
            P(("groups", "ctx"), None),
            P("ctx", None, None),
            P("groups"),
            P("groups"),
        ),
        out_specs=P(("groups", "ctx"), None),
        check_vma=False,
    )
```

```python
import functools
import math

import jax
import jax.numpy as jnp
import numpy as np
from jax import lax
from jax.experimental import pallas as pl
from jax.experimental.pallas import tpu as pltpu
from jax.sharding import PartitionSpec as P

LATENT = 512
V_HEAD = 128
CORES = 2
LANES = 128

score_scale = 192.0 ** (-0.5) * math.log2(math.e)
neg_large = -1e30
least_max = -1e29
f32 = jnp.float32
bf16 = jnp.bfloat16


def chip_cycle(chips):
    wide = max(1, int(round(chips ** (1 / 3))))
    tall = chips // wide
    if wide * tall != chips or wide < 2 or tall < 2:
        return list(range(chips))
    walk = []
    for z in range(tall):
        across = range(1, wide) if z % 2 == 0 else range(wide - 1, 0, -1)
        walk += [z * wide + x for x in across]
    return walk + [z * wide for z in reversed(range(tall))]


def scores_of(q_ref, part, pieces):
    total, at = None, 0
    for piece in pieces:
        s = jnp.dot(
            q_ref[part, at:at + piece.shape[0]], piece[...], preferred_element_type=f32
        )
        total, at = s if total is None else total + s, at + piece.shape[0]
    return total


def values_of(weights, pieces):
    summed, at = [], 0
    for piece in pieces:
        wide = min(piece.shape[0], LATENT - at)
        summed.append(lax.dot_general(
            weights, piece[:wide, :], (((1,), (1,)), ((), ())), preferred_element_type=f32
        ))
        at += wide
    return summed[0] if len(summed) == 1 else jnp.concatenate(summed, axis=1)


def fold_block(part, q_ref, shards, length, old=None, span=None):
    m_old = least_max if old is None else old[0][part, :][:, :1]
    m_new = m_old
    scores = []
    for base, key_ref in shards:
        slot = base + lax.broadcasted_iota(jnp.int32, (1, key_ref[0].shape[1]), 1)
        s = scores_of(q_ref, part, key_ref) * score_scale
        s = jnp.where(slot < length, s, neg_large)
        m_new = jnp.maximum(m_new, jnp.max(s, axis=1, keepdims=True))
        scores.append(s)
    if span is not None:
        keys, shown = span
        s = lax.dot_general(
            q_ref[part, :], keys, (((1,), (1,)), ((), ())), preferred_element_type=f32
        )
        span_s = jnp.where(shown, s * score_scale, neg_large)
        m_new = jnp.maximum(m_new, jnp.max(span_s, axis=1, keepdims=True))
    l_new, summed = 0.0, 0.0
    if old is not None:
        shrink = jnp.exp2(m_old - m_new)
        l_new = old[1][part, :][:, :1] * shrink
        summed = old[2][part, :] * shrink
    for s, (_, key_ref) in zip(scores, shards):
        probs = jnp.exp2(s - m_new)
        l_new += jnp.sum(probs, axis=1, keepdims=True)
        summed += values_of(probs.astype(bf16), key_ref)
    if span is not None:
        probs = jnp.exp2(span_s - m_new)
        l_new += jnp.sum(probs, axis=1, keepdims=True)
        summed += jnp.dot(
            probs.astype(bf16), keys[:, :LATENT], preferred_element_type=f32
        )
    return m_new, l_new, summed


def fold_shards(q_ref, shards, length, old, new, span=None):
    rows = q_ref.shape[0]
    block = min(256, rows)
    for start in range(0, rows, block):
        part = pl.ds(start, block)
        shown = None if span is None else (span[0], span[1](start, block))
        m_new, l_new, summed = fold_block(part, q_ref, shards, length, old, shown)
        new[0][part, :] = jnp.broadcast_to(m_new, (block, LANES))
        new[1][part, :] = jnp.broadcast_to(l_new, (block, LANES))
        new[2][part, :] = summed


def parted(index, size):
    return index >> (size.bit_length() - 1), index & (size - 1)


def token_of(index, tokens, chips):
    device, t = parted(index, tokens)
    core, chip = parted(device, chips)
    return (chip * CORES + ((lax.axis_index("ctx") % CORES) ^ core)) * tokens + t


def with_base(table_ref, at, key_refs):
    me = lax.axis_index("ctx")
    count = table_ref.shape[0] // lax.axis_size("ctx")
    return [
        (table_ref[me * count + at + j] * key_ref.shape[1], (key_ref,))
        for j, key_ref in enumerate(key_refs)
    ]


def pieces_kernel(queries_ref, span_ref, out_ref):
    chips = out_ref.shape[0]
    part = queries_ref.shape[1] // chips
    for chip in range(chips):
        out_ref[chip, :, :part] = queries_ref[:, chip * part:(chip + 1) * part]
        out_ref[chip, :, part:] = span_ref[...]


def first_kernel(heads, count, length_ref, table_ref, here_ref, there_ref, *rest):
    keys, (q_ref, m_ref, l_ref, acc_ref) = rest[:count], rest[count:]
    half = here_ref.shape[0]
    width = q_ref.shape[1]
    for core, piece_ref in enumerate((here_ref, there_ref)):
        for head in range(heads):
            row = (head * CORES + core) * half
            q_ref[row:row + half, :] = piece_ref[:, head * width:(head + 1) * width]
    shards = with_base(table_ref, 0, keys)
    fold_shards(q_ref, shards, length_ref[0], None, (m_ref, l_ref, acc_ref))


def middle_kernel(at, count, length_ref, table_ref, q_ref, m_in, l_in, acc_in, *rest):
    keys, new = rest[:count], rest[count:]
    fold_shards(q_ref, with_base(table_ref, at, keys), length_ref[0], (m_in, l_in, acc_in), new)


def span_kernel(at, count, length_ref, offset_ref, table_ref, q_ref, m_in, l_in, acc_in,
                here_ref, *rest):
    keys, new = rest[:count], rest[count:]
    chips = lax.axis_size("ctx") // CORES
    half = here_ref.shape[0]
    tokens = half // chips
    width = q_ref.shape[1]
    key_index = lax.broadcasted_iota(jnp.int32, (1, half), 1)
    key_token = token_of(key_index, tokens, chips)

    def shown(start, block):
        row_index = start + lax.broadcasted_iota(jnp.int32, (block, 1), 0)
        row_token = token_of(row_index & (half * CORES - 1), tokens, chips)
        return (key_token >= offset_ref[0]) & (key_token <= row_token)

    fold_shards(
        q_ref, with_base(table_ref, at, keys), length_ref[0], (m_in, l_in, acc_in), new,
        (here_ref[:, here_ref.shape[1] - width:], shown),
    )


def last_kernel(at, heads, length_ref, table_ref, q_ref, m_ref, l_ref, acc_ref,
                top_ref, bottom_ref, own_up, far_up, keep_ref, give_ref, flat_ref):
    core = lax.axis_index("ctx") % CORES
    shards = [(with_base(table_ref, at, (top_ref,))[0][0], (top_ref, bottom_ref))]
    everyone = flat_ref.shape[0]
    per_core = heads // CORES
    rows = per_core * everyone
    pair = min(2, per_core)
    tail = jnp.zeros((everyone, LANES), f32)
    lane = lax.broadcasted_iota(jnp.int32, (everyone, LANES), 1)
    for side, up_ref in enumerate((own_up, far_up)):
        part = pl.ds(pl.multiple_of((core ^ side) * rows, rows), rows)
        m_new, l_new, summed = fold_block(
            part, q_ref, shards, length_ref[0], (m_ref, l_ref, acc_ref)
        )
        context = (summed * (1.0 / l_new)).astype(bf16)
        weight = m_new + jnp.log2(l_new)
        for j in range(0, per_core, pair):
            lifted = jnp.dot(
                context[j * everyone:(j + pair) * everyone, :],
                jnp.concatenate([up_ref[j + i] for i in range(pair)], axis=1),
                preferred_element_type=f32,
            )
            for i in range(pair):
                head = (core ^ side) * per_core + j + i
                here = slice((j + i) * everyone, (j + i + 1) * everyone)
                tail = jnp.where(lane == head, weight[here], tail)
                lanes = pl.ds(pl.multiple_of(head * V_HEAD, V_HEAD), V_HEAD)
                flat_ref[:, lanes] = lifted[
                    i * everyone:(i + 1) * everyone, i * V_HEAD:(i + 1) * V_HEAD
                ]
    high = tail.astype(bf16).astype(f32)
    mid = (tail - high).astype(bf16).astype(f32)
    low = tail - high - mid
    flat_ref[:, heads * V_HEAD:] = (
        high + pltpu.roll(mid, heads, 1) + pltpu.roll(low, 2 * heads, 1)
    )
    keep_ref[...] = flat_ref[:everyone // CORES, :]
    give_ref[...] = flat_ref[everyone // CORES:, :].astype(bf16)


def merge_kernel(heads, keep_ref, got_ref, out_ref, flat_ref):
    width = heads * V_HEAD
    gap = keep_ref[:, width:] - got_ref[:, width:].astype(f32)
    delta = gap[:, :heads] + (gap[:, heads:2 * heads] + gap[:, 2 * heads:3 * heads])
    share = 1.0 / (1.0 + jnp.exp2(-delta))
    rest = 1.0 / (1.0 + jnp.exp2(delta))
    for j in range(heads):
        lanes = slice(j * V_HEAD, (j + 1) * V_HEAD)
        flat_ref[:, lanes] = (
            keep_ref[:, lanes] * share[:, j:j + 1]
            + got_ref[:, lanes].astype(f32) * rest[:, j:j + 1]
        )
    chips, tokens, _ = out_ref.shape
    for chip in range(chips):
        out_ref[chip] = flat_ref[chip * tokens:(chip + 1) * tokens, :].astype(bf16)


VMEM = pl.BlockSpec(memory_space=pltpu.VMEM)
SMEM = pl.BlockSpec(memory_space=pltpu.SMEM)
PARAMS = pltpu.CompilerParams(vmem_limit_bytes=32 * 1024 * 1024)


def shape(*dims, dtype=f32):
    return jax.ShapeDtypeStruct(dims, dtype)


def on_device(ctx, queries, prefix_latents, span_latents, value_up, prefix_length, span_offset):
    slots, width = prefix_latents.shape
    tokens = queries.shape[0]
    all_heads = queries.shape[1] // width
    chips = ctx // CORES
    heads = all_heads // chips
    rows = tokens * heads
    total = rows * ctx
    everyone = tokens * ctx
    walk = chip_cycle(chips)
    spot = np.argsort(np.array(walk))
    steps = chips // 2

    def across(step):
        return [
            (walk[r] * CORES + c, walk[(r + (-step if c else step)) % chips] * CORES + c)
            for r in range(chips) for c in range(CORES)
        ]

    other_core = [(d, d ^ 1) for d in range(ctx)]
    same_core = [[p * CORES + c for p in range(chips)] for c in range(CORES)]

    turns = [0]
    for s in range(1, steps):
        turns += [-s, s]
    turns.append(steps)
    owner_table = np.array(
        [
            [walk[(spot[p] + (-t if c else t)) % chips] * CORES + c for t in turns]
            for p in range(chips) for c in range(CORES)
        ],
        np.int32,
    )
    table = jnp.asarray(owner_table.reshape(-1))
    state_shapes = [shape(total, LANES), shape(total, LANES), shape(total, LATENT)]

    def fold_first(keys):
        return pl.pallas_call(
            functools.partial(first_kernel, heads, len(keys)),
            out_shape=[shape(total, width, dtype=bf16)] + state_shapes,
            in_specs=[SMEM] * 2 + [VMEM] * (2 + len(keys)),
            out_specs=[VMEM] * 4,
            compiler_params=PARAMS,
            name="first",
        )(prefix_length, table, here, there, *keys)

    def fold_more(at, q, state, keys):
        return pl.pallas_call(
            functools.partial(middle_kernel, at, len(keys)),
            out_shape=state_shapes,
            in_specs=[SMEM] * 2 + [VMEM] * (4 + len(keys)),
            out_specs=[VMEM] * 3,
            compiler_params=PARAMS,
            name="middle",
        )(prefix_length, table, q, *state, *keys)

    onward = functools.partial(lax.ppermute, axis_name="ctx", perm=across(1))
    backward = functools.partial(lax.ppermute, axis_name="ctx", perm=across(-1))
    cut = LATENT // 2
    own = prefix_latents.T
    right, left = onward(own), backward(own)

    pieces = pl.pallas_call(
        pieces_kernel,
        out_shape=shape(chips, tokens, (heads + 1) * width, dtype=bf16),
        in_specs=[VMEM] * 2,
        out_specs=VMEM,
        compiler_params=PARAMS,
        name="pieces",
    )(queries, span_latents)
    here = lax.all_to_all(
        pieces, "ctx", split_axis=0, concat_axis=0, axis_index_groups=same_core, tiled=True
    )

    right, left, up = lax.optimization_barrier((right, left, value_up))
    far_up = lax.ppermute(up, "ctx", other_core)
    keys, state, at = [own, right, left], None, 0
    for s in range(2, steps):
        right, left = onward(right), backward(left)
        if s == 2:
            here = here.reshape(chips * tokens, (heads + 1) * width)
            there = lax.ppermute(here, "ctx", other_core)
            keys += [right, left]
            continue
        if state is None:
            q, *state = fold_first(keys)
        else:
            state = fold_more(at, q, state, keys)
        at += len(keys)
        keys = [right, left]
    top = onward(right[:cut])
    left, state = lax.optimization_barrier((left, state))
    bottom = backward(left[cut:])
    state = pl.pallas_call(
        functools.partial(span_kernel, at, len(keys)),
        out_shape=state_shapes,
        in_specs=[SMEM] * 3 + [VMEM] * (5 + len(keys)),
        out_specs=[VMEM] * 3,
        compiler_params=PARAMS,
        name="middle",
    )(prefix_length, span_offset, table, q, *state, here, *keys)
    flat = heads * V_HEAD + LANES
    half = everyone // CORES
    keep, give = pl.pallas_call(
        functools.partial(last_kernel, chips - 1, heads),
        out_shape=[shape(half, flat), shape(half, flat, dtype=bf16)],
        in_specs=[SMEM] * 2 + [VMEM] * 8,
        out_specs=[VMEM] * 2,
        scratch_shapes=[pltpu.VMEM((everyone, flat), f32)],
        compiler_params=PARAMS,
        name="last",
    )(prefix_length, table, q, *state, top, bottom, value_up, far_up)
    got = lax.ppermute(give, "ctx", other_core)
    merged = pl.pallas_call(
        functools.partial(merge_kernel, heads),
        out_shape=shape(chips, tokens, heads * V_HEAD, dtype=bf16),
        in_specs=[VMEM] * 2,
        out_specs=VMEM,
        scratch_shapes=[pltpu.VMEM((half, heads * V_HEAD), f32)],
        compiler_params=PARAMS,
        name="merge",
    )(keep, got)
    returned = lax.all_to_all(
        merged, "ctx", split_axis=0, concat_axis=0, axis_index_groups=same_core, tiled=True
    )
    return returned.transpose(1, 0, 2).reshape(tokens, all_heads * V_HEAD)


def solution(mesh):
    return jax.shard_map(
        functools.partial(on_device, mesh.shape["ctx"]),
        mesh=mesh,
        in_specs=(
            P(("groups", "ctx"), None),
            P(("groups", "ctx"), None),
            P(("groups", "ctx"), None),
            P("ctx", None, None),
            P("groups"),
            P("groups"),
        ),
        out_specs=P(("groups", "ctx"), None),
        check_vma=False,
    )
```

```python
import functools
import math

import jax
import jax.numpy as jnp
import numpy as np
from jax import lax
from jax.experimental import pallas as pl
from jax.experimental.pallas import tpu as pltpu
from jax.sharding import PartitionSpec as P

LATENT = 512
V_HEAD = 128
CORES = 2
LANES = 128

score_scale = 192.0 ** (-0.5) * math.log2(math.e)
neg_large = -1e30
least_max = -1e29
f32 = jnp.float32
bf16 = jnp.bfloat16


def chip_cycle(chips):
    wide = max(1, int(round(chips ** (1 / 3))))
    tall = chips // wide
    if wide * tall != chips or wide < 2 or tall < 2:
        return list(range(chips))
    walk = []
    for z in range(tall):
        across = range(1, wide) if z % 2 == 0 else range(wide - 1, 0, -1)
        walk += [z * wide + x for x in across]
    return walk + [z * wide for z in reversed(range(tall))]


def scores_of(q_ref, part, pieces):
    total, at = None, 0
    for piece in pieces:
        s = jnp.dot(
            q_ref[part, at:at + piece.shape[0]], piece[...], preferred_element_type=f32
        )
        total, at = s if total is None else total + s, at + piece.shape[0]
    return total


def values_of(weights, pieces):
    summed, at = [], 0
    for piece in pieces:
        wide = min(piece.shape[0], LATENT - at)
        summed.append(lax.dot_general(
            weights, piece[:wide, :], (((1,), (1,)), ((), ())), preferred_element_type=f32
        ))
        at += wide
    return summed[0] if len(summed) == 1 else jnp.concatenate(summed, axis=1)


def fold_block(part, q_ref, shards, length, old=None, span=None):
    m_old = least_max if old is None else old[0][part, :][:, :1]
    m_new = m_old
    scores = []
    for base, key_ref in shards:
        slot = base + lax.broadcasted_iota(jnp.int32, (1, key_ref[0].shape[1]), 1)
        s = scores_of(q_ref, part, key_ref) * score_scale
        s = jnp.where(slot < length, s, neg_large)
        m_new = jnp.maximum(m_new, jnp.max(s, axis=1, keepdims=True))
        scores.append(s)
    if span is not None:
        keys, shown = span
        s = lax.dot_general(
            q_ref[part, :], keys, (((1,), (1,)), ((), ())), preferred_element_type=f32
        )
        span_s = jnp.where(shown, s * score_scale, neg_large)
        m_new = jnp.maximum(m_new, jnp.max(span_s, axis=1, keepdims=True))
    l_new, summed = 0.0, 0.0
    if old is not None:
        shrink = jnp.exp2(m_old - m_new)
        l_new = old[1][part, :][:, :1] * shrink
        summed = old[2][part, :] * shrink
    for s, (_, key_ref) in zip(scores, shards):
        probs = jnp.exp2(s - m_new)
        l_new += jnp.sum(probs, axis=1, keepdims=True)
        summed += values_of(probs.astype(bf16), key_ref)
    if span is not None:
        probs = jnp.exp2(span_s - m_new)
        l_new += jnp.sum(probs, axis=1, keepdims=True)
        summed += jnp.dot(
            probs.astype(bf16), keys[:, :LATENT], preferred_element_type=f32
        )
    return m_new, l_new, summed


def fold_shards(q_ref, shards, length, old, new, span=None):
    rows = q_ref.shape[0]
    block = min(256, rows)
    for start in range(0, rows, block):
        part = pl.ds(start, block)
        shown = None if span is None else (span[0], span[1](start, block))
        m_new, l_new, summed = fold_block(part, q_ref, shards, length, old, shown)
        new[0][part, :] = jnp.broadcast_to(m_new, (block, LANES))
        new[1][part, :] = jnp.broadcast_to(l_new, (block, LANES))
        new[2][part, :] = summed


def parted(index, size):
    return index >> (size.bit_length() - 1), index & (size - 1)


def token_of(index, tokens, chips):
    device, t = parted(index, tokens)
    core, chip = parted(device, chips)
    return (chip * CORES + ((lax.axis_index("ctx") % CORES) ^ core)) * tokens + t


def with_base(table_ref, at, key_refs):
    me = lax.axis_index("ctx")
    count = table_ref.shape[0] // lax.axis_size("ctx")
    return [
        (table_ref[me * count + at + j] * key_ref.shape[1], (key_ref,))
        for j, key_ref in enumerate(key_refs)
    ]


def pieces_kernel(queries_ref, span_ref, out_ref):
    chips = out_ref.shape[0]
    part = queries_ref.shape[1] // chips
    for chip in range(chips):
        out_ref[chip, :, :part] = queries_ref[:, chip * part:(chip + 1) * part]
        out_ref[chip, :, part:] = span_ref[...]


def first_kernel(heads, count, length_ref, table_ref, here_ref, there_ref, *rest):
    keys, (q_ref, m_ref, l_ref, acc_ref) = rest[:count], rest[count:]
    half = here_ref.shape[0]
    width = q_ref.shape[1]
    for core, piece_ref in enumerate((here_ref, there_ref)):
        for head in range(heads):
            row = (head * CORES + core) * half
            q_ref[row:row + half, :] = piece_ref[:, head * width:(head + 1) * width]
    shards = with_base(table_ref, 0, keys)
    fold_shards(q_ref, shards, length_ref[0], None, (m_ref, l_ref, acc_ref))


def middle_kernel(at, count, length_ref, table_ref, q_ref, m_in, l_in, acc_in, *rest):
    keys, new = rest[:count], rest[count:]
    fold_shards(q_ref, with_base(table_ref, at, keys), length_ref[0], (m_in, l_in, acc_in), new)


def span_kernel(at, count, length_ref, offset_ref, table_ref, q_ref, m_in, l_in, acc_in,
                here_ref, *rest):
    keys, new = rest[:count], rest[count:]
    chips = lax.axis_size("ctx") // CORES
    half = here_ref.shape[0]
    tokens = half // chips
    width = q_ref.shape[1]
    key_index = lax.broadcasted_iota(jnp.int32, (1, half), 1)
    key_token = token_of(key_index, tokens, chips)

    def shown(start, block):
        row_index = start + lax.broadcasted_iota(jnp.int32, (block, 1), 0)
        row_token = token_of(row_index & (half * CORES - 1), tokens, chips)
        return (key_token >= offset_ref[0]) & (key_token <= row_token)

    fold_shards(
        q_ref, with_base(table_ref, at, keys), length_ref[0], (m_in, l_in, acc_in), new,
        (here_ref[:, here_ref.shape[1] - width:], shown),
    )


def last_kernel(at, heads, length_ref, table_ref, q_ref, m_ref, l_ref, acc_ref,
                top_ref, bottom_ref, keep_ref, give_ref):
    core = lax.axis_index("ctx") % CORES
    shards = [(with_base(table_ref, at, (top_ref,))[0][0], (top_ref, bottom_ref))]
    rows = keep_ref.shape[0]
    lane = lax.broadcasted_iota(jnp.int32, (rows, LANES), 1)
    for side in (1, 0):
        part = pl.ds(pl.multiple_of((core ^ side) * rows, rows), rows)
        m_new, l_new, summed = fold_block(
            part, q_ref, shards, length_ref[0], (m_ref, l_ref, acc_ref)
        )
        context = summed * (1.0 / l_new)
        weight = jnp.broadcast_to(m_new + jnp.log2(l_new), (rows, LANES))
        if side:
            high = weight.astype(bf16).astype(f32)
            mid = (weight - high).astype(bf16).astype(f32)
            terms = jnp.where(lane == 0, high, jnp.where(lane == 1, mid, weight - high - mid))
            give_ref[:, :LATENT] = context.astype(bf16)
            give_ref[:, LATENT:] = terms.astype(bf16)
        else:
            keep_ref[:, :LATENT] = context
            keep_ref[:, LATENT:] = weight


def merge_kernel(keep_ref, got_ref, up_ref, out_ref, flat_ref):
    core = lax.axis_index("ctx") % CORES
    heads = up_ref.shape[0]
    everyone = flat_ref.shape[0]
    half = everyone // CORES
    pair = min(2, heads)
    for j in range(0, heads, pair):
        contexts = []
        for head in range(j, j + pair):
            row = head * everyone
            got = jnp.concatenate(
                [got_ref[row + half:row + everyone, :], got_ref[row:row + half, :]], axis=0
            ).astype(f32)
            keep = keep_ref[row:row + everyone, :]
            gap = keep[:, LATENT:LATENT + 1] - got[:, LATENT:LATENT + 1]
            gap = gap - got[:, LATENT + 1:LATENT + 2] - got[:, LATENT + 2:LATENT + 3]
            share = 1.0 / (1.0 + jnp.exp2(-gap))
            rest = 1.0 / (1.0 + jnp.exp2(gap))
            contexts.append(
                (keep[:, :LATENT] * share + got[:, :LATENT] * rest).astype(bf16)
            )
        lifted = jnp.dot(
            jnp.concatenate(contexts, axis=0),
            jnp.concatenate([up_ref[j + i] for i in range(pair)], axis=1),
            preferred_element_type=f32,
        )
        for i in range(pair):
            flat_ref[:, (j + i) * V_HEAD:(j + i + 1) * V_HEAD] = lifted[
                i * everyone:(i + 1) * everyone, i * V_HEAD:(i + 1) * V_HEAD
            ]
    devices, tokens, _ = out_ref.shape
    chips = devices // CORES
    for i in range(devices):
        out_ref[(i % chips) * CORES + (core ^ (i // chips))] = (
            flat_ref[i * tokens:(i + 1) * tokens, :].astype(bf16)
        )


VMEM = pl.BlockSpec(memory_space=pltpu.VMEM)
SMEM = pl.BlockSpec(memory_space=pltpu.SMEM)
PARAMS = pltpu.CompilerParams(vmem_limit_bytes=32 * 1024 * 1024)


def shape(*dims, dtype=f32):
    return jax.ShapeDtypeStruct(dims, dtype)


def on_device(ctx, queries, prefix_latents, span_latents, value_up, prefix_length, span_offset):
    slots, width = prefix_latents.shape
    tokens = queries.shape[0]
    all_heads = queries.shape[1] // width
    chips = ctx // CORES
    heads = all_heads // chips
    rows = tokens * heads
    total = rows * ctx
    everyone = tokens * ctx
    walk = chip_cycle(chips)
    spot = np.argsort(np.array(walk))
    steps = chips // 2

    def across(step):
        return [
            (walk[r] * CORES + c, walk[(r + (-step if c else step)) % chips] * CORES + c)
            for r in range(chips) for c in range(CORES)
        ]

    other_core = [(d, d ^ 1) for d in range(ctx)]
    same_core = [[p * CORES + c for p in range(chips)] for c in range(CORES)]

    turns = [0]
    for s in range(1, steps):
        turns += [-s, s]
    turns.append(steps)
    owner_table = np.array(
        [
            [walk[(spot[p] + (-t if c else t)) % chips] * CORES + c for t in turns]
            for p in range(chips) for c in range(CORES)
        ],
        np.int32,
    )
    table = jnp.asarray(owner_table.reshape(-1))
    state_shapes = [shape(total, LANES), shape(total, LANES), shape(total, LATENT)]

    def fold_first(keys):
        return pl.pallas_call(
            functools.partial(first_kernel, heads, len(keys)),
            out_shape=[shape(total, width, dtype=bf16)] + state_shapes,
            in_specs=[SMEM] * 2 + [VMEM] * (2 + len(keys)),
            out_specs=[VMEM] * 4,
            compiler_params=PARAMS,
            name="first",
        )(prefix_length, table, here, there, *keys)

    def fold_more(at, q, state, keys):
        return pl.pallas_call(
            functools.partial(middle_kernel, at, len(keys)),
            out_shape=state_shapes,
            in_specs=[SMEM] * 2 + [VMEM] * (4 + len(keys)),
            out_specs=[VMEM] * 3,
            compiler_params=PARAMS,
            name="middle",
        )(prefix_length, table, q, *state, *keys)

    onward = functools.partial(lax.ppermute, axis_name="ctx", perm=across(1))
    backward = functools.partial(lax.ppermute, axis_name="ctx", perm=across(-1))
    cut = LATENT // 2
    own = prefix_latents.T
    right, left = onward(own), backward(own)

    pieces = pl.pallas_call(
        pieces_kernel,
        out_shape=shape(chips, tokens, (heads + 1) * width, dtype=bf16),
        in_specs=[VMEM] * 2,
        out_specs=VMEM,
        compiler_params=PARAMS,
        name="pieces",
    )(queries, span_latents)
    here = lax.all_to_all(
        pieces, "ctx", split_axis=0, concat_axis=0, axis_index_groups=same_core, tiled=True
    )

    right, left = lax.optimization_barrier((right, left))
    keys, state, at = [own, right, left], None, 0
    for s in range(2, steps):
        right, left = onward(right), backward(left)
        if s == 2:
            here = here.reshape(chips * tokens, (heads + 1) * width)
            there = lax.ppermute(here, "ctx", other_core)
            keys += [right, left]
            continue
        if state is None:
            q, *state = fold_first(keys)
        else:
            state = fold_more(at, q, state, keys)
        at += len(keys)
        keys = [right, left]
    top = onward(right[:cut])
    left, state = lax.optimization_barrier((left, state))
    bottom = backward(left[cut:])
    state = pl.pallas_call(
        functools.partial(span_kernel, at, len(keys)),
        out_shape=state_shapes,
        in_specs=[SMEM] * 3 + [VMEM] * (5 + len(keys)),
        out_specs=[VMEM] * 3,
        compiler_params=PARAMS,
        name="middle",
    )(prefix_length, span_offset, table, q, *state, here, *keys)
    per_core = heads // CORES
    part = per_core * everyone
    keep, give = pl.pallas_call(
        functools.partial(last_kernel, chips - 1, heads),
        out_shape=[shape(part, LATENT + LANES), shape(part, LATENT + LANES, dtype=bf16)],
        in_specs=[SMEM] * 2 + [VMEM] * 6,
        out_specs=[VMEM] * 2,
        compiler_params=PARAMS,
        name="last",
    )(prefix_length, table, q, *state, top, bottom)
    got = lax.ppermute(give, "ctx", other_core)
    merged = pl.pallas_call(
        merge_kernel,
        out_shape=shape(ctx, tokens, per_core * V_HEAD, dtype=bf16),
        in_specs=[VMEM] * 3,
        out_specs=VMEM,
        scratch_shapes=[pltpu.VMEM((everyone, per_core * V_HEAD), f32)],
        compiler_params=PARAMS,
        name="merge",
    )(keep, got, value_up)
    returned = lax.all_to_all(merged, "ctx", split_axis=0, concat_axis=0, tiled=True)
    return returned.transpose(1, 0, 2).reshape(tokens, all_heads * V_HEAD)


def solution(mesh):
    return jax.shard_map(
        functools.partial(on_device, mesh.shape["ctx"]),
        mesh=mesh,
        in_specs=(
            P(("groups", "ctx"), None),
            P(("groups", "ctx"), None),
            P(("groups", "ctx"), None),
            P("ctx", None, None),
            P("groups"),
            P("groups"),
        ),
        out_specs=P(("groups", "ctx"), None),
        check_vma=False,
    )
```

```python
import functools
import math

import jax
import jax.numpy as jnp
import numpy as np
from jax import lax
from jax.experimental import pallas as pl
from jax.experimental.pallas import tpu as pltpu
from jax.sharding import PartitionSpec as P

LATENT = 512
V_HEAD = 128
CORES = 2
LANES = 128

score_scale = 192.0 ** (-0.5) * math.log2(math.e)
neg_large = -1e30
least_max = -1e29
f32 = jnp.float32
bf16 = jnp.bfloat16


def chip_cycle(chips):
    wide = max(1, int(round(chips ** (1 / 3))))
    tall = chips // wide
    if wide * tall != chips or wide < 2 or tall < 2:
        return list(range(chips))
    walk = []
    for z in range(tall):
        across = range(1, wide) if z % 2 == 0 else range(wide - 1, 0, -1)
        walk += [z * wide + x for x in across]
    return walk + [z * wide for z in reversed(range(tall))]


def scores_of(q_ref, part, pieces):
    total, at = None, 0
    for piece in pieces:
        s = jnp.dot(
            q_ref[part, at:at + piece.shape[0]], piece[...], preferred_element_type=f32
        )
        total, at = s if total is None else total + s, at + piece.shape[0]
    return total


def values_of(weights, pieces):
    summed, at = [], 0
    for piece in pieces:
        wide = min(piece.shape[0], LATENT - at)
        summed.append(lax.dot_general(
            weights, piece[:wide, :], (((1,), (1,)), ((), ())), preferred_element_type=f32
        ))
        at += wide
    return summed[0] if len(summed) == 1 else jnp.concatenate(summed, axis=1)


def fold_block(part, q_ref, shards, length, old=None, span=None):
    m_old = least_max if old is None else old[0][part, :][:, :1]
    m_new = m_old
    scores = []
    for base, key_ref in shards:
        slot = base + lax.broadcasted_iota(jnp.int32, (1, key_ref[0].shape[1]), 1)
        s = scores_of(q_ref, part, key_ref) * score_scale
        s = jnp.where(slot < length, s, neg_large)
        m_new = jnp.maximum(m_new, jnp.max(s, axis=1, keepdims=True))
        scores.append(s)
    if span is not None:
        keys, shown = span
        s = lax.dot_general(
            q_ref[part, :], keys, (((1,), (1,)), ((), ())), preferred_element_type=f32
        )
        span_s = jnp.where(shown, s * score_scale, neg_large)
        m_new = jnp.maximum(m_new, jnp.max(span_s, axis=1, keepdims=True))
    l_new, summed = 0.0, 0.0
    if old is not None:
        shrink = jnp.exp2(m_old - m_new)
        l_new = old[1][part, :][:, :1] * shrink
        summed = old[2][part, :] * shrink
    for s, (_, key_ref) in zip(scores, shards):
        probs = jnp.exp2(s - m_new)
        l_new += jnp.sum(probs, axis=1, keepdims=True)
        summed += values_of(probs.astype(bf16), key_ref)
    if span is not None:
        probs = jnp.exp2(span_s - m_new)
        l_new += jnp.sum(probs, axis=1, keepdims=True)
        summed += jnp.dot(
            probs.astype(bf16), keys[:, :LATENT], preferred_element_type=f32
        )
    return m_new, l_new, summed


def fold_shards(q_ref, shards, length, old, new, span=None):
    rows = q_ref.shape[0]
    block = min(256, rows)
    for start in range(0, rows, block):
        part = pl.ds(start, block)
        shown = None if span is None else (span[0], span[1](start, block))
        m_new, l_new, summed = fold_block(part, q_ref, shards, length, old, shown)
        new[0][part, :] = jnp.broadcast_to(m_new, (block, LANES))
        new[1][part, :] = jnp.broadcast_to(l_new, (block, LANES))
        new[2][part, :] = summed


def parted(index, size):
    return index >> (size.bit_length() - 1), index & (size - 1)


def token_of(index, tokens, chips):
    device, t = parted(index, tokens)
    core, chip = parted(device, chips)
    return (chip * CORES + ((lax.axis_index("ctx") % CORES) ^ core)) * tokens + t


def with_base(table_ref, at, key_refs):
    me = lax.axis_index("ctx")
    count = table_ref.shape[0] // lax.axis_size("ctx")
    return [
        (table_ref[me * count + at + j] * key_ref.shape[1], (key_ref,))
        for j, key_ref in enumerate(key_refs)
    ]


def pieces_kernel(queries_ref, span_ref, out_ref):
    chips = out_ref.shape[0]
    part = queries_ref.shape[1] // chips
    for chip in range(chips):
        out_ref[chip, :, :part] = queries_ref[:, chip * part:(chip + 1) * part]
        out_ref[chip, :, part:] = span_ref[...]


def first_kernel(heads, count, length_ref, table_ref, here_ref, there_ref, *rest):
    keys, (q_ref, m_ref, l_ref, acc_ref) = rest[:count], rest[count:]
    half = here_ref.shape[0]
    width = q_ref.shape[1]
    for core, piece_ref in enumerate((here_ref, there_ref)):
        for head in range(heads):
            row = (head * CORES + core) * half
            q_ref[row:row + half, :] = piece_ref[:, head * width:(head + 1) * width]
    shards = with_base(table_ref, 0, keys)
    fold_shards(q_ref, shards, length_ref[0], None, (m_ref, l_ref, acc_ref))


def middle_kernel(at, count, length_ref, table_ref, q_ref, m_in, l_in, acc_in, *rest):
    keys, new = rest[:count], rest[count:]
    fold_shards(q_ref, with_base(table_ref, at, keys), length_ref[0], (m_in, l_in, acc_in), new)


def span_kernel(at, count, length_ref, offset_ref, table_ref, q_ref, m_in, l_in, acc_in,
                here_ref, *rest):
    keys, new = rest[:count], rest[count:]
    chips = lax.axis_size("ctx") // CORES
    half = here_ref.shape[0]
    tokens = half // chips
    width = q_ref.shape[1]
    key_index = lax.broadcasted_iota(jnp.int32, (1, half), 1)
    key_token = token_of(key_index, tokens, chips)

    def shown(start, block):
        row_index = start + lax.broadcasted_iota(jnp.int32, (block, 1), 0)
        row_token = token_of(row_index & (half * CORES - 1), tokens, chips)
        return (key_token >= offset_ref[0]) & (key_token <= row_token)

    fold_shards(
        q_ref, with_base(table_ref, at, keys), length_ref[0], (m_in, l_in, acc_in), new,
        (here_ref[:, here_ref.shape[1] - width:], shown),
    )


def last_kernel(at, side, length_ref, table_ref, q_ref, m_ref, l_ref, acc_ref,
                top_ref, bottom_ref, out_ref):
    core = lax.axis_index("ctx") % CORES
    shards = [(with_base(table_ref, at, (top_ref,))[0][0], (top_ref, bottom_ref))]
    rows = out_ref.shape[0]
    part = pl.ds(pl.multiple_of((core ^ side) * rows, rows), rows)
    m_new, l_new, summed = fold_block(
        part, q_ref, shards, length_ref[0], (m_ref, l_ref, acc_ref)
    )
    out_ref[:, :LATENT] = (summed * (1.0 / l_new)).astype(out_ref.dtype)
    weight = jnp.broadcast_to(m_new + jnp.log2(l_new), (rows, LANES))
    if side:
        lane = lax.broadcasted_iota(jnp.int32, (rows, LANES), 1)
        high = weight.astype(bf16).astype(f32)
        mid = (weight - high).astype(bf16).astype(f32)
        weight = jnp.where(lane == 0, high, jnp.where(lane == 1, mid, weight - high - mid))
    out_ref[:, LATENT:] = weight.astype(out_ref.dtype)


def merge_kernel(keep_ref, got_ref, up_ref, out_ref, flat_ref):
    core = lax.axis_index("ctx") % CORES
    heads = up_ref.shape[0]
    everyone = flat_ref.shape[0]
    half = everyone // CORES
    pair = min(2, heads)
    for j in range(0, heads, pair):
        contexts = []
        for head in range(j, j + pair):
            row = head * everyone
            got = jnp.concatenate(
                [got_ref[row + half:row + everyone, :], got_ref[row:row + half, :]], axis=0
            ).astype(f32)
            keep = keep_ref[row:row + everyone, :]
            gap = keep[:, LATENT:LATENT + 1] - got[:, LATENT:LATENT + 1]
            gap = gap - got[:, LATENT + 1:LATENT + 2] - got[:, LATENT + 2:LATENT + 3]
            share = 1.0 / (1.0 + jnp.exp2(-gap))
            rest = 1.0 / (1.0 + jnp.exp2(gap))
            contexts.append(
                (keep[:, :LATENT] * share + got[:, :LATENT] * rest).astype(bf16)
            )
        lifted = jnp.dot(
            jnp.concatenate(contexts, axis=0),
            jnp.concatenate([up_ref[j + i] for i in range(pair)], axis=1),
            preferred_element_type=f32,
        )
        for i in range(pair):
            flat_ref[:, (j + i) * V_HEAD:(j + i + 1) * V_HEAD] = lifted[
                i * everyone:(i + 1) * everyone, i * V_HEAD:(i + 1) * V_HEAD
            ]
    devices, tokens, _ = out_ref.shape
    chips = devices // CORES
    for i in range(devices):
        out_ref[(i % chips) * CORES + (core ^ (i // chips))] = (
            flat_ref[i * tokens:(i + 1) * tokens, :].astype(bf16)
        )


VMEM = pl.BlockSpec(memory_space=pltpu.VMEM)
SMEM = pl.BlockSpec(memory_space=pltpu.SMEM)
PARAMS = pltpu.CompilerParams(vmem_limit_bytes=32 * 1024 * 1024)


def shape(*dims, dtype=f32):
    return jax.ShapeDtypeStruct(dims, dtype)


def on_device(ctx, queries, prefix_latents, span_latents, value_up, prefix_length, span_offset):
    slots, width = prefix_latents.shape
    tokens = queries.shape[0]
    all_heads = queries.shape[1] // width
    chips = ctx // CORES
    heads = all_heads // chips
    rows = tokens * heads
    total = rows * ctx
    everyone = tokens * ctx
    walk = chip_cycle(chips)
    spot = np.argsort(np.array(walk))
    steps = chips // 2

    def across(step):
        return [
            (walk[r] * CORES + c, walk[(r + (-step if c else step)) % chips] * CORES + c)
            for r in range(chips) for c in range(CORES)
        ]

    other_core = [(d, d ^ 1) for d in range(ctx)]
    same_core = [[p * CORES + c for p in range(chips)] for c in range(CORES)]

    turns = [0]
    for s in range(1, steps):
        turns += [-s, s]
    turns.append(steps)
    owner_table = np.array(
        [
            [walk[(spot[p] + (-t if c else t)) % chips] * CORES + c for t in turns]
            for p in range(chips) for c in range(CORES)
        ],
        np.int32,
    )
    table = jnp.asarray(owner_table.reshape(-1))
    state_shapes = [shape(total, LANES), shape(total, LANES), shape(total, LATENT)]

    def fold_first(keys):
        return pl.pallas_call(
            functools.partial(first_kernel, heads, len(keys)),
            out_shape=[shape(total, width, dtype=bf16)] + state_shapes,
            in_specs=[SMEM] * 2 + [VMEM] * (2 + len(keys)),
            out_specs=[VMEM] * 4,
            compiler_params=PARAMS,
            name="first",
        )(prefix_length, table, here, there, *keys)

    def fold_more(at, q, state, keys):
        return pl.pallas_call(
            functools.partial(middle_kernel, at, len(keys)),
            out_shape=state_shapes,
            in_specs=[SMEM] * 2 + [VMEM] * (4 + len(keys)),
            out_specs=[VMEM] * 3,
            compiler_params=PARAMS,
            name="middle",
        )(prefix_length, table, q, *state, *keys)

    onward = functools.partial(lax.ppermute, axis_name="ctx", perm=across(1))
    backward = functools.partial(lax.ppermute, axis_name="ctx", perm=across(-1))
    cut = LATENT // 2
    own = prefix_latents.T
    right, left = onward(own), backward(own)

    pieces = pl.pallas_call(
        pieces_kernel,
        out_shape=shape(chips, tokens, (heads + 1) * width, dtype=bf16),
        in_specs=[VMEM] * 2,
        out_specs=VMEM,
        compiler_params=PARAMS,
        name="pieces",
    )(queries, span_latents)
    here = lax.all_to_all(
        pieces, "ctx", split_axis=0, concat_axis=0, axis_index_groups=same_core, tiled=True
    )

    right, left = lax.optimization_barrier((right, left))
    keys, state, at = [own, right, left], None, 0
    for s in range(2, steps):
        right, left = onward(right), backward(left)
        if s == 2:
            here = here.reshape(chips * tokens, (heads + 1) * width)
            there = lax.ppermute(here, "ctx", other_core)
            keys += [right, left]
            continue
        if state is None:
            q, *state = fold_first(keys)
        else:
            state = fold_more(at, q, state, keys)
        at += len(keys)
        keys = [right, left]
    top = onward(right[:cut])
    left, state = lax.optimization_barrier((left, state))
    bottom = backward(left[cut:])
    state = pl.pallas_call(
        functools.partial(span_kernel, at, len(keys)),
        out_shape=state_shapes,
        in_specs=[SMEM] * 3 + [VMEM] * (5 + len(keys)),
        out_specs=[VMEM] * 3,
        compiler_params=PARAMS,
        name="middle",
    )(prefix_length, span_offset, table, q, *state, here, *keys)
    per_core = heads // CORES
    part = per_core * everyone

    def fold_last(side, dtype):
        return pl.pallas_call(
            functools.partial(last_kernel, chips - 1, side),
            out_shape=shape(part, LATENT + LANES, dtype=dtype),
            in_specs=[SMEM] * 2 + [VMEM] * 6,
            out_specs=VMEM,
            compiler_params=PARAMS,
            name="keep" if side == 0 else "give",
        )(prefix_length, table, q, *state, top, bottom)

    got = lax.ppermute(fold_last(1, bf16), "ctx", other_core)
    keep = fold_last(0, f32)
    merged = pl.pallas_call(
        merge_kernel,
        out_shape=shape(ctx, tokens, per_core * V_HEAD, dtype=bf16),
        in_specs=[VMEM] * 3,
        out_specs=VMEM,
        scratch_shapes=[pltpu.VMEM((everyone, per_core * V_HEAD), f32)],
        compiler_params=PARAMS,
        name="merge",
    )(keep, got, value_up)
    returned = lax.all_to_all(merged, "ctx", split_axis=0, concat_axis=0, tiled=True)
    return returned.transpose(1, 0, 2).reshape(tokens, all_heads * V_HEAD)


def solution(mesh):
    return jax.shard_map(
        functools.partial(on_device, mesh.shape["ctx"]),
        mesh=mesh,
        in_specs=(
            P(("groups", "ctx"), None),
            P(("groups", "ctx"), None),
            P(("groups", "ctx"), None),
            P("ctx", None, None),
            P("groups"),
            P("groups"),
        ),
        out_specs=P(("groups", "ctx"), None),
        check_vma=False,
    )
```

```python
import functools
import math

import jax
import jax.numpy as jnp
import numpy as np
from jax import lax
from jax.experimental import pallas as pl
from jax.experimental.pallas import tpu as pltpu
from jax.sharding import PartitionSpec as P

LATENT = 512
V_HEAD = 128
CORES = 2
LANES = 128

score_scale = 192.0 ** (-0.5) * math.log2(math.e)
neg_large = -1e30
least_max = -1e29
f32 = jnp.float32
bf16 = jnp.bfloat16


def chip_cycle(chips):
    wide = max(1, int(round(chips ** (1 / 3))))
    tall = chips // wide
    if wide * tall != chips or wide < 2 or tall < 2:
        return list(range(chips))
    walk = []
    for z in range(tall):
        across = range(1, wide) if z % 2 == 0 else range(wide - 1, 0, -1)
        walk += [z * wide + x for x in across]
    return walk + [z * wide for z in reversed(range(tall))]


def scores_of(q_ref, part, pieces):
    total, at = None, 0
    for piece in pieces:
        s = jnp.dot(
            q_ref[part, at:at + piece.shape[0]], piece[...], preferred_element_type=f32
        )
        total, at = s if total is None else total + s, at + piece.shape[0]
    return total


def values_of(weights, pieces):
    summed, at = [], 0
    for piece in pieces:
        wide = min(piece.shape[0], LATENT - at)
        summed.append(lax.dot_general(
            weights, piece[:wide, :], (((1,), (1,)), ((), ())), preferred_element_type=f32
        ))
        at += wide
    return summed[0] if len(summed) == 1 else jnp.concatenate(summed, axis=1)


def fold_block(part, q_ref, shards, length, old=None, span=None):
    m_old = least_max if old is None else old[0][part, :][:, :1]
    m_new = m_old
    scores = []
    for base, key_ref in shards:
        slot = base + lax.broadcasted_iota(jnp.int32, (1, key_ref[0].shape[1]), 1)
        s = scores_of(q_ref, part, key_ref) * score_scale
        s = jnp.where(slot < length, s, neg_large)
        m_new = jnp.maximum(m_new, jnp.max(s, axis=1, keepdims=True))
        scores.append(s)
    if span is not None:
        keys, shown = span
        s = lax.dot_general(
            q_ref[part, :], keys, (((1,), (1,)), ((), ())), preferred_element_type=f32
        )
        span_s = jnp.where(shown, s * score_scale, neg_large)
        m_new = jnp.maximum(m_new, jnp.max(span_s, axis=1, keepdims=True))
    l_new, summed = 0.0, 0.0
    if old is not None:
        shrink = jnp.exp2(m_old - m_new)
        l_new = old[1][part, :][:, :1] * shrink
        summed = old[2][part, :] * shrink
    for s, (_, key_ref) in zip(scores, shards):
        probs = jnp.exp2(s - m_new)
        l_new += jnp.sum(probs, axis=1, keepdims=True)
        summed += values_of(probs.astype(bf16), key_ref)
    if span is not None:
        probs = jnp.exp2(span_s - m_new)
        l_new += jnp.sum(probs, axis=1, keepdims=True)
        summed += jnp.dot(
            probs.astype(bf16), keys[:, :LATENT], preferred_element_type=f32
        )
    return m_new, l_new, summed


def fold_shards(q_ref, shards, length, old, new, span=None):
    rows = q_ref.shape[0]
    block = min(256, rows)
    for start in range(0, rows, block):
        part = pl.ds(start, block)
        shown = None if span is None else (span[0], span[1](start, block))
        m_new, l_new, summed = fold_block(part, q_ref, shards, length, old, shown)
        new[0][part, :] = jnp.broadcast_to(m_new, (block, LANES))
        new[1][part, :] = jnp.broadcast_to(l_new, (block, LANES))
        new[2][part, :] = summed


def parted(index, size):
    return index >> (size.bit_length() - 1), index & (size - 1)


def token_of(index, tokens, chips):
    device, t = parted(index, tokens)
    core, chip = parted(device, chips)
    return (chip * CORES + ((lax.axis_index("ctx") % CORES) ^ core)) * tokens + t


def with_base(table_ref, at, key_refs):
    me = lax.axis_index("ctx")
    count = table_ref.shape[0] // lax.axis_size("ctx")
    return [
        (table_ref[me * count + at + j] * key_ref.shape[1], (key_ref,))
        for j, key_ref in enumerate(key_refs)
    ]


def first_kernel(heads, count, length_ref, table_ref, here_ref, there_ref, *rest):
    keys, (q_ref, m_ref, l_ref, acc_ref) = rest[:count], rest[count:]
    half = here_ref.shape[0]
    width = q_ref.shape[1]
    for core, piece_ref in enumerate((here_ref, there_ref)):
        for head in range(heads):
            row = (head * CORES + core) * half
            q_ref[row:row + half, :] = piece_ref[:, head * width:(head + 1) * width]
    shards = with_base(table_ref, 0, keys)
    fold_shards(q_ref, shards, length_ref[0], None, (m_ref, l_ref, acc_ref))


def middle_kernel(at, count, length_ref, table_ref, q_ref, m_in, l_in, acc_in, *rest):
    keys, new = rest[:count], rest[count:]
    fold_shards(q_ref, with_base(table_ref, at, keys), length_ref[0], (m_in, l_in, acc_in), new)


def span_kernel(at, count, length_ref, offset_ref, table_ref, q_ref, m_in, l_in, acc_in,
                span_ref, *rest):
    keys, new = rest[:count], rest[count:]
    chips = lax.axis_size("ctx") // CORES
    half = span_ref.shape[0]
    tokens = half // chips
    slot, t = parted(lax.broadcasted_iota(jnp.int32, (1, half), 1), tokens)
    me = lax.axis_index("ctx")
    key_token = (((me // CORES) ^ slot) * CORES + me % CORES) * tokens + t

    def shown(start, block):
        row_index = start + lax.broadcasted_iota(jnp.int32, (block, 1), 0)
        row_token = token_of(row_index & (half * CORES - 1), tokens, chips)
        return (key_token >= offset_ref[0]) & (key_token <= row_token)

    fold_shards(
        q_ref, with_base(table_ref, at, keys), length_ref[0], (m_in, l_in, acc_in), new,
        (span_ref[...], shown),
    )


def last_kernel(at, side, length_ref, table_ref, q_ref, m_ref, l_ref, acc_ref,
                top_ref, bottom_ref, out_ref):
    core = lax.axis_index("ctx") % CORES
    shards = [(with_base(table_ref, at, (top_ref,))[0][0], (top_ref, bottom_ref))]
    rows = out_ref.shape[0]
    part = pl.ds(pl.multiple_of((core ^ side) * rows, rows), rows)
    m_new, l_new, summed = fold_block(
        part, q_ref, shards, length_ref[0], (m_ref, l_ref, acc_ref)
    )
    out_ref[:, :LATENT] = (summed * (1.0 / l_new)).astype(out_ref.dtype)
    weight = jnp.broadcast_to(m_new + jnp.log2(l_new), (rows, LANES))
    if side:
        lane = lax.broadcasted_iota(jnp.int32, (rows, LANES), 1)
        high = weight.astype(bf16).astype(f32)
        mid = (weight - high).astype(bf16).astype(f32)
        weight = jnp.where(lane == 0, high, jnp.where(lane == 1, mid, weight - high - mid))
    out_ref[:, LATENT:] = weight.astype(out_ref.dtype)


def merge_kernel(keep_ref, got_ref, up_ref, out_ref, flat_ref):
    core = lax.axis_index("ctx") % CORES
    heads = up_ref.shape[0]
    everyone = flat_ref.shape[0]
    half = everyone // CORES
    pair = min(2, heads)
    for j in range(0, heads, pair):
        contexts = []
        for head in range(j, j + pair):
            row = head * everyone
            got = jnp.concatenate(
                [got_ref[row + half:row + everyone, :], got_ref[row:row + half, :]], axis=0
            ).astype(f32)
            keep = keep_ref[row:row + everyone, :]
            gap = keep[:, LATENT:LATENT + 1] - got[:, LATENT:LATENT + 1]
            gap = gap - got[:, LATENT + 1:LATENT + 2] - got[:, LATENT + 2:LATENT + 3]
            share = 1.0 / (1.0 + jnp.exp2(-gap))
            rest = 1.0 / (1.0 + jnp.exp2(gap))
            contexts.append(
                (keep[:, :LATENT] * share + got[:, :LATENT] * rest).astype(bf16)
            )
        lifted = jnp.dot(
            jnp.concatenate(contexts, axis=0),
            jnp.concatenate([up_ref[j + i] for i in range(pair)], axis=1),
            preferred_element_type=f32,
        )
        for i in range(pair):
            flat_ref[:, (j + i) * V_HEAD:(j + i + 1) * V_HEAD] = lifted[
                i * everyone:(i + 1) * everyone, i * V_HEAD:(i + 1) * V_HEAD
            ]
    devices, tokens, _ = out_ref.shape
    chips = devices // CORES
    for i in range(devices):
        out_ref[(i % chips) * CORES + (core ^ (i // chips))] = (
            flat_ref[i * tokens:(i + 1) * tokens, :].astype(bf16)
        )


VMEM = pl.BlockSpec(memory_space=pltpu.VMEM)
SMEM = pl.BlockSpec(memory_space=pltpu.SMEM)
PARAMS = pltpu.CompilerParams(vmem_limit_bytes=32 * 1024 * 1024)


def shape(*dims, dtype=f32):
    return jax.ShapeDtypeStruct(dims, dtype)


def on_device(ctx, queries, prefix_latents, span_latents, value_up, prefix_length, span_offset):
    slots, width = prefix_latents.shape
    tokens = queries.shape[0]
    all_heads = queries.shape[1] // width
    chips = ctx // CORES
    heads = all_heads // chips
    rows = tokens * heads
    total = rows * ctx
    everyone = tokens * ctx
    walk = chip_cycle(chips)
    spot = np.argsort(np.array(walk))
    steps = chips // 2

    def across(step):
        return [
            (walk[r] * CORES + c, walk[(r + (-step if c else step)) % chips] * CORES + c)
            for r in range(chips) for c in range(CORES)
        ]

    other_core = [(d, d ^ 1) for d in range(ctx)]
    same_core = [[p * CORES + c for p in range(chips)] for c in range(CORES)]

    turns = [0]
    for s in range(1, steps):
        turns += [-s, s]
    turns.append(steps)
    owner_table = np.array(
        [
            [walk[(spot[p] + (-t if c else t)) % chips] * CORES + c for t in turns]
            for p in range(chips) for c in range(CORES)
        ],
        np.int32,
    )
    table = jnp.asarray(owner_table.reshape(-1))
    state_shapes = [shape(total, LANES), shape(total, LANES), shape(total, LATENT)]

    def fold_first(keys):
        return pl.pallas_call(
            functools.partial(first_kernel, heads, len(keys)),
            out_shape=[shape(total, width, dtype=bf16)] + state_shapes,
            in_specs=[SMEM] * 2 + [VMEM] * (2 + len(keys)),
            out_specs=[VMEM] * 4,
            compiler_params=PARAMS,
            name="first",
        )(prefix_length, table, here, there, *keys)

    def fold_more(at, q, state, keys):
        return pl.pallas_call(
            functools.partial(middle_kernel, at, len(keys)),
            out_shape=state_shapes,
            in_specs=[SMEM] * 2 + [VMEM] * (4 + len(keys)),
            out_specs=[VMEM] * 3,
            compiler_params=PARAMS,
            name="middle",
        )(prefix_length, table, q, *state, *keys)

    onward = functools.partial(lax.ppermute, axis_name="ctx", perm=across(1))
    backward = functools.partial(lax.ppermute, axis_name="ctx", perm=across(-1))
    cut = LATENT // 2
    own = prefix_latents.T
    right, left = onward(own), backward(own)

    pieces = queries.reshape(tokens, chips, heads * width).transpose(1, 0, 2)
    here = lax.all_to_all(
        pieces, "ctx", split_axis=0, concat_axis=0, axis_index_groups=same_core, tiled=True
    )

    right, left = lax.optimization_barrier((right, left))
    spans, bit = span_latents, 1
    while bit < chips:
        swap = [(d, d ^ (bit * CORES)) for d in range(ctx)]
        spans = jnp.concatenate([spans, lax.ppermute(spans, "ctx", swap)], axis=0)
        bit *= 2
    keys, state, at = [own, right, left], None, 0
    for s in range(2, steps):
        right, left = onward(right), backward(left)
        if s == 2:
            here, spans = lax.optimization_barrier((here, spans))
            here = here.reshape(chips * tokens, heads * width)
            there = lax.ppermute(here, "ctx", other_core)
            keys += [right, left]
            continue
        if state is None:
            q, *state = fold_first(keys)
        else:
            state = fold_more(at, q, state, keys)
        at += len(keys)
        keys = [right, left]
    top = onward(right[:cut])
    left, state = lax.optimization_barrier((left, state))
    bottom = backward(left[cut:])
    state = pl.pallas_call(
        functools.partial(span_kernel, at, len(keys)),
        out_shape=state_shapes,
        in_specs=[SMEM] * 3 + [VMEM] * (5 + len(keys)),
        out_specs=[VMEM] * 3,
        compiler_params=PARAMS,
        name="middle",
    )(prefix_length, span_offset, table, q, *state, spans, *keys)
    per_core = heads // CORES
    part = per_core * everyone

    def fold_last(side, dtype):
        return pl.pallas_call(
            functools.partial(last_kernel, chips - 1, side),
            out_shape=shape(part, LATENT + LANES, dtype=dtype),
            in_specs=[SMEM] * 2 + [VMEM] * 6,
            out_specs=VMEM,
            compiler_params=PARAMS,
            name="keep" if side == 0 else "give",
        )(prefix_length, table, q, *state, top, bottom)

    got = lax.ppermute(fold_last(1, bf16), "ctx", other_core)
    keep = fold_last(0, f32)
    merged = pl.pallas_call(
        merge_kernel,
        out_shape=shape(ctx, tokens, per_core * V_HEAD, dtype=bf16),
        in_specs=[VMEM] * 3,
        out_specs=VMEM,
        scratch_shapes=[pltpu.VMEM((everyone, per_core * V_HEAD), f32)],
        compiler_params=PARAMS,
        name="merge",
    )(keep, got, value_up)
    returned = lax.all_to_all(merged, "ctx", split_axis=0, concat_axis=0, tiled=True)
    return returned.transpose(1, 0, 2).reshape(tokens, all_heads * V_HEAD)


def solution(mesh):
    return jax.shard_map(
        functools.partial(on_device, mesh.shape["ctx"]),
        mesh=mesh,
        in_specs=(
            P(("groups", "ctx"), None),
            P(("groups", "ctx"), None),
            P(("groups", "ctx"), None),
            P("ctx", None, None),
            P("groups"),
            P("groups"),
        ),
        out_specs=P(("groups", "ctx"), None),
        check_vma=False,
    )
```

```python
import functools
import math

import jax
import jax.numpy as jnp
import numpy as np
from jax import lax
from jax.experimental import pallas as pl
from jax.experimental.pallas import tpu as pltpu
from jax.sharding import PartitionSpec as P

LATENT = 512
V_HEAD = 128
CORES = 2
LANES = 128

score_scale = 192.0 ** (-0.5) * math.log2(math.e)
neg_large = -1e30
least_max = -1e29
f32 = jnp.float32
bf16 = jnp.bfloat16


def chip_cycle(chips):
    wide = max(1, int(round(chips ** (1 / 3))))
    tall = chips // wide
    if wide * tall != chips or wide < 2 or tall < 2:
        return list(range(chips))
    walk = []
    for z in range(tall):
        across = range(1, wide) if z % 2 == 0 else range(wide - 1, 0, -1)
        walk += [z * wide + x for x in across]
    return walk + [z * wide for z in reversed(range(tall))]


def scores_of(q_ref, part, pieces):
    total, at = None, 0
    for piece in pieces:
        s = jnp.dot(
            q_ref[part, at:at + piece.shape[0]], piece[...], preferred_element_type=f32
        )
        total, at = s if total is None else total + s, at + piece.shape[0]
    return total


def values_of(weights, pieces):
    summed, at = [], 0
    for piece in pieces:
        wide = min(piece.shape[0], LATENT - at)
        summed.append(lax.dot_general(
            weights, piece[:wide, :], (((1,), (1,)), ((), ())), preferred_element_type=f32
        ))
        at += wide
    return summed[0] if len(summed) == 1 else jnp.concatenate(summed, axis=1)


def fold_block(part, q_ref, shards, length, old=None, span=None):
    m_old = least_max if old is None else old[0][part, :][:, :1]
    m_new = m_old
    scores = []
    for base, key_ref in shards:
        slot = base + lax.broadcasted_iota(jnp.int32, (1, key_ref[0].shape[1]), 1)
        s = scores_of(q_ref, part, key_ref) * score_scale
        s = jnp.where(slot < length, s, neg_large)
        m_new = jnp.maximum(m_new, jnp.max(s, axis=1, keepdims=True))
        scores.append(s)
    if span is not None:
        keys, shown = span
        s = lax.dot_general(
            q_ref[part, :], keys, (((1,), (1,)), ((), ())), preferred_element_type=f32
        )
        span_s = jnp.where(shown, s * score_scale, neg_large)
        m_new = jnp.maximum(m_new, jnp.max(span_s, axis=1, keepdims=True))
    l_new, summed = 0.0, 0.0
    if old is not None:
        shrink = jnp.exp2(m_old - m_new)
        l_new = old[1][part, :][:, :1] * shrink
        summed = old[2][part, :] * shrink
    for s, (_, key_ref) in zip(scores, shards):
        probs = jnp.exp2(s - m_new)
        l_new += jnp.sum(probs, axis=1, keepdims=True)
        summed += values_of(probs.astype(bf16), key_ref)
    if span is not None:
        probs = jnp.exp2(span_s - m_new)
        l_new += jnp.sum(probs, axis=1, keepdims=True)
        summed += jnp.dot(
            probs.astype(bf16), keys[:, :LATENT], preferred_element_type=f32
        )
    return m_new, l_new, summed


def fold_shards(q_ref, shards, length, old, new, span=None):
    rows = q_ref.shape[0]
    block = min(256, rows)
    for start in range(0, rows, block):
        part = pl.ds(start, block)
        shown = None if span is None else (span[0], span[1](start, block))
        m_new, l_new, summed = fold_block(part, q_ref, shards, length, old, shown)
        new[0][part, :] = jnp.broadcast_to(m_new, (block, LANES))
        new[1][part, :] = jnp.broadcast_to(l_new, (block, LANES))
        new[2][part, :] = summed


def parted(index, size):
    return index >> (size.bit_length() - 1), index & (size - 1)


def token_of(index, tokens, chips):
    device, t = parted(index, tokens)
    core, chip = parted(device, chips)
    return (chip * CORES + ((lax.axis_index("ctx") % CORES) ^ core)) * tokens + t


def with_base(table_ref, at, key_refs):
    me = lax.axis_index("ctx")
    count = table_ref.shape[0] // lax.axis_size("ctx")
    return [
        (table_ref[me * count + at + j] * key_ref.shape[1], (key_ref,))
        for j, key_ref in enumerate(key_refs)
    ]


def pieces_kernel(queries_hbm, span_hbm, out_ref, queries_ref, span_ref, sems):
    copies = [
        pltpu.make_async_copy(queries_hbm, queries_ref, sems.at[0]),
        pltpu.make_async_copy(span_hbm, span_ref, sems.at[1]),
    ]
    for copy in copies:
        copy.start()
    for copy in copies:
        copy.wait()
    chips = out_ref.shape[0]
    part = queries_ref.shape[1] // chips
    for chip in range(chips):
        out_ref[chip, :, :part] = queries_ref[:, chip * part:(chip + 1) * part]
        out_ref[chip, :, part:] = span_ref[...]


def first_kernel(heads, count, length_ref, table_ref, here_ref, there_ref, *rest):
    keys, (q_ref, m_ref, l_ref, acc_ref) = rest[:count], rest[count:]
    half = here_ref.shape[0]
    width = q_ref.shape[1]
    for core, piece_ref in enumerate((here_ref, there_ref)):
        for head in range(heads):
            row = (head * CORES + core) * half
            q_ref[row:row + half, :] = piece_ref[:, head * width:(head + 1) * width]
    shards = with_base(table_ref, 0, keys)
    fold_shards(q_ref, shards, length_ref[0], None, (m_ref, l_ref, acc_ref))


def middle_kernel(at, count, length_ref, table_ref, q_ref, m_in, l_in, acc_in, *rest):
    keys, new = rest[:count], rest[count:]
    fold_shards(q_ref, with_base(table_ref, at, keys), length_ref[0], (m_in, l_in, acc_in), new)


def span_kernel(at, count, length_ref, offset_ref, table_ref, q_ref, m_in, l_in, acc_in,
                here_ref, *rest):
    keys, new = rest[:count], rest[count:]
    chips = lax.axis_size("ctx") // CORES
    half = here_ref.shape[0]
    tokens = half // chips
    width = q_ref.shape[1]
    key_index = lax.broadcasted_iota(jnp.int32, (1, half), 1)
    key_token = token_of(key_index, tokens, chips)

    def shown(start, block):
        row_index = start + lax.broadcasted_iota(jnp.int32, (block, 1), 0)
        row_token = token_of(row_index & (half * CORES - 1), tokens, chips)
        return (key_token >= offset_ref[0]) & (key_token <= row_token)

    fold_shards(
        q_ref, with_base(table_ref, at, keys), length_ref[0], (m_in, l_in, acc_in), new,
        (here_ref[:, here_ref.shape[1] - width:], shown),
    )


def last_kernel(at, side, length_ref, table_ref, q_ref, m_ref, l_ref, acc_ref,
                top_ref, bottom_ref, out_ref):
    core = lax.axis_index("ctx") % CORES
    shards = [(with_base(table_ref, at, (top_ref,))[0][0], (top_ref, bottom_ref))]
    rows = out_ref.shape[0]
    part = pl.ds(pl.multiple_of((core ^ side) * rows, rows), rows)
    m_new, l_new, summed = fold_block(
        part, q_ref, shards, length_ref[0], (m_ref, l_ref, acc_ref)
    )
    out_ref[:, :LATENT] = (summed * (1.0 / l_new)).astype(out_ref.dtype)
    weight = jnp.broadcast_to(m_new + jnp.log2(l_new), (rows, LANES))
    if side:
        lane = lax.broadcasted_iota(jnp.int32, (rows, LANES), 1)
        high = weight.astype(bf16).astype(f32)
        mid = (weight - high).astype(bf16).astype(f32)
        weight = jnp.where(lane == 0, high, jnp.where(lane == 1, mid, weight - high - mid))
    out_ref[:, LATENT:] = weight.astype(out_ref.dtype)


def merge_kernel(keep_ref, got_ref, up_ref, out_ref, flat_ref):
    core = lax.axis_index("ctx") % CORES
    heads = up_ref.shape[0]
    everyone = flat_ref.shape[0]
    half = everyone // CORES
    pair = min(2, heads)
    for j in range(0, heads, pair):
        contexts = []
        for head in range(j, j + pair):
            row = head * everyone
            got = jnp.concatenate(
                [got_ref[row + half:row + everyone, :], got_ref[row:row + half, :]], axis=0
            ).astype(f32)
            keep = keep_ref[row:row + everyone, :]
            gap = keep[:, LATENT:LATENT + 1] - got[:, LATENT:LATENT + 1]
            gap = gap - got[:, LATENT + 1:LATENT + 2] - got[:, LATENT + 2:LATENT + 3]
            share = 1.0 / (1.0 + jnp.exp2(-gap))
            rest = 1.0 / (1.0 + jnp.exp2(gap))
            contexts.append(
                (keep[:, :LATENT] * share + got[:, :LATENT] * rest).astype(bf16)
            )
        lifted = jnp.dot(
            jnp.concatenate(contexts, axis=0),
            jnp.concatenate([up_ref[j + i] for i in range(pair)], axis=1),
            preferred_element_type=f32,
        )
        for i in range(pair):
            flat_ref[:, (j + i) * V_HEAD:(j + i + 1) * V_HEAD] = lifted[
                i * everyone:(i + 1) * everyone, i * V_HEAD:(i + 1) * V_HEAD
            ]
    devices, tokens, _ = out_ref.shape
    chips = devices // CORES
    for i in range(devices):
        out_ref[(i % chips) * CORES + (core ^ (i // chips))] = (
            flat_ref[i * tokens:(i + 1) * tokens, :].astype(bf16)
        )


VMEM = pl.BlockSpec(memory_space=pltpu.VMEM)
SMEM = pl.BlockSpec(memory_space=pltpu.SMEM)
PARAMS = pltpu.CompilerParams(vmem_limit_bytes=32 * 1024 * 1024)


def shape(*dims, dtype=f32):
    return jax.ShapeDtypeStruct(dims, dtype)


def on_device(ctx, queries, prefix_latents, span_latents, value_up, prefix_length, span_offset):
    slots, width = prefix_latents.shape
    tokens = queries.shape[0]
    all_heads = queries.shape[1] // width
    chips = ctx // CORES
    heads = all_heads // chips
    rows = tokens * heads
    total = rows * ctx
    everyone = tokens * ctx
    walk = chip_cycle(chips)
    spot = np.argsort(np.array(walk))
    steps = chips // 2

    def across(step):
        return [
            (walk[r] * CORES + c, walk[(r + (-step if c else step)) % chips] * CORES + c)
            for r in range(chips) for c in range(CORES)
        ]

    other_core = [(d, d ^ 1) for d in range(ctx)]
    same_core = [[p * CORES + c for p in range(chips)] for c in range(CORES)]

    turns = [0]
    for s in range(1, steps):
        turns += [-s, s]
    turns.append(steps)
    owner_table = np.array(
        [
            [walk[(spot[p] + (-t if c else t)) % chips] * CORES + c for t in turns]
            for p in range(chips) for c in range(CORES)
        ],
        np.int32,
    )
    table = jnp.asarray(owner_table.reshape(-1))
    state_shapes = [shape(total, LANES), shape(total, LANES), shape(total, LATENT)]

    def fold_first(keys):
        return pl.pallas_call(
            functools.partial(first_kernel, heads, len(keys)),
            out_shape=[shape(total, width, dtype=bf16)] + state_shapes,
            in_specs=[SMEM] * 2 + [VMEM] * (2 + len(keys)),
            out_specs=[VMEM] * 4,
            compiler_params=PARAMS,
            name="first",
        )(prefix_length, table, here, there, *keys)

    def fold_more(at, q, state, keys):
        return pl.pallas_call(
            functools.partial(middle_kernel, at, len(keys)),
            out_shape=state_shapes,
            in_specs=[SMEM] * 2 + [VMEM] * (4 + len(keys)),
            out_specs=[VMEM] * 3,
            compiler_params=PARAMS,
            name="middle",
        )(prefix_length, table, q, *state, *keys)

    onward = functools.partial(lax.ppermute, axis_name="ctx", perm=across(1))
    backward = functools.partial(lax.ppermute, axis_name="ctx", perm=across(-1))
    cut = LATENT // 2
    own = prefix_latents.T
    right, left = onward(own), backward(own)

    anywhere = pl.BlockSpec(memory_space=pl.ANY)
    pieces = pl.pallas_call(
        pieces_kernel,
        out_shape=shape(chips, tokens, (heads + 1) * width, dtype=bf16),
        in_specs=[anywhere] * 2,
        out_specs=VMEM,
        scratch_shapes=[
            pltpu.VMEM(queries.shape, bf16),
            pltpu.VMEM(span_latents.shape, bf16),
            pltpu.SemaphoreType.DMA((2,)),
        ],
        compiler_params=pltpu.CompilerParams(vmem_limit_bytes=56 * 1024 * 1024),
        name="pieces",
    )(queries, span_latents)
    here = lax.all_to_all(
        pieces, "ctx", split_axis=0, concat_axis=0, axis_index_groups=same_core, tiled=True
    )

    right, left = lax.optimization_barrier((right, left))
    keys, state, at = [own, right, left], None, 0
    for s in range(2, steps):
        right, left = onward(right), backward(left)
        if s == 2:
            here = here.reshape(chips * tokens, (heads + 1) * width)
            there = lax.ppermute(here, "ctx", other_core)
            keys += [right, left]
            continue
        if state is None:
            q, *state = fold_first(keys)
        else:
            state = fold_more(at, q, state, keys)
        at += len(keys)
        keys = [right, left]
    top = onward(right[:cut])
    left, state = lax.optimization_barrier((left, state))
    bottom = backward(left[cut:])
    state = pl.pallas_call(
        functools.partial(span_kernel, at, len(keys)),
        out_shape=state_shapes,
        in_specs=[SMEM] * 3 + [VMEM] * (5 + len(keys)),
        out_specs=[VMEM] * 3,
        compiler_params=PARAMS,
        name="middle",
    )(prefix_length, span_offset, table, q, *state, here, *keys)
    per_core = heads // CORES
    part = per_core * everyone

    def fold_last(side, dtype):
        return pl.pallas_call(
            functools.partial(last_kernel, chips - 1, side),
            out_shape=shape(part, LATENT + LANES, dtype=dtype),
            in_specs=[SMEM] * 2 + [VMEM] * 6,
            out_specs=VMEM,
            compiler_params=PARAMS,
            name="keep" if side == 0 else "give",
        )(prefix_length, table, q, *state, top, bottom)

    got = lax.ppermute(fold_last(1, bf16), "ctx", other_core)
    keep = fold_last(0, f32)
    merged = pl.pallas_call(
        merge_kernel,
        out_shape=shape(ctx, tokens, per_core * V_HEAD, dtype=bf16),
        in_specs=[VMEM] * 3,
        out_specs=VMEM,
        scratch_shapes=[pltpu.VMEM((everyone, per_core * V_HEAD), f32)],
        compiler_params=PARAMS,
        name="merge",
    )(keep, got, value_up)
    returned = lax.all_to_all(merged, "ctx", split_axis=0, concat_axis=0, tiled=True)
    return returned.transpose(1, 0, 2).reshape(tokens, all_heads * V_HEAD)


def solution(mesh):
    return jax.shard_map(
        functools.partial(on_device, mesh.shape["ctx"]),
        mesh=mesh,
        in_specs=(
            P(("groups", "ctx"), None),
            P(("groups", "ctx"), None),
            P(("groups", "ctx"), None),
            P("ctx", None, None),
            P("groups"),
            P("groups"),
        ),
        out_specs=P(("groups", "ctx"), None),
        check_vma=False,
    )
```

```python
import functools
import math

import jax
import jax.numpy as jnp
import numpy as np
from jax import lax
from jax.experimental import pallas as pl
from jax.experimental.pallas import tpu as pltpu
from jax.sharding import PartitionSpec as P

LATENT = 512
V_HEAD = 128
CORES = 2
LANES = 128

score_scale = 192.0 ** (-0.5) * math.log2(math.e)
neg_large = -1e30
least_max = -1e29
f32 = jnp.float32
bf16 = jnp.bfloat16


def chip_cycle(chips):
    wide = max(1, int(round(chips ** (1 / 3))))
    tall = chips // wide
    if wide * tall != chips or wide < 2 or tall < 2:
        return list(range(chips))
    walk = []
    for z in range(tall):
        across = range(1, wide) if z % 2 == 0 else range(wide - 1, 0, -1)
        walk += [z * wide + x for x in across]
    return walk + [z * wide for z in reversed(range(tall))]


def scores_of(q_ref, part, pieces):
    total, at = None, 0
    for piece in pieces:
        s = jnp.dot(
            q_ref[part, at:at + piece.shape[0]], piece[...], preferred_element_type=f32
        )
        total, at = s if total is None else total + s, at + piece.shape[0]
    return total


def values_of(weights, pieces):
    summed, at = [], 0
    for piece in pieces:
        wide = min(piece.shape[0], LATENT - at)
        summed.append(lax.dot_general(
            weights, piece[:wide, :], (((1,), (1,)), ((), ())), preferred_element_type=f32
        ))
        at += wide
    return summed[0] if len(summed) == 1 else jnp.concatenate(summed, axis=1)


def fold_block(part, q_ref, shards, length, old=None, span=None):
    m_old = least_max if old is None else old[0][part, :][:, :1]
    m_new = m_old
    scores = []
    for base, key_ref in shards:
        slot = base + lax.broadcasted_iota(jnp.int32, (1, key_ref[0].shape[1]), 1)
        s = scores_of(q_ref, part, key_ref) * score_scale
        s = jnp.where(slot < length, s, neg_large)
        m_new = jnp.maximum(m_new, jnp.max(s, axis=1, keepdims=True))
        scores.append(s)
    if span is not None:
        keys, shown = span
        s = lax.dot_general(
            q_ref[part, :], keys, (((1,), (1,)), ((), ())), preferred_element_type=f32
        )
        span_s = jnp.where(shown, s * score_scale, neg_large)
        m_new = jnp.maximum(m_new, jnp.max(span_s, axis=1, keepdims=True))
    l_new, summed = 0.0, 0.0
    if old is not None:
        shrink = jnp.exp2(m_old - m_new)
        l_new = old[1][part, :][:, :1] * shrink
        summed = old[2][part, :] * shrink
    for s, (_, key_ref) in zip(scores, shards):
        probs = jnp.exp2(s - m_new)
        l_new += jnp.sum(probs, axis=1, keepdims=True)
        summed += values_of(probs.astype(bf16), key_ref)
    if span is not None:
        probs = jnp.exp2(span_s - m_new)
        l_new += jnp.sum(probs, axis=1, keepdims=True)
        summed += jnp.dot(
            probs.astype(bf16), keys[:, :LATENT], preferred_element_type=f32
        )
    return m_new, l_new, summed


def fold_shards(q_ref, shards, length, old, new, span=None):
    rows = q_ref.shape[0]
    block = min(256, rows)
    for start in range(0, rows, block):
        part = pl.ds(start, block)
        shown = None if span is None else (span[0], span[1](start, block))
        m_new, l_new, summed = fold_block(part, q_ref, shards, length, old, shown)
        new[0][part, :] = jnp.broadcast_to(m_new, (block, LANES))
        new[1][part, :] = jnp.broadcast_to(l_new, (block, LANES))
        new[2][part, :] = summed


def parted(index, size):
    return index >> (size.bit_length() - 1), index & (size - 1)


def token_of(index, tokens, chips):
    device, t = parted(index, tokens)
    core, chip = parted(device, chips)
    return (chip * CORES + ((lax.axis_index("ctx") % CORES) ^ core)) * tokens + t


def with_base(table_ref, at, key_refs):
    me = lax.axis_index("ctx")
    count = table_ref.shape[0] // lax.axis_size("ctx")
    return [
        (table_ref[me * count + at + j] * key_ref.shape[1], (key_ref,))
        for j, key_ref in enumerate(key_refs)
    ]


def pieces_kernel(queries_hbm, span_hbm, out_ref, sems):
    chips = out_ref.shape[0]
    part = queries_hbm.shape[1] // chips
    copies = []
    for chip in range(chips):
        copies.append(pltpu.make_async_copy(
            queries_hbm.at[:, chip * part:(chip + 1) * part],
            out_ref.at[chip, :, :part], sems.at[2 * chip],
        ))
        copies.append(pltpu.make_async_copy(
            span_hbm, out_ref.at[chip, :, part:], sems.at[2 * chip + 1],
        ))
    for copy in copies:
        copy.start()
    for copy in copies:
        copy.wait()


def first_kernel(heads, count, length_ref, table_ref, here_ref, there_ref, *rest):
    keys, (q_ref, m_ref, l_ref, acc_ref) = rest[:count], rest[count:]
    half = here_ref.shape[0]
    width = q_ref.shape[1]
    for core, piece_ref in enumerate((here_ref, there_ref)):
        for head in range(heads):
            row = (head * CORES + core) * half
            q_ref[row:row + half, :] = piece_ref[:, head * width:(head + 1) * width]
    shards = with_base(table_ref, 0, keys)
    fold_shards(q_ref, shards, length_ref[0], None, (m_ref, l_ref, acc_ref))


def middle_kernel(at, count, length_ref, table_ref, q_ref, m_in, l_in, acc_in, *rest):
    keys, new = rest[:count], rest[count:]
    fold_shards(q_ref, with_base(table_ref, at, keys), length_ref[0], (m_in, l_in, acc_in), new)


def span_kernel(at, count, length_ref, offset_ref, table_ref, q_ref, m_in, l_in, acc_in,
                here_ref, *rest):
    keys, new = rest[:count], rest[count:]
    chips = lax.axis_size("ctx") // CORES
    half = here_ref.shape[0]
    tokens = half // chips
    width = q_ref.shape[1]
    key_index = lax.broadcasted_iota(jnp.int32, (1, half), 1)
    key_token = token_of(key_index, tokens, chips)

    def shown(start, block):
        row_index = start + lax.broadcasted_iota(jnp.int32, (block, 1), 0)
        row_token = token_of(row_index & (half * CORES - 1), tokens, chips)
        return (key_token >= offset_ref[0]) & (key_token <= row_token)

    fold_shards(
        q_ref, with_base(table_ref, at, keys), length_ref[0], (m_in, l_in, acc_in), new,
        (here_ref[:, here_ref.shape[1] - width:], shown),
    )


def last_kernel(at, side, length_ref, table_ref, q_ref, m_ref, l_ref, acc_ref,
                top_ref, bottom_ref, out_ref):
    core = lax.axis_index("ctx") % CORES
    shards = [(with_base(table_ref, at, (top_ref,))[0][0], (top_ref, bottom_ref))]
    rows = out_ref.shape[0]
    part = pl.ds(pl.multiple_of((core ^ side) * rows, rows), rows)
    m_new, l_new, summed = fold_block(
        part, q_ref, shards, length_ref[0], (m_ref, l_ref, acc_ref)
    )
    out_ref[:, :LATENT] = (summed * (1.0 / l_new)).astype(out_ref.dtype)
    weight = jnp.broadcast_to(m_new + jnp.log2(l_new), (rows, LANES))
    if side:
        lane = lax.broadcasted_iota(jnp.int32, (rows, LANES), 1)
        high = weight.astype(bf16).astype(f32)
        mid = (weight - high).astype(bf16).astype(f32)
        weight = jnp.where(lane == 0, high, jnp.where(lane == 1, mid, weight - high - mid))
    out_ref[:, LATENT:] = weight.astype(out_ref.dtype)


def merge_kernel(keep_ref, got_ref, up_ref, out_ref, flat_ref):
    core = lax.axis_index("ctx") % CORES
    heads = up_ref.shape[0]
    everyone = flat_ref.shape[0]
    half = everyone // CORES
    pair = min(2, heads)
    for j in range(0, heads, pair):
        contexts = []
        for head in range(j, j + pair):
            row = head * everyone
            got = jnp.concatenate(
                [got_ref[row + half:row + everyone, :], got_ref[row:row + half, :]], axis=0
            ).astype(f32)
            keep = keep_ref[row:row + everyone, :]
            gap = keep[:, LATENT:LATENT + 1] - got[:, LATENT:LATENT + 1]
            gap = gap - got[:, LATENT + 1:LATENT + 2] - got[:, LATENT + 2:LATENT + 3]
            share = 1.0 / (1.0 + jnp.exp2(-gap))
            rest = 1.0 / (1.0 + jnp.exp2(gap))
            contexts.append(
                (keep[:, :LATENT] * share + got[:, :LATENT] * rest).astype(bf16)
            )
        lifted = jnp.dot(
            jnp.concatenate(contexts, axis=0),
            jnp.concatenate([up_ref[j + i] for i in range(pair)], axis=1),
            preferred_element_type=f32,
        )
        for i in range(pair):
            flat_ref[:, (j + i) * V_HEAD:(j + i + 1) * V_HEAD] = lifted[
                i * everyone:(i + 1) * everyone, i * V_HEAD:(i + 1) * V_HEAD
            ]
    devices, tokens, _ = out_ref.shape
    chips = devices // CORES
    for i in range(devices):
        out_ref[(i % chips) * CORES + (core ^ (i // chips))] = (
            flat_ref[i * tokens:(i + 1) * tokens, :].astype(bf16)
        )


VMEM = pl.BlockSpec(memory_space=pltpu.VMEM)
SMEM = pl.BlockSpec(memory_space=pltpu.SMEM)
PARAMS = pltpu.CompilerParams(vmem_limit_bytes=32 * 1024 * 1024)


def shape(*dims, dtype=f32):
    return jax.ShapeDtypeStruct(dims, dtype)


def on_device(ctx, queries, prefix_latents, span_latents, value_up, prefix_length, span_offset):
    slots, width = prefix_latents.shape
    tokens = queries.shape[0]
    all_heads = queries.shape[1] // width
    chips = ctx // CORES
    heads = all_heads // chips
    rows = tokens * heads
    total = rows * ctx
    everyone = tokens * ctx
    walk = chip_cycle(chips)
    spot = np.argsort(np.array(walk))
    steps = chips // 2

    def across(step):
        return [
            (walk[r] * CORES + c, walk[(r + (-step if c else step)) % chips] * CORES + c)
            for r in range(chips) for c in range(CORES)
        ]

    other_core = [(d, d ^ 1) for d in range(ctx)]
    same_core = [[p * CORES + c for p in range(chips)] for c in range(CORES)]

    turns = [0]
    for s in range(1, steps):
        turns += [-s, s]
    turns.append(steps)
    owner_table = np.array(
        [
            [walk[(spot[p] + (-t if c else t)) % chips] * CORES + c for t in turns]
            for p in range(chips) for c in range(CORES)
        ],
        np.int32,
    )
    table = jnp.asarray(owner_table.reshape(-1))
    state_shapes = [shape(total, LANES), shape(total, LANES), shape(total, LATENT)]

    def fold_first(keys):
        return pl.pallas_call(
            functools.partial(first_kernel, heads, len(keys)),
            out_shape=[shape(total, width, dtype=bf16)] + state_shapes,
            in_specs=[SMEM] * 2 + [VMEM] * (2 + len(keys)),
            out_specs=[VMEM] * 4,
            compiler_params=PARAMS,
            name="first",
        )(prefix_length, table, here, there, *keys)

    def fold_more(at, q, state, keys):
        return pl.pallas_call(
            functools.partial(middle_kernel, at, len(keys)),
            out_shape=state_shapes,
            in_specs=[SMEM] * 2 + [VMEM] * (4 + len(keys)),
            out_specs=[VMEM] * 3,
            compiler_params=PARAMS,
            name="middle",
        )(prefix_length, table, q, *state, *keys)

    onward = functools.partial(lax.ppermute, axis_name="ctx", perm=across(1))
    backward = functools.partial(lax.ppermute, axis_name="ctx", perm=across(-1))
    cut = LATENT // 2
    own = prefix_latents.T
    right, left = onward(own), backward(own)

    anywhere = pl.BlockSpec(memory_space=pl.ANY)
    pieces = pl.pallas_call(
        pieces_kernel,
        out_shape=shape(chips, tokens, (heads + 1) * width, dtype=bf16),
        in_specs=[anywhere] * 2,
        out_specs=VMEM,
        scratch_shapes=[pltpu.SemaphoreType.DMA((2 * chips,))],
        compiler_params=pltpu.CompilerParams(vmem_limit_bytes=56 * 1024 * 1024),
        name="pieces",
    )(queries, span_latents)
    here = lax.all_to_all(
        pieces, "ctx", split_axis=0, concat_axis=0, axis_index_groups=same_core, tiled=True
    )

    right, left = lax.optimization_barrier((right, left))
    keys, state, at = [own, right, left], None, 0
    for s in range(2, steps):
        right, left = onward(right), backward(left)
        if s == 2:
            here = here.reshape(chips * tokens, (heads + 1) * width)
            there = lax.ppermute(here, "ctx", other_core)
            keys += [right, left]
            continue
        if state is None:
            q, *state = fold_first(keys)
        else:
            state = fold_more(at, q, state, keys)
        at += len(keys)
        keys = [right, left]
    top = onward(right[:cut])
    left, state = lax.optimization_barrier((left, state))
    bottom = backward(left[cut:])
    state = pl.pallas_call(
        functools.partial(span_kernel, at, len(keys)),
        out_shape=state_shapes,
        in_specs=[SMEM] * 3 + [VMEM] * (5 + len(keys)),
        out_specs=[VMEM] * 3,
        compiler_params=PARAMS,
        name="middle",
    )(prefix_length, span_offset, table, q, *state, here, *keys)
    per_core = heads // CORES
    part = per_core * everyone

    def fold_last(side, dtype):
        return pl.pallas_call(
            functools.partial(last_kernel, chips - 1, side),
            out_shape=shape(part, LATENT + LANES, dtype=dtype),
            in_specs=[SMEM] * 2 + [VMEM] * 6,
            out_specs=VMEM,
            compiler_params=PARAMS,
            name="keep" if side == 0 else "give",
        )(prefix_length, table, q, *state, top, bottom)

    got = lax.ppermute(fold_last(1, bf16), "ctx", other_core)
    keep = fold_last(0, f32)
    merged = pl.pallas_call(
        merge_kernel,
        out_shape=shape(ctx, tokens, per_core * V_HEAD, dtype=bf16),
        in_specs=[VMEM] * 3,
        out_specs=VMEM,
        scratch_shapes=[pltpu.VMEM((everyone, per_core * V_HEAD), f32)],
        compiler_params=PARAMS,
        name="merge",
    )(keep, got, value_up)
    returned = lax.all_to_all(merged, "ctx", split_axis=0, concat_axis=0, tiled=True)
    return returned.transpose(1, 0, 2).reshape(tokens, all_heads * V_HEAD)


def solution(mesh):
    return jax.shard_map(
        functools.partial(on_device, mesh.shape["ctx"]),
        mesh=mesh,
        in_specs=(
            P(("groups", "ctx"), None),
            P(("groups", "ctx"), None),
            P(("groups", "ctx"), None),
            P("ctx", None, None),
            P("groups"),
            P("groups"),
        ),
        out_specs=P(("groups", "ctx"), None),
        check_vma=False,
    )
```

```python
import functools
import math

import jax
import jax.numpy as jnp
import numpy as np
from jax import lax
from jax.experimental import pallas as pl
from jax.experimental.pallas import tpu as pltpu
from jax.sharding import PartitionSpec as P

LATENT = 512
V_HEAD = 128
CORES = 2
LANES = 128

score_scale = 192.0 ** (-0.5) * math.log2(math.e)
neg_large = -1e30
least_max = -1e29
f32 = jnp.float32
bf16 = jnp.bfloat16


def chip_cycle(chips):
    wide = max(1, int(round(chips ** (1 / 3))))
    tall = chips // wide
    if wide * tall != chips or wide < 2 or tall < 2:
        return list(range(chips))
    walk = []
    for z in range(tall):
        across = range(1, wide) if z % 2 == 0 else range(wide - 1, 0, -1)
        walk += [z * wide + x for x in across]
    return walk + [z * wide for z in reversed(range(tall))]


def scores_of(q_ref, part, pieces):
    total, at = None, 0
    for piece in pieces:
        s = jnp.dot(
            q_ref[part, at:at + piece.shape[0]], piece[...], preferred_element_type=f32
        )
        total, at = s if total is None else total + s, at + piece.shape[0]
    return total


def values_of(weights, pieces):
    summed, at = [], 0
    for piece in pieces:
        wide = min(piece.shape[0], LATENT - at)
        summed.append(lax.dot_general(
            weights, piece[:wide, :], (((1,), (1,)), ((), ())), preferred_element_type=f32
        ))
        at += wide
    return summed[0] if len(summed) == 1 else jnp.concatenate(summed, axis=1)


def fold_block(part, q_ref, shards, length, old=None, span=None):
    m_old = least_max if old is None else old[0][part, :][:, :1]
    m_new = m_old
    scores = []
    for base, key_ref in shards:
        slot = base + lax.broadcasted_iota(jnp.int32, (1, key_ref[0].shape[1]), 1)
        s = scores_of(q_ref, part, key_ref) * score_scale
        s = jnp.where(slot < length, s, neg_large)
        m_new = jnp.maximum(m_new, jnp.max(s, axis=1, keepdims=True))
        scores.append(s)
    if span is not None:
        keys, shown = span
        s = lax.dot_general(
            q_ref[part, :], keys, (((1,), (1,)), ((), ())), preferred_element_type=f32
        )
        span_s = jnp.where(shown, s * score_scale, neg_large)
        m_new = jnp.maximum(m_new, jnp.max(span_s, axis=1, keepdims=True))
    l_new, summed = 0.0, 0.0
    if old is not None:
        shrink = jnp.exp2(m_old - m_new)
        l_new = old[1][part, :][:, :1] * shrink
        summed = old[2][part, :] * shrink
    for s, (_, key_ref) in zip(scores, shards):
        probs = jnp.exp2(s - m_new)
        l_new += jnp.sum(probs, axis=1, keepdims=True)
        summed += values_of(probs.astype(bf16), key_ref)
    if span is not None:
        probs = jnp.exp2(span_s - m_new)
        l_new += jnp.sum(probs, axis=1, keepdims=True)
        summed += jnp.dot(
            probs.astype(bf16), keys[:, :LATENT], preferred_element_type=f32
        )
    return m_new, l_new, summed


def fold_shards(q_ref, shards, length, old, new, span=None):
    rows = q_ref.shape[0]
    block = min(256, rows)
    for start in range(0, rows, block):
        part = pl.ds(start, block)
        shown = None if span is None else (span[0], span[1](start, block))
        m_new, l_new, summed = fold_block(part, q_ref, shards, length, old, shown)
        new[0][part, :] = jnp.broadcast_to(m_new, (block, LANES))
        new[1][part, :] = jnp.broadcast_to(l_new, (block, LANES))
        new[2][part, :] = summed


def parted(index, size):
    return index >> (size.bit_length() - 1), index & (size - 1)


def token_of(index, tokens, chips):
    device, t = parted(index, tokens)
    core, chip = parted(device, chips)
    return (chip * CORES + ((lax.axis_index("ctx") % CORES) ^ core)) * tokens + t


def with_base(table_ref, at, key_refs):
    me = lax.axis_index("ctx")
    count = table_ref.shape[0] // lax.axis_size("ctx")
    return [
        (table_ref[me * count + at + j] * key_ref.shape[1], (key_ref,))
        for j, key_ref in enumerate(key_refs)
    ]


def pieces_kernel(queries_hbm, span_hbm, out_ref, queries_ref, span_ref, sems):
    chips = out_ref.shape[0]
    part = queries_ref.shape[1] // chips
    span_copy = pltpu.make_async_copy(span_hbm, span_ref, sems.at[0])
    span_copy.start()
    copies = []
    for i, first in enumerate((0, chips // 2)):
        lanes = slice(first * part, (first + chips // 2) * part)
        copies.append(pltpu.make_async_copy(
            queries_hbm.at[:, lanes], queries_ref.at[:, lanes], sems.at[1 + i]
        ))
        copies[-1].start()
    span_copy.wait()
    for i, first in enumerate((0, chips // 2)):
        copies[i].wait()
        for chip in range(first, first + chips // 2):
            out_ref[chip, :, :part] = queries_ref[:, chip * part:(chip + 1) * part]
            out_ref[chip, :, part:] = span_ref[...]


def first_kernel(heads, count, length_ref, table_ref, here_ref, there_ref, *rest):
    keys, (q_ref, m_ref, l_ref, acc_ref) = rest[:count], rest[count:]
    half = here_ref.shape[0]
    width = q_ref.shape[1]
    for core, piece_ref in enumerate((here_ref, there_ref)):
        for head in range(heads):
            row = (head * CORES + core) * half
            q_ref[row:row + half, :] = piece_ref[:, head * width:(head + 1) * width]
    shards = with_base(table_ref, 0, keys)
    fold_shards(q_ref, shards, length_ref[0], None, (m_ref, l_ref, acc_ref))


def middle_kernel(at, count, length_ref, table_ref, q_ref, m_in, l_in, acc_in, *rest):
    keys, new = rest[:count], rest[count:]
    fold_shards(q_ref, with_base(table_ref, at, keys), length_ref[0], (m_in, l_in, acc_in), new)


def span_kernel(at, count, length_ref, offset_ref, table_ref, q_ref, m_in, l_in, acc_in,
                here_ref, *rest):
    keys, new = rest[:count], rest[count:]
    chips = lax.axis_size("ctx") // CORES
    half = here_ref.shape[0]
    tokens = half // chips
    width = q_ref.shape[1]
    key_index = lax.broadcasted_iota(jnp.int32, (1, half), 1)
    key_token = token_of(key_index, tokens, chips)

    def shown(start, block):
        row_index = start + lax.broadcasted_iota(jnp.int32, (block, 1), 0)
        row_token = token_of(row_index & (half * CORES - 1), tokens, chips)
        return (key_token >= offset_ref[0]) & (key_token <= row_token)

    fold_shards(
        q_ref, with_base(table_ref, at, keys), length_ref[0], (m_in, l_in, acc_in), new,
        (here_ref[:, here_ref.shape[1] - width:], shown),
    )


def last_kernel(at, side, length_ref, table_ref, q_ref, m_ref, l_ref, acc_ref,
                top_ref, bottom_ref, out_ref):
    core = lax.axis_index("ctx") % CORES
    shards = [(with_base(table_ref, at, (top_ref,))[0][0], (top_ref, bottom_ref))]
    rows = out_ref.shape[0]
    block = min(128, rows)
    for start in range(0, rows, block):
        part = pl.ds(pl.multiple_of((core ^ side) * rows + start, block), block)
        m_new, l_new, summed = fold_block(
            part, q_ref, shards, length_ref[0], (m_ref, l_ref, acc_ref)
        )
        here = slice(start, start + block)
        out_ref[here, :LATENT] = (summed * (1.0 / l_new)).astype(out_ref.dtype)
        weight = jnp.broadcast_to(m_new + jnp.log2(l_new), (block, LANES))
        if side:
            lane = lax.broadcasted_iota(jnp.int32, (block, LANES), 1)
            high = weight.astype(bf16).astype(f32)
            mid = (weight - high).astype(bf16).astype(f32)
            weight = jnp.where(lane == 0, high, jnp.where(lane == 1, mid, weight - high - mid))
        out_ref[here, LATENT:] = weight.astype(out_ref.dtype)


def merge_kernel(keep_ref, got_ref, up_ref, out_ref, flat_ref):
    core = lax.axis_index("ctx") % CORES
    heads = up_ref.shape[0]
    everyone = flat_ref.shape[0]
    half = everyone // CORES
    pair = min(2, heads)
    for j in range(0, heads, pair):
        contexts = []
        for head in range(j, j + pair):
            row = head * everyone
            got = jnp.concatenate(
                [got_ref[row + half:row + everyone, :], got_ref[row:row + half, :]], axis=0
            ).astype(f32)
            keep = keep_ref[row:row + everyone, :]
            gap = keep[:, LATENT:LATENT + 1] - got[:, LATENT:LATENT + 1]
            gap = gap - got[:, LATENT + 1:LATENT + 2] - got[:, LATENT + 2:LATENT + 3]
            share = 1.0 / (1.0 + jnp.exp2(-gap))
            rest = 1.0 / (1.0 + jnp.exp2(gap))
            contexts.append(
                (keep[:, :LATENT] * share + got[:, :LATENT] * rest).astype(bf16)
            )
        lifted = jnp.dot(
            jnp.concatenate(contexts, axis=0),
            jnp.concatenate([up_ref[j + i] for i in range(pair)], axis=1),
            preferred_element_type=f32,
        )
        for i in range(pair):
            flat_ref[:, (j + i) * V_HEAD:(j + i + 1) * V_HEAD] = lifted[
                i * everyone:(i + 1) * everyone, i * V_HEAD:(i + 1) * V_HEAD
            ]
    devices, tokens, _ = out_ref.shape
    chips = devices // CORES
    for i in range(devices):
        out_ref[(i % chips) * CORES + (core ^ (i // chips))] = (
            flat_ref[i * tokens:(i + 1) * tokens, :].astype(bf16)
        )


VMEM = pl.BlockSpec(memory_space=pltpu.VMEM)
SMEM = pl.BlockSpec(memory_space=pltpu.SMEM)
PARAMS = pltpu.CompilerParams(vmem_limit_bytes=32 * 1024 * 1024)


def shape(*dims, dtype=f32):
    return jax.ShapeDtypeStruct(dims, dtype)


def on_device(ctx, queries, prefix_latents, span_latents, value_up, prefix_length, span_offset):
    slots, width = prefix_latents.shape
    tokens = queries.shape[0]
    all_heads = queries.shape[1] // width
    chips = ctx // CORES
    heads = all_heads // chips
    rows = tokens * heads
    total = rows * ctx
    everyone = tokens * ctx
    walk = chip_cycle(chips)
    spot = np.argsort(np.array(walk))
    steps = chips // 2

    def across(step):
        return [
            (walk[r] * CORES + c, walk[(r + (-step if c else step)) % chips] * CORES + c)
            for r in range(chips) for c in range(CORES)
        ]

    other_core = [(d, d ^ 1) for d in range(ctx)]
    same_core = [[p * CORES + c for p in range(chips)] for c in range(CORES)]

    turns = [0]
    for s in range(1, steps):
        turns += [-s, s]
    turns.append(steps)
    owner_table = np.array(
        [
            [walk[(spot[p] + (-t if c else t)) % chips] * CORES + c for t in turns]
            for p in range(chips) for c in range(CORES)
        ],
        np.int32,
    )
    table = jnp.asarray(owner_table.reshape(-1))
    state_shapes = [shape(total, LANES), shape(total, LANES), shape(total, LATENT)]

    def fold_first(keys):
        return pl.pallas_call(
            functools.partial(first_kernel, heads, len(keys)),
            out_shape=[shape(total, width, dtype=bf16)] + state_shapes,
            in_specs=[SMEM] * 2 + [VMEM] * (2 + len(keys)),
            out_specs=[VMEM] * 4,
            compiler_params=PARAMS,
            name="first",
        )(prefix_length, table, here, there, *keys)

    def fold_more(at, q, state, keys):
        return pl.pallas_call(
            functools.partial(middle_kernel, at, len(keys)),
            out_shape=state_shapes,
            in_specs=[SMEM] * 2 + [VMEM] * (4 + len(keys)),
            out_specs=[VMEM] * 3,
            compiler_params=PARAMS,
            name="middle",
        )(prefix_length, table, q, *state, *keys)

    onward = functools.partial(lax.ppermute, axis_name="ctx", perm=across(1))
    backward = functools.partial(lax.ppermute, axis_name="ctx", perm=across(-1))
    cut = LATENT // 2
    own = prefix_latents.T
    right, left = onward(own), backward(own)

    anywhere = pl.BlockSpec(memory_space=pl.ANY)
    pieces = pl.pallas_call(
        pieces_kernel,
        out_shape=shape(chips, tokens, (heads + 1) * width, dtype=bf16),
        in_specs=[anywhere] * 2,
        out_specs=VMEM,
        scratch_shapes=[
            pltpu.VMEM(queries.shape, bf16),
            pltpu.VMEM(span_latents.shape, bf16),
            pltpu.SemaphoreType.DMA((3,)),
        ],
        compiler_params=pltpu.CompilerParams(vmem_limit_bytes=56 * 1024 * 1024),
        name="pieces",
    )(queries, span_latents)
    here = lax.all_to_all(
        pieces, "ctx", split_axis=0, concat_axis=0, axis_index_groups=same_core, tiled=True
    )

    right, left = lax.optimization_barrier((right, left))
    keys, state, at = [own, right, left], None, 0
    for s in range(2, steps):
        right, left = onward(right), backward(left)
        if s == 2:
            here = here.reshape(chips * tokens, (heads + 1) * width)
            there = lax.ppermute(here, "ctx", other_core)
            keys += [right, left]
            continue
        if state is None:
            q, *state = fold_first(keys)
        else:
            state = fold_more(at, q, state, keys)
        at += len(keys)
        keys = [right, left]
    top = onward(right[:cut])
    left, state = lax.optimization_barrier((left, state))
    bottom = backward(left[cut:])
    state = pl.pallas_call(
        functools.partial(span_kernel, at, len(keys)),
        out_shape=state_shapes,
        in_specs=[SMEM] * 3 + [VMEM] * (5 + len(keys)),
        out_specs=[VMEM] * 3,
        compiler_params=PARAMS,
        name="middle",
    )(prefix_length, span_offset, table, q, *state, here, *keys)
    per_core = heads // CORES
    part = per_core * everyone

    def fold_last(side, dtype):
        return pl.pallas_call(
            functools.partial(last_kernel, chips - 1, side),
            out_shape=shape(part, LATENT + LANES, dtype=dtype),
            in_specs=[SMEM] * 2 + [VMEM] * 6,
            out_specs=VMEM,
            compiler_params=PARAMS,
            name="keep" if side == 0 else "give",
        )(prefix_length, table, q, *state, top, bottom)

    got = lax.ppermute(fold_last(1, bf16), "ctx", other_core)
    keep = fold_last(0, f32)
    merged = pl.pallas_call(
        merge_kernel,
        out_shape=shape(ctx, tokens, per_core * V_HEAD, dtype=bf16),
        in_specs=[VMEM] * 3,
        out_specs=VMEM,
        scratch_shapes=[pltpu.VMEM((everyone, per_core * V_HEAD), f32)],
        compiler_params=PARAMS,
        name="merge",
    )(keep, got, value_up)
    returned = lax.all_to_all(merged, "ctx", split_axis=0, concat_axis=0, tiled=True)
    return returned.transpose(1, 0, 2).reshape(tokens, all_heads * V_HEAD)


def solution(mesh):
    return jax.shard_map(
        functools.partial(on_device, mesh.shape["ctx"]),
        mesh=mesh,
        in_specs=(
            P(("groups", "ctx"), None),
            P(("groups", "ctx"), None),
            P(("groups", "ctx"), None),
            P("ctx", None, None),
            P("groups"),
            P("groups"),
        ),
        out_specs=P(("groups", "ctx"), None),
        check_vma=False,
    )
```

```python
import functools
import math

import jax
import jax.numpy as jnp
import numpy as np
from jax import lax
from jax.experimental import pallas as pl
from jax.experimental.pallas import tpu as pltpu
from jax.sharding import PartitionSpec as P

LATENT = 512
V_HEAD = 128
CORES = 2
LANES = 128

score_scale = 192.0 ** (-0.5) * math.log2(math.e)
neg_large = -1e30
least_max = -1e29
f32 = jnp.float32
bf16 = jnp.bfloat16


def chip_cycle(chips):
    wide = max(1, int(round(chips ** (1 / 3))))
    tall = chips // wide
    if wide * tall != chips or wide < 2 or tall < 2:
        return list(range(chips))
    walk = []
    for z in range(tall):
        across = range(1, wide) if z % 2 == 0 else range(wide - 1, 0, -1)
        walk += [z * wide + x for x in across]
    return walk + [z * wide for z in reversed(range(tall))]


def scores_of(q_ref, part, pieces):
    total, at = None, 0
    for piece in pieces:
        s = jnp.dot(
            q_ref[part, at:at + piece.shape[0]], piece[...], preferred_element_type=f32
        )
        total, at = s if total is None else total + s, at + piece.shape[0]
    return total


def values_of(weights, pieces):
    summed, at = [], 0
    for piece in pieces:
        wide = min(piece.shape[0], LATENT - at)
        summed.append(lax.dot_general(
            weights, piece[:wide, :], (((1,), (1,)), ((), ())), preferred_element_type=f32
        ))
        at += wide
    return summed[0] if len(summed) == 1 else jnp.concatenate(summed, axis=1)


def fold_block(part, q_ref, shards, length, old=None, span=None):
    m_old = least_max if old is None else old[0][part, :][:, :1]
    m_new = m_old
    scores = []
    for base, key_ref in shards:
        slot = base + lax.broadcasted_iota(jnp.int32, (1, key_ref[0].shape[1]), 1)
        s = scores_of(q_ref, part, key_ref) * score_scale
        s = jnp.where(slot < length, s, neg_large)
        m_new = jnp.maximum(m_new, jnp.max(s, axis=1, keepdims=True))
        scores.append(s)
    if span is not None:
        keys, shown = span
        s = lax.dot_general(
            q_ref[part, :], keys, (((1,), (1,)), ((), ())), preferred_element_type=f32
        )
        span_s = jnp.where(shown, s * score_scale, neg_large)
        m_new = jnp.maximum(m_new, jnp.max(span_s, axis=1, keepdims=True))
    l_new, summed = 0.0, 0.0
    if old is not None:
        shrink = jnp.exp2(m_old - m_new)
        l_new = old[1][part, :][:, :1] * shrink
        summed = old[2][part, :] * shrink
    for s, (_, key_ref) in zip(scores, shards):
        probs = jnp.exp2(s - m_new)
        l_new += jnp.sum(probs, axis=1, keepdims=True)
        summed += values_of(probs.astype(bf16), key_ref)
    if span is not None:
        probs = jnp.exp2(span_s - m_new)
        l_new += jnp.sum(probs, axis=1, keepdims=True)
        summed += jnp.dot(
            probs.astype(bf16), keys[:, :LATENT], preferred_element_type=f32
        )
    return m_new, l_new, summed


def fold_shards(q_ref, shards, length, old, new, span=None):
    rows = q_ref.shape[0]
    block = min(256, rows)
    for start in range(0, rows, block):
        part = pl.ds(start, block)
        shown = None if span is None else (span[0], span[1](start, block))
        m_new, l_new, summed = fold_block(part, q_ref, shards, length, old, shown)
        new[0][part, :] = jnp.broadcast_to(m_new, (block, LANES))
        new[1][part, :] = jnp.broadcast_to(l_new, (block, LANES))
        new[2][part, :] = summed


def parted(index, size):
    return index >> (size.bit_length() - 1), index & (size - 1)


def token_of(index, tokens, chips):
    device, t = parted(index, tokens)
    core, chip = parted(device, chips)
    return (chip * CORES + ((lax.axis_index("ctx") % CORES) ^ core)) * tokens + t


def with_base(table_ref, at, key_refs):
    me = lax.axis_index("ctx")
    count = table_ref.shape[0] // lax.axis_size("ctx")
    return [
        (table_ref[me * count + at + j] * key_ref.shape[1], (key_ref,))
        for j, key_ref in enumerate(key_refs)
    ]


def pieces_kernel(queries_hbm, span_hbm, out_ref, span_ref, sems):
    part = queries_hbm.shape[2]
    copies = [
        pltpu.make_async_copy(queries_hbm, out_ref.at[:, :, :part], sems.at[0]),
        pltpu.make_async_copy(span_hbm, span_ref, sems.at[1]),
    ]
    for copy in copies:
        copy.start()
    for copy in copies:
        copy.wait()
    for chip in range(out_ref.shape[0]):
        out_ref[chip, :, part:] = span_ref[...]


def first_kernel(heads, count, length_ref, table_ref, here_ref, there_ref, *rest):
    keys, (q_ref, m_ref, l_ref, acc_ref) = rest[:count], rest[count:]
    half = here_ref.shape[0]
    width = q_ref.shape[1]
    for core, piece_ref in enumerate((here_ref, there_ref)):
        for head in range(heads):
            row = (head * CORES + core) * half
            q_ref[row:row + half, :] = piece_ref[:, head * width:(head + 1) * width]
    shards = with_base(table_ref, 0, keys)
    fold_shards(q_ref, shards, length_ref[0], None, (m_ref, l_ref, acc_ref))


def middle_kernel(at, count, length_ref, table_ref, q_ref, m_in, l_in, acc_in, *rest):
    keys, new = rest[:count], rest[count:]
    fold_shards(q_ref, with_base(table_ref, at, keys), length_ref[0], (m_in, l_in, acc_in), new)


def span_kernel(at, count, length_ref, offset_ref, table_ref, q_ref, m_in, l_in, acc_in,
                here_ref, *rest):
    keys, new = rest[:count], rest[count:]
    chips = lax.axis_size("ctx") // CORES
    half = here_ref.shape[0]
    tokens = half // chips
    width = q_ref.shape[1]
    key_index = lax.broadcasted_iota(jnp.int32, (1, half), 1)
    key_token = token_of(key_index, tokens, chips)

    def shown(start, block):
        row_index = start + lax.broadcasted_iota(jnp.int32, (block, 1), 0)
        row_token = token_of(row_index & (half * CORES - 1), tokens, chips)
        return (key_token >= offset_ref[0]) & (key_token <= row_token)

    fold_shards(
        q_ref, with_base(table_ref, at, keys), length_ref[0], (m_in, l_in, acc_in), new,
        (here_ref[:, here_ref.shape[1] - width:], shown),
    )


def last_kernel(at, side, length_ref, table_ref, q_ref, m_ref, l_ref, acc_ref,
                top_ref, bottom_ref, out_ref):
    core = lax.axis_index("ctx") % CORES
    shards = [(with_base(table_ref, at, (top_ref,))[0][0], (top_ref, bottom_ref))]
    rows = out_ref.shape[0]
    part = pl.ds(pl.multiple_of((core ^ side) * rows, rows), rows)
    m_new, l_new, summed = fold_block(
        part, q_ref, shards, length_ref[0], (m_ref, l_ref, acc_ref)
    )
    out_ref[:, :LATENT] = (summed * (1.0 / l_new)).astype(out_ref.dtype)
    weight = jnp.broadcast_to(m_new + jnp.log2(l_new), (rows, LANES))
    if side:
        lane = lax.broadcasted_iota(jnp.int32, (rows, LANES), 1)
        high = weight.astype(bf16).astype(f32)
        mid = (weight - high).astype(bf16).astype(f32)
        weight = jnp.where(lane == 0, high, jnp.where(lane == 1, mid, weight - high - mid))
    out_ref[:, LATENT:] = weight.astype(out_ref.dtype)


def merge_kernel(keep_ref, got_ref, up_ref, out_ref, flat_ref):
    core = lax.axis_index("ctx") % CORES
    heads = up_ref.shape[0]
    everyone = flat_ref.shape[0]
    half = everyone // CORES
    pair = min(2, heads)
    for j in range(0, heads, pair):
        contexts = []
        for head in range(j, j + pair):
            row = head * everyone
            got = jnp.concatenate(
                [got_ref[row + half:row + everyone, :], got_ref[row:row + half, :]], axis=0
            ).astype(f32)
            keep = keep_ref[row:row + everyone, :]
            gap = keep[:, LATENT:LATENT + 1] - got[:, LATENT:LATENT + 1]
            gap = gap - got[:, LATENT + 1:LATENT + 2] - got[:, LATENT + 2:LATENT + 3]
            share = 1.0 / (1.0 + jnp.exp2(-gap))
            rest = 1.0 / (1.0 + jnp.exp2(gap))
            contexts.append(
                (keep[:, :LATENT] * share + got[:, :LATENT] * rest).astype(bf16)
            )
        lifted = jnp.dot(
            jnp.concatenate(contexts, axis=0),
            jnp.concatenate([up_ref[j + i] for i in range(pair)], axis=1),
            preferred_element_type=f32,
        )
        for i in range(pair):
            flat_ref[:, (j + i) * V_HEAD:(j + i + 1) * V_HEAD] = lifted[
                i * everyone:(i + 1) * everyone, i * V_HEAD:(i + 1) * V_HEAD
            ]
    devices, tokens, _ = out_ref.shape
    chips = devices // CORES
    for i in range(devices):
        out_ref[(i % chips) * CORES + (core ^ (i // chips))] = (
            flat_ref[i * tokens:(i + 1) * tokens, :].astype(bf16)
        )


VMEM = pl.BlockSpec(memory_space=pltpu.VMEM)
SMEM = pl.BlockSpec(memory_space=pltpu.SMEM)
PARAMS = pltpu.CompilerParams(vmem_limit_bytes=32 * 1024 * 1024)


def shape(*dims, dtype=f32):
    return jax.ShapeDtypeStruct(dims, dtype)


def on_device(ctx, queries, prefix_latents, span_latents, value_up, prefix_length, span_offset):
    slots, width = prefix_latents.shape
    tokens = queries.shape[0]
    all_heads = queries.shape[1] // width
    chips = ctx // CORES
    heads = all_heads // chips
    rows = tokens * heads
    total = rows * ctx
    everyone = tokens * ctx
    walk = chip_cycle(chips)
    spot = np.argsort(np.array(walk))
    steps = chips // 2

    def across(step):
        return [
            (walk[r] * CORES + c, walk[(r + (-step if c else step)) % chips] * CORES + c)
            for r in range(chips) for c in range(CORES)
        ]

    other_core = [(d, d ^ 1) for d in range(ctx)]
    same_core = [[p * CORES + c for p in range(chips)] for c in range(CORES)]

    turns = [0]
    for s in range(1, steps):
        turns += [-s, s]
    turns.append(steps)
    owner_table = np.array(
        [
            [walk[(spot[p] + (-t if c else t)) % chips] * CORES + c for t in turns]
            for p in range(chips) for c in range(CORES)
        ],
        np.int32,
    )
    table = jnp.asarray(owner_table.reshape(-1))
    state_shapes = [shape(total, LANES), shape(total, LANES), shape(total, LATENT)]

    def fold_first(keys):
        return pl.pallas_call(
            functools.partial(first_kernel, heads, len(keys)),
            out_shape=[shape(total, width, dtype=bf16)] + state_shapes,
            in_specs=[SMEM] * 2 + [VMEM] * (2 + len(keys)),
            out_specs=[VMEM] * 4,
            compiler_params=PARAMS,
            name="first",
        )(prefix_length, table, here, there, *keys)

    def fold_more(at, q, state, keys):
        return pl.pallas_call(
            functools.partial(middle_kernel, at, len(keys)),
            out_shape=state_shapes,
            in_specs=[SMEM] * 2 + [VMEM] * (4 + len(keys)),
            out_specs=[VMEM] * 3,
            compiler_params=PARAMS,
            name="middle",
        )(prefix_length, table, q, *state, *keys)

    onward = functools.partial(lax.ppermute, axis_name="ctx", perm=across(1))
    backward = functools.partial(lax.ppermute, axis_name="ctx", perm=across(-1))
    cut = LATENT // 2
    own = prefix_latents.T
    right, left = onward(own), backward(own)

    anywhere = pl.BlockSpec(memory_space=pl.ANY)
    pieces = pl.pallas_call(
        pieces_kernel,
        out_shape=shape(chips, tokens, (heads + 1) * width, dtype=bf16),
        in_specs=[anywhere] * 2,
        out_specs=VMEM,
        scratch_shapes=[
            pltpu.VMEM(span_latents.shape, bf16),
            pltpu.SemaphoreType.DMA((2,)),
        ],
        compiler_params=pltpu.CompilerParams(vmem_limit_bytes=56 * 1024 * 1024),
        name="pieces",
    )(queries.reshape(tokens, chips, heads * width).transpose(1, 0, 2), span_latents)
    here = lax.all_to_all(
        pieces, "ctx", split_axis=0, concat_axis=0, axis_index_groups=same_core, tiled=True
    )

    right, left = lax.optimization_barrier((right, left))
    keys, state, at = [own, right, left], None, 0
    for s in range(2, steps):
        right, left = onward(right), backward(left)
        if s == 2:
            here = here.reshape(chips * tokens, (heads + 1) * width)
            there = lax.ppermute(here, "ctx", other_core)
            keys += [right, left]
            continue
        if state is None:
            q, *state = fold_first(keys)
        else:
            state = fold_more(at, q, state, keys)
        at += len(keys)
        keys = [right, left]
    top = onward(right[:cut])
    left, state = lax.optimization_barrier((left, state))
    bottom = backward(left[cut:])
    state = pl.pallas_call(
        functools.partial(span_kernel, at, len(keys)),
        out_shape=state_shapes,
        in_specs=[SMEM] * 3 + [VMEM] * (5 + len(keys)),
        out_specs=[VMEM] * 3,
        compiler_params=PARAMS,
        name="middle",
    )(prefix_length, span_offset, table, q, *state, here, *keys)
    per_core = heads // CORES
    part = per_core * everyone

    def fold_last(side, dtype):
        return pl.pallas_call(
            functools.partial(last_kernel, chips - 1, side),
            out_shape=shape(part, LATENT + LANES, dtype=dtype),
            in_specs=[SMEM] * 2 + [VMEM] * 6,
            out_specs=VMEM,
            compiler_params=PARAMS,
            name="keep" if side == 0 else "give",
        )(prefix_length, table, q, *state, top, bottom)

    got = lax.ppermute(fold_last(1, bf16), "ctx", other_core)
    keep = fold_last(0, f32)
    merged = pl.pallas_call(
        merge_kernel,
        out_shape=shape(ctx, tokens, per_core * V_HEAD, dtype=bf16),
        in_specs=[VMEM] * 3,
        out_specs=VMEM,
        scratch_shapes=[pltpu.VMEM((everyone, per_core * V_HEAD), f32)],
        compiler_params=PARAMS,
        name="merge",
    )(keep, got, value_up)
    returned = lax.all_to_all(merged, "ctx", split_axis=0, concat_axis=0, tiled=True)
    return returned.transpose(1, 0, 2).reshape(tokens, all_heads * V_HEAD)


def solution(mesh):
    return jax.shard_map(
        functools.partial(on_device, mesh.shape["ctx"]),
        mesh=mesh,
        in_specs=(
            P(("groups", "ctx"), None),
            P(("groups", "ctx"), None),
            P(("groups", "ctx"), None),
            P("ctx", None, None),
            P("groups"),
            P("groups"),
        ),
        out_specs=P(("groups", "ctx"), None),
        check_vma=False,
    )
```

```python
import functools
import math

import jax
import jax.numpy as jnp
import numpy as np
from jax import lax
from jax.experimental import pallas as pl
from jax.experimental.pallas import tpu as pltpu
from jax.sharding import PartitionSpec as P

LATENT = 512
V_HEAD = 128
CORES = 2
LANES = 128

score_scale = 192.0 ** (-0.5) * math.log2(math.e)
neg_large = -1e30
least_max = -1e29
f32 = jnp.float32
bf16 = jnp.bfloat16


def chip_cycle(chips):
    wide = max(1, int(round(chips ** (1 / 3))))
    tall = chips // wide
    if wide * tall != chips or wide < 2 or tall < 2:
        return list(range(chips))
    walk = []
    for z in range(tall):
        across = range(1, wide) if z % 2 == 0 else range(wide - 1, 0, -1)
        walk += [z * wide + x for x in across]
    return walk + [z * wide for z in reversed(range(tall))]


def scores_of(q_ref, part, pieces):
    total, at = None, 0
    for piece in pieces:
        s = jnp.dot(
            q_ref[part, at:at + piece.shape[0]], piece[...], preferred_element_type=f32
        )
        total, at = s if total is None else total + s, at + piece.shape[0]
    return total


def values_of(weights, pieces):
    summed, at = [], 0
    for piece in pieces:
        wide = min(piece.shape[0], LATENT - at)
        summed.append(lax.dot_general(
            weights, piece[:wide, :], (((1,), (1,)), ((), ())), preferred_element_type=f32
        ))
        at += wide
    return summed[0] if len(summed) == 1 else jnp.concatenate(summed, axis=1)


def fold_block(part, q_ref, shards, length, old=None, span=None):
    m_old = least_max if old is None else old[0][part, :][:, :1]
    m_new = m_old
    scores = []
    for base, key_ref in shards:
        slot = base + lax.broadcasted_iota(jnp.int32, (1, key_ref[0].shape[1]), 1)
        s = scores_of(q_ref, part, key_ref) * score_scale
        s = jnp.where(slot < length, s, neg_large)
        m_new = jnp.maximum(m_new, jnp.max(s, axis=1, keepdims=True))
        scores.append(s)
    if span is not None:
        keys, shown = span
        s = lax.dot_general(
            q_ref[part, :], keys, (((1,), (1,)), ((), ())), preferred_element_type=f32
        )
        span_s = jnp.where(shown, s * score_scale, neg_large)
        m_new = jnp.maximum(m_new, jnp.max(span_s, axis=1, keepdims=True))
    l_new, summed = 0.0, 0.0
    if old is not None:
        shrink = jnp.exp2(m_old - m_new)
        l_new = old[1][part, :][:, :1] * shrink
        summed = old[2][part, :] * shrink
    for s, (_, key_ref) in zip(scores, shards):
        probs = jnp.exp2(s - m_new)
        l_new += jnp.sum(probs, axis=1, keepdims=True)
        summed += values_of(probs.astype(bf16), key_ref)
    if span is not None:
        probs = jnp.exp2(span_s - m_new)
        l_new += jnp.sum(probs, axis=1, keepdims=True)
        summed += jnp.dot(
            probs.astype(bf16), keys[:, :LATENT], preferred_element_type=f32
        )
    return m_new, l_new, summed


def fold_shards(q_ref, shards, length, old, new, span=None):
    rows = q_ref.shape[0]
    block = min(256, rows)
    for start in range(0, rows, block):
        part = pl.ds(start, block)
        shown = None if span is None else (span[0], span[1](start, block))
        m_new, l_new, summed = fold_block(part, q_ref, shards, length, old, shown)
        new[0][part, :] = jnp.broadcast_to(m_new, (block, LANES))
        new[1][part, :] = jnp.broadcast_to(l_new, (block, LANES))
        new[2][part, :] = summed


def parted(index, size):
    return index >> (size.bit_length() - 1), index & (size - 1)


def token_of(index, tokens, chips):
    device, t = parted(index, tokens)
    core, chip = parted(device, chips)
    return (chip * CORES + ((lax.axis_index("ctx") % CORES) ^ core)) * tokens + t


def with_base(table_ref, at, key_refs):
    me = lax.axis_index("ctx")
    count = table_ref.shape[0] // lax.axis_size("ctx")
    return [
        (table_ref[me * count + at + j] * key_ref.shape[1], (key_ref,))
        for j, key_ref in enumerate(key_refs)
    ]


def pieces_kernel(queries_hbm, span_hbm, out_hbm, sems):
    part = queries_hbm.shape[2]
    copies = [pltpu.make_async_copy(queries_hbm, out_hbm.at[:, :, :part], sems.at[0])]
    for chip in range(out_hbm.shape[0]):
        copies.append(pltpu.make_async_copy(
            span_hbm, out_hbm.at[chip, :, part:], sems.at[1 + chip]
        ))
    for copy in copies:
        copy.start()
    for copy in copies:
        copy.wait()


def first_kernel(heads, count, length_ref, table_ref, here_ref, there_ref, *rest):
    keys, (q_ref, m_ref, l_ref, acc_ref) = rest[:count], rest[count:]
    half = here_ref.shape[0]
    width = q_ref.shape[1]
    for core, piece_ref in enumerate((here_ref, there_ref)):
        for head in range(heads):
            row = (head * CORES + core) * half
            q_ref[row:row + half, :] = piece_ref[:, head * width:(head + 1) * width]
    shards = with_base(table_ref, 0, keys)
    fold_shards(q_ref, shards, length_ref[0], None, (m_ref, l_ref, acc_ref))


def middle_kernel(at, count, length_ref, table_ref, q_ref, m_in, l_in, acc_in, *rest):
    keys, new = rest[:count], rest[count:]
    fold_shards(q_ref, with_base(table_ref, at, keys), length_ref[0], (m_in, l_in, acc_in), new)


def span_kernel(at, count, length_ref, offset_ref, table_ref, q_ref, m_in, l_in, acc_in,
                here_ref, *rest):
    keys, new = rest[:count], rest[count:]
    chips = lax.axis_size("ctx") // CORES
    half = here_ref.shape[0]
    tokens = half // chips
    width = q_ref.shape[1]
    key_index = lax.broadcasted_iota(jnp.int32, (1, half), 1)
    key_token = token_of(key_index, tokens, chips)

    def shown(start, block):
        row_index = start + lax.broadcasted_iota(jnp.int32, (block, 1), 0)
        row_token = token_of(row_index & (half * CORES - 1), tokens, chips)
        return (key_token >= offset_ref[0]) & (key_token <= row_token)

    fold_shards(
        q_ref, with_base(table_ref, at, keys), length_ref[0], (m_in, l_in, acc_in), new,
        (here_ref[:, here_ref.shape[1] - width:], shown),
    )


def last_kernel(at, side, length_ref, table_ref, q_ref, m_ref, l_ref, acc_ref,
                top_ref, bottom_ref, out_ref):
    core = lax.axis_index("ctx") % CORES
    shards = [(with_base(table_ref, at, (top_ref,))[0][0], (top_ref, bottom_ref))]
    rows = out_ref.shape[0]
    part = pl.ds(pl.multiple_of((core ^ side) * rows, rows), rows)
    m_new, l_new, summed = fold_block(
        part, q_ref, shards, length_ref[0], (m_ref, l_ref, acc_ref)
    )
    out_ref[:, :LATENT] = (summed * (1.0 / l_new)).astype(out_ref.dtype)
    weight = jnp.broadcast_to(m_new + jnp.log2(l_new), (rows, LANES))
    if side:
        lane = lax.broadcasted_iota(jnp.int32, (rows, LANES), 1)
        high = weight.astype(bf16).astype(f32)
        mid = (weight - high).astype(bf16).astype(f32)
        weight = jnp.where(lane == 0, high, jnp.where(lane == 1, mid, weight - high - mid))
    out_ref[:, LATENT:] = weight.astype(out_ref.dtype)


def merge_kernel(keep_ref, got_ref, up_ref, out_ref, flat_ref):
    core = lax.axis_index("ctx") % CORES
    heads = up_ref.shape[0]
    everyone = flat_ref.shape[0]
    half = everyone // CORES
    pair = min(2, heads)
    for j in range(0, heads, pair):
        contexts = []
        for head in range(j, j + pair):
            row = head * everyone
            got = jnp.concatenate(
                [got_ref[row + half:row + everyone, :], got_ref[row:row + half, :]], axis=0
            ).astype(f32)
            keep = keep_ref[row:row + everyone, :]
            gap = keep[:, LATENT:LATENT + 1] - got[:, LATENT:LATENT + 1]
            gap = gap - got[:, LATENT + 1:LATENT + 2] - got[:, LATENT + 2:LATENT + 3]
            share = 1.0 / (1.0 + jnp.exp2(-gap))
            rest = 1.0 / (1.0 + jnp.exp2(gap))
            contexts.append(
                (keep[:, :LATENT] * share + got[:, :LATENT] * rest).astype(bf16)
            )
        lifted = jnp.dot(
            jnp.concatenate(contexts, axis=0),
            jnp.concatenate([up_ref[j + i] for i in range(pair)], axis=1),
            preferred_element_type=f32,
        )
        for i in range(pair):
            flat_ref[:, (j + i) * V_HEAD:(j + i + 1) * V_HEAD] = lifted[
                i * everyone:(i + 1) * everyone, i * V_HEAD:(i + 1) * V_HEAD
            ]
    devices, tokens, _ = out_ref.shape
    chips = devices // CORES
    for i in range(devices):
        out_ref[(i % chips) * CORES + (core ^ (i // chips))] = (
            flat_ref[i * tokens:(i + 1) * tokens, :].astype(bf16)
        )


VMEM = pl.BlockSpec(memory_space=pltpu.VMEM)
SMEM = pl.BlockSpec(memory_space=pltpu.SMEM)
PARAMS = pltpu.CompilerParams(vmem_limit_bytes=32 * 1024 * 1024)


def shape(*dims, dtype=f32):
    return jax.ShapeDtypeStruct(dims, dtype)


def on_device(ctx, queries, prefix_latents, span_latents, value_up, prefix_length, span_offset):
    slots, width = prefix_latents.shape
    tokens = queries.shape[0]
    all_heads = queries.shape[1] // width
    chips = ctx // CORES
    heads = all_heads // chips
    rows = tokens * heads
    total = rows * ctx
    everyone = tokens * ctx
    walk = chip_cycle(chips)
    spot = np.argsort(np.array(walk))
    steps = chips // 2

    def across(step):
        return [
            (walk[r] * CORES + c, walk[(r + (-step if c else step)) % chips] * CORES + c)
            for r in range(chips) for c in range(CORES)
        ]

    other_core = [(d, d ^ 1) for d in range(ctx)]
    same_core = [[p * CORES + c for p in range(chips)] for c in range(CORES)]

    turns = [0]
    for s in range(1, steps):
        turns += [-s, s]
    turns.append(steps)
    owner_table = np.array(
        [
            [walk[(spot[p] + (-t if c else t)) % chips] * CORES + c for t in turns]
            for p in range(chips) for c in range(CORES)
        ],
        np.int32,
    )
    table = jnp.asarray(owner_table.reshape(-1))
    state_shapes = [shape(total, LANES), shape(total, LANES), shape(total, LATENT)]

    def fold_first(keys):
        return pl.pallas_call(
            functools.partial(first_kernel, heads, len(keys)),
            out_shape=[shape(total, width, dtype=bf16)] + state_shapes,
            in_specs=[SMEM] * 2 + [VMEM] * (2 + len(keys)),
            out_specs=[VMEM] * 4,
            compiler_params=PARAMS,
            name="first",
        )(prefix_length, table, here, there, *keys)

    def fold_more(at, q, state, keys):
        return pl.pallas_call(
            functools.partial(middle_kernel, at, len(keys)),
            out_shape=state_shapes,
            in_specs=[SMEM] * 2 + [VMEM] * (4 + len(keys)),
            out_specs=[VMEM] * 3,
            compiler_params=PARAMS,
            name="middle",
        )(prefix_length, table, q, *state, *keys)

    onward = functools.partial(lax.ppermute, axis_name="ctx", perm=across(1))
    backward = functools.partial(lax.ppermute, axis_name="ctx", perm=across(-1))
    cut = LATENT // 2
    own = prefix_latents.T
    right, left = onward(own), backward(own)

    anywhere = pl.BlockSpec(memory_space=pl.ANY)
    pieces = pl.pallas_call(
        pieces_kernel,
        out_shape=shape(chips, tokens, (heads + 1) * width, dtype=bf16),
        in_specs=[anywhere] * 2,
        out_specs=anywhere,
        scratch_shapes=[pltpu.SemaphoreType.DMA((1 + chips,))],
        compiler_params=pltpu.CompilerParams(vmem_limit_bytes=56 * 1024 * 1024),
        name="pieces",
    )(queries.reshape(tokens, chips, heads * width).transpose(1, 0, 2), span_latents)
    here = lax.all_to_all(
        pieces, "ctx", split_axis=0, concat_axis=0, axis_index_groups=same_core, tiled=True
    )

    right, left = lax.optimization_barrier((right, left))
    keys, state, at = [own, right, left], None, 0
    for s in range(2, steps):
        right, left = onward(right), backward(left)
        if s == 2:
            here = here.reshape(chips * tokens, (heads + 1) * width)
            there = lax.ppermute(here, "ctx", other_core)
            keys += [right, left]
            continue
        if state is None:
            q, *state = fold_first(keys)
        else:
            state = fold_more(at, q, state, keys)
        at += len(keys)
        keys = [right, left]
    top = onward(right[:cut])
    left, state = lax.optimization_barrier((left, state))
    bottom = backward(left[cut:])
    state = pl.pallas_call(
        functools.partial(span_kernel, at, len(keys)),
        out_shape=state_shapes,
        in_specs=[SMEM] * 3 + [VMEM] * (5 + len(keys)),
        out_specs=[VMEM] * 3,
        compiler_params=PARAMS,
        name="middle",
    )(prefix_length, span_offset, table, q, *state, here, *keys)
    per_core = heads // CORES
    part = per_core * everyone

    def fold_last(side, dtype):
        return pl.pallas_call(
            functools.partial(last_kernel, chips - 1, side),
            out_shape=shape(part, LATENT + LANES, dtype=dtype),
            in_specs=[SMEM] * 2 + [VMEM] * 6,
            out_specs=VMEM,
            compiler_params=PARAMS,
            name="keep" if side == 0 else "give",
        )(prefix_length, table, q, *state, top, bottom)

    got = lax.ppermute(fold_last(1, bf16), "ctx", other_core)
    keep = fold_last(0, f32)
    merged = pl.pallas_call(
        merge_kernel,
        out_shape=shape(ctx, tokens, per_core * V_HEAD, dtype=bf16),
        in_specs=[VMEM] * 3,
        out_specs=VMEM,
        scratch_shapes=[pltpu.VMEM((everyone, per_core * V_HEAD), f32)],
        compiler_params=PARAMS,
        name="merge",
    )(keep, got, value_up)
    returned = lax.all_to_all(merged, "ctx", split_axis=0, concat_axis=0, tiled=True)
    return returned.transpose(1, 0, 2).reshape(tokens, all_heads * V_HEAD)


def solution(mesh):
    return jax.shard_map(
        functools.partial(on_device, mesh.shape["ctx"]),
        mesh=mesh,
        in_specs=(
            P(("groups", "ctx"), None),
            P(("groups", "ctx"), None),
            P(("groups", "ctx"), None),
            P("ctx", None, None),
            P("groups"),
            P("groups"),
        ),
        out_specs=P(("groups", "ctx"), None),
        check_vma=False,
    )
```

```python
import functools
import math

import jax
import jax.numpy as jnp
import numpy as np
from jax import lax
from jax.experimental import pallas as pl
from jax.experimental.pallas import tpu as pltpu
from jax.sharding import PartitionSpec as P

LATENT = 512
V_HEAD = 128
CORES = 2
LANES = 128

score_scale = 192.0 ** (-0.5) * math.log2(math.e)
neg_large = -1e30
least_max = -1e29
f32 = jnp.float32
bf16 = jnp.bfloat16


def chip_cycle(chips):
    wide = max(1, int(round(chips ** (1 / 3))))
    tall = chips // wide
    if wide * tall != chips or wide < 2 or tall < 2:
        return list(range(chips))
    walk = []
    for z in range(tall):
        across = range(1, wide) if z % 2 == 0 else range(wide - 1, 0, -1)
        walk += [z * wide + x for x in across]
    return walk + [z * wide for z in reversed(range(tall))]


def scores_of(q_ref, part, pieces):
    total, at = None, 0
    for piece in pieces:
        s = jnp.dot(
            q_ref[part, at:at + piece.shape[0]], piece[...], preferred_element_type=f32
        )
        total, at = s if total is None else total + s, at + piece.shape[0]
    return total


def values_of(weights, pieces):
    summed, at = [], 0
    for piece in pieces:
        wide = min(piece.shape[0], LATENT - at)
        summed.append(lax.dot_general(
            weights, piece[:wide, :], (((1,), (1,)), ((), ())), preferred_element_type=f32
        ))
        at += wide
    return summed[0] if len(summed) == 1 else jnp.concatenate(summed, axis=1)


def fold_block(part, q_ref, shards, length, old=None, span=None):
    m_old = least_max if old is None else old[0][part, :][:, :1]
    m_new = m_old
    scores = []
    for base, key_ref in shards:
        slot = base + lax.broadcasted_iota(jnp.int32, (1, key_ref[0].shape[1]), 1)
        s = scores_of(q_ref, part, key_ref) * score_scale
        s = jnp.where(slot < length, s, neg_large)
        m_new = jnp.maximum(m_new, jnp.max(s, axis=1, keepdims=True))
        scores.append(s)
    if span is not None:
        keys, shown = span
        s = lax.dot_general(
            q_ref[part, :], keys, (((1,), (1,)), ((), ())), preferred_element_type=f32
        )
        span_s = jnp.where(shown, s * score_scale, neg_large)
        m_new = jnp.maximum(m_new, jnp.max(span_s, axis=1, keepdims=True))
    l_new, summed = 0.0, 0.0
    if old is not None:
        shrink = jnp.exp2(m_old - m_new)
        l_new = old[1][part, :][:, :1] * shrink
        summed = old[2][part, :] * shrink
    for s, (_, key_ref) in zip(scores, shards):
        probs = jnp.exp2(s - m_new)
        l_new += jnp.sum(probs, axis=1, keepdims=True)
        summed += values_of(probs.astype(bf16), key_ref)
    if span is not None:
        probs = jnp.exp2(span_s - m_new)
        l_new += jnp.sum(probs, axis=1, keepdims=True)
        summed += jnp.dot(
            probs.astype(bf16), keys[:, :LATENT], preferred_element_type=f32
        )
    return m_new, l_new, summed


def fold_shards(q_ref, shards, length, old, new, span=None):
    rows = q_ref.shape[0]
    block = min(256, rows)
    for start in range(0, rows, block):
        part = pl.ds(start, block)
        shown = None if span is None else (span[0], span[1](start, block))
        m_new, l_new, summed = fold_block(part, q_ref, shards, length, old, shown)
        new[0][part, :] = jnp.broadcast_to(m_new, (block, LANES))
        new[1][part, :] = jnp.broadcast_to(l_new, (block, LANES))
        new[2][part, :] = summed


def parted(index, size):
    return index >> (size.bit_length() - 1), index & (size - 1)


def token_of(index, tokens, chips):
    device, t = parted(index, tokens)
    core, chip = parted(device, chips)
    return (chip * CORES + ((lax.axis_index("ctx") % CORES) ^ core)) * tokens + t


def with_base(table_ref, at, key_refs):
    me = lax.axis_index("ctx")
    count = table_ref.shape[0] // lax.axis_size("ctx")
    return [
        (table_ref[me * count + at + j] * key_ref.shape[1], (key_ref,))
        for j, key_ref in enumerate(key_refs)
    ]


def pieces_kernel(queries_hbm, span_hbm, out_ref, span_ref, sems):
    part = queries_hbm.shape[2]
    copies = [
        pltpu.make_async_copy(queries_hbm, out_ref.at[:, :, :part], sems.at[0]),
        pltpu.make_async_copy(span_hbm, span_ref, sems.at[1]),
    ]
    for copy in copies:
        copy.start()
    for copy in copies:
        copy.wait()
    for chip in range(out_ref.shape[0]):
        out_ref[chip, :, part:] = span_ref[...]


def first_kernel(heads, count, length_ref, table_ref, here_ref, there_ref, *rest):
    keys, (q_ref, m_ref, l_ref, acc_ref) = rest[:count], rest[count:]
    half = here_ref.shape[0]
    width = q_ref.shape[1]
    for core, piece_ref in enumerate((here_ref, there_ref)):
        for head in range(heads):
            row = (head * CORES + core) * half
            q_ref[row:row + half, :] = piece_ref[:, head * width:(head + 1) * width]
    shards = with_base(table_ref, 0, keys)
    fold_shards(q_ref, shards, length_ref[0], None, (m_ref, l_ref, acc_ref))


def middle_kernel(at, count, length_ref, table_ref, q_ref, m_in, l_in, acc_in, *rest):
    keys, new = rest[:count], rest[count:]
    fold_shards(q_ref, with_base(table_ref, at, keys), length_ref[0], (m_in, l_in, acc_in), new)


def span_kernel(at, count, length_ref, offset_ref, table_ref, q_ref, m_in, l_in, acc_in,
                here_ref, *rest):
    keys, new = rest[:count], rest[count:]
    chips = lax.axis_size("ctx") // CORES
    half = here_ref.shape[0]
    tokens = half // chips
    width = q_ref.shape[1]
    key_index = lax.broadcasted_iota(jnp.int32, (1, half), 1)
    key_token = token_of(key_index, tokens, chips)

    def shown(start, block):
        row_index = start + lax.broadcasted_iota(jnp.int32, (block, 1), 0)
        row_token = token_of(row_index & (half * CORES - 1), tokens, chips)
        return (key_token >= offset_ref[0]) & (key_token <= row_token)

    fold_shards(
        q_ref, with_base(table_ref, at, keys), length_ref[0], (m_in, l_in, acc_in), new,
        (here_ref[:, here_ref.shape[1] - width:], shown),
    )


def last_kernel(at, side, length_ref, table_ref, q_ref, m_ref, l_ref, acc_ref,
                top_ref, bottom_ref, out_ref):
    core = lax.axis_index("ctx") % CORES
    shards = [(with_base(table_ref, at, (top_ref,))[0][0], (top_ref, bottom_ref))]
    rows = out_ref.shape[0]
    part = pl.ds(pl.multiple_of((core ^ side) * rows, rows), rows)
    m_new, l_new, summed = fold_block(
        part, q_ref, shards, length_ref[0], (m_ref, l_ref, acc_ref)
    )
    out_ref[:, :LATENT] = (summed * (1.0 / l_new)).astype(out_ref.dtype)
    weight = jnp.broadcast_to(m_new + jnp.log2(l_new), (rows, LANES))
    if side:
        lane = lax.broadcasted_iota(jnp.int32, (rows, LANES), 1)
        high = weight.astype(bf16).astype(f32)
        mid = (weight - high).astype(bf16).astype(f32)
        weight = jnp.where(lane == 0, high, jnp.where(lane == 1, mid, weight - high - mid))
    out_ref[:, LATENT:] = weight.astype(out_ref.dtype)


def merge_kernel(keep_ref, got_ref, up_ref, out_ref, flat_ref):
    core = lax.axis_index("ctx") % CORES
    heads = up_ref.shape[0]
    everyone = flat_ref.shape[0]
    half = everyone // CORES
    pair = min(2, heads)
    for j in range(0, heads, pair):
        contexts = []
        for head in range(j, j + pair):
            row = head * everyone
            got = jnp.concatenate(
                [got_ref[row + half:row + everyone, :], got_ref[row:row + half, :]], axis=0
            ).astype(f32)
            keep = keep_ref[row:row + everyone, :]
            gap = keep[:, LATENT:LATENT + 1] - got[:, LATENT:LATENT + 1]
            gap = gap - got[:, LATENT + 1:LATENT + 2] - got[:, LATENT + 2:LATENT + 3]
            share = 1.0 / (1.0 + jnp.exp2(-gap))
            rest = 1.0 / (1.0 + jnp.exp2(gap))
            contexts.append(
                (keep[:, :LATENT] * share + got[:, :LATENT] * rest).astype(bf16)
            )
        lifted = jnp.dot(
            jnp.concatenate(contexts, axis=0),
            jnp.concatenate([up_ref[j + i] for i in range(pair)], axis=1),
            preferred_element_type=f32,
        )
        for i in range(pair):
            flat_ref[:, (j + i) * V_HEAD:(j + i + 1) * V_HEAD] = lifted[
                i * everyone:(i + 1) * everyone, i * V_HEAD:(i + 1) * V_HEAD
            ]
    devices, tokens, _ = out_ref.shape
    chips = devices // CORES
    for i in range(devices):
        out_ref[devices - 1 - (i % chips) * CORES - (core ^ (i // chips))] = (
            flat_ref[i * tokens:(i + 1) * tokens, :].astype(bf16)
        )


VMEM = pl.BlockSpec(memory_space=pltpu.VMEM)
SMEM = pl.BlockSpec(memory_space=pltpu.SMEM)
PARAMS = pltpu.CompilerParams(vmem_limit_bytes=32 * 1024 * 1024)


def shape(*dims, dtype=f32):
    return jax.ShapeDtypeStruct(dims, dtype)


def on_device(ctx, queries, prefix_latents, span_latents, value_up, prefix_length, span_offset):
    slots, width = prefix_latents.shape
    tokens = queries.shape[0]
    all_heads = queries.shape[1] // width
    chips = ctx // CORES
    heads = all_heads // chips
    rows = tokens * heads
    total = rows * ctx
    everyone = tokens * ctx
    walk = chip_cycle(chips)
    spot = np.argsort(np.array(walk))
    steps = chips // 2

    def across(step):
        return [
            (walk[r] * CORES + c, walk[(r + (-step if c else step)) % chips] * CORES + c)
            for r in range(chips) for c in range(CORES)
        ]

    other_core = [(d, d ^ 1) for d in range(ctx)]
    same_core = [[p * CORES + c for p in range(chips)] for c in range(CORES)]

    turns = [0]
    for s in range(1, steps):
        turns += [-s, s]
    turns.append(steps)
    owner_table = np.array(
        [
            [walk[(spot[p] + (-t if c else t)) % chips] * CORES + c for t in turns]
            for p in range(chips) for c in range(CORES)
        ],
        np.int32,
    )
    table = jnp.asarray(owner_table.reshape(-1))
    state_shapes = [shape(total, LANES), shape(total, LANES), shape(total, LATENT)]

    def fold_first(keys):
        return pl.pallas_call(
            functools.partial(first_kernel, heads, len(keys)),
            out_shape=[shape(total, width, dtype=bf16)] + state_shapes,
            in_specs=[SMEM] * 2 + [VMEM] * (2 + len(keys)),
            out_specs=[VMEM] * 4,
            compiler_params=PARAMS,
            name="first",
        )(prefix_length, table, here, there, *keys)

    def fold_more(at, q, state, keys):
        return pl.pallas_call(
            functools.partial(middle_kernel, at, len(keys)),
            out_shape=state_shapes,
            in_specs=[SMEM] * 2 + [VMEM] * (4 + len(keys)),
            out_specs=[VMEM] * 3,
            compiler_params=PARAMS,
            name="middle",
        )(prefix_length, table, q, *state, *keys)

    onward = functools.partial(lax.ppermute, axis_name="ctx", perm=across(1))
    backward = functools.partial(lax.ppermute, axis_name="ctx", perm=across(-1))
    cut = LATENT // 2
    own = prefix_latents.T
    right, left = onward(own), backward(own)

    anywhere = pl.BlockSpec(memory_space=pl.ANY)
    pieces = pl.pallas_call(
        pieces_kernel,
        out_shape=shape(chips, tokens, (heads + 1) * width, dtype=bf16),
        in_specs=[anywhere] * 2,
        out_specs=VMEM,
        scratch_shapes=[
            pltpu.VMEM(span_latents.shape, bf16),
            pltpu.SemaphoreType.DMA((2,)),
        ],
        compiler_params=pltpu.CompilerParams(vmem_limit_bytes=56 * 1024 * 1024),
        name="pieces",
    )(queries.reshape(tokens, chips, heads * width).transpose(1, 0, 2), span_latents)
    here = lax.all_to_all(
        pieces, "ctx", split_axis=0, concat_axis=0, axis_index_groups=same_core, tiled=True
    )

    right, left = lax.optimization_barrier((right, left))
    keys, state, at = [own, right, left], None, 0
    for s in range(2, steps):
        right, left = onward(right), backward(left)
        if s == 2:
            here = here.reshape(chips * tokens, (heads + 1) * width)
            there = lax.ppermute(here, "ctx", other_core)
            keys += [right, left]
            continue
        if state is None:
            q, *state = fold_first(keys)
        else:
            state = fold_more(at, q, state, keys)
        at += len(keys)
        keys = [right, left]
    top = onward(right[:cut])
    left, state = lax.optimization_barrier((left, state))
    bottom = backward(left[cut:])
    state = pl.pallas_call(
        functools.partial(span_kernel, at, len(keys)),
        out_shape=state_shapes,
        in_specs=[SMEM] * 3 + [VMEM] * (5 + len(keys)),
        out_specs=[VMEM] * 3,
        compiler_params=PARAMS,
        name="middle",
    )(prefix_length, span_offset, table, q, *state, here, *keys)
    per_core = heads // CORES
    part = per_core * everyone

    def fold_last(side, dtype):
        return pl.pallas_call(
            functools.partial(last_kernel, chips - 1, side),
            out_shape=shape(part, LATENT + LANES, dtype=dtype),
            in_specs=[SMEM] * 2 + [VMEM] * 6,
            out_specs=VMEM,
            compiler_params=PARAMS,
            name="keep" if side == 0 else "give",
        )(prefix_length, table, q, *state, top, bottom)

    got = lax.ppermute(fold_last(1, bf16), "ctx", other_core)
    keep = fold_last(0, f32)
    merged = pl.pallas_call(
        merge_kernel,
        out_shape=shape(ctx, tokens, per_core * V_HEAD, dtype=bf16),
        in_specs=[VMEM] * 3,
        out_specs=VMEM,
        scratch_shapes=[pltpu.VMEM((everyone, per_core * V_HEAD), f32)],
        compiler_params=PARAMS,
        name="merge",
    )(keep, got, value_up)
    returned = lax.all_to_all(
        merged, "ctx", split_axis=0, concat_axis=0, tiled=True,
        axis_index_groups=[list(range(ctx))[::-1]],
    )
    return returned[::-1].transpose(1, 0, 2).reshape(tokens, all_heads * V_HEAD)


def solution(mesh):
    return jax.shard_map(
        functools.partial(on_device, mesh.shape["ctx"]),
        mesh=mesh,
        in_specs=(
            P(("groups", "ctx"), None),
            P(("groups", "ctx"), None),
            P(("groups", "ctx"), None),
            P("ctx", None, None),
            P("groups"),
            P("groups"),
        ),
        out_specs=P(("groups", "ctx"), None),
        check_vma=False,
    )
```

```python
import functools
import math

import jax
import jax.numpy as jnp
import numpy as np
from jax import lax
from jax.experimental import pallas as pl
from jax.experimental.pallas import tpu as pltpu
from jax.sharding import PartitionSpec as P

LATENT = 512
V_HEAD = 128
CORES = 2
LANES = 128

score_scale = 192.0 ** (-0.5) * math.log2(math.e)
neg_large = -1e30
least_max = -1e29
f32 = jnp.float32
bf16 = jnp.bfloat16


def chip_cycle(chips):
    wide = max(1, int(round(chips ** (1 / 3))))
    tall = chips // wide
    if wide * tall != chips or wide < 2 or tall < 2:
        return list(range(chips))
    walk = []
    for z in range(tall):
        across = range(1, wide) if z % 2 == 0 else range(wide - 1, 0, -1)
        walk += [z * wide + x for x in across]
    return walk + [z * wide for z in reversed(range(tall))]


def scores_of(q_ref, part, pieces):
    total, at = None, 0
    for piece in pieces:
        s = jnp.dot(
            q_ref[part, at:at + piece.shape[0]], piece[...], preferred_element_type=f32
        )
        total, at = s if total is None else total + s, at + piece.shape[0]
    return total


def values_of(weights, pieces):
    summed, at = [], 0
    for piece in pieces:
        wide = min(piece.shape[0], LATENT - at)
        summed.append(lax.dot_general(
            weights, piece[:wide, :], (((1,), (1,)), ((), ())), preferred_element_type=f32
        ))
        at += wide
    return summed[0] if len(summed) == 1 else jnp.concatenate(summed, axis=1)


def fold_block(part, q_ref, shards, length, old=None, span=None):
    m_old = least_max if old is None else old[0][part, :][:, :1]
    m_new = m_old
    scores = []
    for base, key_ref in shards:
        slot = base + lax.broadcasted_iota(jnp.int32, (1, key_ref[0].shape[1]), 1)
        s = scores_of(q_ref, part, key_ref) * score_scale
        s = jnp.where(slot < length, s, neg_large)
        m_new = jnp.maximum(m_new, jnp.max(s, axis=1, keepdims=True))
        scores.append(s)
    if span is not None:
        keys, shown = span
        s = lax.dot_general(
            q_ref[part, :], keys, (((1,), (1,)), ((), ())), preferred_element_type=f32
        )
        span_s = jnp.where(shown, s * score_scale, neg_large)
        m_new = jnp.maximum(m_new, jnp.max(span_s, axis=1, keepdims=True))
    l_new, summed = 0.0, 0.0
    if old is not None:
        shrink = jnp.exp2(m_old - m_new)
        l_new = old[1][part, :][:, :1] * shrink
        summed = old[2][part, :] * shrink
    for s, (_, key_ref) in zip(scores, shards):
        probs = jnp.exp2(s - m_new)
        l_new += jnp.sum(probs, axis=1, keepdims=True)
        summed += values_of(probs.astype(bf16), key_ref)
    if span is not None:
        probs = jnp.exp2(span_s - m_new)
        l_new += jnp.sum(probs, axis=1, keepdims=True)
        summed += jnp.dot(
            probs.astype(bf16), keys[:, :LATENT], preferred_element_type=f32
        )
    return m_new, l_new, summed


def fold_shards(q_ref, shards, length, old, new, span=None):
    rows = q_ref.shape[0]
    block = min(256, rows)
    for start in range(0, rows, block):
        part = pl.ds(start, block)
        shown = None if span is None else (span[0], span[1](start, block))
        m_new, l_new, summed = fold_block(part, q_ref, shards, length, old, shown)
        new[0][part, :] = jnp.broadcast_to(m_new, (block, LANES))
        new[1][part, :] = jnp.broadcast_to(l_new, (block, LANES))
        new[2][part, :] = summed


def parted(index, size):
    return index >> (size.bit_length() - 1), index & (size - 1)


def token_of(index, tokens, chips):
    device, t = parted(index, tokens)
    core, chip = parted(device, chips)
    return ((chips - 1 - chip) * CORES + ((lax.axis_index("ctx") % CORES) ^ core)) * tokens + t


def with_base(table_ref, at, key_refs):
    me = lax.axis_index("ctx")
    count = table_ref.shape[0] // lax.axis_size("ctx")
    return [
        (table_ref[me * count + at + j] * key_ref.shape[1], (key_ref,))
        for j, key_ref in enumerate(key_refs)
    ]


def pieces_kernel(queries_hbm, span_hbm, out_ref, queries_ref, span_ref, sems):
    copies = [
        pltpu.make_async_copy(queries_hbm, queries_ref, sems.at[0]),
        pltpu.make_async_copy(span_hbm, span_ref, sems.at[1]),
    ]
    for copy in copies:
        copy.start()
    for copy in copies:
        copy.wait()
    chips = out_ref.shape[0]
    part = queries_ref.shape[1] // chips
    for chip in range(chips):
        out_ref[chips - 1 - chip, :, :part] = queries_ref[:, chip * part:(chip + 1) * part]
        out_ref[chip, :, part:] = span_ref[...]


def first_kernel(heads, count, length_ref, table_ref, here_ref, there_ref, *rest):
    keys, (q_ref, m_ref, l_ref, acc_ref) = rest[:count], rest[count:]
    half = here_ref.shape[0]
    width = q_ref.shape[1]
    for core, piece_ref in enumerate((here_ref, there_ref)):
        for head in range(heads):
            row = (head * CORES + core) * half
            q_ref[row:row + half, :] = piece_ref[:, head * width:(head + 1) * width]
    shards = with_base(table_ref, 0, keys)
    fold_shards(q_ref, shards, length_ref[0], None, (m_ref, l_ref, acc_ref))


def middle_kernel(at, count, length_ref, table_ref, q_ref, m_in, l_in, acc_in, *rest):
    keys, new = rest[:count], rest[count:]
    fold_shards(q_ref, with_base(table_ref, at, keys), length_ref[0], (m_in, l_in, acc_in), new)


def span_kernel(at, count, length_ref, offset_ref, table_ref, q_ref, m_in, l_in, acc_in,
                here_ref, *rest):
    keys, new = rest[:count], rest[count:]
    chips = lax.axis_size("ctx") // CORES
    half = here_ref.shape[0]
    tokens = half // chips
    width = q_ref.shape[1]
    key_index = lax.broadcasted_iota(jnp.int32, (1, half), 1)
    key_token = token_of(key_index, tokens, chips)

    def shown(start, block):
        row_index = start + lax.broadcasted_iota(jnp.int32, (block, 1), 0)
        row_token = token_of(row_index & (half * CORES - 1), tokens, chips)
        return (key_token >= offset_ref[0]) & (key_token <= row_token)

    fold_shards(
        q_ref, with_base(table_ref, at, keys), length_ref[0], (m_in, l_in, acc_in), new,
        (here_ref[:, here_ref.shape[1] - width:], shown),
    )


def last_kernel(at, side, length_ref, table_ref, q_ref, m_ref, l_ref, acc_ref,
                top_ref, bottom_ref, out_ref):
    core = lax.axis_index("ctx") % CORES
    shards = [(with_base(table_ref, at, (top_ref,))[0][0], (top_ref, bottom_ref))]
    rows = out_ref.shape[0]
    part = pl.ds(pl.multiple_of((core ^ side) * rows, rows), rows)
    m_new, l_new, summed = fold_block(
        part, q_ref, shards, length_ref[0], (m_ref, l_ref, acc_ref)
    )
    out_ref[:, :LATENT] = (summed * (1.0 / l_new)).astype(out_ref.dtype)
    weight = jnp.broadcast_to(m_new + jnp.log2(l_new), (rows, LANES))
    if side:
        lane = lax.broadcasted_iota(jnp.int32, (rows, LANES), 1)
        high = weight.astype(bf16).astype(f32)
        mid = (weight - high).astype(bf16).astype(f32)
        weight = jnp.where(lane == 0, high, jnp.where(lane == 1, mid, weight - high - mid))
    out_ref[:, LATENT:] = weight.astype(out_ref.dtype)


def merge_kernel(keep_ref, got_ref, up_ref, out_ref, flat_ref):
    core = lax.axis_index("ctx") % CORES
    heads = up_ref.shape[0]
    everyone = flat_ref.shape[0]
    half = everyone // CORES
    pair = min(2, heads)
    for j in range(0, heads, pair):
        contexts = []
        for head in range(j, j + pair):
            row = head * everyone
            got = jnp.concatenate(
                [got_ref[row + half:row + everyone, :], got_ref[row:row + half, :]], axis=0
            ).astype(f32)
            keep = keep_ref[row:row + everyone, :]
            gap = keep[:, LATENT:LATENT + 1] - got[:, LATENT:LATENT + 1]
            gap = gap - got[:, LATENT + 1:LATENT + 2] - got[:, LATENT + 2:LATENT + 3]
            share = 1.0 / (1.0 + jnp.exp2(-gap))
            rest = 1.0 / (1.0 + jnp.exp2(gap))
            contexts.append(
                (keep[:, :LATENT] * share + got[:, :LATENT] * rest).astype(bf16)
            )
        lifted = jnp.dot(
            jnp.concatenate(contexts, axis=0),
            jnp.concatenate([up_ref[j + i] for i in range(pair)], axis=1),
            preferred_element_type=f32,
        )
        for i in range(pair):
            flat_ref[:, (j + i) * V_HEAD:(j + i + 1) * V_HEAD] = lifted[
                i * everyone:(i + 1) * everyone, i * V_HEAD:(i + 1) * V_HEAD
            ]
    devices, tokens, _ = out_ref.shape
    chips = devices // CORES
    for i in range(devices):
        out_ref[1 + (i % chips) * CORES - (core ^ (i // chips))] = (
            flat_ref[i * tokens:(i + 1) * tokens, :].astype(bf16)
        )


VMEM = pl.BlockSpec(memory_space=pltpu.VMEM)
SMEM = pl.BlockSpec(memory_space=pltpu.SMEM)
PARAMS = pltpu.CompilerParams(vmem_limit_bytes=32 * 1024 * 1024)


def shape(*dims, dtype=f32):
    return jax.ShapeDtypeStruct(dims, dtype)


def on_device(ctx, queries, prefix_latents, span_latents, value_up, prefix_length, span_offset):
    slots, width = prefix_latents.shape
    tokens = queries.shape[0]
    all_heads = queries.shape[1] // width
    chips = ctx // CORES
    heads = all_heads // chips
    rows = tokens * heads
    total = rows * ctx
    everyone = tokens * ctx
    walk = chip_cycle(chips)
    spot = np.argsort(np.array(walk))
    steps = chips // 2

    def across(step):
        return [
            (walk[r] * CORES + c, walk[(r + (-step if c else step)) % chips] * CORES + c)
            for r in range(chips) for c in range(CORES)
        ]

    other_core = [(d, d ^ 1) for d in range(ctx)]
    same_core = [[p * CORES + c for p in reversed(range(chips))] for c in range(CORES)]

    turns = [0]
    for s in range(1, steps):
        turns += [-s, s]
    turns.append(steps)
    owner_table = np.array(
        [
            [walk[(spot[p] + (-t if c else t)) % chips] * CORES + c for t in turns]
            for p in range(chips) for c in range(CORES)
        ],
        np.int32,
    )
    table = jnp.asarray(owner_table.reshape(-1))
    state_shapes = [shape(total, LANES), shape(total, LANES), shape(total, LATENT)]

    def fold_first(keys):
        return pl.pallas_call(
            functools.partial(first_kernel, heads, len(keys)),
            out_shape=[shape(total, width, dtype=bf16)] + state_shapes,
            in_specs=[SMEM] * 2 + [VMEM] * (2 + len(keys)),
            out_specs=[VMEM] * 4,
            compiler_params=PARAMS,
            name="first",
        )(prefix_length, table, here, there, *keys)

    def fold_more(at, q, state, keys):
        return pl.pallas_call(
            functools.partial(middle_kernel, at, len(keys)),
            out_shape=state_shapes,
            in_specs=[SMEM] * 2 + [VMEM] * (4 + len(keys)),
            out_specs=[VMEM] * 3,
            compiler_params=PARAMS,
            name="middle",
        )(prefix_length, table, q, *state, *keys)

    onward = functools.partial(lax.ppermute, axis_name="ctx", perm=across(1))
    backward = functools.partial(lax.ppermute, axis_name="ctx", perm=across(-1))
    cut = LATENT // 2
    own = prefix_latents.T
    right, left = onward(own), backward(own)

    anywhere = pl.BlockSpec(memory_space=pl.ANY)
    pieces = pl.pallas_call(
        pieces_kernel,
        out_shape=shape(chips, tokens, (heads + 1) * width, dtype=bf16),
        in_specs=[anywhere] * 2,
        out_specs=VMEM,
        scratch_shapes=[
            pltpu.VMEM(queries.shape, bf16),
            pltpu.VMEM(span_latents.shape, bf16),
            pltpu.SemaphoreType.DMA((2,)),
        ],
        compiler_params=pltpu.CompilerParams(vmem_limit_bytes=56 * 1024 * 1024),
        name="pieces",
    )(queries, span_latents)
    here = lax.all_to_all(
        pieces, "ctx", split_axis=0, concat_axis=0, axis_index_groups=same_core, tiled=True
    )

    right, left = lax.optimization_barrier((right, left))
    keys, state, at = [own, right, left], None, 0
    for s in range(2, steps):
        right, left = onward(right), backward(left)
        if s == 2:
            here = here.reshape(chips * tokens, (heads + 1) * width)
            there = lax.ppermute(here, "ctx", other_core)
            keys += [right, left]
            continue
        if state is None:
            q, *state = fold_first(keys)
        else:
            state = fold_more(at, q, state, keys)
        at += len(keys)
        keys = [right, left]
    top = onward(right[:cut])
    left, state = lax.optimization_barrier((left, state))
    bottom = backward(left[cut:])
    state = pl.pallas_call(
        functools.partial(span_kernel, at, len(keys)),
        out_shape=state_shapes,
        in_specs=[SMEM] * 3 + [VMEM] * (5 + len(keys)),
        out_specs=[VMEM] * 3,
        compiler_params=PARAMS,
        name="middle",
    )(prefix_length, span_offset, table, q, *state, here, *keys)
    per_core = heads // CORES
    part = per_core * everyone

    def fold_last(side, dtype):
        return pl.pallas_call(
            functools.partial(last_kernel, chips - 1, side),
            out_shape=shape(part, LATENT + LANES, dtype=dtype),
            in_specs=[SMEM] * 2 + [VMEM] * 6,
            out_specs=VMEM,
            compiler_params=PARAMS,
            name="keep" if side == 0 else "give",
        )(prefix_length, table, q, *state, top, bottom)

    got = lax.ppermute(fold_last(1, bf16), "ctx", other_core)
    keep = fold_last(0, f32)
    merged = pl.pallas_call(
        merge_kernel,
        out_shape=shape(ctx, tokens, per_core * V_HEAD, dtype=bf16),
        in_specs=[VMEM] * 3,
        out_specs=VMEM,
        scratch_shapes=[pltpu.VMEM((everyone, per_core * V_HEAD), f32)],
        compiler_params=PARAMS,
        name="merge",
    )(keep, got, value_up)
    returned = lax.all_to_all(
        merged, "ctx", split_axis=0, concat_axis=0, tiled=True,
        axis_index_groups=[list(range(ctx))[::-1]],
    )
    return returned[::-1].transpose(1, 0, 2).reshape(tokens, all_heads * V_HEAD)


def solution(mesh):
    return jax.shard_map(
        functools.partial(on_device, mesh.shape["ctx"]),
        mesh=mesh,
        in_specs=(
            P(("groups", "ctx"), None),
            P(("groups", "ctx"), None),
            P(("groups", "ctx"), None),
            P("ctx", None, None),
            P("groups"),
            P("groups"),
        ),
        out_specs=P(("groups", "ctx"), None),
        check_vma=False,
    )
```

```python
import functools
import math

import jax
import jax.numpy as jnp
import numpy as np
from jax import lax
from jax.experimental import pallas as pl
from jax.experimental.pallas import tpu as pltpu
from jax.sharding import PartitionSpec as P

LATENT = 512
V_HEAD = 128
CORES = 2
LANES = 128

score_scale = 192.0 ** (-0.5) * math.log2(math.e)
neg_large = -1e30
least_max = -1e29
f32 = jnp.float32
bf16 = jnp.bfloat16


def chip_cycle(chips):
    wide = max(1, int(round(chips ** (1 / 3))))
    tall = chips // wide
    if wide * tall != chips or wide < 2 or tall < 2:
        return list(range(chips))
    walk = []
    for z in range(tall):
        across = range(1, wide) if z % 2 == 0 else range(wide - 1, 0, -1)
        walk += [z * wide + x for x in across]
    return walk + [z * wide for z in reversed(range(tall))]


def scores_of(q_ref, part, pieces):
    total, at = None, 0
    for piece in pieces:
        s = jnp.dot(
            q_ref[part, at:at + piece.shape[0]], piece[...], preferred_element_type=f32
        )
        total, at = s if total is None else total + s, at + piece.shape[0]
    return total


def values_of(weights, pieces):
    summed, at = [], 0
    for piece in pieces:
        wide = min(piece.shape[0], LATENT - at)
        summed.append(lax.dot_general(
            weights, piece[:wide, :], (((1,), (1,)), ((), ())), preferred_element_type=f32
        ))
        at += wide
    return summed[0] if len(summed) == 1 else jnp.concatenate(summed, axis=1)


def fold_block(part, q_ref, shards, length, old=None, span=None):
    m_old = least_max if old is None else old[0][part, :][:, :1]
    m_new = m_old
    scores = []
    for base, key_ref in shards:
        slot = base + lax.broadcasted_iota(jnp.int32, (1, key_ref[0].shape[1]), 1)
        s = scores_of(q_ref, part, key_ref) * score_scale
        s = jnp.where(slot < length, s, neg_large)
        m_new = jnp.maximum(m_new, jnp.max(s, axis=1, keepdims=True))
        scores.append(s)
    if span is not None:
        keys, shown = span
        s = lax.dot_general(
            q_ref[part, :], keys, (((1,), (1,)), ((), ())), preferred_element_type=f32
        )
        span_s = jnp.where(shown, s * score_scale, neg_large)
        m_new = jnp.maximum(m_new, jnp.max(span_s, axis=1, keepdims=True))
    l_new, summed = 0.0, 0.0
    if old is not None:
        shrink = jnp.exp2(m_old - m_new)
        l_new = old[1][part, :][:, :1] * shrink
        summed = old[2][part, :] * shrink
    for s, (_, key_ref) in zip(scores, shards):
        probs = jnp.exp2(s - m_new)
        l_new += jnp.sum(probs, axis=1, keepdims=True)
        summed += values_of(probs.astype(bf16), key_ref)
    if span is not None:
        probs = jnp.exp2(span_s - m_new)
        l_new += jnp.sum(probs, axis=1, keepdims=True)
        summed += jnp.dot(
            probs.astype(bf16), keys[:, :LATENT], preferred_element_type=f32
        )
    return m_new, l_new, summed


def fold_shards(q_ref, shards, length, old, new, span=None):
    rows = q_ref.shape[0]
    block = min(256, rows)
    for start in range(0, rows, block):
        part = pl.ds(start, block)
        shown = None if span is None else (span[0], span[1](start, block))
        m_new, l_new, summed = fold_block(part, q_ref, shards, length, old, shown)
        new[0][part, :] = jnp.broadcast_to(m_new, (block, LANES))
        new[1][part, :] = jnp.broadcast_to(l_new, (block, LANES))
        new[2][part, :] = summed


def parted(index, size):
    return index >> (size.bit_length() - 1), index & (size - 1)


def token_of(index, tokens, chips):
    device, t = parted(index, tokens)
    core, chip = parted(device, chips)
    return (chip * CORES + ((lax.axis_index("ctx") % CORES) ^ core)) * tokens + t


def with_base(table_ref, at, key_refs):
    me = lax.axis_index("ctx")
    count = table_ref.shape[0] // lax.axis_size("ctx")
    return [
        (table_ref[me * count + at + j] * key_ref.shape[1], (key_ref,))
        for j, key_ref in enumerate(key_refs)
    ]


def pieces_kernel(queries_hbm, span_hbm, out_ref, span_ref, sems):
    part = queries_hbm.shape[2]
    copies = [
        pltpu.make_async_copy(queries_hbm, out_ref.at[:, :, :part], sems.at[0]),
        pltpu.make_async_copy(span_hbm, span_ref, sems.at[1]),
    ]
    for copy in copies:
        copy.start()
    for copy in copies:
        copy.wait()
    for chip in range(out_ref.shape[0]):
        out_ref[chip, :, part:] = span_ref[...]


def first_kernel(heads, count, length_ref, table_ref, here_ref, there_ref, *rest):
    keys, (q_ref, m_ref, l_ref, acc_ref) = rest[:count], rest[count:]
    half = here_ref.shape[0]
    width = q_ref.shape[1]
    for core, piece_ref in enumerate((here_ref, there_ref)):
        for head in range(heads):
            row = (head * CORES + core) * half
            q_ref[row:row + half, :] = piece_ref[:, head * width:(head + 1) * width]
    shards = with_base(table_ref, 0, keys)
    fold_shards(q_ref, shards, length_ref[0], None, (m_ref, l_ref, acc_ref))


def middle_kernel(at, count, length_ref, table_ref, q_ref, m_in, l_in, acc_in, *rest):
    keys, new = rest[:count], rest[count:]
    fold_shards(q_ref, with_base(table_ref, at, keys), length_ref[0], (m_in, l_in, acc_in), new)


def span_kernel(at, count, length_ref, offset_ref, table_ref, q_ref, m_in, l_in, acc_in,
                here_ref, *rest):
    keys, new = rest[:count], rest[count:]
    chips = lax.axis_size("ctx") // CORES
    half = here_ref.shape[0]
    tokens = half // chips
    width = q_ref.shape[1]
    key_index = lax.broadcasted_iota(jnp.int32, (1, half), 1)
    key_token = token_of(key_index, tokens, chips)

    def shown(start, block):
        row_index = start + lax.broadcasted_iota(jnp.int32, (block, 1), 0)
        row_token = token_of(row_index & (half * CORES - 1), tokens, chips)
        return (key_token >= offset_ref[0]) & (key_token <= row_token)

    fold_shards(
        q_ref, with_base(table_ref, at, keys), length_ref[0], (m_in, l_in, acc_in), new,
        (here_ref[:, here_ref.shape[1] - width:], shown),
    )


def last_kernel(at, side, length_ref, table_ref, q_ref, m_ref, l_ref, acc_ref,
                top_ref, bottom_ref, out_ref):
    core = lax.axis_index("ctx") % CORES
    shards = [(with_base(table_ref, at, (top_ref,))[0][0], (top_ref, bottom_ref))]
    rows = out_ref.shape[0]
    part = pl.ds(pl.multiple_of((core ^ side) * rows, rows), rows)
    m_new, l_new, summed = fold_block(
        part, q_ref, shards, length_ref[0], (m_ref, l_ref, acc_ref)
    )
    out_ref[:, :LATENT] = (summed * (1.0 / l_new)).astype(out_ref.dtype)
    weight = jnp.broadcast_to(m_new + jnp.log2(l_new), (rows, LANES))
    if side:
        lane = lax.broadcasted_iota(jnp.int32, (rows, LANES), 1)
        high = weight.astype(bf16).astype(f32)
        mid = (weight - high).astype(bf16).astype(f32)
        weight = jnp.where(lane == 0, high, jnp.where(lane == 1, mid, weight - high - mid))
    out_ref[:, LATENT:] = weight.astype(out_ref.dtype)


def merge_kernel(keep_ref, got_ref, up_ref, out_ref, flat_ref):
    core = lax.axis_index("ctx") % CORES
    heads = up_ref.shape[0]
    everyone = flat_ref.shape[0]
    half = everyone // CORES
    pair = min(2, heads)
    for j in range(0, heads, pair):
        contexts = []
        for head in range(j, j + pair):
            row = head * everyone
            got = jnp.concatenate(
                [got_ref[row + half:row + everyone, :], got_ref[row:row + half, :]], axis=0
            ).astype(f32)
            keep = keep_ref[row:row + everyone, :]
            gap = keep[:, LATENT:LATENT + 1] - got[:, LATENT:LATENT + 1]
            gap = gap - got[:, LATENT + 1:LATENT + 2] - got[:, LATENT + 2:LATENT + 3]
            share = 1.0 / (1.0 + jnp.exp2(-gap))
            rest = 1.0 / (1.0 + jnp.exp2(gap))
            contexts.append(
                (keep[:, :LATENT] * share + got[:, :LATENT] * rest).astype(bf16)
            )
        lifted = jnp.dot(
            jnp.concatenate(contexts, axis=0),
            jnp.concatenate([up_ref[j + i] for i in range(pair)], axis=1),
            preferred_element_type=f32,
        )
        for i in range(pair):
            flat_ref[:, (j + i) * V_HEAD:(j + i + 1) * V_HEAD] = lifted[
                i * everyone:(i + 1) * everyone, i * V_HEAD:(i + 1) * V_HEAD
            ]
    devices, tokens, _ = out_ref.shape
    chips = devices // CORES
    for i in range(devices):
        out_ref[(1 - (core ^ (i // chips))) * chips + chips - 1 - i % chips] = (
            flat_ref[i * tokens:(i + 1) * tokens, :].astype(bf16)
        )


def place_kernel(parts_ref, out_ref):
    devices, _, width = parts_ref.shape
    chips = devices // CORES
    for i in range(devices):
        core, chip = 1 - i // chips, chips - 1 - i % chips
        at = (chip * CORES + core) * width
        out_ref[:, at:at + width] = parts_ref[i]


VMEM = pl.BlockSpec(memory_space=pltpu.VMEM)
SMEM = pl.BlockSpec(memory_space=pltpu.SMEM)
PARAMS = pltpu.CompilerParams(vmem_limit_bytes=32 * 1024 * 1024)


def shape(*dims, dtype=f32):
    return jax.ShapeDtypeStruct(dims, dtype)


def on_device(ctx, queries, prefix_latents, span_latents, value_up, prefix_length, span_offset):
    slots, width = prefix_latents.shape
    tokens = queries.shape[0]
    all_heads = queries.shape[1] // width
    chips = ctx // CORES
    heads = all_heads // chips
    rows = tokens * heads
    total = rows * ctx
    everyone = tokens * ctx
    walk = chip_cycle(chips)
    spot = np.argsort(np.array(walk))
    steps = chips // 2

    def across(step):
        return [
            (walk[r] * CORES + c, walk[(r + (-step if c else step)) % chips] * CORES + c)
            for r in range(chips) for c in range(CORES)
        ]

    other_core = [(d, d ^ 1) for d in range(ctx)]
    same_core = [[p * CORES + c for p in range(chips)] for c in range(CORES)]

    turns = [0]
    for s in range(1, steps):
        turns += [-s, s]
    turns.append(steps)
    owner_table = np.array(
        [
            [walk[(spot[p] + (-t if c else t)) % chips] * CORES + c for t in turns]
            for p in range(chips) for c in range(CORES)
        ],
        np.int32,
    )
    table = jnp.asarray(owner_table.reshape(-1))
    state_shapes = [shape(total, LANES), shape(total, LANES), shape(total, LATENT)]

    def fold_first(keys):
        return pl.pallas_call(
            functools.partial(first_kernel, heads, len(keys)),
            out_shape=[shape(total, width, dtype=bf16)] + state_shapes,
            in_specs=[SMEM] * 2 + [VMEM] * (2 + len(keys)),
            out_specs=[VMEM] * 4,
            compiler_params=PARAMS,
            name="first",
        )(prefix_length, table, here, there, *keys)

    def fold_more(at, q, state, keys):
        return pl.pallas_call(
            functools.partial(middle_kernel, at, len(keys)),
            out_shape=state_shapes,
            in_specs=[SMEM] * 2 + [VMEM] * (4 + len(keys)),
            out_specs=[VMEM] * 3,
            compiler_params=PARAMS,
            name="middle",
        )(prefix_length, table, q, *state, *keys)

    onward = functools.partial(lax.ppermute, axis_name="ctx", perm=across(1))
    backward = functools.partial(lax.ppermute, axis_name="ctx", perm=across(-1))
    cut = LATENT // 2
    own = prefix_latents.T
    right, left = onward(own), backward(own)

    anywhere = pl.BlockSpec(memory_space=pl.ANY)
    pieces = pl.pallas_call(
        pieces_kernel,
        out_shape=shape(chips, tokens, (heads + 1) * width, dtype=bf16),
        in_specs=[anywhere] * 2,
        out_specs=VMEM,
        scratch_shapes=[
            pltpu.VMEM(span_latents.shape, bf16),
            pltpu.SemaphoreType.DMA((2,)),
        ],
        compiler_params=pltpu.CompilerParams(vmem_limit_bytes=56 * 1024 * 1024),
        name="pieces",
    )(queries.reshape(tokens, chips, heads * width).transpose(1, 0, 2), span_latents)
    here = lax.all_to_all(
        pieces, "ctx", split_axis=0, concat_axis=0, axis_index_groups=same_core, tiled=True
    )

    right, left = lax.optimization_barrier((right, left))
    keys, state, at = [own, right, left], None, 0
    for s in range(2, steps):
        right, left = onward(right), backward(left)
        if s == 2:
            here = here.reshape(chips * tokens, (heads + 1) * width)
            there = lax.ppermute(here, "ctx", other_core)
            keys += [right, left]
            continue
        if state is None:
            q, *state = fold_first(keys)
        else:
            state = fold_more(at, q, state, keys)
        at += len(keys)
        keys = [right, left]
    top = onward(right[:cut])
    left, state = lax.optimization_barrier((left, state))
    bottom = backward(left[cut:])
    state = pl.pallas_call(
        functools.partial(span_kernel, at, len(keys)),
        out_shape=state_shapes,
        in_specs=[SMEM] * 3 + [VMEM] * (5 + len(keys)),
        out_specs=[VMEM] * 3,
        compiler_params=PARAMS,
        name="middle",
    )(prefix_length, span_offset, table, q, *state, here, *keys)
    per_core = heads // CORES
    part = per_core * everyone

    def fold_last(side, dtype):
        return pl.pallas_call(
            functools.partial(last_kernel, chips - 1, side),
            out_shape=shape(part, LATENT + LANES, dtype=dtype),
            in_specs=[SMEM] * 2 + [VMEM] * 6,
            out_specs=VMEM,
            compiler_params=PARAMS,
            name="keep" if side == 0 else "give",
        )(prefix_length, table, q, *state, top, bottom)

    got = lax.ppermute(fold_last(1, bf16), "ctx", other_core)
    keep = fold_last(0, f32)
    merged = pl.pallas_call(
        merge_kernel,
        out_shape=shape(ctx, tokens, per_core * V_HEAD, dtype=bf16),
        in_specs=[VMEM] * 3,
        out_specs=VMEM,
        scratch_shapes=[pltpu.VMEM((everyone, per_core * V_HEAD), f32)],
        compiler_params=PARAMS,
        name="merge",
    )(keep, got, value_up)
    returned = lax.all_to_all(
        merged, "ctx", split_axis=0, concat_axis=0, tiled=True,
        axis_index_groups=[
            [p * CORES + c for c in reversed(range(CORES)) for p in reversed(range(chips))]
        ],
    )
    return pl.pallas_call(
        place_kernel,
        out_shape=shape(tokens, all_heads * V_HEAD, dtype=bf16),
        in_specs=[VMEM],
        out_specs=VMEM,
        compiler_params=PARAMS,
        name="place",
    )(returned)


def solution(mesh):
    return jax.shard_map(
        functools.partial(on_device, mesh.shape["ctx"]),
        mesh=mesh,
        in_specs=(
            P(("groups", "ctx"), None),
            P(("groups", "ctx"), None),
            P(("groups", "ctx"), None),
            P("ctx", None, None),
            P("groups"),
            P("groups"),
        ),
        out_specs=P(("groups", "ctx"), None),
        check_vma=False,
    )
```

```python
import functools
import math

import jax
import jax.numpy as jnp
import numpy as np
from jax import lax
from jax.experimental import pallas as pl
from jax.experimental.pallas import tpu as pltpu
from jax.sharding import PartitionSpec as P

LATENT = 512
V_HEAD = 128
CORES = 2
LANES = 128

score_scale = 192.0 ** (-0.5) * math.log2(math.e)
neg_large = -1e30
least_max = -1e29
f32 = jnp.float32
bf16 = jnp.bfloat16


def chip_cycle(chips):
    wide = max(1, int(round(chips ** (1 / 3))))
    tall = chips // wide
    if wide * tall != chips or wide < 2 or tall < 2:
        return list(range(chips))
    walk = []
    for z in range(tall):
        across = range(1, wide) if z % 2 == 0 else range(wide - 1, 0, -1)
        walk += [z * wide + x for x in across]
    return walk + [z * wide for z in reversed(range(tall))]


def scores_of(q_ref, part, pieces):
    total, at = None, 0
    for piece in pieces:
        s = jnp.dot(
            q_ref[part, at:at + piece.shape[0]], piece[...], preferred_element_type=f32
        )
        total, at = s if total is None else total + s, at + piece.shape[0]
    return total


def values_of(weights, pieces):
    summed, at = [], 0
    for piece in pieces:
        wide = min(piece.shape[0], LATENT - at)
        summed.append(lax.dot_general(
            weights, piece[:wide, :], (((1,), (1,)), ((), ())), preferred_element_type=f32
        ))
        at += wide
    return summed[0] if len(summed) == 1 else jnp.concatenate(summed, axis=1)


def fold_block(part, q_ref, shards, length, old=None, span=None):
    m_old = least_max if old is None else old[0][part, :][:, :1]
    m_new = m_old
    scores = []
    for base, key_ref in shards:
        slot = base + lax.broadcasted_iota(jnp.int32, (1, key_ref[0].shape[1]), 1)
        s = scores_of(q_ref, part, key_ref) * score_scale
        s = jnp.where(slot < length, s, neg_large)
        m_new = jnp.maximum(m_new, jnp.max(s, axis=1, keepdims=True))
        scores.append(s)
    if span is not None:
        keys, shown = span
        s = lax.dot_general(
            q_ref[part, :], keys, (((1,), (1,)), ((), ())), preferred_element_type=f32
        )
        span_s = jnp.where(shown, s * score_scale, neg_large)
        m_new = jnp.maximum(m_new, jnp.max(span_s, axis=1, keepdims=True))
    l_new, summed = 0.0, 0.0
    if old is not None:
        shrink = jnp.exp2(m_old - m_new)
        l_new = old[1][part, :][:, :1] * shrink
        summed = old[2][part, :] * shrink
    for s, (_, key_ref) in zip(scores, shards):
        probs = jnp.exp2(s - m_new)
        l_new += jnp.sum(probs, axis=1, keepdims=True)
        summed += values_of(probs.astype(bf16), key_ref)
    if span is not None:
        probs = jnp.exp2(span_s - m_new)
        l_new += jnp.sum(probs, axis=1, keepdims=True)
        summed += jnp.dot(
            probs.astype(bf16), keys[:, :LATENT], preferred_element_type=f32
        )
    return m_new, l_new, summed


def fold_shards(q_ref, shards, length, old, new, span=None):
    rows = q_ref.shape[0]
    block = min(256, rows)
    for start in range(0, rows, block):
        part = pl.ds(start, block)
        shown = None if span is None else (span[0], span[1](start, block))
        m_new, l_new, summed = fold_block(part, q_ref, shards, length, old, shown)
        new[0][part, :] = jnp.broadcast_to(m_new, (block, LANES))
        new[1][part, :] = jnp.broadcast_to(l_new, (block, LANES))
        new[2][part, :] = summed


def parted(index, size):
    return index >> (size.bit_length() - 1), index & (size - 1)


def token_of(index, tokens, chips):
    device, t = parted(index, tokens)
    core, chip = parted(device, chips)
    return (chip * CORES + ((lax.axis_index("ctx") % CORES) ^ core)) * tokens + t


def with_base(table_ref, at, key_refs):
    me = lax.axis_index("ctx")
    count = table_ref.shape[0] // lax.axis_size("ctx")
    return [
        (table_ref[me * count + at + j] * key_ref.shape[1], (key_ref,))
        for j, key_ref in enumerate(key_refs)
    ]


def pieces_kernel(queries_hbm, span_hbm, out_ref, span_ref, sems):
    part = queries_hbm.shape[2]
    copies = [
        pltpu.make_async_copy(queries_hbm, out_ref.at[:, :, :part], sems.at[0]),
        pltpu.make_async_copy(span_hbm, span_ref, sems.at[1]),
    ]
    for copy in copies:
        copy.start()
    for copy in copies:
        copy.wait()
    for chip in range(out_ref.shape[0]):
        out_ref[chip, :, part:] = span_ref[...]


def first_kernel(heads, count, length_ref, table_ref, here_ref, there_ref, *rest):
    keys, (q_ref, m_ref, l_ref, acc_ref) = rest[:count], rest[count:]
    half = here_ref.shape[0]
    width = q_ref.shape[1]
    for core, piece_ref in enumerate((here_ref, there_ref)):
        for head in range(heads):
            row = (head * CORES + core) * half
            q_ref[row:row + half, :] = piece_ref[:, head * width:(head + 1) * width]
    shards = with_base(table_ref, 0, keys)
    fold_shards(q_ref, shards, length_ref[0], None, (m_ref, l_ref, acc_ref))


def middle_kernel(at, count, length_ref, table_ref, q_ref, m_in, l_in, acc_in, *rest):
    keys, new = rest[:count], rest[count:]
    fold_shards(q_ref, with_base(table_ref, at, keys), length_ref[0], (m_in, l_in, acc_in), new)


def span_kernel(at, count, length_ref, offset_ref, table_ref, q_ref, m_in, l_in, acc_in,
                here_ref, *rest):
    keys, new = rest[:count], rest[count:]
    chips = lax.axis_size("ctx") // CORES
    half = here_ref.shape[0]
    tokens = half // chips
    width = q_ref.shape[1]
    key_index = lax.broadcasted_iota(jnp.int32, (1, half), 1)
    key_token = token_of(key_index, tokens, chips)

    def shown(start, block):
        row_index = start + lax.broadcasted_iota(jnp.int32, (block, 1), 0)
        row_token = token_of(row_index & (half * CORES - 1), tokens, chips)
        return (key_token >= offset_ref[0]) & (key_token <= row_token)

    fold_shards(
        q_ref, with_base(table_ref, at, keys), length_ref[0], (m_in, l_in, acc_in), new,
        (here_ref[:, here_ref.shape[1] - width:], shown),
    )


def last_kernel(at, side, length_ref, table_ref, q_ref, m_ref, l_ref, acc_ref,
                top_ref, bottom_ref, out_ref):
    core = lax.axis_index("ctx") % CORES
    shards = [(with_base(table_ref, at, (top_ref,))[0][0], (top_ref, bottom_ref))]
    rows = out_ref.shape[0]
    part = pl.ds(pl.multiple_of((core ^ side) * rows, rows), rows)
    m_new, l_new, summed = fold_block(
        part, q_ref, shards, length_ref[0], (m_ref, l_ref, acc_ref)
    )
    out_ref[:, :LATENT] = (summed * (1.0 / l_new)).astype(out_ref.dtype)
    weight = jnp.broadcast_to(m_new + jnp.log2(l_new), (rows, LANES))
    if side:
        lane = lax.broadcasted_iota(jnp.int32, (rows, LANES), 1)
        high = weight.astype(bf16).astype(f32)
        mid = (weight - high).astype(bf16).astype(f32)
        weight = jnp.where(lane == 0, high, jnp.where(lane == 1, mid, weight - high - mid))
    out_ref[:, LATENT:] = weight.astype(out_ref.dtype)


def merge_kernel(keep_ref, got_ref, up_ref, out_ref, flat_ref):
    core = lax.axis_index("ctx") % CORES
    heads = up_ref.shape[0]
    everyone = flat_ref.shape[0]
    half = everyone // CORES
    pair = min(2, heads)
    for j in range(0, heads, pair):
        contexts = []
        for head in range(j, j + pair):
            row = head * everyone
            got = jnp.concatenate(
                [got_ref[row + half:row + everyone, :], got_ref[row:row + half, :]], axis=0
            ).astype(f32)
            keep = keep_ref[row:row + everyone, :]
            gap = keep[:, LATENT:LATENT + 1] - got[:, LATENT:LATENT + 1]
            gap = gap - got[:, LATENT + 1:LATENT + 2] - got[:, LATENT + 2:LATENT + 3]
            share = 1.0 / (1.0 + jnp.exp2(-gap))
            rest = 1.0 / (1.0 + jnp.exp2(gap))
            contexts.append(
                (keep[:, :LATENT] * share + got[:, :LATENT] * rest).astype(bf16)
            )
        lifted = jnp.dot(
            jnp.concatenate(contexts, axis=0),
            jnp.concatenate([up_ref[j + i] for i in range(pair)], axis=1),
            preferred_element_type=f32,
        )
        for i in range(pair):
            flat_ref[:, (j + i) * V_HEAD:(j + i + 1) * V_HEAD] = lifted[
                i * everyone:(i + 1) * everyone, i * V_HEAD:(i + 1) * V_HEAD
            ]
    devices, tokens, _ = out_ref.shape
    chips = devices // CORES
    for i in range(devices):
        out_ref[devices - 1 - (i % chips) * CORES - (core ^ (i // chips))] = (
            flat_ref[i * tokens:(i + 1) * tokens, :].astype(bf16)
        )


VMEM = pl.BlockSpec(memory_space=pltpu.VMEM)
SMEM = pl.BlockSpec(memory_space=pltpu.SMEM)
PARAMS = pltpu.CompilerParams(vmem_limit_bytes=32 * 1024 * 1024)


def shape(*dims, dtype=f32):
    return jax.ShapeDtypeStruct(dims, dtype)


def on_device(ctx, queries, prefix_latents, span_latents, value_up, prefix_length, span_offset):
    slots, width = prefix_latents.shape
    tokens = queries.shape[0]
    all_heads = queries.shape[1] // width
    chips = ctx // CORES
    heads = all_heads // chips
    rows = tokens * heads
    total = rows * ctx
    everyone = tokens * ctx
    walk = chip_cycle(chips)
    spot = np.argsort(np.array(walk))
    steps = chips // 2

    def across(step):
        return [
            (walk[r] * CORES + c, walk[(r + (step if c else -step)) % chips] * CORES + c)
            for r in range(chips) for c in range(CORES)
        ]

    other_core = [(d, d ^ 1) for d in range(ctx)]
    same_core = [[p * CORES + c for p in range(chips)] for c in range(CORES)]

    turns = [0]
    for s in range(1, steps):
        turns += [-s, s]
    turns.append(steps)
    owner_table = np.array(
        [
            [walk[(spot[p] + (t if c else -t)) % chips] * CORES + c for t in turns]
            for p in range(chips) for c in range(CORES)
        ],
        np.int32,
    )
    table = jnp.asarray(owner_table.reshape(-1))
    state_shapes = [shape(total, LANES), shape(total, LANES), shape(total, LATENT)]

    def fold_first(keys):
        return pl.pallas_call(
            functools.partial(first_kernel, heads, len(keys)),
            out_shape=[shape(total, width, dtype=bf16)] + state_shapes,
            in_specs=[SMEM] * 2 + [VMEM] * (2 + len(keys)),
            out_specs=[VMEM] * 4,
            compiler_params=PARAMS,
            name="first",
        )(prefix_length, table, here, there, *keys)

    def fold_more(at, q, state, keys):
        return pl.pallas_call(
            functools.partial(middle_kernel, at, len(keys)),
            out_shape=state_shapes,
            in_specs=[SMEM] * 2 + [VMEM] * (4 + len(keys)),
            out_specs=[VMEM] * 3,
            compiler_params=PARAMS,
            name="middle",
        )(prefix_length, table, q, *state, *keys)

    onward = functools.partial(lax.ppermute, axis_name="ctx", perm=across(1))
    backward = functools.partial(lax.ppermute, axis_name="ctx", perm=across(-1))
    cut = LATENT // 2
    own = prefix_latents.T
    right, left = onward(own), backward(own)

    anywhere = pl.BlockSpec(memory_space=pl.ANY)
    pieces = pl.pallas_call(
        pieces_kernel,
        out_shape=shape(chips, tokens, (heads + 1) * width, dtype=bf16),
        in_specs=[anywhere] * 2,
        out_specs=VMEM,
        scratch_shapes=[
            pltpu.VMEM(span_latents.shape, bf16),
            pltpu.SemaphoreType.DMA((2,)),
        ],
        compiler_params=pltpu.CompilerParams(vmem_limit_bytes=56 * 1024 * 1024),
        name="pieces",
    )(queries.reshape(tokens, chips, heads * width).transpose(1, 0, 2), span_latents)
    here = lax.all_to_all(
        pieces, "ctx", split_axis=0, concat_axis=0, axis_index_groups=same_core, tiled=True
    )

    right, left = lax.optimization_barrier((right, left))
    keys, state, at = [own, right, left], None, 0
    for s in range(2, steps):
        right, left = onward(right), backward(left)
        if s == 2:
            here = here.reshape(chips * tokens, (heads + 1) * width)
            there = lax.ppermute(here, "ctx", other_core)
            keys += [right, left]
            continue
        if state is None:
            q, *state = fold_first(keys)
        else:
            state = fold_more(at, q, state, keys)
        at += len(keys)
        keys = [right, left]
    top = onward(right[:cut])
    left, state = lax.optimization_barrier((left, state))
    bottom = backward(left[cut:])
    state = pl.pallas_call(
        functools.partial(span_kernel, at, len(keys)),
        out_shape=state_shapes,
        in_specs=[SMEM] * 3 + [VMEM] * (5 + len(keys)),
        out_specs=[VMEM] * 3,
        compiler_params=PARAMS,
        name="middle",
    )(prefix_length, span_offset, table, q, *state, here, *keys)
    per_core = heads // CORES
    part = per_core * everyone

    def fold_last(side, dtype):
        return pl.pallas_call(
            functools.partial(last_kernel, chips - 1, side),
            out_shape=shape(part, LATENT + LANES, dtype=dtype),
            in_specs=[SMEM] * 2 + [VMEM] * 6,
            out_specs=VMEM,
            compiler_params=PARAMS,
            name="keep" if side == 0 else "give",
        )(prefix_length, table, q, *state, top, bottom)

    got = lax.ppermute(fold_last(1, bf16), "ctx", other_core)
    keep = fold_last(0, f32)
    merged = pl.pallas_call(
        merge_kernel,
        out_shape=shape(ctx, tokens, per_core * V_HEAD, dtype=bf16),
        in_specs=[VMEM] * 3,
        out_specs=VMEM,
        scratch_shapes=[pltpu.VMEM((everyone, per_core * V_HEAD), f32)],
        compiler_params=PARAMS,
        name="merge",
    )(keep, got, value_up)
    returned = lax.all_to_all(
        merged, "ctx", split_axis=0, concat_axis=0, tiled=True,
        axis_index_groups=[list(range(ctx))[::-1]],
    )
    return returned[::-1].transpose(1, 0, 2).reshape(tokens, all_heads * V_HEAD)


def solution(mesh):
    return jax.shard_map(
        functools.partial(on_device, mesh.shape["ctx"]),
        mesh=mesh,
        in_specs=(
            P(("groups", "ctx"), None),
            P(("groups", "ctx"), None),
            P(("groups", "ctx"), None),
            P("ctx", None, None),
            P("groups"),
            P("groups"),
        ),
        out_specs=P(("groups", "ctx"), None),
        check_vma=False,
    )
```

```python
import functools
import math

import jax
import jax.numpy as jnp
import numpy as np
from jax import lax
from jax.experimental import pallas as pl
from jax.experimental.pallas import tpu as pltpu
from jax.sharding import PartitionSpec as P

LATENT = 512
V_HEAD = 128
CORES = 2
LANES = 128

score_scale = 192.0 ** (-0.5) * math.log2(math.e)
neg_large = -1e30
least_max = -1e29
f32 = jnp.float32
bf16 = jnp.bfloat16


def chip_cycle(chips):
    wide = max(1, int(round(chips ** (1 / 3))))
    tall = chips // wide
    if wide * tall != chips or wide < 2 or tall < 2:
        return list(range(chips))
    walk = []
    for z in range(tall):
        across = range(1, wide) if z % 2 == 0 else range(wide - 1, 0, -1)
        walk += [z * wide + x for x in across]
    return walk + [z * wide for z in reversed(range(tall))]


def scores_of(q_ref, part, pieces):
    total, at = None, 0
    for piece in pieces:
        s = jnp.dot(
            q_ref[part, at:at + piece.shape[0]], piece[...], preferred_element_type=f32
        )
        total, at = s if total is None else total + s, at + piece.shape[0]
    return total


def values_of(weights, pieces):
    summed, at = [], 0
    for piece in pieces:
        wide = min(piece.shape[0], LATENT - at)
        summed.append(lax.dot_general(
            weights, piece[:wide, :], (((1,), (1,)), ((), ())), preferred_element_type=f32
        ))
        at += wide
    return summed[0] if len(summed) == 1 else jnp.concatenate(summed, axis=1)


def fold_block(part, q_ref, shards, length, old=None, span=None):
    m_old = least_max if old is None else old[0][part, :][:, :1]
    m_new = m_old
    scores = []
    for base, key_ref in shards:
        slot = base + lax.broadcasted_iota(jnp.int32, (1, key_ref[0].shape[1]), 1)
        s = scores_of(q_ref, part, key_ref) * score_scale
        s = jnp.where(slot < length, s, neg_large)
        m_new = jnp.maximum(m_new, jnp.max(s, axis=1, keepdims=True))
        scores.append(s)
    if span is not None:
        keys, shown = span
        s = lax.dot_general(
            q_ref[part, :], keys, (((1,), (1,)), ((), ())), preferred_element_type=f32
        )
        span_s = jnp.where(shown, s * score_scale, neg_large)
        m_new = jnp.maximum(m_new, jnp.max(span_s, axis=1, keepdims=True))
    l_new, summed = 0.0, 0.0
    if old is not None:
        shrink = jnp.exp2(m_old - m_new)
        l_new = old[1][part, :][:, :1] * shrink
        summed = old[2][part, :] * shrink
    for s, (_, key_ref) in zip(scores, shards):
        probs = jnp.exp2(s - m_new)
        l_new += jnp.sum(probs, axis=1, keepdims=True)
        summed += values_of(probs.astype(bf16), key_ref)
    if span is not None:
        probs = jnp.exp2(span_s - m_new)
        l_new += jnp.sum(probs, axis=1, keepdims=True)
        summed += jnp.dot(
            probs.astype(bf16), keys[:, :LATENT], preferred_element_type=f32
        )
    return m_new, l_new, summed


def fold_shards(q_ref, shards, length, old, new, span=None):
    rows = q_ref.shape[0]
    block = min(256, rows)
    for start in range(0, rows, block):
        part = pl.ds(start, block)
        shown = None if span is None else (span[0], span[1](start, block))
        m_new, l_new, summed = fold_block(part, q_ref, shards, length, old, shown)
        new[0][part, :] = jnp.broadcast_to(m_new, (block, LANES))
        new[1][part, :] = jnp.broadcast_to(l_new, (block, LANES))
        new[2][part, :] = summed


def parted(index, size):
    return index >> (size.bit_length() - 1), index & (size - 1)


def token_of(index, tokens, chips):
    device, t = parted(index, tokens)
    core, chip = parted(device, chips)
    return (chip * CORES + ((lax.axis_index("ctx") % CORES) ^ core)) * tokens + t


def with_base(table_ref, at, key_refs):
    me = lax.axis_index("ctx")
    count = table_ref.shape[0] // lax.axis_size("ctx")
    return [
        (table_ref[me * count + at + j] * key_ref.shape[1], (key_ref,))
        for j, key_ref in enumerate(key_refs)
    ]


def pieces_kernel(queries_hbm, span_hbm, out_ref, span_ref, sems):
    part = queries_hbm.shape[2]
    copies = [
        pltpu.make_async_copy(queries_hbm, out_ref.at[:, :, :part], sems.at[0]),
        pltpu.make_async_copy(span_hbm, span_ref, sems.at[1]),
    ]
    for copy in copies:
        copy.start()
    for copy in copies:
        copy.wait()
    for chip in range(out_ref.shape[0]):
        out_ref[chip, :, part:] = span_ref[...]


def first_kernel(heads, count, length_ref, table_ref, here_ref, there_ref, *rest):
    keys, (q_ref, m_ref, l_ref, acc_ref) = rest[:count], rest[count:]
    half = here_ref.shape[0]
    width = q_ref.shape[1]
    for core, piece_ref in enumerate((here_ref, there_ref)):
        for head in range(heads):
            row = (head * CORES + core) * half
            q_ref[row:row + half, :] = piece_ref[:, head * width:(head + 1) * width]
    shards = with_base(table_ref, 0, keys)
    fold_shards(q_ref, shards, length_ref[0], None, (m_ref, l_ref, acc_ref))


def middle_kernel(at, count, length_ref, table_ref, q_ref, m_in, l_in, acc_in, *rest):
    keys, new = rest[:count], rest[count:]
    fold_shards(q_ref, with_base(table_ref, at, keys), length_ref[0], (m_in, l_in, acc_in), new)


def span_kernel(at, count, length_ref, offset_ref, table_ref, q_ref, m_in, l_in, acc_in,
                here_ref, *rest):
    keys, new = rest[:count], rest[count:]
    chips = lax.axis_size("ctx") // CORES
    half = here_ref.shape[0]
    tokens = half // chips
    width = q_ref.shape[1]
    key_index = lax.broadcasted_iota(jnp.int32, (1, half), 1)
    key_token = token_of(key_index, tokens, chips)

    def shown(start, block):
        row_index = start + lax.broadcasted_iota(jnp.int32, (block, 1), 0)
        row_token = token_of(row_index & (half * CORES - 1), tokens, chips)
        return (key_token >= offset_ref[0]) & (key_token <= row_token)

    fold_shards(
        q_ref, with_base(table_ref, at, keys), length_ref[0], (m_in, l_in, acc_in), new,
        (here_ref[:, here_ref.shape[1] - width:], shown),
    )


def last_kernel(at, side, length_ref, table_ref, q_ref, m_ref, l_ref, acc_ref,
                top_ref, bottom_ref, out_ref):
    core = lax.axis_index("ctx") % CORES
    shards = [(with_base(table_ref, at, (top_ref,))[0][0], (top_ref, bottom_ref))]
    rows = out_ref.shape[0]
    part = pl.ds(pl.multiple_of((core ^ side) * rows, rows), rows)
    m_new, l_new, summed = fold_block(
        part, q_ref, shards, length_ref[0], (m_ref, l_ref, acc_ref)
    )
    out_ref[:, :LATENT] = (summed * (1.0 / l_new)).astype(out_ref.dtype)
    weight = jnp.broadcast_to(m_new + jnp.log2(l_new), (rows, LANES))
    if side:
        lane = lax.broadcasted_iota(jnp.int32, (rows, LANES), 1)
        high = weight.astype(bf16).astype(f32)
        mid = (weight - high).astype(bf16).astype(f32)
        weight = jnp.where(lane == 0, high, jnp.where(lane == 1, mid, weight - high - mid))
    out_ref[:, LATENT:] = weight.astype(out_ref.dtype)


def merge_kernel(keep_ref, got_ref, up_ref, out_ref, flat_ref):
    core = lax.axis_index("ctx") % CORES
    heads = up_ref.shape[0]
    everyone = flat_ref.shape[0]
    half = everyone // CORES
    pair = min(2, heads)
    for j in range(0, heads, pair):
        contexts = []
        for head in range(j, j + pair):
            row = head * everyone
            got = jnp.concatenate(
                [got_ref[row + half:row + everyone, :], got_ref[row:row + half, :]], axis=0
            ).astype(f32)
            keep = keep_ref[row:row + everyone, :]
            gap = keep[:, LATENT:LATENT + 1] - got[:, LATENT:LATENT + 1]
            gap = gap - got[:, LATENT + 1:LATENT + 2] - got[:, LATENT + 2:LATENT + 3]
            share = 1.0 / (1.0 + jnp.exp2(-gap))
            rest = 1.0 / (1.0 + jnp.exp2(gap))
            contexts.append(
                (keep[:, :LATENT] * share + got[:, :LATENT] * rest).astype(bf16)
            )
        lifted = jnp.dot(
            jnp.concatenate(contexts, axis=0),
            jnp.concatenate([up_ref[j + i] for i in range(pair)], axis=1),
            preferred_element_type=f32,
        )
        for i in range(pair):
            flat_ref[:, (j + i) * V_HEAD:(j + i + 1) * V_HEAD] = lifted[
                i * everyone:(i + 1) * everyone, i * V_HEAD:(i + 1) * V_HEAD
            ]
    devices, tokens, _ = out_ref.shape
    chips = devices // CORES
    for i in range(devices):
        out_ref[(i % chips) * CORES + 1 - (core ^ (i // chips))] = (
            flat_ref[i * tokens:(i + 1) * tokens, :].astype(bf16)
        )


def place_kernel(parts_ref, out_ref):
    devices, _, width = parts_ref.shape
    for i in range(devices):
        core, chip = 1 - i % CORES, i // CORES
        at = (chip * CORES + core) * width
        out_ref[:, at:at + width] = parts_ref[i]


VMEM = pl.BlockSpec(memory_space=pltpu.VMEM)
SMEM = pl.BlockSpec(memory_space=pltpu.SMEM)
PARAMS = pltpu.CompilerParams(vmem_limit_bytes=32 * 1024 * 1024)


def shape(*dims, dtype=f32):
    return jax.ShapeDtypeStruct(dims, dtype)


def on_device(ctx, queries, prefix_latents, span_latents, value_up, prefix_length, span_offset):
    slots, width = prefix_latents.shape
    tokens = queries.shape[0]
    all_heads = queries.shape[1] // width
    chips = ctx // CORES
    heads = all_heads // chips
    rows = tokens * heads
    total = rows * ctx
    everyone = tokens * ctx
    walk = chip_cycle(chips)
    spot = np.argsort(np.array(walk))
    steps = chips // 2

    def across(step):
        return [
            (walk[r] * CORES + c, walk[(r + (-step if c else step)) % chips] * CORES + c)
            for r in range(chips) for c in range(CORES)
        ]

    other_core = [(d, d ^ 1) for d in range(ctx)]
    same_core = [[p * CORES + c for p in range(chips)] for c in range(CORES)]

    turns = [0]
    for s in range(1, steps):
        turns += [-s, s]
    turns.append(steps)
    owner_table = np.array(
        [
            [walk[(spot[p] + (-t if c else t)) % chips] * CORES + c for t in turns]
            for p in range(chips) for c in range(CORES)
        ],
        np.int32,
    )
    table = jnp.asarray(owner_table.reshape(-1))
    state_shapes = [shape(total, LANES), shape(total, LANES), shape(total, LATENT)]

    def fold_first(keys):
        return pl.pallas_call(
            functools.partial(first_kernel, heads, len(keys)),
            out_shape=[shape(total, width, dtype=bf16)] + state_shapes,
            in_specs=[SMEM] * 2 + [VMEM] * (2 + len(keys)),
            out_specs=[VMEM] * 4,
            compiler_params=PARAMS,
            name="first",
        )(prefix_length, table, here, there, *keys)

    def fold_more(at, q, state, keys):
        return pl.pallas_call(
            functools.partial(middle_kernel, at, len(keys)),
            out_shape=state_shapes,
            in_specs=[SMEM] * 2 + [VMEM] * (4 + len(keys)),
            out_specs=[VMEM] * 3,
            compiler_params=PARAMS,
            name="middle",
        )(prefix_length, table, q, *state, *keys)

    onward = functools.partial(lax.ppermute, axis_name="ctx", perm=across(1))
    backward = functools.partial(lax.ppermute, axis_name="ctx", perm=across(-1))
    cut = LATENT // 2
    own = prefix_latents.T
    right, left = onward(own), backward(own)

    anywhere = pl.BlockSpec(memory_space=pl.ANY)
    pieces = pl.pallas_call(
        pieces_kernel,
        out_shape=shape(chips, tokens, (heads + 1) * width, dtype=bf16),
        in_specs=[anywhere] * 2,
        out_specs=VMEM,
        scratch_shapes=[
            pltpu.VMEM(span_latents.shape, bf16),
            pltpu.SemaphoreType.DMA((2,)),
        ],
        compiler_params=pltpu.CompilerParams(vmem_limit_bytes=56 * 1024 * 1024),
        name="pieces",
    )(queries.reshape(tokens, chips, heads * width).transpose(1, 0, 2), span_latents)
    here = lax.all_to_all(
        pieces, "ctx", split_axis=0, concat_axis=0, axis_index_groups=same_core, tiled=True
    )

    right, left = lax.optimization_barrier((right, left))
    keys, state, at = [own, right, left], None, 0
    for s in range(2, steps):
        right, left = onward(right), backward(left)
        if s == 2:
            here = here.reshape(chips * tokens, (heads + 1) * width)
            there = lax.ppermute(here, "ctx", other_core)
            keys += [right, left]
            continue
        if state is None:
            q, *state = fold_first(keys)
        else:
            state = fold_more(at, q, state, keys)
        at += len(keys)
        keys = [right, left]
    top = onward(right[:cut])
    left, state = lax.optimization_barrier((left, state))
    bottom = backward(left[cut:])
    state = pl.pallas_call(
        functools.partial(span_kernel, at, len(keys)),
        out_shape=state_shapes,
        in_specs=[SMEM] * 3 + [VMEM] * (5 + len(keys)),
        out_specs=[VMEM] * 3,
        compiler_params=PARAMS,
        name="middle",
    )(prefix_length, span_offset, table, q, *state, here, *keys)
    per_core = heads // CORES
    part = per_core * everyone

    def fold_last(side, dtype):
        return pl.pallas_call(
            functools.partial(last_kernel, chips - 1, side),
            out_shape=shape(part, LATENT + LANES, dtype=dtype),
            in_specs=[SMEM] * 2 + [VMEM] * 6,
            out_specs=VMEM,
            compiler_params=PARAMS,
            name="keep" if side == 0 else "give",
        )(prefix_length, table, q, *state, top, bottom)

    got = lax.ppermute(fold_last(1, bf16), "ctx", other_core)
    keep = fold_last(0, f32)
    merged = pl.pallas_call(
        merge_kernel,
        out_shape=shape(ctx, tokens, per_core * V_HEAD, dtype=bf16),
        in_specs=[VMEM] * 3,
        out_specs=VMEM,
        scratch_shapes=[pltpu.VMEM((everyone, per_core * V_HEAD), f32)],
        compiler_params=PARAMS,
        name="merge",
    )(keep, got, value_up)
    returned = lax.all_to_all(
        merged, "ctx", split_axis=0, concat_axis=0, tiled=True,
        axis_index_groups=[
            [p * CORES + c for p in range(chips) for c in reversed(range(CORES))]
        ],
    )
    return pl.pallas_call(
        place_kernel,
        out_shape=shape(tokens, all_heads * V_HEAD, dtype=bf16),
        in_specs=[VMEM],
        out_specs=VMEM,
        compiler_params=PARAMS,
        name="place",
    )(returned)


def solution(mesh):
    return jax.shard_map(
        functools.partial(on_device, mesh.shape["ctx"]),
        mesh=mesh,
        in_specs=(
            P(("groups", "ctx"), None),
            P(("groups", "ctx"), None),
            P(("groups", "ctx"), None),
            P("ctx", None, None),
            P("groups"),
            P("groups"),
        ),
        out_specs=P(("groups", "ctx"), None),
        check_vma=False,
    )
```
